32 devices in a mesh: win: 2 (over x), seq: 8 (over z, y), ch: 2 (over core).
Axes of the slice: x: 2, y: 2, z: 4, core: 2. Of those that a mesh axis runs over, the one named last changes fastest.
Arguments:
- tokens: int32 [8192], P(('win', 'seq')), parts along dimension 0, may hold values from 0 to 3
- hidden: bfloat16 [8192, 1024], P(('win', 'seq')), parts along dimension 0, may hold values from -6 to 6
- embedding: bfloat16 [4, 1024], replicated, may hold values from -3 to 3
- w_gate: bfloat16 [1024, 2048], P(None, 'ch'), may hold values from -0.1875 to 0.1875
- w_inner: bfloat16 [1024, 2048], P(None, 'ch'), may hold values from -0.1875 to 0.1875
- w_state: bfloat16 [1024, 256], replicated, may hold values from -0.1875 to 0.1875
- w_step: bfloat16 [1024, 32], P(None, 'ch'), may hold values from -0.75 to 0.75
- conv_inner: float32 [4, 2048], P(None, 'ch'), may hold values from -3 to 3
- conv_state: float32 [4, 256], replicated, may hold values from -3 to 3
- step_bias: float32 [32], P('ch'), may hold values from -1 to 1
- decay_rate: float32 [32], P('ch'), may hold values from 1.2207031e-05 to 0.05, as said below
- norm_gain: float32 [2048], P('ch'), may hold values from 0.1 to 1.9
- w_output: bfloat16 [2048, 1024], P('ch'), may hold values from -0.125 to 0.125
Outputs:
- mixed: bfloat16 [8192, 1024], P(('win', 'seq'), 'ch'), parts along dimension 0
The draws below stay inside these ranges and needn't reach their ends.
There are 2 independent parts, one for each index of `win`. The reference program is written for one: setup_inputs(seed, part) draws one part's arguments, and reference() takes and returns one part's arrays. A program takes and returns all parts, laid end to end along the dimension named above; an argument that names none is the same for every part. Nothing has to cross between parts.
Inputs may be any that keep to these rules, and one draw needn't show every extreme that they name: `decay_rate`: each head's decay rate per unit step.
All inputs are finite; a program needn't handle non-finite values.
Results may differ from the reference program's by a relative error of at most 0.013.
Values may be sent and summed in bfloat16 or wider, within the bound.
No kernel may reach another device: no remote copies, remote signals or barrier semaphores. Data moves between devices by JAX's collectives and lax.ppermute only.
A program may use at most 128 MiB of HBM per device.

```python
import jax
import jax.numpy as jnp
from jax import lax

D = 1024
HEADS = 32
HDIM = 64
NS = 128
CONV = 4
ROWS = 512
DI = 2048
SEQ_LEN = 4096


def draw_decay_rate(key, part):
    lowest = 0.05 / SEQ_LEN
    highest = 0.05
    fraction = jax.random.uniform(key, (HEADS,), jnp.float32)
    log_low = jnp.log(jnp.float32(lowest))
    log_high = jnp.log(jnp.float32(highest))
    return jnp.exp(log_low + (log_high - log_low) * fraction).astype(jnp.float32)


def touch_ends(array, rng, low, high):
    index_at = [jax.random.randint(jax.random.fold_in(rng, axis), (), 0, length) for axis, length in enumerate(array.shape)]
    main_axis = array.shape.index(max(array.shape))
    next_to = index_at[:main_axis] + [(index_at[main_axis] + 1) % array.shape[main_axis]] + index_at[main_axis + 1:]
    return array.at[tuple(index_at)].set(low).at[tuple(next_to)].set(high)


def levels(rng, shape, cuts, low, top_value):
    factor_of, own = 1.0, jax.random.fold_in(rng, 6)
    for dim, shards_of in cuts:
        steps = jnp.exp(jax.random.uniform(jax.random.fold_in(own, dim), (shards_of,), jnp.float32, low / len(cuts), top_value / len(cuts)))
        factor_of = factor_of * jnp.repeat(steps, shape[dim] // shards_of).reshape([-1 if axis == dim else 1 for axis in range(len(shape))])
    return factor_of


def centred(rng, extent, scale, reach, shards=(), held_as=jnp.bfloat16):
    result = jax.random.normal(rng, extent, jnp.float32) * scale
    if len(shards) > 0:
        result = levels(rng, extent, shards, -0.22, 0.18) * result
    return jnp.clip(result, min=-reach, max=reach).astype(held_as)


def setup_inputs(seed: int = 0, part: int = 0) -> dict:
    streams_of = jax.random.split(jax.random.key(seed), 14)
    own_keys = jax.random.split(jax.random.fold_in(streams_of[13], part), 14)
    tokens = touch_ends(jax.random.randint(own_keys[0], (SEQ_LEN,), 0, 4), jax.random.fold_in(own_keys[0], 1), 0, 3).astype(jnp.int32)
    hidden = centred(own_keys[1], (SEQ_LEN, D), 1.0, 6.0, ((0, 8),))
    embedding = centred(streams_of[2], (4, D), 0.5, 3.0)
    w_gate = centred(streams_of[3], (D, DI), D ** -0.5, 0.1875, ((1, 2),))
    w_inner = centred(streams_of[4], (D, DI), D ** -0.5, 0.1875, ((1, 2),))
    w_state = centred(streams_of[5], (D, 2 * NS), D ** -0.5, 0.1875)
    w_step = centred(streams_of[6], (D, HEADS), (D // 16) ** -0.5, 0.75, ((1, 2),))
    conv_inner = centred(streams_of[7], (CONV, DI), CONV ** -0.5, 3.0, ((1, 2),), jnp.float32)
    conv_state = centred(streams_of[8], (CONV, 2 * NS), CONV ** -0.5, 3.0, (), jnp.float32)
    step_bias = jnp.clip(jax.random.uniform(streams_of[9], (HEADS,), jnp.float32, -1.0, 1.0) * levels(streams_of[9], (HEADS,), ((0, 2),), -0.4, 0.0), -1.0, 1.0)
    decay_rate = draw_decay_rate(jax.random.fold_in(streams_of[13], 71), part)
    norm_gain = jnp.clip(1.0 + 0.18 * jax.random.normal(streams_of[11], (DI,), jnp.float32), 0.1, 1.9)
    w_output = centred(streams_of[12], (DI, D), DI ** -0.5, 0.125, ((0, 2),))
    return dict(tokens=tokens, hidden=hidden, embedding=embedding, w_gate=w_gate, w_inner=w_inner, w_state=w_state, w_step=w_step, conv_inner=conv_inner, conv_state=conv_state, step_bias=step_bias, decay_rate=decay_rate, norm_gain=norm_gain, w_output=w_output)


def block_step(state, pieces):
    inner_blk, bmat_blk, cmat_blk, bmat_half, cmat_half, step_blk, logd_blk = pieces
    blen = inner_blk.shape[0]
    head_count = state.shape[0]
    head_size = state.shape[1]
    inner3 = inner_blk.reshape(blen, head_count, head_size)
    cumlog = jnp.cumsum(logd_blk, axis=0).T
    position = jnp.arange(blen)
    lower = (position[:, None] >= position[None, :])[None]
    spread = jnp.where(lower, cumlog[:, :, None] - cumlog[:, None, :], 0.0)
    decay = jnp.where(lower, jnp.exp(spread), 0.0)
    scores = jnp.dot(cmat_half, bmat_half.T, preferred_element_type=jnp.float32)
    weights = decay * scores[None] * step_blk.T[:, None, :]
    inside = jnp.einsum('hij,jhp->ihp', weights, inner3, precision=lax.Precision.HIGHEST)
    carried = jnp.einsum('in,hpn->ihp', cmat_blk, state, precision=lax.Precision.HIGHEST) * jnp.exp(cumlog).T[:, :, None]
    final_log = cumlog[:, -1]
    to_end = jnp.exp(final_log[:, None] - cumlog) * step_blk.T
    added = jnp.einsum('hj,jhp,jn->hpn', to_end, inner3, bmat_blk, precision=lax.Precision.HIGHEST)
    new_state = state * jnp.exp(final_log)[:, None, None] + added
    return (new_state, inside + carried)

def run_blocks(state, inner_f, bmat, cmat, bmat_half, cmat_half, step, logdecay, blocklen):
    count = inner_f.shape[0] // blocklen
    pieces = (inner_f.reshape(count, blocklen, -1), bmat.reshape(count, blocklen, -1), cmat.reshape(count, blocklen, -1), bmat_half.reshape(count, blocklen, -1), cmat_half.reshape(count, blocklen, -1), step.reshape(count, blocklen, -1), logdecay.reshape(count, blocklen, -1))
    final_state, outputs = lax.scan(block_step, state, pieces)
    return (final_state, outputs.reshape(inner_f.shape[0], state.shape[0], state.shape[1]))

def causal_conv(before, rows, weights):
    width = weights.shape[0]
    count = rows.shape[0]
    extended = jnp.concatenate([before, rows], axis=0).astype(jnp.float32)
    total = jnp.zeros((count, rows.shape[1]), jnp.float32)
    for offset in range(width):
        total = total + weights[offset][None, :] * extended[offset:offset + count]
    return jax.nn.silu(total).astype(jnp.bfloat16)

def mixer(strand_rows, w_gate, w_inner, w_state, w_step, conv_inner, conv_state, step_bias, decay_rate, norm_gain, w_output):
    as_f32 = strand_rows.astype(jnp.float32)
    normed = (as_f32 * lax.rsqrt(lax.optimization_barrier(jnp.mean(as_f32 * as_f32, axis=-1, keepdims=True)) + 1e-05)).astype(jnp.bfloat16)
    gate_rows = jnp.dot(normed, w_gate, preferred_element_type=jnp.float32).astype(jnp.bfloat16)
    inner_rows = jnp.dot(normed, w_inner, preferred_element_type=jnp.float32).astype(jnp.bfloat16)
    state_rows = jnp.dot(normed, w_state, preferred_element_type=jnp.float32).astype(jnp.bfloat16)
    step_raw = jnp.dot(normed, w_step, preferred_element_type=jnp.float32)
    width = conv_inner.shape[0]
    inner_conv = causal_conv(jnp.zeros((width - 1, inner_rows.shape[1]), jnp.bfloat16), inner_rows, conv_inner)
    state_conv = causal_conv(jnp.zeros((width - 1, state_rows.shape[1]), jnp.bfloat16), state_rows, conv_state)
    state_f = state_conv.astype(jnp.float32)
    bmat = state_f[:, :NS]
    cmat = state_f[:, NS:]
    bmat_half = state_conv[:, :NS]
    cmat_half = state_conv[:, NS:]
    step = jax.nn.softplus(step_raw + step_bias[None, :])
    logdecay = -step * decay_rate[None, :]
    inner_f = inner_conv.astype(jnp.float32)
    zero_state = jnp.zeros((HEADS, HDIM, NS), jnp.float32)
    blocklen = min(256, ROWS)
    final_state, out3 = run_blocks(zero_state, inner_f, bmat, cmat, bmat_half, cmat_half, step, logdecay, blocklen)
    gated = out3.reshape(inner_f.shape[0], HEADS * HDIM) * jax.nn.silu(gate_rows.astype(jnp.float32))
    normed_out = (gated * lax.rsqrt(lax.optimization_barrier(jnp.mean(gated * gated, axis=-1, keepdims=True)) + 1e-05) * norm_gain[None, :]).astype(jnp.bfloat16)
    return jnp.dot(normed_out, w_output, preferred_element_type=jnp.float32)

def reference(tokens, hidden, embedding, w_gate, w_inner, w_state, w_step, conv_inner, conv_state, step_bias, decay_rate, norm_gain, w_output):
    onehot = (tokens[:, None] == jnp.arange(4, dtype=jnp.int32)[None, :]).astype(jnp.bfloat16)
    base_rows = jnp.dot(onehot, embedding, preferred_element_type=jnp.float32)
    merged = (hidden.astype(jnp.float32) + base_rows).astype(jnp.bfloat16)
    forward = mixer(merged, w_gate, w_inner, w_state, w_step, conv_inner, conv_state, step_bias, decay_rate, norm_gain, w_output)
    mirrored = mixer(merged[::-1, ::-1], w_gate, w_inner, w_state, w_step, conv_inner, conv_state, step_bias, decay_rate, norm_gain, w_output)
    return (forward + mirrored[::-1, ::-1]).astype(jnp.bfloat16)
```

```python
import functools

import jax
import jax.numpy as jnp
from jax import lax
from jax.experimental import pallas as pl
from jax.experimental.pallas import tpu as pltpu
from jax.sharding import PartitionSpec as P

F32 = jnp.float32
BF16 = jnp.bfloat16
EPS = 1e-05
HALO = 16
EXTRA = 16
CHUNK = 128
TILE = 256
VMEM_LIMIT = 40 * 1024 * 1024


def params(limit=VMEM_LIMIT, dims=("arbitrary",)):
    return pltpu.CompilerParams(vmem_limit_bytes=limit, dimension_semantics=dims)


def dot(a, b):
    return jnp.dot(a, b, preferred_element_type=F32)


def dot_nt(a, b):
    return lax.dot_general(a, b, (((1,), (1,)), ((), ())), preferred_element_type=F32)


def dot_tn(a, b):
    return lax.dot_general(a, b, (((0,), (0,)), ((), ())), preferred_element_type=F32)


def flip_matrix(size):
    rows = lax.broadcasted_iota(jnp.int32, (size, size), 0)
    columns = lax.broadcasted_iota(jnp.int32, (size, size), 1)
    return jnp.where(rows + columns == size - 1, 1.0, 0.0).astype(BF16)


def flip_lanes(value):
    width = value.shape[1]
    anti = flip_matrix(TILE)
    count = width // TILE
    blocks = [
        dot(value[:, (count - 1 - k) * TILE : (count - k) * TILE], anti).astype(BF16)
        for k in range(count)
    ]
    return jnp.concatenate(blocks, axis=1)


def normalise(rows):
    wide = rows.astype(F32)
    return (wide * lax.rsqrt(jnp.mean(wide * wide, axis=-1, keepdims=True) + EPS)).astype(BF16)


def silu(v):
    return v / (1.0 + jnp.exp(-v))


def two_parts(value):
    high = value.astype(BF16)
    low = (value - high.astype(F32)).astype(BF16)
    return jnp.concatenate([high, low], axis=1)


def spread(value, width, head_size, first_head):
    heads = value.shape[1]
    source = lax.broadcasted_iota(jnp.int32, (2 * heads, width), 0)
    source = jnp.where(source >= heads, source - heads, source)
    target = lax.broadcasted_iota(jnp.int32, (2 * heads, width), 1) // head_size + first_head
    onehot = jnp.where(source == target, 1.0, 0.0).astype(BF16)
    return dot(two_parts(value), onehot)


def gate_kernel(merged_ref, wg_ref, nf_ref, nb_ref, gf_ref, gb_ref):
    @pl.when(pl.program_id(0) == 0)
    def _():
        normed = normalise(merged_ref[...])
        nf_ref[...] = normed
        nb_ref[...] = flip_lanes(normed)

    weights = wg_ref[...]
    for rows_ref, out_ref in ((nf_ref, gf_ref), (nb_ref, gb_ref)):
        gate = dot(rows_ref[...], weights).astype(BF16).astype(F32)
        out_ref[...] = silu(gate).astype(BF16)


def gate_call(merged, w_gate):
    rows, width = merged.shape
    inner = w_gate.shape[1]
    whole = pl.BlockSpec((rows, width), lambda g: (0, 0))
    tile = pl.BlockSpec((rows, TILE), lambda g: (0, g))
    return pl.pallas_call(
        gate_kernel,
        grid=(inner // TILE,),
        in_specs=[whole, pl.BlockSpec((width, TILE), lambda g: (0, g))],
        out_specs=[whole, whole, tile, tile],
        out_shape=[jax.ShapeDtypeStruct((rows, width), BF16)] * 2
        + [jax.ShapeDtypeStruct((rows, inner), BF16)] * 2,
        compiler_params=params(),
        name="gate",
    )(merged, w_gate)


def conv_silu(rows_ref, weights, rows, backward):
    taps = weights.shape[0]
    total = None
    for k in range(taps):
        offset = (taps - 1 - k) if backward else HALO - (taps - 1) + k
        term = weights[k : k + 1, :] * rows_ref[offset : offset + rows, :]
        total = term if total is None else total + term
    return silu(total).astype(BF16)


def local_kernel(
    backward,
    head_size,
    normed_ref,
    halo_ref,
    wi_ref,
    ws_ref,
    wt_ref,
    ci_ref,
    cs_ref,
    bias_ref,
    rate_ref,
    xs_ref,
    bc_ref,
    cum_ref,
    cumt_ref,
    state_ref,
    ext_ref,
    rows_ref,
    step_ref,
    bt_ref,
):
    rows = normed_ref.shape[0]
    states = bc_ref.shape[1] // 2
    g = pl.program_id(0)

    @pl.when(g == 0)
    def _():
        halo = normalise(halo_ref[...])
        main = normed_ref[...]
        if backward:
            ext_ref[:rows, :] = main
            ext_ref[rows:, :] = flip_lanes(halo)
        else:
            ext_ref[:HALO, :] = halo
            ext_ref[HALO:, :] = main
        rows_ref[...] = dot(ext_ref[...], ws_ref[...]).astype(BF16).astype(F32)
        state_conv = conv_silu(rows_ref, cs_ref[...], rows, backward)
        bc_ref[...] = state_conv
        bt_ref[...] = state_conv[:, :states].astype(F32).T.astype(BF16)
        raw = dot(main, wt_ref[...]) + bias_ref[...]
        step = jnp.maximum(raw, 0.0) + jnp.log1p(jnp.exp(-jnp.abs(raw)))
        step_ref[...] = step
        logdecay = -step * rate_ref[...]
        high = logdecay.astype(BF16)
        rest = logdecay - high.astype(F32)
        mid = rest.astype(BF16)
        low = (rest - mid.astype(F32)).astype(BF16)
        parts = jnp.concatenate([high, mid, low], axis=1)
        heads = step.shape[1]
        to = lax.broadcasted_iota(jnp.int32, (rows, rows), 0)
        frm = lax.broadcasted_iota(jnp.int32, (rows, rows), 1)
        reach = (to <= frm) if backward else (to >= frm)
        sums = dot(jnp.where(reach, 1.0, 0.0).astype(BF16), parts)
        cum = sums[:, :heads] + sums[:, heads : 2 * heads] + sums[:, 2 * heads :]
        cum_ref[...] = cum
        cumt_ref[...] = cum.T

    projected = dot(ext_ref[...], wi_ref[...]).astype(BF16).astype(F32)
    rows_ref[...] = projected
    x = conv_silu(rows_ref, ci_ref[...], rows, backward).astype(F32)
    first = g * (TILE // head_size)
    xs = x * spread(step_ref[...], TILE, head_size, first)
    xs_ref[...] = xs.astype(BF16)
    cum = cum_ref[...]
    total = cum[:1, :] if backward else cum[rows - 1 :, :]
    left = spread(jnp.exp(total - cum), TILE, head_size, first)
    state_ref[:states, :] = dot(bt_ref[...], (xs * left).astype(BF16)).astype(BF16)
    whole = spread(jnp.broadcast_to(jnp.exp(total), (EXTRA, total.shape[1])), TILE, head_size, first)
    high = whole.astype(BF16).astype(F32)
    place = lax.broadcasted_iota(jnp.int32, whole.shape, 0)
    state_ref[states:, :] = jnp.where(place == 0, high, whole - high).astype(BF16)


def local_call(backward, normed, halo, w_inner, w_state, w_step, ci, cs, bias, rate):
    rows, width = normed.shape
    inner = w_inner.shape[1]
    heads = w_step.shape[1]
    both = w_state.shape[1]
    states = both // 2
    taps = ci.shape[0]

    def whole(*shape):
        return pl.BlockSpec(shape, lambda g: (0, 0))

    def tile(count):
        return pl.BlockSpec((count, TILE), lambda g: (0, g))

    return pl.pallas_call(
        functools.partial(local_kernel, backward, inner // heads),
        grid=(inner // TILE,),
        in_specs=[
            whole(rows, width),
            whole(HALO, width),
            tile(width),
            whole(width, both),
            whole(width, heads),
            tile(taps),
            whole(taps, both),
            whole(1, heads),
            whole(1, heads),
        ],
        out_specs=[
            tile(rows),
            whole(rows, both),
            whole(rows, heads),
            whole(heads, rows),
            tile(states + EXTRA),
        ],
        out_shape=[
            jax.ShapeDtypeStruct((rows, inner), BF16),
            jax.ShapeDtypeStruct((rows, both), BF16),
            jax.ShapeDtypeStruct((rows, heads), F32),
            jax.ShapeDtypeStruct((heads, rows), F32),
            jax.ShapeDtypeStruct((states + EXTRA, inner), BF16),
        ],
        scratch_shapes=[
            pltpu.VMEM((rows + HALO, width), BF16),
            pltpu.VMEM((rows + HALO, TILE), F32),
            pltpu.VMEM((rows, heads), F32),
            pltpu.VMEM((states, rows), BF16),
        ],
        compiler_params=params(),
        name="local_b" if backward else "local_f",
    )(normed, halo, w_inner, w_state, w_step, ci, cs, bias, rate)


def inside_kernel(backward, head_size, xs_ref, bc_ref, cum_ref, cumt_ref, y_ref, state_ref, prev_ref):
    length, inner = xs_ref.shape
    states = bc_ref.shape[1] // 2
    heads = cum_ref.shape[1]

    @pl.when(pl.program_id(0) == 0)
    def _():
        state_ref[...] = jnp.zeros_like(state_ref)
        prev_ref[...] = jnp.zeros_like(prev_ref)

    bmat = bc_ref[:, :states]
    cmat = bc_ref[:, states:]
    to = lax.broadcasted_iota(jnp.int32, (length, length), 0)
    frm = lax.broadcasted_iota(jnp.int32, (length, length), 1)
    reach = (to <= frm) if backward else (to >= frm)
    scores = jnp.where(reach, dot_nt(cmat, bmat), 0.0)
    cum = cum_ref[...]
    cumt = cumt_ref[...]
    last = 0 if backward else length - 1
    end = cum[last : last + 1, :]
    since = spread(jnp.exp(cum - prev_ref[...]), inner, head_size, 0)
    left = spread(jnp.exp(end - cum), inner, head_size, 0)
    state = state_ref[...]
    carried = dot(cmat, state.astype(BF16)) * since
    xs = xs_ref[...]
    scaled = (xs.astype(F32) * left).astype(BF16)
    state_ref[...] = state * since[last : last + 1, :] + dot_tn(bmat, scaled)
    prev_ref[...] = end
    pair = 2 * head_size
    lane = lax.broadcasted_iota(jnp.int32, (length, pair), 1)
    for p in range(heads // 2):
        weights = []
        for h in (2 * p, 2 * p + 1):
            apart = jnp.minimum(cum[:, h : h + 1] - cumt[h : h + 1, :], 0.0)
            weights.append((jnp.exp(apart) * scores).astype(BF16))
        mine = xs[:, p * pair : (p + 1) * pair]
        none = jnp.zeros_like(mine)
        stacked = jnp.concatenate(
            [jnp.where(lane < head_size, mine, none), jnp.where(lane < head_size, none, mine)], axis=0
        )
        inside = dot(jnp.concatenate(weights, axis=1), stacked)
        y_ref[:, p * pair : (p + 1) * pair] = (
            inside + carried[:, p * pair : (p + 1) * pair]
        ).astype(BF16)


def inside_call(backward, xs, bc, cum, cumt):
    rows, inner = xs.shape
    heads = cum.shape[1]
    both = bc.shape[1]
    count = rows // CHUNK
    at = (lambda c: count - 1 - c) if backward else (lambda c: c)

    def block(width):
        return pl.BlockSpec((CHUNK, width), lambda c: (at(c), 0))

    return pl.pallas_call(
        functools.partial(inside_kernel, backward, inner // heads),
        grid=(count,),
        in_specs=[
            block(inner),
            block(both),
            block(heads),
            pl.BlockSpec((heads, CHUNK), lambda c: (0, at(c))),
        ],
        out_specs=block(inner),
        out_shape=jax.ShapeDtypeStruct((rows, inner), BF16),
        scratch_shapes=[pltpu.VMEM((both // 2, inner), F32), pltpu.VMEM((1, heads), F32)],
        compiler_params=params(),
        name="inside_b" if backward else "inside_f",
    )(xs, bc, cum, cumt)


def parts_of(payload):
    states = payload.shape[0] - EXTRA
    wide = payload.astype(F32)
    return wide[:states], wide[states : states + 1] + wide[states + 1 : states + 2]


def write_payload(out_ref, state, decay):
    states = state.shape[0]
    out_ref[:states, :] = state.astype(BF16)
    decay = jnp.broadcast_to(decay, (EXTRA, decay.shape[1]))
    high = decay.astype(BF16).astype(F32)
    place = lax.broadcasted_iota(jnp.int32, decay.shape, 0)
    out_ref[states:, :] = jnp.where(place == 0, high, decay - high).astype(BF16)


def pair_kernel(first_ref, mine_ref, other_ref, out_ref):
    mine, mine_a = parts_of(mine_ref[...])
    other, other_a = parts_of(other_ref[...])
    is_first = first_ref[0] == 1
    early = jnp.where(is_first, mine, other)
    late = jnp.where(is_first, other, mine)
    late_a = jnp.where(is_first, other_a, mine_a)
    write_payload(out_ref, late_a * early + late, mine_a * other_a)


def chain_kernel(pair_ref, before_ref, out_ref):
    pair, pair_a = parts_of(pair_ref[...])
    before, before_a = parts_of(before_ref[...])
    write_payload(out_ref, pair_a * before + pair, pair_a * before_a)


def longer_kernel(before_ref, farther_ref, out_ref):
    before, before_a = parts_of(before_ref[...])
    farther, farther_a = parts_of(farther_ref[...])
    write_payload(out_ref, before + before_a * farther, before_a * farther_a)


def entry_kernel(first_ref, mine_ref, other_ref, before_ref, farther_ref, keep_ref, send_ref):
    mine, mine_a = parts_of(mine_ref[...])
    other, other_a = parts_of(other_ref[...])
    before, before_a = parts_of(before_ref[...])
    farther, _ = parts_of(farther_ref[...])
    is_first = first_ref[0] == 1
    entry_first = before + before_a * farther
    early = jnp.where(is_first, mine, other)
    early_a = jnp.where(is_first, mine_a, other_a)
    entry_second = early_a * entry_first + early
    keep_ref[...] = jnp.where(is_first, entry_first, entry_second).astype(BF16)
    send_ref[...] = jnp.where(is_first, entry_second, entry_first).astype(BF16)


def small_call(kernel, name, flags, arrays, shapes):
    vmem = pl.BlockSpec(memory_space=pltpu.VMEM)
    smem = pl.BlockSpec(memory_space=pltpu.SMEM)
    return pl.pallas_call(
        kernel,
        in_specs=[smem] * len(flags) + [vmem] * len(arrays),
        out_specs=[vmem] * len(shapes),
        out_shape=[jax.ShapeDtypeStruct(s, BF16) for s in shapes],
        compiler_params=pltpu.CompilerParams(vmem_limit_bytes=16 * 1024 * 1024),
        name=name,
    )(*flags, *arrays)


def entering(backward, state):
    tag = "_b" if backward else "_f"
    count = lax.axis_size("seq")
    place = lax.axis_index("seq")
    parity = place % 2
    first = (parity if backward else 1 - parity).astype(jnp.int32).reshape(1)
    height, inner = state.shape
    half = inner // 2
    swap = [(i, i ^ 1) for i in range(count)]
    send = lax.dynamic_slice_in_dim(state, (1 - parity) * half, half, 1)
    mine = lax.dynamic_slice_in_dim(state, parity * half, half, 1)
    other = lax.ppermute(send, "seq", swap)
    shape = (height, half)
    (pair,) = small_call(pair_kernel, "pair" + tag, [first], [mine, other], [shape])
    before = None
    running = pair
    apart = 2
    while apart < count:
        by = -apart if backward else apart
        hops = [(i, i + by) for i in range(count) if 0 <= i + by < count]
        arrived = lax.ppermute(running, "seq", hops)
        last = apart * 2 >= count
        if before is None and last:
            farther = jnp.zeros(shape, BF16)
            before = arrived
        elif last:
            farther = arrived
        else:
            if before is None:
                before = arrived
            else:
                (before,) = small_call(longer_kernel, "longer" + tag, [], [before, arrived], [shape])
            (running,) = small_call(chain_kernel, "chain" + tag, [], [pair, before], [shape])
        apart *= 2
    entry = (height - EXTRA, half)
    keep, out = small_call(
        entry_kernel, "entry" + tag, [first], [mine, other, before, farther], [entry, entry]
    )
    return keep, lax.ppermute(out, "seq", swap)


def finish_kernel(
    head_size, place_ref, y_ref, bc_ref, cum_ref, keep_ref, other_ref, gate_ref, gain_ref, wo_ref, own_ref, send_ref, sq_ref
):
    rows, inner = y_ref.shape
    states = bc_ref.shape[1] // 2
    cmat = bc_ref[:, states:]
    swap = place_ref[0] == 1
    keep = keep_ref[...]
    other = other_ref[...]
    entry = jnp.concatenate([jnp.where(swap, other, keep), jnp.where(swap, keep, other)], axis=1)
    carried = dot(cmat, entry) * spread(jnp.exp(cum_ref[...]), inner, head_size, 0)
    gated = (y_ref[...].astype(F32) + carried) * gate_ref[...].astype(F32)
    squares = jnp.sum(gated * gated, axis=-1, keepdims=True)
    scaled = (gated * gain_ref[...]).astype(BF16)
    half = own_ref.shape[1]
    spare = sq_ref.shape[1]
    squares = jnp.broadcast_to(squares, (rows, spare))
    sq_ref[...] = squares
    high = squares.astype(BF16).astype(F32)
    lane = lax.broadcasted_iota(jnp.int32, squares.shape, 1)
    send_ref[:, half:] = jnp.where(lane == 0, high, squares - high).astype(BF16)
    result = dot(scaled, wo_ref[...])
    low, up = result[:, :half], result[:, half:]
    second = place_ref[1] == 1
    own_ref[...] = jnp.where(second, up, low)
    send_ref[:, :half] = jnp.where(second, low, up).astype(BF16)


def finish_call(name, place, y, bc, cum, keep, other, gate, gain, w_output):
    rows, inner = y.shape
    width = w_output.shape[1]
    half = width // 2
    heads = cum.shape[1]
    block_rows = TILE

    def block(columns):
        return pl.BlockSpec((block_rows, columns), lambda r: (r, 0))

    def whole(a):
        return pl.BlockSpec(a.shape, lambda r: (0, 0))

    return pl.pallas_call(
        functools.partial(finish_kernel, inner // heads),
        grid=(rows // block_rows,),
        in_specs=[
            pl.BlockSpec(memory_space=pltpu.SMEM),
            block(inner),
            block(bc.shape[1]),
            block(heads),
            whole(keep),
            whole(other),
            block(inner),
            whole(gain),
            whole(w_output),
        ],
        out_specs=[block(half), block(half + 128), block(128)],
        out_shape=[
            jax.ShapeDtypeStruct((rows, half), F32),
            jax.ShapeDtypeStruct((rows, half + 128), BF16),
            jax.ShapeDtypeStruct((rows, 128), F32),
        ],
        compiler_params=params(),
        name=name,
    )(place, y, bc, cum, keep, other, gate, gain, w_output)


def sum_kernel(full_width, of_ref, sf_ref, rf_ref, ob_ref, sb_ref, rb_ref, out_ref):
    half = out_ref.shape[1]
    total = None
    for own_ref, sq_ref, recv_ref in ((of_ref, sf_ref, rf_ref), (ob_ref, sb_ref, rb_ref)):
        theirs = recv_ref[:, half : half + 1].astype(F32) + recv_ref[:, half + 1 : half + 2].astype(F32)
        squares = sq_ref[:, :1] + theirs
        scale = lax.rsqrt(squares / full_width + EPS)
        part = (own_ref[...] + recv_ref[:, :half].astype(F32)) * scale
        total = part if total is None else total + part
    out_ref[...] = total.astype(BF16)


def sum_call(full_width, arrays):
    rows, half = arrays[0].shape
    block_rows = 128
    return pl.pallas_call(
        functools.partial(sum_kernel, full_width),
        grid=(rows // block_rows,),
        in_specs=[pl.BlockSpec((block_rows, a.shape[1]), lambda r: (r, 0)) for a in arrays],
        out_specs=pl.BlockSpec((block_rows, half), lambda r: (r, 0)),
        out_shape=jax.ShapeDtypeStruct((rows, half), BF16),
        compiler_params=params(),
        name="total",
    )(*arrays)


def flip_kernel(w_ref, out_ref):
    out_ref[...] = dot(w_ref[...], flip_matrix(TILE)).astype(BF16)


def flip_call(w):
    rows, width = w.shape
    count = width // TILE
    return pl.pallas_call(
        flip_kernel,
        grid=(count,),
        in_specs=[pl.BlockSpec((rows, TILE), lambda g: (0, count - 1 - g))],
        out_specs=pl.BlockSpec((rows, TILE), lambda g: (0, g)),
        out_shape=jax.ShapeDtypeStruct((rows, width), BF16),
        compiler_params=params(),
        name="flip",
    )(w)


def body(
    tokens,
    hidden,
    embedding,
    w_gate,
    w_inner,
    w_state,
    w_step,
    conv_inner,
    conv_state,
    step_bias,
    decay_rate,
    norm_gain,
    w_output,
):
    rows = hidden.shape[0]
    count = lax.axis_size("seq")
    base = jnp.zeros(hidden.shape, F32)
    for t in range(embedding.shape[0]):
        base = jnp.where((tokens == t)[:, None], embedding[t].astype(F32)[None, :], base)
    merged = (hidden.astype(F32) + base).astype(BF16)
    halo_f = lax.ppermute(merged[rows - HALO :], "seq", [(i, i + 1) for i in range(count - 1)])
    halo_b = lax.ppermute(merged[:HALO], "seq", [(i + 1, i) for i in range(count - 1)])
    normed_f, normed_b, gate_f, gate_b = gate_call(merged, w_gate)
    bias = step_bias.reshape(1, -1)
    rate = decay_rate.reshape(1, -1)
    gain = norm_gain.reshape(1, -1)
    place = jnp.stack([lax.axis_index("seq") % 2, lax.axis_index("ch")]).astype(jnp.int32)
    weights = (w_inner, w_state, w_step, conv_inner, conv_state, bias, rate)
    xs_f, bc_f, cum_f, cumt_f, state_f = local_call(False, normed_f, halo_f, *weights)
    xs_b, bc_b, cum_b, cumt_b, state_b = local_call(True, normed_b, halo_b, *weights)
    keep_f, other_f = entering(False, state_f)
    keep_b, other_b = entering(True, state_b)
    y_f = inside_call(False, xs_f, bc_f, cum_f, cumt_f)
    y_b = inside_call(True, xs_b, bc_b, cum_b, cumt_b)
    w_back = flip_call(w_output)
    swap = [(0, 1), (1, 0)]
    own_f, send_f, sq_f = finish_call("finish_f", place, y_f, bc_f, cum_f, keep_f, other_f, gate_f, gain, w_output)
    recv_f = lax.ppermute(send_f, "ch", swap)
    own_b, send_b, sq_b = finish_call("finish_b", place, y_b, bc_b, cum_b, keep_b, other_b, gate_b, gain, w_back)
    recv_b = lax.ppermute(send_b, "ch", swap)
    full_width = w_inner.shape[1] * lax.axis_size("ch")
    return sum_call(float(full_width), (own_f, sq_f, recv_f, own_b, sq_b, recv_b))


def solution(mesh):
    return jax.shard_map(
        body,
        mesh=mesh,
        in_specs=(
            P(("win", "seq")),
            P(("win", "seq"), None),
            P(),
            P(None, "ch"),
            P(None, "ch"),
            P(),
            P(None, "ch"),
            P(None, "ch"),
            P(),
            P("ch"),
            P("ch"),
            P("ch"),
            P("ch", None),
        ),
        out_specs=P(("win", "seq"), "ch"),
        check_vma=False,
    )
```

```python
import functools

import jax
import jax.numpy as jnp
from jax import lax
from jax.experimental import pallas as pl
from jax.experimental.pallas import tpu as pltpu
from jax.sharding import PartitionSpec as P

F32 = jnp.float32
BF16 = jnp.bfloat16
EPS = 1e-05
HALO = 16
EXTRA = 16
CHUNK = 128
TILE = 256
MB = 1024 * 1024


def call(kernel, name, *, vmem, cost, scalars=(), grid=(), in_specs, out_specs, out_shape, scratch=()):
    flops, moved, special = cost
    return pl.pallas_call(
        kernel,
        grid_spec=pltpu.PrefetchScalarGridSpec(
            num_scalar_prefetch=len(scalars),
            grid=grid,
            in_specs=in_specs,
            out_specs=out_specs,
            scratch_shapes=scratch,
        ),
        out_shape=out_shape,
        compiler_params=pltpu.CompilerParams(
            vmem_limit_bytes=vmem * MB, dimension_semantics=("arbitrary",) * len(grid)
        ),
        cost_estimate=pl.CostEstimate(flops=flops, bytes_accessed=moved, transcendentals=special),
        name=name,
    )


def micros(us):
    return (int(us * 1.1e9), int(us * 1e6), 0)


def dot(a, b):
    return jnp.dot(a, b, preferred_element_type=F32)


def dot_nt(a, b):
    return lax.dot_general(a, b, (((1,), (1,)), ((), ())), preferred_element_type=F32)


def dot_tn(a, b):
    return lax.dot_general(a, b, (((0,), (0,)), ((), ())), preferred_element_type=F32)


def flip_matrix(size):
    rows = lax.broadcasted_iota(jnp.int32, (size, size), 0)
    columns = lax.broadcasted_iota(jnp.int32, (size, size), 1)
    return jnp.where(rows + columns == size - 1, 1.0, 0.0).astype(BF16)


def flip_both(value):
    rows, width = value.shape
    turned = dot(flip_matrix(rows), value).astype(BF16)
    anti = flip_matrix(TILE)
    count = width // TILE
    blocks = [
        dot(turned[:, (count - 1 - k) * TILE : (count - k) * TILE], anti).astype(BF16)
        for k in range(count)
    ]
    return jnp.concatenate(blocks, axis=1)


def silu(v):
    half = 0.5 * v
    return half + half * jnp.tanh(half)


def two_parts(value):
    high = value.astype(BF16)
    low = (value - high.astype(F32)).astype(BF16)
    return jnp.concatenate([high, low], axis=1)


def spread(value, width, head_size, first_head):
    heads = value.shape[1]
    source = lax.broadcasted_iota(jnp.int32, (2 * heads, width), 0)
    source = jnp.where(source >= heads, source - heads, source)
    target = lax.broadcasted_iota(jnp.int32, (2 * heads, width), 1) // head_size + first_head
    onehot = jnp.where(source == target, 1.0, 0.0).astype(BF16)
    return dot(two_parts(value), onehot)


def prepare_kernel(back_ref, tokens_ref, hidden_ref, emb_ref, out_ref, tail_ref):
    length = hidden_ref.shape[0]
    kinds = emb_ref.shape[0]
    back = back_ref[0] == 1
    r = pl.program_id(0)
    final = pl.num_programs(0) - 1
    kind = lax.broadcasted_iota(jnp.int32, (kinds, length), 0)
    onehot = jnp.where(kind == tokens_ref[...], 1.0, 0.0).astype(BF16)
    merged = (hidden_ref[...].astype(F32) + dot_tn(onehot, emb_ref[...])).astype(BF16).astype(F32)
    mean = jnp.mean(merged * merged, axis=-1, keepdims=True)
    normed = (merged * lax.rsqrt(mean + EPS)).astype(BF16)

    @pl.when(back)
    def _():
        out_ref[...] = flip_both(normed)

    @pl.when(jnp.logical_not(back))
    def _():
        out_ref[...] = normed

    @pl.when(r == jnp.where(back, 0, final))
    def _():
        tail_ref[...] = out_ref[length - HALO :, :]


def prepare_call(back, tokens, hidden, embedding):
    rows, width = hidden.shape
    count = rows // CHUNK

    def turned(r, back):
        return (jnp.where(back[0] == 1, count - 1 - r, r), 0)

    return call(
        prepare_kernel,
        "prepare",
        vmem=12,
        cost=micros(1.5),
        scalars=(back,),
        grid=(count,),
        in_specs=[
            pl.BlockSpec((1, CHUNK), lambda r, back: (0, r)),
            pl.BlockSpec((CHUNK, width), lambda r, back: (r, 0)),
            pl.BlockSpec(embedding.shape, lambda r, back: (0, 0)),
        ],
        out_specs=[
            pl.BlockSpec((CHUNK, width), turned),
            pl.BlockSpec((HALO, width), lambda r, back: (0, 0)),
        ],
        out_shape=[
            jax.ShapeDtypeStruct((rows, width), BF16),
            jax.ShapeDtypeStruct((HALO, width), BF16),
        ],
    )(back, tokens.reshape(1, rows), hidden, embedding)


def gate_kernel(rows_ref, wg_ref, out_ref):
    gate = dot(rows_ref[...], wg_ref[...]).astype(BF16).astype(F32)
    out_ref[...] = silu(gate).astype(BF16)


def gate_call(tag, normed, w_gate):
    rows, width = normed.shape
    inner = w_gate.shape[1]
    return call(
        gate_kernel,
        "gate_" + tag,
        vmem=8,
        cost=micros(2.4),
        grid=(inner // TILE,),
        in_specs=[
            pl.BlockSpec((rows, width), lambda g: (0, 0)),
            pl.BlockSpec((width, TILE), lambda g: (0, g)),
        ],
        out_specs=pl.BlockSpec((rows, TILE), lambda g: (0, g)),
        out_shape=jax.ShapeDtypeStruct((rows, inner), BF16),
    )(normed, w_gate)


def conv_silu(rows_ref, weights, rows):
    taps = weights.shape[0]
    total = None
    for k in range(taps):
        offset = HALO - (taps - 1) + k
        term = weights[k : k + 1, :] * rows_ref[offset : offset + rows, :]
        total = term if total is None else total + term
    return silu(total).astype(BF16)


def maps_kernel(normed_ref, halo_ref, ws_ref, cs_ref, bc_ref, bt_ref, rows_ref):
    rows = normed_ref.shape[0]
    states = bc_ref.shape[1] // 2
    rows_ref[:HALO, :] = dot(halo_ref[...], ws_ref[...]).astype(BF16).astype(F32)
    rows_ref[HALO:, :] = dot(normed_ref[...], ws_ref[...]).astype(BF16).astype(F32)
    state_conv = conv_silu(rows_ref, cs_ref[...], rows)
    bc_ref[...] = state_conv
    bt_ref[...] = state_conv[:, :states].astype(F32).T.astype(BF16)


def maps_call(normed, halo, w_state, conv_state):
    rows = normed.shape[0]
    both = w_state.shape[1]
    vmem = pl.BlockSpec(memory_space=pltpu.VMEM)
    return call(
        maps_kernel,
        "maps",
        vmem=8,
        cost=micros(1.5),
        in_specs=[vmem] * 4,
        out_specs=[vmem] * 2,
        out_shape=[
            jax.ShapeDtypeStruct((rows, both), BF16),
            jax.ShapeDtypeStruct((both // 2, rows), BF16),
        ],
        scratch=[pltpu.VMEM((rows + HALO, both), F32)],
    )(normed, halo, w_state, conv_state)


def local_kernel(
    head_size,
    normed_ref,
    halo_ref,
    bt_ref,
    wi_ref,
    wt_ref,
    small_ref,
    xs_ref,
    cum_ref,
    cumt_ref,
    state_ref,
    rows_ref,
    step_ref,
):
    rows = normed_ref.shape[0]
    states = bt_ref.shape[0]
    heads = wt_ref.shape[0]
    taps = SMALL_TAPS
    g = pl.program_id(0)

    @pl.when(g == 0)
    def _():
        bias = small_ref[taps + 1 : taps + 2, :heads]
        rate = small_ref[taps + 2 : taps + 3, :heads]
        raw = dot_nt(normed_ref[...], wt_ref[...]) + bias
        step = jnp.maximum(raw, 0.0) + jnp.log1p(jnp.exp(-jnp.abs(raw)))
        step_ref[...] = step
        logdecay = -step * rate
        high = logdecay.astype(BF16)
        rest = logdecay - high.astype(F32)
        mid = rest.astype(BF16)
        low = (rest - mid.astype(F32)).astype(BF16)
        parts = jnp.concatenate([high, mid, low], axis=1)
        to = lax.broadcasted_iota(jnp.int32, (rows, rows), 0)
        frm = lax.broadcasted_iota(jnp.int32, (rows, rows), 1)
        sums = dot(jnp.where(to >= frm, 1.0, 0.0).astype(BF16), parts)
        cum = sums[:, :heads] + sums[:, heads : 2 * heads] + sums[:, 2 * heads :]
        cum_ref[...] = cum
        cumt_ref[...] = cum.T

    weights = wi_ref[...]
    rows_ref[:HALO, :] = dot(halo_ref[...], weights).astype(BF16).astype(F32)
    rows_ref[HALO:, :] = dot(normed_ref[...], weights).astype(BF16).astype(F32)
    columns = pl.ds(pl.multiple_of(g * TILE, TILE), TILE)
    x = conv_silu(rows_ref, small_ref[:taps, columns], rows).astype(F32)
    first = g * (TILE // head_size)
    xs = x * spread(step_ref[...], TILE, head_size, first)
    xs_ref[...] = xs.astype(BF16)
    cum = cum_ref[...]
    total = cum[rows - 1 :, :]
    left = spread(jnp.exp(total - cum), TILE, head_size, first)
    state_ref[:states, :] = dot(bt_ref[...], (xs * left).astype(BF16)).astype(BF16)
    whole = spread(jnp.broadcast_to(jnp.exp(total), (EXTRA, heads)), TILE, head_size, first)
    high = whole.astype(BF16).astype(F32)
    place = lax.broadcasted_iota(jnp.int32, whole.shape, 0)
    state_ref[states:, :] = jnp.where(place == 0, high, whole - high).astype(BF16)


SMALL_TAPS = 4
SMALL_ROWS = 8


def small_params(conv, gain, bias, rate):
    inner = gain.shape[0]
    rest = SMALL_ROWS - SMALL_TAPS - 3

    def row(a):
        return jnp.pad(a, (0, inner - a.shape[0]))[None, :]

    return jnp.concatenate([conv, row(gain), row(bias), row(rate), jnp.zeros((rest, inner), F32)], axis=0)


def local_call(tag, normed, halo, bt, w_inner, w_step_t, small):
    rows, width = normed.shape
    inner = w_inner.shape[1]
    heads = w_step_t.shape[0]
    states = bt.shape[0]

    def whole(a):
        return pl.BlockSpec(a.shape, lambda g: (0, 0))

    def tile(count):
        return pl.BlockSpec((count, TILE), lambda g: (0, g))

    return call(
        functools.partial(local_kernel, inner // heads),
        "local_" + tag,
        vmem=12,
        cost=micros(5.0),
        grid=(inner // TILE,),
        in_specs=[whole(normed), whole(halo), whole(bt), tile(width), whole(w_step_t), whole(small)],
        out_specs=[
            tile(rows),
            pl.BlockSpec((rows, heads), lambda g: (0, 0)),
            pl.BlockSpec((heads, rows), lambda g: (0, 0)),
            tile(states + EXTRA),
        ],
        out_shape=[
            jax.ShapeDtypeStruct((rows, inner), BF16),
            jax.ShapeDtypeStruct((rows, heads), F32),
            jax.ShapeDtypeStruct((heads, rows), F32),
            jax.ShapeDtypeStruct((states + EXTRA, inner), BF16),
        ],
        scratch=[pltpu.VMEM((rows + HALO, TILE), F32), pltpu.VMEM((rows, heads), F32)],
    )(normed, halo, bt, w_inner, w_step_t, small)


def inside_kernel(head_size, xs_ref, bc_ref, cum_ref, cumt_ref, y_ref, state_ref, prev_ref):
    length, inner = xs_ref.shape
    states = bc_ref.shape[1] // 2
    heads = cum_ref.shape[1]

    @pl.when(pl.program_id(0) == 0)
    def _():
        state_ref[...] = jnp.zeros_like(state_ref)
        prev_ref[...] = jnp.zeros_like(prev_ref)

    bmat = bc_ref[:, :states]
    cmat = bc_ref[:, states:]
    to = lax.broadcasted_iota(jnp.int32, (length, length), 0)
    frm = lax.broadcasted_iota(jnp.int32, (length, length), 1)
    scores = jnp.where(to >= frm, dot_nt(cmat, bmat), 0.0)
    cum = cum_ref[...]
    cumt = cumt_ref[...]
    last = length - 1
    end = cum[last:, :]
    since = spread(jnp.exp(cum - prev_ref[...]), inner, head_size, 0)
    left = spread(jnp.exp(end - cum), inner, head_size, 0)
    state = state_ref[...]
    carried = dot(cmat, state.astype(BF16)) * since
    xs = xs_ref[...]
    scaled = (xs.astype(F32) * left).astype(BF16)
    state_ref[...] = state * since[last:, :] + dot_tn(bmat, scaled)
    prev_ref[...] = end
    pair = 2 * head_size
    lane = lax.broadcasted_iota(jnp.int32, (length, pair), 1)
    for p in range(heads // 2):
        weights = []
        for h in (2 * p, 2 * p + 1):
            apart = jnp.minimum(cum[:, h : h + 1] - cumt[h : h + 1, :], 0.0)
            weights.append((jnp.exp(apart) * scores).astype(BF16))
        mine = xs[:, p * pair : (p + 1) * pair]
        none = jnp.zeros_like(mine)
        stacked = jnp.concatenate(
            [jnp.where(lane < head_size, mine, none), jnp.where(lane < head_size, none, mine)], axis=0
        )
        inside = dot(jnp.concatenate(weights, axis=1), stacked)
        y_ref[:, p * pair : (p + 1) * pair] = (
            inside + carried[:, p * pair : (p + 1) * pair]
        ).astype(BF16)


def inside_call(tag, xs, bc, cum, cumt):
    rows, inner = xs.shape
    heads = cum.shape[1]
    both = bc.shape[1]

    def block(width):
        return pl.BlockSpec((CHUNK, width), lambda c: (c, 0))

    return call(
        functools.partial(inside_kernel, inner // heads),
        "inside_" + tag,
        vmem=8,
        cost=micros(3.2),
        grid=(rows // CHUNK,),
        in_specs=[
            block(inner),
            block(both),
            block(heads),
            pl.BlockSpec((heads, CHUNK), lambda c: (0, c)),
        ],
        out_specs=block(inner),
        out_shape=jax.ShapeDtypeStruct((rows, inner), BF16),
        scratch=[pltpu.VMEM((both // 2, inner), F32), pltpu.VMEM((1, heads), F32)],
    )(xs, bc, cum, cumt)


def parts_of(payload):
    states = payload.shape[0] - EXTRA
    wide = payload.astype(F32)
    return wide[:states], wide[states : states + 1] + wide[states + 1 : states + 2]


def write_payload(out_ref, state, decay):
    states = state.shape[0]
    out_ref[:states, :] = state.astype(BF16)
    decay = jnp.broadcast_to(decay, (EXTRA, decay.shape[1]))
    high = decay.astype(BF16).astype(F32)
    place = lax.broadcasted_iota(jnp.int32, decay.shape, 0)
    out_ref[states:, :] = jnp.where(place == 0, high, decay - high).astype(BF16)


def pair_kernel(first_ref, mine_ref, other_ref, out_ref):
    mine, mine_a = parts_of(mine_ref[...])
    other, other_a = parts_of(other_ref[...])
    is_first = first_ref[0] == 1
    early = jnp.where(is_first, mine, other)
    late = jnp.where(is_first, other, mine)
    late_a = jnp.where(is_first, other_a, mine_a)
    write_payload(out_ref, late_a * early + late, mine_a * other_a)


def chain_kernel(pair_ref, before_ref, out_ref):
    pair, pair_a = parts_of(pair_ref[...])
    before, before_a = parts_of(before_ref[...])
    write_payload(out_ref, pair_a * before + pair, pair_a * before_a)


def longer_kernel(before_ref, farther_ref, out_ref):
    before, before_a = parts_of(before_ref[...])
    farther, farther_a = parts_of(farther_ref[...])
    write_payload(out_ref, before + before_a * farther, before_a * farther_a)


def entry_kernel(first_ref, mine_ref, other_ref, before_ref, farther_ref, keep_ref, send_ref):
    mine, mine_a = parts_of(mine_ref[...])
    other, other_a = parts_of(other_ref[...])
    before, before_a = parts_of(before_ref[...])
    farther, _ = parts_of(farther_ref[...])
    is_first = first_ref[0] == 1
    entry_first = before + before_a * farther
    early = jnp.where(is_first, mine, other)
    early_a = jnp.where(is_first, mine_a, other_a)
    entry_second = early_a * entry_first + early
    keep_ref[...] = jnp.where(is_first, entry_first, entry_second).astype(BF16)
    send_ref[...] = jnp.where(is_first, entry_second, entry_first).astype(BF16)


def small_call(kernel, name, flags, arrays, shapes):
    vmem = pl.BlockSpec(memory_space=pltpu.VMEM)
    smem = pl.BlockSpec(memory_space=pltpu.SMEM)
    return call(
        kernel,
        name,
        vmem=4,
        cost=micros(0.5),
        in_specs=[smem] * len(flags) + [vmem] * len(arrays),
        out_specs=[vmem] * len(shapes),
        out_shape=[jax.ShapeDtypeStruct(s, BF16) for s in shapes],
    )(*flags, *arrays)


def onward(value, by):
    count = lax.axis_size("seq")
    cores = lax.axis_size("ch")
    pairs = []
    for core in range(cores):
        step = -by if core == 1 else by
        pairs += [
            (i * cores + core, (i + step) * cores + core) for i in range(count) if 0 <= i + step < count
        ]
    return lax.ppermute(value, ("seq", "ch"), pairs)


def entering(tag, back, state):
    count = lax.axis_size("seq")
    parity = lax.axis_index("seq") % 2
    first = jnp.where(back == 1, parity, 1 - parity).astype(jnp.int32)
    height, inner = state.shape
    half = inner // 2
    swap = [(i, i ^ 1) for i in range(count)]
    send = lax.dynamic_slice_in_dim(state, (1 - parity) * half, half, 1)
    mine = lax.dynamic_slice_in_dim(state, parity * half, half, 1)
    other = lax.ppermute(send, "seq", swap)
    shape = (height, half)
    (pair,) = small_call(pair_kernel, "pair_" + tag, [first], [mine, other], [shape])
    before = None
    farther = None
    running = pair
    apart = 2
    while apart < count:
        arrived = onward(running, apart)
        last = apart * 2 >= count
        if before is None:
            before = arrived
        elif last:
            farther = arrived
        else:
            (before,) = small_call(longer_kernel, "longer_" + tag, [], [before, arrived], [shape])
        if not last:
            (running,) = small_call(chain_kernel, "chain_" + tag, [], [pair, before], [shape])
        apart *= 2
    if before is None:
        before = jnp.zeros(shape, BF16)
    if farther is None:
        farther = jnp.zeros(shape, BF16)
    entry = (height - EXTRA, half)
    keep, out = small_call(
        entry_kernel, "entry_" + tag, [first], [mine, other, before, farther], [entry, entry]
    )
    return keep, lax.ppermute(out, "seq", swap)


def gated_part(head_size, swap, y_ref, bc_ref, cum_ref, keep_ref, other_ref, gate_ref, small_ref, wo_ref):
    inner = y_ref.shape[1]
    states = bc_ref.shape[1] // 2
    cmat = bc_ref[:, states:]
    keep = keep_ref[...]
    other = other_ref[...]
    entry = jnp.concatenate([jnp.where(swap, other, keep), jnp.where(swap, keep, other)], axis=1)
    carried = dot(cmat, entry) * spread(jnp.exp(cum_ref[...]), inner, head_size, 0)
    gated = (y_ref[...].astype(F32) + carried) * gate_ref[...].astype(F32)
    squares = jnp.sum(gated * gated, axis=-1, keepdims=True)
    gain = small_ref[SMALL_TAPS : SMALL_TAPS + 1, :]
    return dot((gated * gain).astype(BF16), wo_ref[...]), squares


def part_kernel(head_size, flags_ref, *refs):
    *ins, out_ref, sq_ref = refs
    result, squares = gated_part(head_size, flags_ref[0] == 1, *ins)
    out_ref[...] = result
    sq_ref[...] = jnp.broadcast_to(squares, sq_ref.shape)


def finish_kernel(head_size, full_width, flags_ref, *refs):
    *ins, part_ref, psq_ref, own_ref, send_ref = refs
    result, squares = gated_part(head_size, flags_ref[0] == 1, *ins)
    squares = squares + psq_ref[:, :1]
    result = (result + part_ref[...]) * lax.rsqrt(squares / full_width + EPS)
    result = result.astype(BF16)
    half = own_ref.shape[1]

    @pl.when(flags_ref[1] == 1)
    def _():
        turned = flip_both(result)
        own_ref[...] = turned[:, half:]
        send_ref[...] = turned[:, :half]

    @pl.when(flags_ref[1] != 1)
    def _():
        own_ref[...] = result[:, :half]
        send_ref[...] = result[:, half:]


def finish_call(flags, y, bc, cum, keep, other, gate, small, w_output, full_width=None, partial=None):
    rows, inner = y.shape
    width = w_output.shape[1]
    half = width // 2
    heads = cum.shape[1]
    count = rows // TILE

    def block(columns):
        return pl.BlockSpec((TILE, columns), lambda r, flags: (r, 0))

    def whole(a):
        return pl.BlockSpec(a.shape, lambda r, flags: (0, 0))

    def turned(r, flags):
        return (jnp.where(flags[1] == 1, count - 1 - r, r), 0)

    in_specs = [
        block(inner),
        block(bc.shape[1]),
        block(heads),
        whole(keep),
        whole(other),
        block(inner),
        whole(small),
        whole(w_output),
    ]
    arrays = [y, bc, cum, keep, other, gate, small, w_output]
    if partial is None:
        kernel = functools.partial(part_kernel, inner // heads)
        out_specs = [block(width), block(128)]
        out_shape = [jax.ShapeDtypeStruct((rows, width), F32), jax.ShapeDtypeStruct((rows, 128), F32)]
    else:
        kernel = functools.partial(finish_kernel, inner // heads, full_width)
        in_specs += [block(width), block(128)]
        arrays += list(partial)
        out_specs = [pl.BlockSpec((TILE, half), turned)] * 2
        out_shape = [jax.ShapeDtypeStruct((rows, half), BF16)] * 2
    return call(
        kernel,
        "part" if partial is None else "finish",
        vmem=16,
        cost=micros(3.5),
        scalars=(flags,),
        grid=(count,),
        in_specs=in_specs,
        out_specs=out_specs,
        out_shape=out_shape,
    )(flags, *arrays)


def body(
    tokens,
    hidden,
    embedding,
    w_gate,
    w_inner,
    w_state,
    w_step,
    conv_inner,
    conv_state,
    step_bias,
    decay_rate,
    norm_gain,
    w_output,
):
    swap = [(0, 1), (1, 0)]

    def theirs(a):
        return lax.ppermute(a, "ch", swap)

    back = lax.axis_index("ch").astype(jnp.int32).reshape(1)
    parity = (lax.axis_index("seq") % 2).astype(jnp.int32).reshape(1)
    flags = jnp.concatenate([parity, back])
    normed, tail = prepare_call(back, tokens, hidden, embedding)
    halo = onward(tail, 1)
    small = small_params(conv_inner, norm_gain, step_bias, decay_rate)
    own = (w_inner, w_step.T, small)
    other = tuple(theirs(a) for a in own)
    w_gate_2 = theirs(w_gate)
    w_output_2 = theirs(w_output)
    gate_1 = gate_call("own", normed, w_gate)
    bc, bt = maps_call(normed, halo, w_state, conv_state)
    xs_1, cum_1, cumt_1, state_1 = local_call("own", normed, halo, bt, *own)
    xs_2, cum_2, cumt_2, state_2 = local_call("other", normed, halo, bt, *other)
    entry_1 = entering("own", back, state_1)
    entry_2 = entering("other", back, state_2)
    y_1 = inside_call("own", xs_1, bc, cum_1, cumt_1)
    y_2 = inside_call("other", xs_2, bc, cum_2, cumt_2)
    gate_2 = gate_call("other", normed, w_gate_2)
    partial = finish_call(flags, y_1, bc, cum_1, *entry_1, gate_1, small, w_output)
    full_width = float(w_inner.shape[1] * lax.axis_size("ch"))
    mine, send = finish_call(
        flags, y_2, bc, cum_2, *entry_2, gate_2, other[2], w_output_2, full_width, partial
    )
    return (mine.astype(F32) + theirs(send).astype(F32)).astype(BF16)


def solution(mesh):
    return jax.shard_map(
        body,
        mesh=mesh,
        in_specs=(
            P(("win", "seq")),
            P(("win", "seq"), None),
            P(),
            P(None, "ch"),
            P(None, "ch"),
            P(),
            P(None, "ch"),
            P(None, "ch"),
            P(),
            P("ch"),
            P("ch"),
            P("ch"),
            P("ch", None),
        ),
        out_specs=P(("win", "seq"), "ch"),
        check_vma=False,
    )
```

```python
import functools

import jax
import jax.numpy as jnp
from jax import lax
from jax.experimental import pallas as pl
from jax.experimental.pallas import tpu as pltpu
from jax.sharding import PartitionSpec as P

F32 = jnp.float32
BF16 = jnp.bfloat16
EPS = 1e-05
HALO = 16
EXTRA = 16
CHUNK = 128
TILE = 256
MB = 1024 * 1024


def call(
    kernel, name, *, vmem, cost, scalars=(), grid=(), in_specs, out_specs, out_shape, scratch=(), after=()
):
    flops, moved, special = cost
    first = len(scalars) + len(in_specs)

    def body(*refs):
        kernel(*refs[:first], *refs[first + len(after) :])

    run = pl.pallas_call(
        body,
        grid_spec=pltpu.PrefetchScalarGridSpec(
            num_scalar_prefetch=len(scalars),
            grid=grid,
            in_specs=list(in_specs) + [pl.BlockSpec(memory_space=pl.ANY)] * len(after),
            out_specs=out_specs,
            scratch_shapes=scratch,
        ),
        out_shape=out_shape,
        compiler_params=pltpu.CompilerParams(
            vmem_limit_bytes=vmem * MB, dimension_semantics=("arbitrary",) * len(grid)
        ),
        cost_estimate=pl.CostEstimate(flops=flops, bytes_accessed=moved, transcendentals=special),
        name=name,
    )
    return lambda *arrays: run(*arrays, *after)


def micros(us):
    return (int(us * 1.1e9), int(us * 1e6), 0)


def dot(a, b):
    return jnp.dot(a, b, preferred_element_type=F32)


def dot_nt(a, b):
    return lax.dot_general(a, b, (((1,), (1,)), ((), ())), preferred_element_type=F32)


def dot_tn(a, b):
    return lax.dot_general(a, b, (((0,), (0,)), ((), ())), preferred_element_type=F32)


def flip_matrix(size):
    rows = lax.broadcasted_iota(jnp.int32, (size, size), 0)
    columns = lax.broadcasted_iota(jnp.int32, (size, size), 1)
    return jnp.where(rows + columns == size - 1, 1.0, 0.0).astype(BF16)


def flip_both(value):
    rows, width = value.shape
    turned = dot(flip_matrix(rows), value).astype(BF16)
    anti = flip_matrix(TILE)
    count = width // TILE
    blocks = [
        dot(turned[:, (count - 1 - k) * TILE : (count - k) * TILE], anti).astype(BF16)
        for k in range(count)
    ]
    return jnp.concatenate(blocks, axis=1)


def silu(v):
    half = 0.5 * v
    return half + half * jnp.tanh(half)


def two_parts(value):
    high = value.astype(BF16)
    low = (value - high.astype(F32)).astype(BF16)
    return jnp.concatenate([high, low], axis=1)


def spread(value, width, head_size, first_head):
    heads = value.shape[1]
    source = lax.broadcasted_iota(jnp.int32, (2 * heads, width), 0)
    source = jnp.where(source >= heads, source - heads, source)
    target = lax.broadcasted_iota(jnp.int32, (2 * heads, width), 1) // head_size + first_head
    onehot = jnp.where(source == target, 1.0, 0.0).astype(BF16)
    return dot(two_parts(value), onehot)


def prepare_kernel(
    back_ref,
    tokens_hbm,
    hidden_hbm,
    emb_hbm,
    conv_ref,
    gain_ref,
    bias_ref,
    rate_ref,
    out_ref,
    tail_ref,
    small_ref,
    tokens_ref,
    hidden_ref,
    emb_ref,
    sems,
):
    rows = hidden_ref.shape[0]
    kinds = emb_ref.shape[0]
    taps, inner = conv_ref.shape
    heads = bias_ref.shape[1]
    count = rows // CHUNK
    back = back_ref[0] == 1
    copies = [
        pltpu.make_async_copy(tokens_hbm, tokens_ref, sems.at[0]),
        pltpu.make_async_copy(emb_hbm, emb_ref, sems.at[1]),
    ]
    for r in range(count):
        part = pl.ds(r * CHUNK, CHUNK)
        copies.append(pltpu.make_async_copy(hidden_hbm.at[part, :], hidden_ref.at[part, :], sems.at[2 + r]))
    for copy in copies:
        copy.start()
    small_ref[:taps, :] = conv_ref[...]
    small_ref[taps : taps + 1, :] = gain_ref[...]
    small_ref[taps + 1 :, :] = jnp.zeros((SMALL_ROWS - taps - 1, inner), F32)
    small_ref[taps + 1 : taps + 2, :heads] = bias_ref[...]
    small_ref[taps + 2 : taps + 3, :heads] = rate_ref[...]
    copies[0].wait()
    copies[1].wait()
    kind = lax.broadcasted_iota(jnp.int32, (kinds, rows), 0)
    onehot = jnp.where(kind == tokens_ref[...], 1.0, 0.0).astype(BF16)
    for r in range(count):
        copies[2 + r].wait()
        low, high = r * CHUNK, (r + 1) * CHUNK
        base = dot_tn(onehot[:, low:high], emb_ref[...])
        merged = (hidden_ref[low:high, :].astype(F32) + base).astype(BF16).astype(F32)
        mean = jnp.mean(merged * merged, axis=-1, keepdims=True)
        normed = (merged * lax.rsqrt(mean + EPS)).astype(BF16)

        @pl.when(back)
        def _():
            turned = flip_both(normed)
            out_ref[rows - high : rows - low, :] = turned
            if r == 0:
                tail_ref[...] = turned[CHUNK - HALO :, :]

        @pl.when(jnp.logical_not(back))
        def _():
            out_ref[low:high, :] = normed
            if r == count - 1:
                tail_ref[...] = normed[CHUNK - HALO :, :]


def prepare_call(back, tokens, hidden, embedding, conv, gain, bias, rate):
    rows, width = hidden.shape
    inner = conv.shape[1]
    vmem = pl.BlockSpec(memory_space=pltpu.VMEM)
    hbm = pl.BlockSpec(memory_space=pltpu.HBM)
    return call(
        prepare_kernel,
        "prepare",
        vmem=12,
        cost=micros(1.5),
        scalars=(back,),
        grid=(),
        in_specs=[hbm] * 3 + [vmem] * 4,
        out_specs=[vmem] * 3,
        out_shape=[
            jax.ShapeDtypeStruct((rows, width), BF16),
            jax.ShapeDtypeStruct((HALO, width), BF16),
            jax.ShapeDtypeStruct((SMALL_ROWS, inner), F32),
        ],
        scratch=[
            pltpu.VMEM((1, rows), jnp.int32),
            pltpu.VMEM((rows, width), BF16),
            pltpu.VMEM(embedding.shape, BF16),
            pltpu.SemaphoreType.DMA((2 + rows // CHUNK,)),
        ],
    )(
        back,
        tokens.reshape(1, rows),
        hidden,
        embedding,
        conv,
        gain.reshape(1, -1),
        bias.reshape(1, -1),
        rate.reshape(1, -1),
    )


def gate_kernel(rows_ref, wg_ref, out_ref):
    gate = dot(rows_ref[...], wg_ref[...]).astype(BF16).astype(F32)
    out_ref[...] = silu(gate).astype(BF16)


def gate_call(tag, normed, w_gate, after=()):
    rows, width = normed.shape
    inner = w_gate.shape[1]
    return call(
        gate_kernel,
        "gate_" + tag,
        vmem=8,
        cost=micros(2.4),
        grid=(inner // TILE,),
        in_specs=[
            pl.BlockSpec((rows, width), lambda g: (0, 0)),
            pl.BlockSpec((width, TILE), lambda g: (0, g)),
        ],
        out_specs=pl.BlockSpec((rows, TILE), lambda g: (0, g)),
        out_shape=jax.ShapeDtypeStruct((rows, inner), BF16),
        after=after,
    )(normed, w_gate)


def conv_silu(rows_ref, weights, rows):
    taps = weights.shape[0]
    total = None
    for k in range(taps):
        offset = HALO - (taps - 1) + k
        term = weights[k : k + 1, :] * rows_ref[offset : offset + rows, :]
        total = term if total is None else total + term
    return silu(total).astype(BF16)


def maps_kernel(place_ref, normed_ref, halo_ref, ws_ref, cs_ref, bc_ref, bt_ref, rows_ref):
    rows = normed_ref.shape[0]
    states = bc_ref.shape[1] // 2
    before = dot(halo_ref[...], ws_ref[...]).astype(BF16).astype(F32)
    rows_ref[:HALO, :] = jnp.where(place_ref[0] >= 1, before, 0.0)
    rows_ref[HALO:, :] = dot(normed_ref[...], ws_ref[...]).astype(BF16).astype(F32)
    state_conv = conv_silu(rows_ref, cs_ref[...], rows)
    bc_ref[...] = state_conv
    bt_ref[...] = state_conv[:, :states].astype(F32).T.astype(BF16)


def maps_call(place, normed, halo, w_state, conv_state, after=()):
    rows = normed.shape[0]
    both = w_state.shape[1]
    vmem = pl.BlockSpec(memory_space=pltpu.VMEM)
    return call(
        maps_kernel,
        "maps",
        vmem=8,
        cost=micros(1.5),
        scalars=(place,),
        in_specs=[vmem] * 4,
        out_specs=[vmem] * 2,
        out_shape=[
            jax.ShapeDtypeStruct((rows, both), BF16),
            jax.ShapeDtypeStruct((both // 2, rows), BF16),
        ],
        scratch=[pltpu.VMEM((rows + HALO, both), F32)],
        after=after,
    )(place, normed, halo, w_state, conv_state)


def local_kernel(
    head_size,
    place_ref,
    parity_ref,
    normed_ref,
    halo_ref,
    bt_ref,
    wi_ref,
    wt_ref,
    small_ref,
    xs_ref,
    cum_ref,
    cumt_ref,
    send_ref,
    mine_ref,
    rows_ref,
    step_ref,
):
    rows = normed_ref.shape[0]
    states = bt_ref.shape[0]
    heads = wt_ref.shape[0]
    taps = SMALL_TAPS
    tiles = pl.num_programs(0)
    g = pl.program_id(0)
    tile = tile_at(g, tiles, parity_ref)

    @pl.when(g == 0)
    def _():
        bias = small_ref[taps + 1 : taps + 2, :heads]
        rate = small_ref[taps + 2 : taps + 3, :heads]
        raw = dot_nt(normed_ref[...], wt_ref[...]) + bias
        step = jnp.maximum(raw, 0.0) + jnp.log1p(jnp.exp(-jnp.abs(raw)))
        step_ref[...] = step
        logdecay = -step * rate
        high = logdecay.astype(BF16)
        rest = logdecay - high.astype(F32)
        mid = rest.astype(BF16)
        low = (rest - mid.astype(F32)).astype(BF16)
        parts = jnp.concatenate([high, mid, low], axis=1)
        to = lax.broadcasted_iota(jnp.int32, (rows, rows), 0)
        frm = lax.broadcasted_iota(jnp.int32, (rows, rows), 1)
        sums = dot(jnp.where(to >= frm, 1.0, 0.0).astype(BF16), parts)
        cum = sums[:, :heads] + sums[:, heads : 2 * heads] + sums[:, 2 * heads :]
        cum_ref[...] = cum
        cumt_ref[...] = cum.T

    weights = wi_ref[...]
    before = dot(halo_ref[...], weights).astype(BF16).astype(F32)
    rows_ref[:HALO, :] = jnp.where(place_ref[0] >= 1, before, 0.0)
    rows_ref[HALO:, :] = dot(normed_ref[...], weights).astype(BF16).astype(F32)
    columns = pl.ds(pl.multiple_of(tile * TILE, TILE), TILE)
    x = conv_silu(rows_ref, small_ref[:taps, columns], rows).astype(F32)
    first = tile * (TILE // head_size)
    xs = x * spread(step_ref[...], TILE, head_size, first)
    xs_ref[...] = xs.astype(BF16)
    cum = cum_ref[...]
    total = cum[rows - 1 :, :]
    left = spread(jnp.exp(total - cum), TILE, head_size, first)
    state = dot(bt_ref[...], (xs * left).astype(BF16))
    decay = spread(jnp.exp(total), TILE, head_size, first)

    @pl.when(g < tiles // 2)
    def _():
        write_payload(send_ref, state, decay)

    @pl.when(g >= tiles // 2)
    def _():
        write_payload(mine_ref, state, decay)


def tile_at(g, tiles, parity_ref):
    return lax.rem(g + (1 - parity_ref[0]) * (tiles // 2), tiles)


SMALL_TAPS = 4
SMALL_ROWS = 8


def local_call(tag, place, parity, normed, halo, bt, w_inner, w_step_t, small, after=()):
    rows, width = normed.shape
    inner = w_inner.shape[1]
    heads = w_step_t.shape[0]
    states = bt.shape[0]
    tiles = inner // TILE
    half = tiles // 2

    def whole(a):
        return pl.BlockSpec(a.shape, lambda g, place, parity: (0, 0))

    def tile(count):
        return pl.BlockSpec((count, TILE), lambda g, place, parity: (0, tile_at(g, tiles, parity)))

    payload = (states + EXTRA, TILE)
    return call(
        functools.partial(local_kernel, inner // heads),
        "local_" + tag,
        vmem=12,
        cost=micros(5.0),
        scalars=(place, parity),
        grid=(tiles,),
        in_specs=[whole(normed), whole(halo), whole(bt), tile(width), whole(w_step_t), whole(small)],
        out_specs=[
            tile(rows),
            pl.BlockSpec((rows, heads), lambda g, place, parity: (0, 0)),
            pl.BlockSpec((heads, rows), lambda g, place, parity: (0, 0)),
            pl.BlockSpec(payload, lambda g, place, parity: (0, jnp.minimum(g, half - 1))),
            pl.BlockSpec(payload, lambda g, place, parity: (0, jnp.maximum(g - half, 0))),
        ],
        out_shape=[
            jax.ShapeDtypeStruct((rows, inner), BF16),
            jax.ShapeDtypeStruct((rows, heads), F32),
            jax.ShapeDtypeStruct((heads, rows), F32),
            jax.ShapeDtypeStruct((states + EXTRA, inner // 2), BF16),
            jax.ShapeDtypeStruct((states + EXTRA, inner // 2), BF16),
        ],
        scratch=[pltpu.VMEM((rows + HALO, TILE), F32), pltpu.VMEM((rows, heads), F32)],
        after=after,
    )(place, parity, normed, halo, bt, w_inner, w_step_t, small)


def inside_kernel(head_size, xs_ref, bc_ref, cum_ref, cumt_ref, y_ref, state_ref, prev_ref):
    length, inner = xs_ref.shape
    states = bc_ref.shape[1] // 2
    heads = cum_ref.shape[1]

    @pl.when(pl.program_id(0) == 0)
    def _():
        state_ref[...] = jnp.zeros_like(state_ref)
        prev_ref[...] = jnp.zeros_like(prev_ref)

    bmat = bc_ref[:, :states]
    cmat = bc_ref[:, states:]
    to = lax.broadcasted_iota(jnp.int32, (length, length), 0)
    frm = lax.broadcasted_iota(jnp.int32, (length, length), 1)
    scores = jnp.where(to >= frm, dot_nt(cmat, bmat), 0.0)
    cum = cum_ref[...]
    cumt = cumt_ref[...]
    last = length - 1
    end = cum[last:, :]
    since = spread(jnp.exp(cum - prev_ref[...]), inner, head_size, 0)
    left = spread(jnp.exp(end - cum), inner, head_size, 0)
    state = state_ref[...]
    carried = dot(cmat, state.astype(BF16)) * since
    xs = xs_ref[...]
    scaled = (xs.astype(F32) * left).astype(BF16)
    state_ref[...] = state * since[last:, :] + dot_tn(bmat, scaled)
    prev_ref[...] = end
    pair = 2 * head_size
    lane = lax.broadcasted_iota(jnp.int32, (length, pair), 1)
    for p in range(heads // 2):
        weights = []
        for h in (2 * p, 2 * p + 1):
            apart = jnp.minimum(cum[:, h : h + 1] - cumt[h : h + 1, :], 0.0)
            weights.append((jnp.exp(apart) * scores).astype(BF16))
        mine = xs[:, p * pair : (p + 1) * pair]
        none = jnp.zeros_like(mine)
        stacked = jnp.concatenate(
            [jnp.where(lane < head_size, mine, none), jnp.where(lane < head_size, none, mine)], axis=0
        )
        inside = dot(jnp.concatenate(weights, axis=1), stacked)
        y_ref[:, p * pair : (p + 1) * pair] = (
            inside + carried[:, p * pair : (p + 1) * pair]
        ).astype(BF16)


def inside_call(tag, xs, bc, cum, cumt, after=()):
    rows, inner = xs.shape
    heads = cum.shape[1]
    both = bc.shape[1]

    def block(width):
        return pl.BlockSpec((CHUNK, width), lambda c: (c, 0))

    return call(
        functools.partial(inside_kernel, inner // heads),
        "inside_" + tag,
        vmem=8,
        cost=micros(3.2),
        grid=(rows // CHUNK,),
        in_specs=[
            block(inner),
            block(both),
            block(heads),
            pl.BlockSpec((heads, CHUNK), lambda c: (0, c)),
        ],
        out_specs=block(inner),
        out_shape=jax.ShapeDtypeStruct((rows, inner), BF16),
        scratch=[pltpu.VMEM((both // 2, inner), F32), pltpu.VMEM((1, heads), F32)],
        after=after,
    )(xs, bc, cum, cumt)


def parts_of(ref, known=None):
    states = ref.shape[0] - EXTRA
    state = ref[:states, :].astype(F32)
    extra = ref[states:, :].astype(F32)
    decay = extra[:1] + extra[1:2]
    if known is None:
        return state, decay
    return jnp.where(known, state, 0.0), jnp.where(known, decay, 0.0)


def write_payload(out_ref, state, decay):
    states = state.shape[0]
    out_ref[:states, :] = state.astype(BF16)
    decay = jnp.broadcast_to(decay, (EXTRA, decay.shape[1]))
    high = decay.astype(BF16).astype(F32)
    place = lax.broadcasted_iota(jnp.int32, decay.shape, 0)
    out_ref[states:, :] = jnp.where(place == 0, high, decay - high).astype(BF16)


def pair_kernel(place_ref, mine_ref, other_ref, out_ref):
    mine, mine_a = parts_of(mine_ref)
    other, other_a = parts_of(other_ref)
    is_first = lax.rem(place_ref[0], 2) == 0
    early = jnp.where(is_first, mine, other)
    late = jnp.where(is_first, other, mine)
    late_a = jnp.where(is_first, other_a, mine_a)
    write_payload(out_ref, late_a * early + late, mine_a * other_a)


def chain_kernel(reach, place_ref, pair_ref, before_ref, out_ref):
    pair, pair_a = parts_of(pair_ref)
    before, before_a = parts_of(before_ref, place_ref[0] >= reach)
    write_payload(out_ref, pair_a * before + pair, pair_a * before_a)


def longer_kernel(reach, farther_reach, place_ref, before_ref, farther_ref, out_ref):
    before, before_a = parts_of(before_ref, place_ref[0] >= reach)
    farther, farther_a = parts_of(farther_ref, place_ref[0] >= farther_reach)
    write_payload(out_ref, before + before_a * farther, before_a * farther_a)


def entry_kernel(reach, farther_reach, place_ref, mine_ref, other_ref, before_ref, farther_ref, keep_ref, send_ref):
    mine, mine_a = parts_of(mine_ref)
    other, other_a = parts_of(other_ref)
    before, before_a = parts_of(before_ref, place_ref[0] >= reach)
    farther, _ = parts_of(farther_ref, place_ref[0] >= farther_reach)
    is_first = lax.rem(place_ref[0], 2) == 0
    entry_first = before + before_a * farther
    early = jnp.where(is_first, mine, other)
    early_a = jnp.where(is_first, mine_a, other_a)
    entry_second = early_a * entry_first + early
    keep_ref[...] = jnp.where(is_first, entry_first, entry_second).astype(BF16)
    send_ref[...] = jnp.where(is_first, entry_second, entry_first).astype(BF16)


def small_call(kernel, name, place, arrays, shapes, after=()):
    vmem = pl.BlockSpec(memory_space=pltpu.VMEM)
    return call(
        kernel,
        name,
        vmem=4,
        cost=micros(0.5),
        scalars=(place,),
        in_specs=[vmem] * len(arrays),
        out_specs=[vmem] * len(shapes),
        out_shape=[jax.ShapeDtypeStruct(s, BF16) for s in shapes],
        after=after,
    )(place, *arrays)


def onward(value, by):
    count = lax.axis_size("seq")
    pairs = []
    for i in range(count):
        up = (i + by, 0) if i + by < count else (i, 1)
        down = (i - by, 1) if i - by >= 0 else (i, 0)
        pairs += [(2 * i, 2 * up[0] + up[1]), (2 * i + 1, 2 * down[0] + down[1])]
    return lax.ppermute(value, ("seq", "ch"), pairs)


class Chain:
    def __init__(self, tag, place, send, mine):
        self.tag, self.place, self.mine = tag, place, mine
        self.count = lax.axis_size("seq")
        self.swap = [(i, i ^ 1) for i in range(self.count)]
        self.other = lax.ppermute(send, "seq", self.swap)
        self.before = self.farther = None
        self.reach = self.farther_reach = 0
        self.apart = 2

    def pair(self, after):
        (self.pair_state,) = small_call(
            pair_kernel, "pair_" + self.tag, self.place, [self.mine, self.other], [self.mine.shape], after
        )
        self.running = self.pair_state
        self.hop()
        return self.pair_state

    def hop(self):
        if self.apart < self.count:
            self.arrived = onward(self.running, self.apart)

    def middle(self, after):
        while self.apart * 2 < self.count:
            self.take(after)
            (self.running,) = small_call(
                functools.partial(chain_kernel, self.reach),
                "chain_" + self.tag,
                self.place,
                [self.pair_state, self.before],
                [self.mine.shape],
                after,
            )
            self.apart *= 2
            self.hop()
        return self.running

    def take(self, after=()):
        if self.before is None:
            self.before, self.reach = self.arrived, self.apart
        else:
            (self.before,) = small_call(
                functools.partial(longer_kernel, self.reach, self.apart),
                "longer_" + self.tag,
                self.place,
                [self.before, self.arrived],
                [self.mine.shape],
                after,
            )
            self.reach = 0

    def entry(self, after):
        shape = self.mine.shape
        if self.apart < self.count:
            if self.before is None:
                self.before, self.reach = self.arrived, self.apart
                self.farther, self.farther_reach = self.arrived, self.count
            else:
                self.farther, self.farther_reach = self.arrived, self.apart
        else:
            self.before = self.farther = self.mine
            self.reach = self.farther_reach = self.count
        half = (shape[0] - EXTRA, shape[1])
        keep, out = small_call(
            functools.partial(entry_kernel, self.reach, self.farther_reach),
            "entry_" + self.tag,
            self.place,
            [self.mine, self.other, self.before, self.farther],
            [half, half],
            after,
        )
        return keep, lax.ppermute(out, "seq", self.swap)


def gated_part(head_size, swap, y_ref, bc_ref, cum_ref, keep_ref, other_ref, gate_ref, small_ref, wo_ref):
    inner = y_ref.shape[1]
    states = bc_ref.shape[1] // 2
    cmat = bc_ref[:, states:]
    keep = keep_ref[...]
    other = other_ref[...]
    entry = jnp.concatenate([jnp.where(swap, other, keep), jnp.where(swap, keep, other)], axis=1)
    carried = dot(cmat, entry) * spread(jnp.exp(cum_ref[...]), inner, head_size, 0)
    gated = (y_ref[...].astype(F32) + carried) * gate_ref[...].astype(F32)
    squares = jnp.sum(gated * gated, axis=-1, keepdims=True)
    gain = small_ref[SMALL_TAPS : SMALL_TAPS + 1, :]
    return dot((gated * gain).astype(BF16), wo_ref[...]), squares


def part_kernel(head_size, back_ref, parity_ref, *refs):
    *ins, out_ref, sq_ref = refs
    result, squares = gated_part(head_size, parity_ref[0] == 1, *ins)
    out_ref[...] = result
    sq_ref[...] = jnp.broadcast_to(squares, sq_ref.shape)


def finish_kernel(head_size, full_width, back_ref, parity_ref, *refs):
    *ins, part_ref, psq_ref, own_ref, send_ref = refs
    result, squares = gated_part(head_size, parity_ref[0] == 1, *ins)
    squares = squares + psq_ref[:, :1]
    result = (result + part_ref[...]) * lax.rsqrt(squares / full_width + EPS)
    result = result.astype(BF16)
    half = own_ref.shape[1]

    @pl.when(back_ref[0] == 1)
    def _():
        turned = flip_both(result)
        own_ref[...] = turned[:, half:]
        send_ref[...] = turned[:, :half]

    @pl.when(back_ref[0] != 1)
    def _():
        own_ref[...] = result[:, :half]
        send_ref[...] = result[:, half:]


def finish_call(back, parity, y, bc, cum, keep, other, gate, small, w_output, full_width=None, partial=None, after=()):
    rows, inner = y.shape
    width = w_output.shape[1]
    half = width // 2
    heads = cum.shape[1]
    count = rows // TILE

    def block(columns):
        return pl.BlockSpec((TILE, columns), lambda r, back, parity: (r, 0))

    def whole(a):
        return pl.BlockSpec(a.shape, lambda r, back, parity: (0, 0))

    def turned(r, back, parity):
        return (jnp.where(back[0] == 1, count - 1 - r, r), 0)

    in_specs = [
        block(inner),
        block(bc.shape[1]),
        block(heads),
        whole(keep),
        whole(other),
        block(inner),
        whole(small),
        whole(w_output),
    ]
    arrays = [y, bc, cum, keep, other, gate, small, w_output]
    if partial is None:
        kernel = functools.partial(part_kernel, inner // heads)
        out_specs = [block(width), block(128)]
        out_shape = [jax.ShapeDtypeStruct((rows, width), F32), jax.ShapeDtypeStruct((rows, 128), F32)]
    else:
        kernel = functools.partial(finish_kernel, inner // heads, full_width)
        in_specs += [block(width), block(128)]
        arrays += list(partial)
        out_specs = [pl.BlockSpec((TILE, half), turned)] * 2
        out_shape = [jax.ShapeDtypeStruct((rows, half), BF16)] * 2
    return call(
        kernel,
        "part" if partial is None else "finish",
        vmem=16,
        cost=micros(3.5),
        scalars=(back, parity),
        grid=(count,),
        in_specs=in_specs,
        out_specs=out_specs,
        out_shape=out_shape,
        after=after,
    )(back, parity, *arrays)


def total_kernel(mine_ref, theirs_ref, out_ref):
    out_ref[...] = (mine_ref[...].astype(F32) + theirs_ref[...].astype(F32)).astype(BF16)


def total_call(mine, theirs):
    rows, half = mine.shape
    block = pl.BlockSpec((CHUNK, half), lambda r: (r, 0))
    return call(
        total_kernel,
        "total",
        vmem=4,
        cost=micros(0.8),
        grid=(rows // CHUNK,),
        in_specs=[block, block],
        out_specs=block,
        out_shape=jax.ShapeDtypeStruct((rows, half), BF16),
    )(mine, theirs)


def body(
    tokens,
    hidden,
    embedding,
    w_gate,
    w_inner,
    w_state,
    w_step,
    conv_inner,
    conv_state,
    step_bias,
    decay_rate,
    norm_gain,
    w_output,
):
    swap = [(0, 1), (1, 0)]

    def theirs(a):
        return lax.ppermute(a, "ch", swap)

    core = lax.axis_index("ch").astype(jnp.int32)
    index = lax.axis_index("seq").astype(jnp.int32)
    last = lax.axis_size("seq") - 1
    back = core.reshape(1)
    parity = (index % 2).reshape(1)
    place = (index + core * (last - 2 * index)).reshape(1)
    w_inner_2 = theirs(w_inner)
    normed, tail, small = prepare_call(
        back, tokens, hidden, embedding, conv_inner, norm_gain, step_bias, decay_rate
    )
    halo = onward(tail, 1)
    small_2 = theirs(small)
    w_step_t = w_step.T
    w_step_2 = theirs(w_step_t)
    w_gate_2 = theirs(w_gate)
    w_output_2 = theirs(w_output)
    gate_1 = gate_call("own", normed, w_gate)
    bc, bt = maps_call(place, normed, halo, w_state, conv_state, after=[gate_1])
    xs_1, cum_1, cumt_1, send_1, mine_1 = local_call(
        "own", place, parity, normed, halo, bt, w_inner, w_step_t, small
    )
    chain_1 = Chain("own", place, send_1, mine_1)
    xs_2, cum_2, cumt_2, send_2, mine_2 = local_call(
        "other", place, parity, normed, halo, bt, w_inner_2, w_step_2, small_2, after=[mine_1]
    )
    chain_2 = Chain("other", place, send_2, mine_2)
    done = chain_1.pair(after=[xs_2])
    y_1 = inside_call("own", xs_1, bc, cum_1, cumt_1, after=[done])
    done = chain_1.middle(after=[y_1])
    done = chain_2.pair(after=[done])
    entry_1 = chain_1.entry(after=[done])
    y_2 = inside_call("other", xs_2, bc, cum_2, cumt_2, after=[entry_1[0]])
    done = chain_2.middle(after=[y_2])
    gate_2 = gate_call("other", normed, w_gate_2, after=[done])
    entry_2 = chain_2.entry(after=[gate_2])
    partial = finish_call(
        back, parity, y_1, bc, cum_1, *entry_1, gate_1, small, w_output, after=[entry_2[0]]
    )
    full_width = float(w_inner.shape[1] * lax.axis_size("ch"))
    mine, send = finish_call(
        back, parity, y_2, bc, cum_2, *entry_2, gate_2, small_2, w_output_2, full_width, partial
    )
    return total_call(mine, theirs(send))


def solution(mesh):
    return jax.shard_map(
        body,
        mesh=mesh,
        in_specs=(
            P(("win", "seq")),
            P(("win", "seq"), None),
            P(),
            P(None, "ch"),
            P(None, "ch"),
            P(),
            P(None, "ch"),
            P(None, "ch"),
            P(),
            P("ch"),
            P("ch"),
            P("ch"),
            P("ch", None),
        ),
        out_specs=P(("win", "seq"), "ch"),
        check_vma=False,
    )
```

```python
import functools

import jax
import jax.numpy as jnp
from jax import lax
from jax.experimental import pallas as pl
from jax.experimental.pallas import tpu as pltpu
from jax.sharding import PartitionSpec as P

F32 = jnp.float32
BF16 = jnp.bfloat16
EPS = 1e-05
HALO = 16
EXTRA = 16
CHUNK = 128
TILE = 256
MB = 1024 * 1024


def call(
    kernel, name, *, vmem, cost, scalars=(), grid=(), in_specs, out_specs, out_shape, scratch=(), after=()
):
    flops, moved, special = cost
    first = len(scalars) + len(in_specs)

    def body(*refs):
        kernel(*refs[:first], *refs[first + len(after) :])

    run = pl.pallas_call(
        body,
        grid_spec=pltpu.PrefetchScalarGridSpec(
            num_scalar_prefetch=len(scalars),
            grid=grid,
            in_specs=list(in_specs) + [pl.BlockSpec(memory_space=pl.ANY)] * len(after),
            out_specs=out_specs,
            scratch_shapes=scratch,
        ),
        out_shape=out_shape,
        compiler_params=pltpu.CompilerParams(
            vmem_limit_bytes=vmem * MB, dimension_semantics=("arbitrary",) * len(grid)
        ),
        cost_estimate=pl.CostEstimate(flops=flops, bytes_accessed=moved, transcendentals=special),
        name=name,
    )
    return lambda *arrays: run(*arrays, *after)


def micros(us):
    return (int(us * 1.1e9), int(us * 1e6), 0)


def dot(a, b):
    return jnp.dot(a, b, preferred_element_type=F32)


def dot_nt(a, b):
    return lax.dot_general(a, b, (((1,), (1,)), ((), ())), preferred_element_type=F32)


def dot_tn(a, b):
    return lax.dot_general(a, b, (((0,), (0,)), ((), ())), preferred_element_type=F32)


def flip_matrix(size):
    rows = lax.broadcasted_iota(jnp.int32, (size, size), 0)
    columns = lax.broadcasted_iota(jnp.int32, (size, size), 1)
    return jnp.where(rows + columns == size - 1, 1.0, 0.0).astype(BF16)


def flip_both(value):
    rows, width = value.shape
    turned = dot(flip_matrix(rows), value).astype(BF16)
    anti = flip_matrix(TILE)
    count = width // TILE
    blocks = [
        dot(turned[:, (count - 1 - k) * TILE : (count - k) * TILE], anti).astype(BF16)
        for k in range(count)
    ]
    return jnp.concatenate(blocks, axis=1)


def silu(v):
    half = 0.5 * v
    return half + half * jnp.tanh(half)


def two_parts(value):
    high = value.astype(BF16)
    low = (value - high.astype(F32)).astype(BF16)
    return jnp.concatenate([high, low], axis=1)


def spread(value, width, head_size, first_head):
    heads = value.shape[1]
    source = lax.broadcasted_iota(jnp.int32, (2 * heads, width), 0)
    source = jnp.where(source >= heads, source - heads, source)
    target = lax.broadcasted_iota(jnp.int32, (2 * heads, width), 1) // head_size + first_head
    onehot = jnp.where(source == target, 1.0, 0.0).astype(BF16)
    return dot(two_parts(value), onehot)


def prepare_kernel(
    back_ref,
    parity_ref,
    place_ref,
    hidden_hbm,
    tokens_hbm,
    emb_hbm,
    conv_hbm,
    gain_hbm,
    bias_hbm,
    rate_hbm,
    out_ref,
    tail_ref,
    small_ref,
    hidden_ref,
    tokens_ref,
    emb_ref,
    conv_ref,
    gain_ref,
    bias_ref,
    rate_ref,
    sems,
):
    rows = hidden_ref.shape[0]
    kinds = emb_ref.shape[0]
    taps, inner = conv_ref.shape
    heads = bias_ref.shape[1]
    count = rows // CHUNK
    back = back_ref[0] == 1
    whole = [
        (tokens_hbm, tokens_ref),
        (emb_hbm, emb_ref),
        (conv_hbm, conv_ref),
        (gain_hbm, gain_ref),
        (bias_hbm, bias_ref),
        (rate_hbm, rate_ref),
    ]
    small_copies = [pltpu.make_async_copy(src, dst, sems.at[count + i]) for i, (src, dst) in enumerate(whole)]
    parts = [pl.ds(r * CHUNK, CHUNK) for r in range(count)]
    copies = [
        pltpu.make_async_copy(hidden_hbm.at[part, :], hidden_ref.at[part, :], sems.at[r])
        for r, part in enumerate(parts)
    ]
    for copy in small_copies[:2] + copies + small_copies[2:]:
        copy.start()
    for copy in small_copies[:2]:
        copy.wait()
    kind = lax.broadcasted_iota(jnp.int32, (kinds, rows), 0)
    onehot = jnp.where(kind == tokens_ref[...], 1.0, 0.0).astype(BF16)
    for r in range(count):
        copies[r].wait()
        low, high = r * CHUNK, (r + 1) * CHUNK
        base = dot_tn(onehot[:, low:high], emb_ref[...])
        merged = (hidden_ref[low:high, :].astype(F32) + base).astype(BF16).astype(F32)
        mean = jnp.mean(merged * merged, axis=-1, keepdims=True)
        normed = (merged * lax.rsqrt(mean + EPS)).astype(BF16)

        @pl.when(back)
        def _():
            turned = flip_both(normed)
            out_ref[rows - high : rows - low, :] = turned
            if r == 0:
                tail_ref[...] = turned[CHUNK - HALO :, :]

        @pl.when(jnp.logical_not(back))
        def _():
            out_ref[low:high, :] = normed
            if r == count - 1:
                tail_ref[...] = normed[CHUNK - HALO :, :]

    for copy in small_copies[2:]:
        copy.wait()
    small_ref[:taps, :] = conv_ref[...]
    small_ref[taps : taps + 1, :] = gain_ref[...]
    small_ref[taps + 1 :, :] = jnp.zeros((SMALL_ROWS - taps - 1, inner), F32)
    small_ref[taps + 1 : taps + 2, :heads] = bias_ref[...]
    small_ref[taps + 2 : taps + 3, :heads] = rate_ref[...]


def prepare_call(scalars, hidden, tokens, embedding, conv, gain, bias, rate):
    rows, width = hidden.shape
    inner = conv.shape[1]
    vmem = pl.BlockSpec(memory_space=pltpu.VMEM)
    arrays = [hidden, tokens.reshape(1, -1), embedding, conv]
    arrays += [a.reshape(1, -1) for a in (gain, bias, rate)]
    return call(
        prepare_kernel,
        "prepare",
        vmem=12,
        cost=micros(1.5),
        scalars=scalars,
        in_specs=[pl.BlockSpec(memory_space=pltpu.HBM)] * len(arrays),
        out_specs=[vmem] * 3,
        out_shape=[
            jax.ShapeDtypeStruct((rows, width), BF16),
            jax.ShapeDtypeStruct((HALO, width), BF16),
            jax.ShapeDtypeStruct((SMALL_ROWS, inner), F32),
        ],
        scratch=[pltpu.VMEM(a.shape, a.dtype) for a in arrays]
        + [pltpu.SemaphoreType.DMA((rows // CHUNK + len(arrays) - 1,))],
    )(*scalars, *(pltpu.with_memory_space_constraint(a, pltpu.HBM) for a in arrays))


def gate_kernel(rows_ref, wg_ref, out_ref):
    gate = dot(rows_ref[...], wg_ref[...]).astype(BF16).astype(F32)
    out_ref[...] = silu(gate).astype(BF16)


def gate_call(tag, normed, w_gate, after=()):
    rows, width = normed.shape
    inner = w_gate.shape[1]
    return call(
        gate_kernel,
        "gate_" + tag,
        vmem=8,
        cost=micros(2.4),
        grid=(inner // TILE,),
        in_specs=[
            pl.BlockSpec((rows, width), lambda g: (0, 0)),
            pl.BlockSpec((width, TILE), lambda g: (0, g)),
        ],
        out_specs=pl.BlockSpec((rows, TILE), lambda g: (0, g)),
        out_shape=jax.ShapeDtypeStruct((rows, inner), BF16),
        after=after,
    )(normed, w_gate)


def conv_silu(rows_ref, weights, rows):
    taps = weights.shape[0]
    total = None
    for k in range(taps):
        offset = HALO - (taps - 1) + k
        term = weights[k : k + 1, :] * rows_ref[offset : offset + rows, :]
        total = term if total is None else total + term
    return silu(total).astype(BF16)


def maps_kernel(place_ref, normed_ref, halo_ref, ws_ref, cs_ref, bc_ref, bt_ref, rows_ref):
    rows = normed_ref.shape[0]
    states = bc_ref.shape[1] // 2
    before = dot(halo_ref[...], ws_ref[...]).astype(BF16).astype(F32)
    rows_ref[:HALO, :] = jnp.where(place_ref[0] >= 1, before, 0.0)
    rows_ref[HALO:, :] = dot(normed_ref[...], ws_ref[...]).astype(BF16).astype(F32)
    state_conv = conv_silu(rows_ref, cs_ref[...], rows)
    bc_ref[...] = state_conv
    bt_ref[...] = state_conv[:, :states].astype(F32).T.astype(BF16)


def maps_call(place, normed, halo, w_state, conv_state, after=()):
    rows = normed.shape[0]
    both = w_state.shape[1]
    vmem = pl.BlockSpec(memory_space=pltpu.VMEM)
    return call(
        maps_kernel,
        "maps",
        vmem=8,
        cost=micros(1.5),
        scalars=(place,),
        in_specs=[vmem] * 4,
        out_specs=[vmem] * 2,
        out_shape=[
            jax.ShapeDtypeStruct((rows, both), BF16),
            jax.ShapeDtypeStruct((both // 2, rows), BF16),
        ],
        scratch=[pltpu.VMEM((rows + HALO, both), F32)],
        after=after,
    )(place, normed, halo, w_state, conv_state)


def local_kernel(
    head_size,
    place_ref,
    parity_ref,
    normed_ref,
    halo_ref,
    bt_ref,
    wi_ref,
    wt_ref,
    small_ref,
    xs_ref,
    cum_ref,
    cumt_ref,
    send_ref,
    mine_ref,
    rows_ref,
    step_ref,
):
    rows = normed_ref.shape[0]
    states = bt_ref.shape[0]
    heads = wt_ref.shape[0]
    taps = SMALL_TAPS
    tiles = pl.num_programs(0)
    g = pl.program_id(0)
    tile = tile_at(g, tiles, parity_ref)

    @pl.when(g == 0)
    def _():
        bias = small_ref[taps + 1 : taps + 2, :heads]
        rate = small_ref[taps + 2 : taps + 3, :heads]
        raw = dot_nt(normed_ref[...], wt_ref[...]) + bias
        step = jnp.maximum(raw, 0.0) + jnp.log1p(jnp.exp(-jnp.abs(raw)))
        step_ref[...] = step
        logdecay = -step * rate
        high = logdecay.astype(BF16)
        rest = logdecay - high.astype(F32)
        mid = rest.astype(BF16)
        low = (rest - mid.astype(F32)).astype(BF16)
        parts = jnp.concatenate([high, mid, low], axis=1)
        to = lax.broadcasted_iota(jnp.int32, (rows, rows), 0)
        frm = lax.broadcasted_iota(jnp.int32, (rows, rows), 1)
        sums = dot(jnp.where(to >= frm, 1.0, 0.0).astype(BF16), parts)
        cum = sums[:, :heads] + sums[:, heads : 2 * heads] + sums[:, 2 * heads :]
        cum_ref[...] = cum
        cumt_ref[...] = cum.T

    weights = wi_ref[...]
    before = dot(halo_ref[...], weights).astype(BF16).astype(F32)
    rows_ref[:HALO, :] = jnp.where(place_ref[0] >= 1, before, 0.0)
    rows_ref[HALO:, :] = dot(normed_ref[...], weights).astype(BF16).astype(F32)
    columns = pl.ds(pl.multiple_of(tile * TILE, TILE), TILE)
    x = conv_silu(rows_ref, small_ref[:taps, columns], rows).astype(F32)
    first = tile * (TILE // head_size)
    xs = x * spread(step_ref[...], TILE, head_size, first)
    xs_ref[...] = xs.astype(BF16)
    cum = cum_ref[...]
    total = cum[rows - 1 :, :]
    left = spread(jnp.exp(total - cum), TILE, head_size, first)
    state = dot(bt_ref[...], (xs * left).astype(BF16))
    decay = spread(jnp.exp(total), TILE, head_size, first)

    @pl.when(g < tiles // 2)
    def _():
        write_payload(send_ref, state, decay)

    @pl.when(g >= tiles // 2)
    def _():
        write_payload(mine_ref, state, decay)


def tile_at(g, tiles, parity_ref):
    return lax.rem(g + (1 - parity_ref[0]) * (tiles // 2), tiles)


SMALL_TAPS = 4
SMALL_ROWS = 8


def local_call(tag, place, parity, normed, halo, bt, w_inner, w_step_t, small, after=()):
    rows, width = normed.shape
    inner = w_inner.shape[1]
    heads = w_step_t.shape[0]
    states = bt.shape[0]
    tiles = inner // TILE
    half = tiles // 2

    def whole(a):
        return pl.BlockSpec(a.shape, lambda g, place, parity: (0, 0))

    def tile(count):
        return pl.BlockSpec((count, TILE), lambda g, place, parity: (0, tile_at(g, tiles, parity)))

    payload = (states + EXTRA, TILE)
    return call(
        functools.partial(local_kernel, inner // heads),
        "local_" + tag,
        vmem=12,
        cost=micros(5.0),
        scalars=(place, parity),
        grid=(tiles,),
        in_specs=[whole(normed), whole(halo), whole(bt), tile(width), whole(w_step_t), whole(small)],
        out_specs=[
            tile(rows),
            pl.BlockSpec((rows, heads), lambda g, place, parity: (0, 0)),
            pl.BlockSpec((heads, rows), lambda g, place, parity: (0, 0)),
            pl.BlockSpec(payload, lambda g, place, parity: (0, jnp.minimum(g, half - 1))),
            pl.BlockSpec(payload, lambda g, place, parity: (0, jnp.maximum(g - half, 0))),
        ],
        out_shape=[
            jax.ShapeDtypeStruct((rows, inner), BF16),
            jax.ShapeDtypeStruct((rows, heads), F32),
            jax.ShapeDtypeStruct((heads, rows), F32),
            jax.ShapeDtypeStruct((states + EXTRA, inner // 2), BF16),
            jax.ShapeDtypeStruct((states + EXTRA, inner // 2), BF16),
        ],
        scratch=[pltpu.VMEM((rows + HALO, TILE), F32), pltpu.VMEM((rows, heads), F32)],
        after=after,
    )(place, parity, normed, halo, bt, w_inner, w_step_t, small)


def inside_kernel(head_size, xs_ref, bc_ref, cum_ref, cumt_ref, y_ref, state_ref, prev_ref):
    length, inner = xs_ref.shape
    states = bc_ref.shape[1] // 2
    heads = cum_ref.shape[1]

    @pl.when(pl.program_id(0) == 0)
    def _():
        state_ref[...] = jnp.zeros_like(state_ref)
        prev_ref[...] = jnp.zeros_like(prev_ref)

    bmat = bc_ref[:, :states]
    cmat = bc_ref[:, states:]
    to = lax.broadcasted_iota(jnp.int32, (length, length), 0)
    frm = lax.broadcasted_iota(jnp.int32, (length, length), 1)
    scores = jnp.where(to >= frm, dot_nt(cmat, bmat), 0.0)
    cum = cum_ref[...]
    cumt = cumt_ref[...]
    last = length - 1
    end = cum[last:, :]
    since = spread(jnp.exp(cum - prev_ref[...]), inner, head_size, 0)
    left = spread(jnp.exp(end - cum), inner, head_size, 0)
    state = state_ref[...]
    carried = dot(cmat, state.astype(BF16)) * since
    xs = xs_ref[...]
    scaled = (xs.astype(F32) * left).astype(BF16)
    state_ref[...] = state * since[last:, :] + dot_tn(bmat, scaled)
    prev_ref[...] = end
    pair = 2 * head_size
    lane = lax.broadcasted_iota(jnp.int32, (length, pair), 1)
    for p in range(heads // 2):
        weights = []
        for h in (2 * p, 2 * p + 1):
            apart = jnp.minimum(cum[:, h : h + 1] - cumt[h : h + 1, :], 0.0)
            weights.append((jnp.exp(apart) * scores).astype(BF16))
        mine = xs[:, p * pair : (p + 1) * pair]
        none = jnp.zeros_like(mine)
        stacked = jnp.concatenate(
            [jnp.where(lane < head_size, mine, none), jnp.where(lane < head_size, none, mine)], axis=0
        )
        inside = dot(jnp.concatenate(weights, axis=1), stacked)
        y_ref[:, p * pair : (p + 1) * pair] = (
            inside + carried[:, p * pair : (p + 1) * pair]
        ).astype(BF16)


def inside_call(tag, xs, bc, cum, cumt, after=()):
    rows, inner = xs.shape
    heads = cum.shape[1]
    both = bc.shape[1]

    def block(width):
        return pl.BlockSpec((CHUNK, width), lambda c: (c, 0))

    return call(
        functools.partial(inside_kernel, inner // heads),
        "inside_" + tag,
        vmem=8,
        cost=micros(3.2),
        grid=(rows // CHUNK,),
        in_specs=[
            block(inner),
            block(both),
            block(heads),
            pl.BlockSpec((heads, CHUNK), lambda c: (0, c)),
        ],
        out_specs=block(inner),
        out_shape=jax.ShapeDtypeStruct((rows, inner), BF16),
        scratch=[pltpu.VMEM((both // 2, inner), F32), pltpu.VMEM((1, heads), F32)],
        after=after,
    )(xs, bc, cum, cumt)


def parts_of(ref, known=None):
    states = ref.shape[0] - EXTRA
    state = ref[:states, :].astype(F32)
    extra = ref[states:, :].astype(F32)
    decay = extra[:1] + extra[1:2]
    if known is None:
        return state, decay
    return jnp.where(known, state, 0.0), jnp.where(known, decay, 0.0)


def write_payload(out_ref, state, decay):
    states = state.shape[0]
    out_ref[:states, :] = state.astype(BF16)
    decay = jnp.broadcast_to(decay, (EXTRA, decay.shape[1]))
    high = decay.astype(BF16).astype(F32)
    place = lax.broadcasted_iota(jnp.int32, decay.shape, 0)
    out_ref[states:, :] = jnp.where(place == 0, high, decay - high).astype(BF16)


def pair_kernel(place_ref, mine_ref, other_ref, out_ref):
    mine, mine_a = parts_of(mine_ref)
    other, other_a = parts_of(other_ref)
    is_first = lax.rem(place_ref[0], 2) == 0
    early = jnp.where(is_first, mine, other)
    late = jnp.where(is_first, other, mine)
    late_a = jnp.where(is_first, other_a, mine_a)
    write_payload(out_ref, late_a * early + late, mine_a * other_a)


def chain_kernel(reach, place_ref, pair_ref, before_ref, out_ref):
    pair, pair_a = parts_of(pair_ref)
    before, before_a = parts_of(before_ref, place_ref[0] >= reach)
    write_payload(out_ref, pair_a * before + pair, pair_a * before_a)


def longer_kernel(reach, farther_reach, place_ref, before_ref, farther_ref, out_ref):
    before, before_a = parts_of(before_ref, place_ref[0] >= reach)
    farther, farther_a = parts_of(farther_ref, place_ref[0] >= farther_reach)
    write_payload(out_ref, before + before_a * farther, before_a * farther_a)


def entry_kernel(reach, farther_reach, place_ref, mine_ref, other_ref, before_ref, farther_ref, keep_ref, send_ref):
    mine, mine_a = parts_of(mine_ref)
    other, other_a = parts_of(other_ref)
    before, before_a = parts_of(before_ref, place_ref[0] >= reach)
    farther, _ = parts_of(farther_ref, place_ref[0] >= farther_reach)
    is_first = lax.rem(place_ref[0], 2) == 0
    entry_first = before + before_a * farther
    early = jnp.where(is_first, mine, other)
    early_a = jnp.where(is_first, mine_a, other_a)
    entry_second = early_a * entry_first + early
    keep_ref[...] = jnp.where(is_first, entry_first, entry_second).astype(BF16)
    send_ref[...] = jnp.where(is_first, entry_second, entry_first).astype(BF16)


def small_call(kernel, name, place, arrays, shapes, after=()):
    vmem = pl.BlockSpec(memory_space=pltpu.VMEM)
    return call(
        kernel,
        name,
        vmem=4,
        cost=micros(0.5),
        scalars=(place,),
        in_specs=[vmem] * len(arrays),
        out_specs=[vmem] * len(shapes),
        out_shape=[jax.ShapeDtypeStruct(s, BF16) for s in shapes],
        after=after,
    )(place, *arrays)


def onward(value, by):
    count = lax.axis_size("seq")
    pairs = []
    for i in range(count):
        up = (i + by, 0) if i + by < count else (i, 1)
        down = (i - by, 1) if i - by >= 0 else (i, 0)
        pairs += [(2 * i, 2 * up[0] + up[1]), (2 * i + 1, 2 * down[0] + down[1])]
    return lax.ppermute(value, ("seq", "ch"), pairs)


class Chain:
    def __init__(self, tag, place, send, mine):
        self.tag, self.place, self.mine = tag, place, mine
        self.count = lax.axis_size("seq")
        self.swap = [(i, i ^ 1) for i in range(self.count)]
        self.other = lax.ppermute(send, "seq", self.swap)
        self.before = self.farther = None
        self.reach = self.farther_reach = 0
        self.apart = 2

    def pair(self, after):
        (self.pair_state,) = small_call(
            pair_kernel, "pair_" + self.tag, self.place, [self.mine, self.other], [self.mine.shape], after
        )
        self.running = self.pair_state
        self.hop()
        return self.pair_state

    def hop(self):
        if self.apart < self.count:
            self.arrived = onward(self.running, self.apart)

    def middle(self, after):
        while self.apart * 2 < self.count:
            self.take(after)
            (self.running,) = small_call(
                functools.partial(chain_kernel, self.reach),
                "chain_" + self.tag,
                self.place,
                [self.pair_state, self.before],
                [self.mine.shape],
                after,
            )
            self.apart *= 2
            self.hop()
        return self.running

    def take(self, after=()):
        if self.before is None:
            self.before, self.reach = self.arrived, self.apart
        else:
            (self.before,) = small_call(
                functools.partial(longer_kernel, self.reach, self.apart),
                "longer_" + self.tag,
                self.place,
                [self.before, self.arrived],
                [self.mine.shape],
                after,
            )
            self.reach = 0

    def entry(self, after):
        shape = self.mine.shape
        if self.apart < self.count:
            if self.before is None:
                self.before, self.reach = self.arrived, self.apart
                self.farther, self.farther_reach = self.arrived, self.count
            else:
                self.farther, self.farther_reach = self.arrived, self.apart
        else:
            self.before = self.farther = self.mine
            self.reach = self.farther_reach = self.count
        half = (shape[0] - EXTRA, shape[1])
        keep, out = small_call(
            functools.partial(entry_kernel, self.reach, self.farther_reach),
            "entry_" + self.tag,
            self.place,
            [self.mine, self.other, self.before, self.farther],
            [half, half],
            after,
        )
        return keep, lax.ppermute(out, "seq", self.swap)


def gated_part(head_size, swap, y_ref, bc_ref, cum_ref, keep_ref, other_ref, gate_ref, small_ref, wo_ref):
    inner = y_ref.shape[1]
    states = bc_ref.shape[1] // 2
    cmat = bc_ref[:, states:]
    keep = keep_ref[...]
    other = other_ref[...]
    entry = jnp.concatenate([jnp.where(swap, other, keep), jnp.where(swap, keep, other)], axis=1)
    carried = dot(cmat, entry) * spread(jnp.exp(cum_ref[...]), inner, head_size, 0)
    gated = (y_ref[...].astype(F32) + carried) * gate_ref[...].astype(F32)
    squares = jnp.sum(gated * gated, axis=-1, keepdims=True)
    gain = small_ref[SMALL_TAPS : SMALL_TAPS + 1, :]
    return dot((gated * gain).astype(BF16), wo_ref[...]), squares


def part_kernel(head_size, back_ref, parity_ref, *refs):
    *ins, out_ref, sq_ref = refs
    result, squares = gated_part(head_size, parity_ref[0] == 1, *ins)
    out_ref[...] = result
    sq_ref[...] = jnp.broadcast_to(squares, sq_ref.shape)


def finish_kernel(head_size, full_width, back_ref, parity_ref, *refs):
    *ins, part_ref, psq_ref, own_ref, send_ref = refs
    result, squares = gated_part(head_size, parity_ref[0] == 1, *ins)
    squares = squares + psq_ref[:, :1]
    result = (result + part_ref[...]) * lax.rsqrt(squares / full_width + EPS)
    result = result.astype(BF16)
    half = own_ref.shape[1]

    @pl.when(back_ref[0] == 1)
    def _():
        turned = flip_both(result)
        own_ref[...] = turned[:, half:]
        send_ref[...] = turned[:, :half]

    @pl.when(back_ref[0] != 1)
    def _():
        own_ref[...] = result[:, :half]
        send_ref[...] = result[:, half:]


def finish_call(back, parity, y, bc, cum, keep, other, gate, small, w_output, full_width=None, partial=None, after=()):
    rows, inner = y.shape
    width = w_output.shape[1]
    half = width // 2
    heads = cum.shape[1]
    count = rows // TILE

    def block(columns):
        return pl.BlockSpec((TILE, columns), lambda r, back, parity: (r, 0))

    def whole(a):
        return pl.BlockSpec(a.shape, lambda r, back, parity: (0, 0))

    def turned(r, back, parity):
        return (jnp.where(back[0] == 1, count - 1 - r, r), 0)

    in_specs = [
        block(inner),
        block(bc.shape[1]),
        block(heads),
        whole(keep),
        whole(other),
        block(inner),
        whole(small),
        whole(w_output),
    ]
    arrays = [y, bc, cum, keep, other, gate, small, w_output]
    if partial is None:
        kernel = functools.partial(part_kernel, inner // heads)
        out_specs = [block(width), block(128)]
        out_shape = [jax.ShapeDtypeStruct((rows, width), F32), jax.ShapeDtypeStruct((rows, 128), F32)]
    else:
        kernel = functools.partial(finish_kernel, inner // heads, full_width)
        in_specs += [block(width), block(128)]
        arrays += list(partial)
        out_specs = [pl.BlockSpec((TILE, half), turned)] * 2
        out_shape = [jax.ShapeDtypeStruct((rows, half), BF16)] * 2
    return call(
        kernel,
        "part" if partial is None else "finish",
        vmem=16,
        cost=micros(3.5),
        scalars=(back, parity),
        grid=(count,),
        in_specs=in_specs,
        out_specs=out_specs,
        out_shape=out_shape,
        after=after,
    )(back, parity, *arrays)


def total_kernel(mine_ref, theirs_ref, out_ref):
    out_ref[...] = (mine_ref[...].astype(F32) + theirs_ref[...].astype(F32)).astype(BF16)


def total_call(mine, theirs):
    rows, half = mine.shape
    block = pl.BlockSpec((CHUNK, half), lambda r: (r, 0))
    return call(
        total_kernel,
        "total",
        vmem=4,
        cost=micros(0.8),
        grid=(rows // CHUNK,),
        in_specs=[block, block],
        out_specs=block,
        out_shape=jax.ShapeDtypeStruct((rows, half), BF16),
    )(mine, theirs)


def body(
    tokens,
    hidden,
    embedding,
    w_gate,
    w_inner,
    w_state,
    w_step,
    conv_inner,
    conv_state,
    step_bias,
    decay_rate,
    norm_gain,
    w_output,
):
    swap = [(0, 1), (1, 0)]

    def theirs(a):
        return lax.ppermute(a, "ch", swap)

    core = lax.axis_index("ch").astype(jnp.int32)
    index = lax.axis_index("seq").astype(jnp.int32)
    last = lax.axis_size("seq") - 1
    back = core.reshape(1)
    parity = (index & 1).reshape(1)
    place = (index + core * (last - 2 * index)).reshape(1)
    w_inner_2 = theirs(w_inner)
    normed, tail, small = prepare_call(
        (back, parity, place), hidden, tokens, embedding, conv_inner, norm_gain, step_bias, decay_rate
    )
    halo = onward(tail, 1)
    small_2 = theirs(small)
    w_step_t = w_step.T
    w_step_2 = theirs(w_step_t)
    w_gate_2 = theirs(w_gate)
    w_output_2 = theirs(w_output)
    gate_1 = gate_call("own", normed, w_gate)
    bc, bt = maps_call(place, normed, halo, w_state, conv_state, after=[gate_1])
    xs_1, cum_1, cumt_1, send_1, mine_1 = local_call(
        "own", place, parity, normed, halo, bt, w_inner, w_step_t, small
    )
    chain_1 = Chain("own", place, send_1, mine_1)
    xs_2, cum_2, cumt_2, send_2, mine_2 = local_call(
        "other", place, parity, normed, halo, bt, w_inner_2, w_step_2, small_2, after=[mine_1]
    )
    chain_2 = Chain("other", place, send_2, mine_2)
    done = chain_1.pair(after=[xs_2])
    y_1 = inside_call("own", xs_1, bc, cum_1, cumt_1, after=[done])
    done = chain_1.middle(after=[y_1])
    done = chain_2.pair(after=[done])
    entry_1 = chain_1.entry(after=[done])
    y_2 = inside_call("other", xs_2, bc, cum_2, cumt_2, after=[entry_1[0]])
    done = chain_2.middle(after=[y_2])
    gate_2 = gate_call("other", normed, w_gate_2, after=[done])
    entry_2 = chain_2.entry(after=[gate_2])
    partial = finish_call(
        back, parity, y_1, bc, cum_1, *entry_1, gate_1, small, w_output, after=[entry_2[0]]
    )
    full_width = float(w_inner.shape[1] * lax.axis_size("ch"))
    mine, send = finish_call(
        back, parity, y_2, bc, cum_2, *entry_2, gate_2, small_2, w_output_2, full_width, partial
    )
    return total_call(mine, theirs(send))


def solution(mesh):
    return jax.shard_map(
        body,
        mesh=mesh,
        in_specs=(
            P(("win", "seq")),
            P(("win", "seq"), None),
            P(),
            P(None, "ch"),
            P(None, "ch"),
            P(),
            P(None, "ch"),
            P(None, "ch"),
            P(),
            P("ch"),
            P("ch"),
            P("ch"),
            P("ch", None),
        ),
        out_specs=P(("win", "seq"), "ch"),
        check_vma=False,
    )
```

```python
import functools

import jax
import jax.numpy as jnp
from jax import lax
from jax.experimental import pallas as pl
from jax.experimental.pallas import tpu as pltpu
from jax.sharding import PartitionSpec as P

F32 = jnp.float32
BF16 = jnp.bfloat16
EPS = 1e-05
HALO = 16
EXTRA = 16
CHUNK = 128
TILE = 256
BLOCK = 64
MB = 1024 * 1024


def call(
    kernel, name, *, vmem, cost, scalars=(), grid=(), in_specs, out_specs, out_shape, scratch=(), after=()
):
    flops, moved, special = cost
    first = len(scalars) + len(in_specs)

    def body(*refs):
        kernel(*refs[:first], *refs[first + len(after) :])

    run = pl.pallas_call(
        body,
        grid_spec=pltpu.PrefetchScalarGridSpec(
            num_scalar_prefetch=len(scalars),
            grid=grid,
            in_specs=list(in_specs) + [pl.BlockSpec(memory_space=pl.ANY)] * len(after),
            out_specs=out_specs,
            scratch_shapes=scratch,
        ),
        out_shape=out_shape,
        compiler_params=pltpu.CompilerParams(
            vmem_limit_bytes=vmem * MB, dimension_semantics=("arbitrary",) * len(grid)
        ),
        cost_estimate=pl.CostEstimate(flops=flops, bytes_accessed=moved, transcendentals=special),
        name=name,
    )
    return lambda *arrays: run(*arrays, *after)


def micros(us):
    return (int(us * 1.1e9), int(us * 1e6), 0)


def dot(a, b):
    return jnp.dot(a, b, preferred_element_type=F32)


def dot_nt(a, b):
    return lax.dot_general(a, b, (((1,), (1,)), ((), ())), preferred_element_type=F32)


def dot_tn(a, b):
    return lax.dot_general(a, b, (((0,), (0,)), ((), ())), preferred_element_type=F32)


def flip_matrix(size):
    rows = lax.broadcasted_iota(jnp.int32, (size, size), 0)
    columns = lax.broadcasted_iota(jnp.int32, (size, size), 1)
    return jnp.where(rows + columns == size - 1, 1.0, 0.0).astype(BF16)


def flip_both(value):
    rows, width = value.shape
    turned = dot(flip_matrix(rows), value).astype(BF16)
    anti = flip_matrix(TILE)
    count = width // TILE
    blocks = [
        dot(turned[:, (count - 1 - k) * TILE : (count - k) * TILE], anti).astype(BF16)
        for k in range(count)
    ]
    return jnp.concatenate(blocks, axis=1)


def silu(v):
    half = 0.5 * v
    return half + half * jnp.tanh(half)


def two_parts(value):
    high = value.astype(BF16)
    low = (value - high.astype(F32)).astype(BF16)
    return jnp.concatenate([high, low], axis=1)


def head_matrix(heads, width, head_size, first_head):
    source = lax.broadcasted_iota(jnp.int32, (2 * heads, width), 0)
    source = jnp.where(source >= heads, source - heads, source)
    target = lax.broadcasted_iota(jnp.int32, (2 * heads, width), 1) // head_size + first_head
    return jnp.where(source == target, 1.0, 0.0).astype(BF16)


def prepare_kernel(
    back_ref,
    parity_ref,
    place_ref,
    hidden_hbm,
    tokens_hbm,
    emb_hbm,
    conv_hbm,
    gain_hbm,
    bias_hbm,
    rate_hbm,
    out_ref,
    tail_ref,
    small_ref,
    hidden_ref,
    tokens_ref,
    emb_ref,
    conv_ref,
    gain_ref,
    bias_ref,
    rate_ref,
    base_ref,
    normed_ref,
    sems,
):
    rows = hidden_ref.shape[0]
    kinds = emb_ref.shape[0]
    taps, inner = conv_ref.shape
    heads = bias_ref.shape[1]
    count = rows // CHUNK
    back = back_ref[0] == 1
    whole = [
        (tokens_hbm, tokens_ref),
        (emb_hbm, emb_ref),
        (conv_hbm, conv_ref),
        (gain_hbm, gain_ref),
        (bias_hbm, bias_ref),
        (rate_hbm, rate_ref),
    ]
    small_copies = [pltpu.make_async_copy(src, dst, sems.at[count + i]) for i, (src, dst) in enumerate(whole)]
    parts = [pl.ds(r * CHUNK, CHUNK) for r in range(count)]
    copies = [
        pltpu.make_async_copy(hidden_hbm.at[part, :], hidden_ref.at[part, :], sems.at[r])
        for r, part in enumerate(parts)
    ]
    for copy in small_copies[:2] + copies + small_copies[2:]:
        copy.start()
    for copy in small_copies[:2]:
        copy.wait()
    kind = lax.broadcasted_iota(jnp.int32, (kinds, rows), 0)
    onehot = jnp.where(kind == tokens_ref[...], 1.0, 0.0).astype(BF16)
    for r in range(count):
        copies[r].wait()
        low, high = r * CHUNK, (r + 1) * CHUNK
        base_ref[...] = dot_tn(onehot[:, low:high], emb_ref[...])
        for q in range(low, high, HALO):
            block = slice(q, q + HALO)
            merged = hidden_ref[block, :].astype(F32) + base_ref[q - low : q - low + HALO, :]
            merged = merged.astype(BF16).astype(F32)
            mean = jnp.mean(merged * merged, axis=-1, keepdims=True)
            normed_ref[q - low : q - low + HALO, :] = (merged * lax.rsqrt(mean + EPS)).astype(BF16)

        @pl.when(back)
        def _():
            out_ref[rows - high : rows - low, :] = flip_both(normed_ref[...])

        @pl.when(jnp.logical_not(back))
        def _():
            out_ref[low:high, :] = normed_ref[...]

    tail_ref[...] = out_ref[rows - HALO :, :]
    for copy in small_copies[2:]:
        copy.wait()
    small_ref[:taps, :] = conv_ref[...]
    small_ref[taps : taps + 1, :] = gain_ref[...]
    small_ref[taps + 1 :, :] = jnp.zeros((SMALL_ROWS - taps - 1, inner), F32)
    small_ref[taps + 1 : taps + 2, :heads] = bias_ref[...]
    small_ref[taps + 2 : taps + 3, :heads] = rate_ref[...]


def prepare_call(scalars, hidden, tokens, embedding, conv, gain, bias, rate):
    rows, width = hidden.shape
    inner = conv.shape[1]
    vmem = pl.BlockSpec(memory_space=pltpu.VMEM)
    arrays = [hidden, tokens.reshape(1, -1), embedding, conv]
    arrays += [a.reshape(1, -1) for a in (gain, bias, rate)]
    return call(
        prepare_kernel,
        "prepare",
        vmem=12,
        cost=micros(1.5),
        scalars=scalars,
        in_specs=[pl.BlockSpec(memory_space=pltpu.HBM)] * len(arrays),
        out_specs=[vmem] * 3,
        out_shape=[
            jax.ShapeDtypeStruct((rows, width), BF16),
            jax.ShapeDtypeStruct((HALO, width), BF16),
            jax.ShapeDtypeStruct((SMALL_ROWS, inner), F32),
        ],
        scratch=[pltpu.VMEM(a.shape, a.dtype) for a in arrays]
        + [pltpu.VMEM((CHUNK, width), F32), pltpu.VMEM((CHUNK, width), BF16)]
        + [pltpu.SemaphoreType.DMA((rows // CHUNK + len(arrays) - 1,))],
    )(*scalars, *(pltpu.with_memory_space_constraint(a, pltpu.HBM) for a in arrays))


def gate_kernel(rows_ref, wg_ref, out_ref, gate_ref):
    gate_ref[...] = dot(rows_ref[...], wg_ref[...])
    for r in range(0, gate_ref.shape[0], BLOCK):
        gate = gate_ref[r : r + BLOCK, :].astype(BF16).astype(F32)
        out_ref[r : r + BLOCK, :] = silu(gate).astype(BF16)


def gate_call(tag, normed, w_gate, after=()):
    rows, width = normed.shape
    inner = w_gate.shape[1]
    return call(
        gate_kernel,
        "gate_" + tag,
        vmem=8,
        cost=micros(2.4),
        grid=(inner // TILE,),
        in_specs=[
            pl.BlockSpec((rows, width), lambda g: (0, 0)),
            pl.BlockSpec((width, TILE), lambda g: (0, g)),
        ],
        out_specs=pl.BlockSpec((rows, TILE), lambda g: (0, g)),
        out_shape=jax.ShapeDtypeStruct((rows, inner), BF16),
        scratch=[pltpu.VMEM((rows, TILE), F32)],
        after=after,
    )(normed, w_gate)


def conv_silu(rows_ref, weights, row):
    taps = weights.shape[0]
    total = None
    for k in range(taps):
        offset = HALO - (taps - 1) + k + row
        term = weights[k : k + 1, :] * rows_ref[offset : offset + BLOCK, :]
        total = term if total is None else total + term
    return silu(total).astype(BF16)


def maps_kernel(place_ref, normed_ref, halo_ref, ws_ref, cs_ref, bc_ref, bt_ref, rows_ref):
    rows = normed_ref.shape[0]
    states = bc_ref.shape[1] // 2
    before = dot(halo_ref[...], ws_ref[...]).astype(BF16).astype(F32)
    rows_ref[:HALO, :] = jnp.where(place_ref[0] >= 1, before, 0.0)
    rows_ref[HALO:, :] = dot(normed_ref[...], ws_ref[...]).astype(BF16).astype(F32)
    weights = cs_ref[...]
    for r in range(0, rows, BLOCK):
        bc_ref[r : r + BLOCK, :] = conv_silu(rows_ref, weights, r)
    bt_ref[...] = bc_ref[:, :states].astype(F32).T.astype(BF16)


def maps_call(place, normed, halo, w_state, conv_state, after=()):
    rows = normed.shape[0]
    both = w_state.shape[1]
    vmem = pl.BlockSpec(memory_space=pltpu.VMEM)
    return call(
        maps_kernel,
        "maps",
        vmem=8,
        cost=micros(1.5),
        scalars=(place,),
        in_specs=[vmem] * 4,
        out_specs=[vmem] * 2,
        out_shape=[
            jax.ShapeDtypeStruct((rows, both), BF16),
            jax.ShapeDtypeStruct((both // 2, rows), BF16),
        ],
        scratch=[pltpu.VMEM((rows + HALO, both), F32)],
        after=after,
    )(place, normed, halo, w_state, conv_state)


def local_kernel(
    head_size,
    place_ref,
    parity_ref,
    normed_ref,
    halo_ref,
    bt_ref,
    wi_ref,
    wt_ref,
    small_ref,
    xs_ref,
    cum_ref,
    cumt_ref,
    send_ref,
    mine_ref,
    rows_ref,
    spread_ref,
    scaled_ref,
    step_ref,
    left_ref,
    whole_ref,
):
    rows = normed_ref.shape[0]
    states = bt_ref.shape[0]
    heads = wt_ref.shape[0]
    taps = SMALL_TAPS
    tiles = pl.num_programs(0)
    g = pl.program_id(0)
    tile = tile_at(g, tiles, parity_ref)

    @pl.when(g == 0)
    def _():
        bias = small_ref[taps + 1 : taps + 2, :heads]
        rate = small_ref[taps + 2 : taps + 3, :heads]
        raw = dot_nt(normed_ref[...], wt_ref[...]) + bias
        step = jnp.maximum(raw, 0.0) + jnp.log1p(jnp.exp(-jnp.abs(raw)))
        step_ref[...] = two_parts(step)
        logdecay = -step * rate
        high = logdecay.astype(BF16)
        rest = logdecay - high.astype(F32)
        mid = rest.astype(BF16)
        low = (rest - mid.astype(F32)).astype(BF16)
        parts = jnp.concatenate([high, mid, low], axis=1)
        to = lax.broadcasted_iota(jnp.int32, (CHUNK, CHUNK), 0)
        frm = lax.broadcasted_iota(jnp.int32, (CHUNK, CHUNK), 1)
        lower = jnp.where(to >= frm, 1.0, 0.0).astype(BF16)
        run = jnp.zeros((1, heads), F32)
        for r in range(0, rows, CHUNK):
            sums = dot(lower, parts[r : r + CHUNK, :])
            sums = sums[:, :heads] + sums[:, heads : 2 * heads] + sums[:, 2 * heads :] + run
            cum_ref[r : r + CHUNK, :] = sums
            run = sums[CHUNK - 1 :, :]
        cum = cum_ref[...]
        cumt_ref[...] = cum.T
        left_ref[...] = two_parts(jnp.exp(run - cum))
        whole_ref[...] = two_parts(jnp.exp(run))

    weights = wi_ref[...]
    before = dot(halo_ref[...], weights).astype(BF16).astype(F32)
    rows_ref[:HALO, :] = jnp.where(place_ref[0] >= 1, before, 0.0)
    rows_ref[HALO:, :] = dot(normed_ref[...], weights).astype(BF16).astype(F32)
    onehot = head_matrix(heads, TILE, head_size, tile * (TILE // head_size))
    spread_ref[0] = dot(step_ref[...], onehot)
    spread_ref[1] = dot(left_ref[...], onehot)
    columns = pl.ds(pl.multiple_of(tile * TILE, TILE), TILE)
    taps_here = small_ref[:taps, columns]
    for r in range(0, rows, BLOCK):
        xs = conv_silu(rows_ref, taps_here, r).astype(F32) * spread_ref[0, r : r + BLOCK, :]
        xs_ref[r : r + BLOCK, :] = xs.astype(BF16)
        scaled_ref[r : r + BLOCK, :] = (xs * spread_ref[1, r : r + BLOCK, :]).astype(BF16)
    state = dot(bt_ref[...], scaled_ref[...])
    decay = dot(whole_ref[...], onehot)

    @pl.when(g < tiles // 2)
    def _():
        write_payload(send_ref, state, decay)

    @pl.when(g >= tiles // 2)
    def _():
        write_payload(mine_ref, state, decay)


def tile_at(g, tiles, parity_ref):
    return lax.rem(g + (1 - parity_ref[0]) * (tiles // 2), tiles)


SMALL_TAPS = 4
SMALL_ROWS = 8


def local_call(tag, place, parity, normed, halo, bt, w_inner, w_step_t, small, after=()):
    rows, width = normed.shape
    inner = w_inner.shape[1]
    heads = w_step_t.shape[0]
    states = bt.shape[0]
    tiles = inner // TILE
    half = tiles // 2

    def whole(a):
        return pl.BlockSpec(a.shape, lambda g, place, parity: (0, 0))

    def tile(count):
        return pl.BlockSpec((count, TILE), lambda g, place, parity: (0, tile_at(g, tiles, parity)))

    payload = (states + EXTRA, TILE)
    return call(
        functools.partial(local_kernel, inner // heads),
        "local_" + tag,
        vmem=12,
        cost=micros(5.0),
        scalars=(place, parity),
        grid=(tiles,),
        in_specs=[whole(normed), whole(halo), whole(bt), tile(width), whole(w_step_t), whole(small)],
        out_specs=[
            tile(rows),
            pl.BlockSpec((rows, heads), lambda g, place, parity: (0, 0)),
            pl.BlockSpec((heads, rows), lambda g, place, parity: (0, 0)),
            pl.BlockSpec(payload, lambda g, place, parity: (0, jnp.minimum(g, half - 1))),
            pl.BlockSpec(payload, lambda g, place, parity: (0, jnp.maximum(g - half, 0))),
        ],
        out_shape=[
            jax.ShapeDtypeStruct((rows, inner), BF16),
            jax.ShapeDtypeStruct((rows, heads), F32),
            jax.ShapeDtypeStruct((heads, rows), F32),
            jax.ShapeDtypeStruct((states + EXTRA, inner // 2), BF16),
            jax.ShapeDtypeStruct((states + EXTRA, inner // 2), BF16),
        ],
        scratch=[
            pltpu.VMEM((rows + HALO, TILE), F32),
            pltpu.VMEM((2, rows, TILE), F32),
            pltpu.VMEM((rows, TILE), BF16),
            pltpu.VMEM((rows, 2 * heads), BF16),
            pltpu.VMEM((rows, 2 * heads), BF16),
            pltpu.VMEM((1, 2 * heads), BF16),
        ],
        after=after,
    )(place, parity, normed, halo, bt, w_inner, w_step_t, small)


def inside_kernel(head_size, xs_ref, bc_ref, cum_ref, cumt_ref, y_ref, state_ref, prev_ref):
    length, inner = xs_ref.shape
    states = bc_ref.shape[1] // 2
    heads = cum_ref.shape[1]

    @pl.when(pl.program_id(0) == 0)
    def _():
        state_ref[...] = jnp.zeros_like(state_ref)
        prev_ref[...] = jnp.zeros_like(prev_ref)

    bmat = bc_ref[:, :states]
    cmat = bc_ref[:, states:]
    to = lax.broadcasted_iota(jnp.int32, (length, length), 0)
    frm = lax.broadcasted_iota(jnp.int32, (length, length), 1)
    scores = jnp.where(to >= frm, dot_nt(cmat, bmat), 0.0)
    cum = cum_ref[...]
    cumt = cumt_ref[...]
    last = length - 1
    end = cum[last:, :]
    since = two_parts(jnp.exp(cum - prev_ref[...]))
    left = two_parts(jnp.exp(end - cum))
    prev_ref[...] = end
    pair = 2 * head_size
    lane = lax.broadcasted_iota(jnp.int32, (length, pair), 1)
    for first in range(0, heads, TILE // head_size):
        columns = slice(first * head_size, first * head_size + TILE)
        onehot = head_matrix(heads, TILE, head_size, first)
        since_here = dot(since, onehot)
        state = state_ref[:, columns]
        carried = dot(cmat, state.astype(BF16)) * since_here
        scaled = (xs_ref[:, columns].astype(F32) * dot(left, onehot)).astype(BF16)
        state_ref[:, columns] = state * since_here[last:, :] + dot_tn(bmat, scaled)
        for start in range(0, TILE, pair):
            low = first * head_size + start
            weights = []
            for h in (low // head_size, low // head_size + 1):
                apart = jnp.minimum(cum[:, h : h + 1] - cumt[h : h + 1, :], 0.0)
                weights.append((jnp.exp(apart) * scores).astype(BF16))
            mine = xs_ref[:, low : low + pair]
            none = jnp.zeros_like(mine)
            stacked = jnp.concatenate(
                [jnp.where(lane < head_size, mine, none), jnp.where(lane < head_size, none, mine)], axis=0
            )
            inside = dot(jnp.concatenate(weights, axis=1), stacked)
            y_ref[:, low : low + pair] = (inside + carried[:, start : start + pair]).astype(BF16)


def inside_call(tag, xs, bc, cum, cumt, after=()):
    rows, inner = xs.shape
    heads = cum.shape[1]
    both = bc.shape[1]

    def block(width):
        return pl.BlockSpec((CHUNK, width), lambda c: (c, 0))

    return call(
        functools.partial(inside_kernel, inner // heads),
        "inside_" + tag,
        vmem=8,
        cost=micros(3.2),
        grid=(rows // CHUNK,),
        in_specs=[
            block(inner),
            block(both),
            block(heads),
            pl.BlockSpec((heads, CHUNK), lambda c: (0, c)),
        ],
        out_specs=block(inner),
        out_shape=jax.ShapeDtypeStruct((rows, inner), BF16),
        scratch=[pltpu.VMEM((both // 2, inner), F32), pltpu.VMEM((1, heads), F32)],
        after=after,
    )(xs, bc, cum, cumt)


def parts_of(ref, known=None):
    states = ref.shape[0] - EXTRA
    state = ref[:states, :].astype(F32)
    extra = ref[states:, :].astype(F32)
    decay = extra[:1] + extra[1:2]
    if known is None:
        return state, decay
    return jnp.where(known, state, 0.0), jnp.where(known, decay, 0.0)


def write_payload(out_ref, state, decay):
    states = state.shape[0]
    out_ref[:states, :] = state.astype(BF16)
    decay = jnp.broadcast_to(decay, (EXTRA, decay.shape[1]))
    high = decay.astype(BF16).astype(F32)
    place = lax.broadcasted_iota(jnp.int32, decay.shape, 0)
    out_ref[states:, :] = jnp.where(place == 0, high, decay - high).astype(BF16)


def pair_kernel(place_ref, mine_ref, other_ref, out_ref):
    mine, mine_a = parts_of(mine_ref)
    other, other_a = parts_of(other_ref)
    is_first = lax.rem(place_ref[0], 2) == 0
    early = jnp.where(is_first, mine, other)
    late = jnp.where(is_first, other, mine)
    late_a = jnp.where(is_first, other_a, mine_a)
    write_payload(out_ref, late_a * early + late, mine_a * other_a)


def chain_kernel(reach, place_ref, pair_ref, before_ref, out_ref):
    pair, pair_a = parts_of(pair_ref)
    before, before_a = parts_of(before_ref, place_ref[0] >= reach)
    write_payload(out_ref, pair_a * before + pair, pair_a * before_a)


def longer_kernel(reach, farther_reach, place_ref, before_ref, farther_ref, out_ref):
    before, before_a = parts_of(before_ref, place_ref[0] >= reach)
    farther, farther_a = parts_of(farther_ref, place_ref[0] >= farther_reach)
    write_payload(out_ref, before + before_a * farther, before_a * farther_a)


def entry_kernel(reach, farther_reach, place_ref, mine_ref, other_ref, before_ref, farther_ref, keep_ref, send_ref):
    mine, mine_a = parts_of(mine_ref)
    other, other_a = parts_of(other_ref)
    before, before_a = parts_of(before_ref, place_ref[0] >= reach)
    farther, _ = parts_of(farther_ref, place_ref[0] >= farther_reach)
    is_first = lax.rem(place_ref[0], 2) == 0
    entry_first = before + before_a * farther
    early = jnp.where(is_first, mine, other)
    early_a = jnp.where(is_first, mine_a, other_a)
    entry_second = early_a * entry_first + early
    keep_ref[...] = jnp.where(is_first, entry_first, entry_second).astype(BF16)
    send_ref[...] = jnp.where(is_first, entry_second, entry_first).astype(BF16)


def small_call(kernel, name, place, arrays, shapes, after=()):
    vmem = pl.BlockSpec(memory_space=pltpu.VMEM)
    return call(
        kernel,
        name,
        vmem=4,
        cost=micros(0.5),
        scalars=(place,),
        in_specs=[vmem] * len(arrays),
        out_specs=[vmem] * len(shapes),
        out_shape=[jax.ShapeDtypeStruct(s, BF16) for s in shapes],
        after=after,
    )(place, *arrays)


def onward(value, by):
    count = lax.axis_size("seq")
    pairs = []
    for i in range(count):
        up = (i + by, 0) if i + by < count else (i, 1)
        down = (i - by, 1) if i - by >= 0 else (i, 0)
        pairs += [(2 * i, 2 * up[0] + up[1]), (2 * i + 1, 2 * down[0] + down[1])]
    return lax.ppermute(value, ("seq", "ch"), pairs)


class Chain:
    def __init__(self, tag, place, send, mine):
        self.tag, self.place, self.mine = tag, place, mine
        self.count = lax.axis_size("seq")
        self.swap = [(i, i ^ 1) for i in range(self.count)]
        self.other = lax.ppermute(send, "seq", self.swap)
        self.before = self.farther = None
        self.reach = self.farther_reach = 0
        self.apart = 2

    def pair(self, after):
        (self.pair_state,) = small_call(
            pair_kernel, "pair_" + self.tag, self.place, [self.mine, self.other], [self.mine.shape], after
        )
        self.running = self.pair_state
        self.hop()
        return self.pair_state

    def hop(self):
        if self.apart < self.count:
            self.arrived = onward(self.running, self.apart)

    def middle(self, after):
        while self.apart * 2 < self.count:
            self.take(after)
            (self.running,) = small_call(
                functools.partial(chain_kernel, self.reach),
                "chain_" + self.tag,
                self.place,
                [self.pair_state, self.before],
                [self.mine.shape],
                after,
            )
            self.apart *= 2
            self.hop()
        return self.running

    def take(self, after=()):
        if self.before is None:
            self.before, self.reach = self.arrived, self.apart
        else:
            (self.before,) = small_call(
                functools.partial(longer_kernel, self.reach, self.apart),
                "longer_" + self.tag,
                self.place,
                [self.before, self.arrived],
                [self.mine.shape],
                after,
            )
            self.reach = 0

    def entry(self, after):
        shape = self.mine.shape
        if self.apart < self.count:
            if self.before is None:
                self.before, self.reach = self.arrived, self.apart
                self.farther, self.farther_reach = self.arrived, self.count
            else:
                self.farther, self.farther_reach = self.arrived, self.apart
        else:
            self.before = self.farther = self.mine
            self.reach = self.farther_reach = self.count
        half = (shape[0] - EXTRA, shape[1])
        keep, out = small_call(
            functools.partial(entry_kernel, self.reach, self.farther_reach),
            "entry_" + self.tag,
            self.place,
            [self.mine, self.other, self.before, self.farther],
            [half, half],
            after,
        )
        return keep, lax.ppermute(out, "seq", self.swap)


def gated_part(
    head_size, swap, y_ref, bc_ref, cum_ref, keep_ref, other_ref, gate_ref, small_ref, wo_ref, scaled_ref
):
    rows, inner = y_ref.shape
    states = bc_ref.shape[1] // 2
    heads = cum_ref.shape[1]
    half = inner // 2
    cmat = bc_ref[:, states:]
    since = two_parts(jnp.exp(cum_ref[...]))
    squares = [0.0] * (rows // BLOCK)
    for low in range(0, inner, TILE):
        columns = slice(low, low + TILE)
        here = slice(low % half, low % half + TILE)
        use_other = swap if low < half else jnp.logical_not(swap)
        entry = jnp.where(use_other, other_ref[:, here], keep_ref[:, here])
        onehot = head_matrix(heads, TILE, head_size, low // head_size)
        gain = small_ref[SMALL_TAPS : SMALL_TAPS + 1, columns]
        for i, r in enumerate(range(0, rows, BLOCK)):
            block = slice(r, r + BLOCK)
            carried = dot(cmat[block, :], entry) * dot(since[block, :], onehot)
            gated = (y_ref[block, columns].astype(F32) + carried) * gate_ref[block, columns].astype(F32)
            squares[i] += jnp.sum(gated * gated, axis=-1, keepdims=True)
            scaled_ref[block, columns] = (gated * gain).astype(BF16)
    return squares


def part_kernel(head_size, back_ref, parity_ref, *refs):
    *ins, out_ref, sq_ref, scaled_ref = refs
    squares = gated_part(head_size, parity_ref[0] == 1, *ins, scaled_ref)
    for i, square in enumerate(squares):
        sq_ref[i * BLOCK : (i + 1) * BLOCK, :] = jnp.broadcast_to(square, (BLOCK, sq_ref.shape[1]))
    out_ref[...] = dot(scaled_ref[...], ins[-1][...])


def finish_kernel(head_size, full_width, back_ref, parity_ref, *refs):
    *ins, part_ref, psq_ref, own_ref, send_ref, scaled_ref, sum_ref, out_ref = refs
    squares = gated_part(head_size, parity_ref[0] == 1, *ins, scaled_ref)
    sum_ref[...] = dot(scaled_ref[...], ins[-1][...])
    half = own_ref.shape[1]
    for i, square in enumerate(squares):
        block = slice(i * BLOCK, (i + 1) * BLOCK)
        scale = lax.rsqrt((square + psq_ref[block, :1]) / full_width + EPS)
        out_ref[block, :] = ((sum_ref[block, :] + part_ref[block, :]) * scale).astype(BF16)

    @pl.when(back_ref[0] == 1)
    def _():
        turned = flip_both(out_ref[...])
        own_ref[...] = turned[:, half:]
        send_ref[...] = turned[:, :half]

    @pl.when(back_ref[0] != 1)
    def _():
        own_ref[...] = out_ref[:, :half]
        send_ref[...] = out_ref[:, half:]


def finish_call(back, parity, y, bc, cum, keep, other, gate, small, w_output, full_width=None, partial=None, after=()):
    rows, inner = y.shape
    width = w_output.shape[1]
    half = width // 2
    heads = cum.shape[1]
    count = rows // TILE

    def block(columns):
        return pl.BlockSpec((TILE, columns), lambda r, back, parity: (r, 0))

    def whole(a):
        return pl.BlockSpec(a.shape, lambda r, back, parity: (0, 0))

    def turned(r, back, parity):
        return (jnp.where(back[0] == 1, count - 1 - r, r), 0)

    in_specs = [
        block(inner),
        block(bc.shape[1]),
        block(heads),
        whole(keep),
        whole(other),
        block(inner),
        whole(small),
        whole(w_output),
    ]
    arrays = [y, bc, cum, keep, other, gate, small, w_output]
    if partial is None:
        scratch = [pltpu.VMEM((TILE, inner), BF16)]
        kernel = functools.partial(part_kernel, inner // heads)
        out_specs = [block(width), block(128)]
        out_shape = [jax.ShapeDtypeStruct((rows, width), F32), jax.ShapeDtypeStruct((rows, 128), F32)]
    else:
        scratch = [
            pltpu.VMEM((TILE, inner), BF16),
            pltpu.VMEM((TILE, width), F32),
            pltpu.VMEM((TILE, width), BF16),
        ]
        kernel = functools.partial(finish_kernel, inner // heads, full_width)
        in_specs += [block(width), block(128)]
        arrays += list(partial)
        out_specs = [pl.BlockSpec((TILE, half), turned)] * 2
        out_shape = [jax.ShapeDtypeStruct((rows, half), BF16)] * 2
    return call(
        kernel,
        "part" if partial is None else "finish",
        vmem=16,
        cost=micros(3.5),
        scalars=(back, parity),
        grid=(count,),
        in_specs=in_specs,
        out_specs=out_specs,
        out_shape=out_shape,
        scratch=scratch,
        after=after,
    )(back, parity, *arrays)


def total_kernel(mine_ref, theirs_ref, out_ref):
    for r in range(0, mine_ref.shape[0], BLOCK):
        block = slice(r, r + BLOCK)
        out_ref[block, :] = (mine_ref[block, :].astype(F32) + theirs_ref[block, :].astype(F32)).astype(BF16)


def total_call(mine, theirs):
    rows, half = mine.shape
    block = pl.BlockSpec((CHUNK, half), lambda r: (r, 0))
    return call(
        total_kernel,
        "total",
        vmem=4,
        cost=micros(0.8),
        grid=(rows // CHUNK,),
        in_specs=[block, block],
        out_specs=block,
        out_shape=jax.ShapeDtypeStruct((rows, half), BF16),
    )(mine, theirs)


def body(
    tokens,
    hidden,
    embedding,
    w_gate,
    w_inner,
    w_state,
    w_step,
    conv_inner,
    conv_state,
    step_bias,
    decay_rate,
    norm_gain,
    w_output,
):
    swap = [(0, 1), (1, 0)]

    def theirs(a):
        return lax.ppermute(a, "ch", swap)

    core = lax.axis_index("ch").astype(jnp.int32)
    index = lax.axis_index("seq").astype(jnp.int32)
    last = lax.axis_size("seq") - 1
    back = core.reshape(1)
    parity = (index & 1).reshape(1)
    place = (index + core * (last - 2 * index)).reshape(1)
    w_inner_2 = theirs(w_inner)
    normed, tail, small = prepare_call(
        (back, parity, place), hidden, tokens, embedding, conv_inner, norm_gain, step_bias, decay_rate
    )
    halo = onward(tail, 1)
    small_2 = theirs(small)
    w_step_t = w_step.T
    w_step_2 = theirs(w_step_t)
    w_gate_2 = theirs(w_gate)
    w_output_2 = theirs(w_output)
    gate_1 = gate_call("own", normed, w_gate)
    bc, bt = maps_call(place, normed, halo, w_state, conv_state, after=[gate_1])
    xs_1, cum_1, cumt_1, send_1, mine_1 = local_call(
        "own", place, parity, normed, halo, bt, w_inner, w_step_t, small
    )
    chain_1 = Chain("own", place, send_1, mine_1)
    xs_2, cum_2, cumt_2, send_2, mine_2 = local_call(
        "other", place, parity, normed, halo, bt, w_inner_2, w_step_2, small_2, after=[mine_1]
    )
    chain_2 = Chain("other", place, send_2, mine_2)
    done = chain_1.pair(after=[xs_2])
    y_1 = inside_call("own", xs_1, bc, cum_1, cumt_1, after=[done])
    done = chain_1.middle(after=[y_1])
    done = chain_2.pair(after=[done])
    entry_1 = chain_1.entry(after=[done])
    y_2 = inside_call("other", xs_2, bc, cum_2, cumt_2, after=[entry_1[0]])
    done = chain_2.middle(after=[y_2])
    gate_2 = gate_call("other", normed, w_gate_2, after=[done])
    entry_2 = chain_2.entry(after=[gate_2])
    partial = finish_call(
        back, parity, y_1, bc, cum_1, *entry_1, gate_1, small, w_output, after=[entry_2[0]]
    )
    full_width = float(w_inner.shape[1] * lax.axis_size("ch"))
    mine, send = finish_call(
        back, parity, y_2, bc, cum_2, *entry_2, gate_2, small_2, w_output_2, full_width, partial
    )
    return total_call(mine, theirs(send))


def solution(mesh):
    return jax.shard_map(
        body,
        mesh=mesh,
        in_specs=(
            P(("win", "seq")),
            P(("win", "seq"), None),
            P(),
            P(None, "ch"),
            P(None, "ch"),
            P(),
            P(None, "ch"),
            P(None, "ch"),
            P(),
            P("ch"),
            P("ch"),
            P("ch"),
            P("ch", None),
        ),
        out_specs=P(("win", "seq"), "ch"),
        check_vma=False,
    )
```

```python
import functools

import jax
import jax.numpy as jnp
from jax import lax
from jax.experimental import pallas as pl
from jax.experimental.pallas import tpu as pltpu
from jax.sharding import PartitionSpec as P

F32 = jnp.float32
BF16 = jnp.bfloat16
EPS = 1e-05
HALO = 16
EXTRA = 16
CHUNK = 128
TILE = 256
BLOCK = 64
MB = 1024 * 1024
VMEM = pl.BlockSpec(memory_space=pltpu.VMEM)
HBM = pl.BlockSpec(memory_space=pltpu.HBM)


def call(
    kernel, name, *, vmem, cost, scalars=(), grid=(), in_specs, out_specs, out_shape, scratch=(), after=()
):
    flops, moved, special = cost
    first = len(scalars) + len(in_specs)

    def body(*refs):
        kernel(*refs[:first], *refs[first + len(after) :])

    run = pl.pallas_call(
        body,
        grid_spec=pltpu.PrefetchScalarGridSpec(
            num_scalar_prefetch=len(scalars),
            grid=grid,
            in_specs=list(in_specs) + [pl.BlockSpec(memory_space=pl.ANY)] * len(after),
            out_specs=out_specs,
            scratch_shapes=scratch,
        ),
        out_shape=out_shape,
        compiler_params=pltpu.CompilerParams(
            vmem_limit_bytes=vmem * MB, dimension_semantics=("arbitrary",) * len(grid)
        ),
        cost_estimate=pl.CostEstimate(flops=flops, bytes_accessed=moved, transcendentals=special),
        name=name,
    )
    return lambda *arrays: run(*arrays, *after)


def micros(us):
    return (int(us * 1.1e9), int(us * 1e6), 0)


def dot(a, b):
    return jnp.dot(a, b, preferred_element_type=F32)


def dot_nt(a, b):
    return lax.dot_general(a, b, (((1,), (1,)), ((), ())), preferred_element_type=F32)


def dot_tn(a, b):
    return lax.dot_general(a, b, (((0,), (0,)), ((), ())), preferred_element_type=F32)


def flip_matrix(size):
    rows = lax.broadcasted_iota(jnp.int32, (size, size), 0)
    columns = lax.broadcasted_iota(jnp.int32, (size, size), 1)
    return jnp.where(rows + columns == size - 1, 1.0, 0.0).astype(BF16)


def flip_both(value):
    rows, width = value.shape
    turned = dot(flip_matrix(rows), value).astype(BF16)
    anti = flip_matrix(TILE)
    count = width // TILE
    blocks = [
        dot(turned[:, (count - 1 - k) * TILE : (count - k) * TILE], anti).astype(BF16)
        for k in range(count)
    ]
    return jnp.concatenate(blocks, axis=1)


def silu(v):
    half = 0.5 * v
    return half + half * jnp.tanh(half)


def two_parts(value):
    high = value.astype(BF16)
    low = (value - high.astype(F32)).astype(BF16)
    return jnp.concatenate([high, low], axis=1)


def head_matrix(heads, width, head_size, first_head):
    source = lax.broadcasted_iota(jnp.int32, (2 * heads, width), 0)
    source = jnp.where(source >= heads, source - heads, source)
    target = lax.broadcasted_iota(jnp.int32, (2 * heads, width), 1) // head_size + first_head
    return jnp.where(source == target, 1.0, 0.0).astype(BF16)


def prepare_kernel(
    back_ref,
    parity_ref,
    place_ref,
    hidden_hbm,
    tokens_hbm,
    emb_hbm,
    conv_hbm,
    gain_hbm,
    bias_hbm,
    rate_hbm,
    out_ref,
    tail_ref,
    small_ref,
    hidden_ref,
    tokens_ref,
    emb_ref,
    conv_ref,
    gain_ref,
    bias_ref,
    rate_ref,
    base_ref,
    normed_ref,
    sems,
):
    rows = hidden_ref.shape[0]
    kinds = emb_ref.shape[0]
    taps, inner = conv_ref.shape
    heads = bias_ref.shape[1]
    count = rows // CHUNK
    back = back_ref[0] == 1
    whole = [
        (tokens_hbm, tokens_ref),
        (emb_hbm, emb_ref),
        (conv_hbm, conv_ref),
        (gain_hbm, gain_ref),
        (bias_hbm, bias_ref),
        (rate_hbm, rate_ref),
    ]
    small_copies = [pltpu.make_async_copy(src, dst, sems.at[count + i]) for i, (src, dst) in enumerate(whole)]
    parts = [pl.ds(r * CHUNK, CHUNK) for r in range(count)]
    copies = [
        pltpu.make_async_copy(hidden_hbm.at[part, :], hidden_ref.at[part, :], sems.at[r])
        for r, part in enumerate(parts)
    ]
    for copy in small_copies[:2] + copies + small_copies[2:]:
        copy.start()
    for copy in small_copies[:2]:
        copy.wait()
    kind = lax.broadcasted_iota(jnp.int32, (kinds, rows), 0)
    onehot = jnp.where(kind == tokens_ref[...], 1.0, 0.0).astype(BF16)
    for r in range(count):
        copies[r].wait()
        low, high = r * CHUNK, (r + 1) * CHUNK
        base_ref[...] = dot_tn(onehot[:, low:high], emb_ref[...])
        for q in range(low, high, HALO):
            block = slice(q, q + HALO)
            merged = hidden_ref[block, :].astype(F32) + base_ref[q - low : q - low + HALO, :]
            merged = merged.astype(BF16).astype(F32)
            mean = jnp.mean(merged * merged, axis=-1, keepdims=True)
            normed_ref[q - low : q - low + HALO, :] = (merged * lax.rsqrt(mean + EPS)).astype(BF16)

        @pl.when(back)
        def _():
            out_ref[rows - high : rows - low, :] = flip_both(normed_ref[...])

        @pl.when(jnp.logical_not(back))
        def _():
            out_ref[low:high, :] = normed_ref[...]

    tail_ref[...] = out_ref[rows - HALO :, :]
    for copy in small_copies[2:]:
        copy.wait()
    small_ref[:taps, :] = conv_ref[...]
    small_ref[taps : taps + 1, :] = gain_ref[...]
    small_ref[taps + 1 :, :] = jnp.zeros((SMALL_ROWS - taps - 1, inner), F32)
    small_ref[taps + 1 : taps + 2, :heads] = bias_ref[...]
    small_ref[taps + 2 : taps + 3, :heads] = rate_ref[...]


def prepare_call(scalars, hidden, tokens, embedding, conv, gain, bias, rate):
    rows, width = hidden.shape
    inner = conv.shape[1]
    arrays = [hidden, tokens.reshape(1, -1), embedding, conv]
    arrays += [a.reshape(1, -1) for a in (gain, bias, rate)]
    return call(
        prepare_kernel,
        "prepare",
        vmem=12,
        cost=micros(1.5),
        scalars=scalars,
        in_specs=[HBM] * len(arrays),
        out_specs=[VMEM] * 3,
        out_shape=[
            jax.ShapeDtypeStruct((rows, width), BF16),
            jax.ShapeDtypeStruct((HALO, width), BF16),
            jax.ShapeDtypeStruct((SMALL_ROWS, inner), F32),
        ],
        scratch=[pltpu.VMEM(a.shape, a.dtype) for a in arrays]
        + [pltpu.VMEM((CHUNK, width), F32), pltpu.VMEM((CHUNK, width), BF16)]
        + [pltpu.SemaphoreType.DMA((rows // CHUNK + len(arrays) - 1,))],
    )(*scalars, *(pltpu.with_memory_space_constraint(a, pltpu.HBM) for a in arrays))


def gate_kernel(rows_ref, wg_ref, out_ref, gate_ref):
    rows, inner = out_ref.shape
    for low in range(0, inner, TILE):
        columns = slice(low, low + TILE)
        gate_ref[...] = dot(rows_ref[...], wg_ref[:, columns])
        for r in range(0, rows, BLOCK):
            gate = gate_ref[r : r + BLOCK, :].astype(BF16).astype(F32)
            out_ref[r : r + BLOCK, columns] = silu(gate).astype(BF16)


def gate_call(tag, normed, w_gate, after=()):
    rows = normed.shape[0]
    inner = w_gate.shape[1]
    return call(
        gate_kernel,
        "gate_" + tag,
        vmem=8,
        cost=micros(2.4),
        in_specs=[VMEM] * 2,
        out_specs=VMEM,
        out_shape=jax.ShapeDtypeStruct((rows, inner), BF16),
        scratch=[pltpu.VMEM((rows, TILE), F32)],
        after=after,
    )(normed, w_gate)


def conv_silu(rows_ref, weights, row):
    taps = weights.shape[0]
    total = None
    for k in range(taps):
        offset = HALO - (taps - 1) + k + row
        term = weights[k : k + 1, :] * rows_ref[offset : offset + BLOCK, :]
        total = term if total is None else total + term
    return silu(total).astype(BF16)


def maps_kernel(place_ref, normed_ref, halo_ref, ws_ref, cs_ref, bc_ref, bt_ref, rows_ref):
    rows = normed_ref.shape[0]
    states = bc_ref.shape[1] // 2
    before = dot(halo_ref[...], ws_ref[...]).astype(BF16).astype(F32)
    rows_ref[:HALO, :] = jnp.where(place_ref[0] >= 1, before, 0.0)
    rows_ref[HALO:, :] = dot(normed_ref[...], ws_ref[...]).astype(BF16).astype(F32)
    weights = cs_ref[...]
    for r in range(0, rows, BLOCK):
        bc_ref[r : r + BLOCK, :] = conv_silu(rows_ref, weights, r)
    bt_ref[...] = bc_ref[:, :states].astype(F32).T.astype(BF16)


def maps_call(place, normed, halo, w_state, conv_state, after=()):
    rows = normed.shape[0]
    both = w_state.shape[1]
    return call(
        maps_kernel,
        "maps",
        vmem=8,
        cost=micros(1.5),
        scalars=(place,),
        in_specs=[VMEM] * 4,
        out_specs=[VMEM] * 2,
        out_shape=[
            jax.ShapeDtypeStruct((rows, both), BF16),
            jax.ShapeDtypeStruct((both // 2, rows), BF16),
        ],
        scratch=[pltpu.VMEM((rows + HALO, both), F32)],
        after=after,
    )(place, normed, halo, w_state, conv_state)


def local_kernel(
    head_size,
    place_ref,
    parity_ref,
    normed_ref,
    halo_ref,
    bt_ref,
    wi_ref,
    wt_ref,
    small_ref,
    xs_ref,
    cum_ref,
    cumt_ref,
    send_ref,
    mine_ref,
    rows_ref,
    spread_ref,
    scaled_ref,
    step_ref,
    left_ref,
    whole_ref,
):
    rows = normed_ref.shape[0]
    states = bt_ref.shape[0]
    heads = wt_ref.shape[0]
    taps = SMALL_TAPS
    bias = small_ref[taps + 1 : taps + 2, :heads]
    rate = small_ref[taps + 2 : taps + 3, :heads]
    raw = dot_nt(normed_ref[...], wt_ref[...]) + bias
    step = jnp.maximum(raw, 0.0) + jnp.log1p(jnp.exp(-jnp.abs(raw)))
    step_ref[...] = two_parts(step)
    logdecay = -step * rate
    high = logdecay.astype(BF16)
    rest = logdecay - high.astype(F32)
    mid = rest.astype(BF16)
    low = (rest - mid.astype(F32)).astype(BF16)
    parts = jnp.concatenate([high, mid, low], axis=1)
    to = lax.broadcasted_iota(jnp.int32, (CHUNK, CHUNK), 0)
    frm = lax.broadcasted_iota(jnp.int32, (CHUNK, CHUNK), 1)
    lower = jnp.where(to >= frm, 1.0, 0.0).astype(BF16)
    run = jnp.zeros((1, heads), F32)
    for r in range(0, rows, CHUNK):
        sums = dot(lower, parts[r : r + CHUNK, :])
        sums = sums[:, :heads] + sums[:, heads : 2 * heads] + sums[:, 2 * heads :] + run
        cum_ref[r : r + CHUNK, :] = sums
        run = sums[CHUNK - 1 :, :]
    cum = cum_ref[...]
    cumt_ref[...] = cum.T
    left_ref[...] = two_parts(jnp.exp(run - cum))
    whole_ref[...] = two_parts(jnp.exp(run))

    inner = xs_ref.shape[1]
    half = inner // 2
    for low in range(0, inner, TILE):
        columns = slice(low, low + TILE)
        weights = wi_ref[:, columns]
        before = dot(halo_ref[...], weights).astype(BF16).astype(F32)
        rows_ref[:HALO, :] = jnp.where(place_ref[0] >= 1, before, 0.0)
        rows_ref[HALO:, :] = dot(normed_ref[...], weights).astype(BF16).astype(F32)
        onehot = head_matrix(heads, TILE, head_size, low // head_size)
        spread_ref[0] = dot(step_ref[...], onehot)
        spread_ref[1] = dot(left_ref[...], onehot)
        taps_here = small_ref[:taps, columns]
        for r in range(0, rows, BLOCK):
            xs = conv_silu(rows_ref, taps_here, r).astype(F32) * spread_ref[0, r : r + BLOCK, :]
            xs_ref[r : r + BLOCK, columns] = xs.astype(BF16)
            scaled_ref[r : r + BLOCK, :] = (xs * spread_ref[1, r : r + BLOCK, :]).astype(BF16)
        state = dot(bt_ref[...], scaled_ref[...])
        decay = dot(whole_ref[...], onehot)
        here = slice(low % half, low % half + TILE)
        is_mine = parity_ref[0] == low // half

        @pl.when(is_mine)
        def _():
            write_payload(mine_ref, here, state, decay)

        @pl.when(jnp.logical_not(is_mine))
        def _():
            write_payload(send_ref, here, state, decay)


SMALL_TAPS = 4
SMALL_ROWS = 8


def local_call(tag, place, parity, normed, halo, bt, w_inner, w_step_t, small, after=()):
    rows = normed.shape[0]
    inner = w_inner.shape[1]
    heads = w_step_t.shape[0]
    states = bt.shape[0]
    return call(
        functools.partial(local_kernel, inner // heads),
        "local_" + tag,
        vmem=12,
        cost=micros(5.0),
        scalars=(place, parity),
        in_specs=[VMEM] * 6,
        out_specs=[VMEM] * 5,
        out_shape=[
            jax.ShapeDtypeStruct((rows, inner), BF16),
            jax.ShapeDtypeStruct((rows, heads), F32),
            jax.ShapeDtypeStruct((heads, rows), F32),
            jax.ShapeDtypeStruct((states + EXTRA, inner // 2), BF16),
            jax.ShapeDtypeStruct((states + EXTRA, inner // 2), BF16),
        ],
        scratch=[
            pltpu.VMEM((rows + HALO, TILE), F32),
            pltpu.VMEM((2, rows, TILE), F32),
            pltpu.VMEM((rows, TILE), BF16),
            pltpu.VMEM((rows, 2 * heads), BF16),
            pltpu.VMEM((rows, 2 * heads), BF16),
            pltpu.VMEM((1, 2 * heads), BF16),
        ],
        after=after,
    )(place, parity, normed, halo, bt, w_inner, w_step_t, small)


def inside_kernel(head_size, xs_ref, bc_ref, cum_ref, cumt_ref, y_ref, state_ref):
    rows, inner = xs_ref.shape
    states = bc_ref.shape[1] // 2
    heads = cum_ref.shape[1]
    length = CHUNK
    last = length - 1
    pair = 2 * head_size
    lane = lax.broadcasted_iota(jnp.int32, (length, pair), 1)
    to = lax.broadcasted_iota(jnp.int32, (length, length), 0)
    frm = lax.broadcasted_iota(jnp.int32, (length, length), 1)
    state_ref[...] = jnp.zeros_like(state_ref)

    def chunk(c, before):
        at = pl.ds(pl.multiple_of(c * length, length), length)
        bmat = bc_ref[at, :states]
        cmat = bc_ref[at, states:]
        scores = jnp.where(to >= frm, dot_nt(cmat, bmat), 0.0)
        cum = cum_ref[at, :]
        cumt = cumt_ref[:, at]
        end = cum[last:, :]
        since = two_parts(jnp.exp(cum - before))
        left = two_parts(jnp.exp(end - cum))
        for first in range(0, heads, TILE // head_size):
            columns = slice(first * head_size, first * head_size + TILE)
            onehot = head_matrix(heads, TILE, head_size, first)
            since_here = dot(since, onehot)
            state = state_ref[:, columns]
            carried = dot(cmat, state.astype(BF16)) * since_here
            scaled = (xs_ref[at, columns].astype(F32) * dot(left, onehot)).astype(BF16)
            state_ref[:, columns] = state * since_here[last:, :] + dot_tn(bmat, scaled)
            for start in range(0, TILE, pair):
                low = first * head_size + start
                weights = []
                for h in (low // head_size, low // head_size + 1):
                    apart = jnp.minimum(cum[:, h : h + 1] - cumt[h : h + 1, :], 0.0)
                    weights.append((jnp.exp(apart) * scores).astype(BF16))
                mine = xs_ref[at, low : low + pair]
                none = jnp.zeros_like(mine)
                stacked = jnp.concatenate(
                    [jnp.where(lane < head_size, mine, none), jnp.where(lane < head_size, none, mine)], axis=0
                )
                inside = dot(jnp.concatenate(weights, axis=1), stacked)
                y_ref[at, low : low + pair] = (inside + carried[:, start : start + pair]).astype(BF16)
        return end

    lax.fori_loop(0, rows // length, chunk, jnp.zeros((1, heads), F32))


def inside_call(tag, xs, bc, cum, cumt, after=()):
    rows, inner = xs.shape
    heads = cum.shape[1]
    both = bc.shape[1]
    return call(
        functools.partial(inside_kernel, inner // heads),
        "inside_" + tag,
        vmem=8,
        cost=micros(3.2),
        in_specs=[VMEM] * 4,
        out_specs=VMEM,
        out_shape=jax.ShapeDtypeStruct((rows, inner), BF16),
        scratch=[pltpu.VMEM((both // 2, inner), F32)],
        after=after,
    )(xs, bc, cum, cumt)


def parts_of(ref, known=None):
    states = ref.shape[0] - EXTRA
    state = ref[:states, :].astype(F32)
    extra = ref[states:, :].astype(F32)
    decay = extra[:1] + extra[1:2]
    if known is None:
        return state, decay
    return jnp.where(known, state, 0.0), jnp.where(known, decay, 0.0)


def write_payload(out_ref, columns, state, decay):
    states = state.shape[0]
    out_ref[:states, columns] = state.astype(BF16)
    decay = jnp.broadcast_to(decay, (EXTRA, decay.shape[1]))
    high = decay.astype(BF16).astype(F32)
    place = lax.broadcasted_iota(jnp.int32, decay.shape, 0)
    out_ref[states:, columns] = jnp.where(place == 0, high, decay - high).astype(BF16)


ALL = slice(None)


def pair_kernel(place_ref, mine_ref, other_ref, out_ref):
    mine, mine_a = parts_of(mine_ref)
    other, other_a = parts_of(other_ref)
    is_first = lax.rem(place_ref[0], 2) == 0
    early = jnp.where(is_first, mine, other)
    late = jnp.where(is_first, other, mine)
    late_a = jnp.where(is_first, other_a, mine_a)
    write_payload(out_ref, ALL, late_a * early + late, mine_a * other_a)


def chain_kernel(reach, place_ref, pair_ref, before_ref, out_ref):
    pair, pair_a = parts_of(pair_ref)
    before, before_a = parts_of(before_ref, place_ref[0] >= reach)
    write_payload(out_ref, ALL, pair_a * before + pair, pair_a * before_a)


def longer_kernel(reach, farther_reach, place_ref, before_ref, farther_ref, out_ref):
    before, before_a = parts_of(before_ref, place_ref[0] >= reach)
    farther, farther_a = parts_of(farther_ref, place_ref[0] >= farther_reach)
    write_payload(out_ref, ALL, before + before_a * farther, before_a * farther_a)


def entry_kernel(reach, farther_reach, place_ref, mine_ref, other_ref, before_ref, farther_ref, keep_ref, send_ref):
    mine, mine_a = parts_of(mine_ref)
    other, other_a = parts_of(other_ref)
    before, before_a = parts_of(before_ref, place_ref[0] >= reach)
    farther, _ = parts_of(farther_ref, place_ref[0] >= farther_reach)
    is_first = lax.rem(place_ref[0], 2) == 0
    entry_first = before + before_a * farther
    early = jnp.where(is_first, mine, other)
    early_a = jnp.where(is_first, mine_a, other_a)
    entry_second = early_a * entry_first + early
    keep_ref[...] = jnp.where(is_first, entry_first, entry_second).astype(BF16)
    send_ref[...] = jnp.where(is_first, entry_second, entry_first).astype(BF16)


def small_call(kernel, name, place, arrays, shapes, after=()):
    return call(
        kernel,
        name,
        vmem=4,
        cost=micros(0.5),
        scalars=(place,),
        in_specs=[VMEM] * len(arrays),
        out_specs=[VMEM] * len(shapes),
        out_shape=[jax.ShapeDtypeStruct(s, BF16) for s in shapes],
        after=after,
    )(place, *arrays)


def onward(value, by):
    count = lax.axis_size("seq")
    pairs = []
    for i in range(count):
        up = (i + by, 0) if i + by < count else (i, 1)
        down = (i - by, 1) if i - by >= 0 else (i, 0)
        pairs += [(2 * i, 2 * up[0] + up[1]), (2 * i + 1, 2 * down[0] + down[1])]
    return lax.ppermute(value, ("seq", "ch"), pairs)


class Chain:
    def __init__(self, tag, place, send, mine):
        self.tag, self.place, self.mine = tag, place, mine
        self.count = lax.axis_size("seq")
        self.swap = [(i, i ^ 1) for i in range(self.count)]
        self.other = lax.ppermute(send, "seq", self.swap)
        self.before = self.farther = None
        self.reach = self.farther_reach = 0
        self.apart = 2

    def pair(self, after):
        (self.pair_state,) = small_call(
            pair_kernel, "pair_" + self.tag, self.place, [self.mine, self.other], [self.mine.shape], after
        )
        self.running = self.pair_state
        self.hop()
        return self.pair_state

    def hop(self):
        if self.apart < self.count:
            self.arrived = onward(self.running, self.apart)

    def middle(self, after):
        while self.apart * 2 < self.count:
            self.take(after)
            (self.running,) = small_call(
                functools.partial(chain_kernel, self.reach),
                "chain_" + self.tag,
                self.place,
                [self.pair_state, self.before],
                [self.mine.shape],
                after,
            )
            self.apart *= 2
            self.hop()
        return self.running

    def take(self, after=()):
        if self.before is None:
            self.before, self.reach = self.arrived, self.apart
        else:
            (self.before,) = small_call(
                functools.partial(longer_kernel, self.reach, self.apart),
                "longer_" + self.tag,
                self.place,
                [self.before, self.arrived],
                [self.mine.shape],
                after,
            )
            self.reach = 0

    def entry(self, after):
        shape = self.mine.shape
        if self.apart < self.count:
            if self.before is None:
                self.before, self.reach = self.arrived, self.apart
                self.farther, self.farther_reach = self.arrived, self.count
            else:
                self.farther, self.farther_reach = self.arrived, self.apart
        else:
            self.before = self.farther = self.mine
            self.reach = self.farther_reach = self.count
        half = (shape[0] - EXTRA, shape[1])
        keep, out = small_call(
            functools.partial(entry_kernel, self.reach, self.farther_reach),
            "entry_" + self.tag,
            self.place,
            [self.mine, self.other, self.before, self.farther],
            [half, half],
            after,
        )
        return keep, lax.ppermute(out, "seq", self.swap)


def gated_part(
    head_size, swap, y_ref, bc_ref, cum_ref, keep_ref, other_ref, gate_ref, small_ref, wo_ref, scaled_ref, tile_ref
):
    rows, inner = y_ref.shape
    states = bc_ref.shape[1] // 2
    heads = cum_ref.shape[1]
    half = inner // 2
    since = two_parts(jnp.exp(cum_ref[...]))
    squares = [0.0] * (rows // BLOCK)
    for low in range(0, inner, TILE):
        columns = slice(low, low + TILE)
        here = slice(low % half, low % half + TILE)
        use_other = swap if low < half else jnp.logical_not(swap)
        entry = jnp.where(use_other, other_ref[:, here], keep_ref[:, here])
        tile_ref[0] = dot(bc_ref[:, states:], entry)
        tile_ref[1] = dot(since, head_matrix(heads, TILE, head_size, low // head_size))
        gain = small_ref[SMALL_TAPS : SMALL_TAPS + 1, columns]
        for i, r in enumerate(range(0, rows, BLOCK)):
            block = slice(r, r + BLOCK)
            gated = y_ref[block, columns].astype(F32) + tile_ref[0, block, :] * tile_ref[1, block, :]
            gated = gated * gate_ref[block, columns].astype(F32)
            squares[i] += jnp.sum(gated * gated, axis=-1, keepdims=True)
            scaled_ref[block, columns] = (gated * gain).astype(BF16)
    return squares


def part_kernel(head_size, parity_ref, *refs):
    *ins, out_ref, sq_ref, scaled_ref, tile_ref = refs
    squares = gated_part(head_size, parity_ref[0] == 1, *ins, scaled_ref, tile_ref)
    for i, square in enumerate(squares):
        sq_ref[i * BLOCK : (i + 1) * BLOCK, :] = jnp.broadcast_to(square, (BLOCK, sq_ref.shape[1]))
    for low in range(0, out_ref.shape[1], TILE):
        out_ref[:, low : low + TILE] = dot(scaled_ref[...], ins[-1][:, low : low + TILE])


def finish_kernel(head_size, full_width, back_ref, parity_ref, *refs):
    *ins, part_ref, psq_ref, own_ref, send_ref, scaled_ref, tile_ref, out_ref = refs
    squares = gated_part(head_size, parity_ref[0] == 1, *ins, scaled_ref, tile_ref)
    rows, half = own_ref.shape
    width = 2 * half
    scales = []
    for i, square in enumerate(squares):
        block = slice(i * BLOCK, (i + 1) * BLOCK)
        scales.append(lax.rsqrt((square + psq_ref[block, :1]) / full_width + EPS))
    for low in range(0, width, TILE):
        columns = slice(low, low + TILE)
        tile_ref[0] = dot(scaled_ref[...], ins[-1][:, columns])
        for i, scale in enumerate(scales):
            block = slice(i * BLOCK, (i + 1) * BLOCK)
            out_ref[block, columns] = ((tile_ref[0, block, :] + part_ref[block, columns]) * scale).astype(BF16)

    @pl.when(back_ref[0] == 1)
    def _():
        turn = flip_matrix(TILE)
        for r in range(0, rows, TILE):
            for low in range(0, width, TILE):
                tile = dot(turn, out_ref[r : r + TILE, low : low + TILE]).astype(BF16)
                tile = dot(tile, turn).astype(BF16)
                to_row, to = rows - TILE - r, width - TILE - low
                target, to = (own_ref, to - half) if to >= half else (send_ref, to)
                target[to_row : to_row + TILE, to : to + TILE] = tile

    @pl.when(back_ref[0] != 1)
    def _():
        own_ref[...] = out_ref[:, :half]
        send_ref[...] = out_ref[:, half:]


def finish_call(back, parity, y, bc, cum, keep, other, gate, small, w_output, full_width=None, partial=None, after=()):
    rows, inner = y.shape
    width = w_output.shape[1]
    half = width // 2
    heads = cum.shape[1]
    arrays = [y, bc, cum, keep, other, gate, small, w_output]
    scratch = [pltpu.VMEM((rows, inner), BF16), pltpu.VMEM((2, rows, TILE), F32)]
    if partial is None:
        scalars = (parity,)
        kernel = functools.partial(part_kernel, inner // heads)
        out_shape = [jax.ShapeDtypeStruct((rows, width), F32), jax.ShapeDtypeStruct((rows, 128), F32)]
    else:
        scalars = (back, parity)
        scratch.append(pltpu.VMEM((rows, width), BF16))
        kernel = functools.partial(finish_kernel, inner // heads, full_width)
        arrays += list(partial)
        out_shape = [jax.ShapeDtypeStruct((rows, half), BF16)] * 2
    return call(
        kernel,
        "part" if partial is None else "finish",
        vmem=16,
        cost=micros(3.5),
        scalars=scalars,
        in_specs=[VMEM] * len(arrays),
        out_specs=[VMEM] * 2,
        out_shape=out_shape,
        scratch=scratch,
        after=after,
    )(*scalars, *arrays)


def total_kernel(mine_ref, theirs_ref, out_hbm, out_ref, sems):
    copies = []
    for i, r in enumerate(range(0, mine_ref.shape[0], CHUNK)):
        for q in range(r, r + CHUNK, BLOCK):
            block = slice(q, q + BLOCK)
            out_ref[block, :] = (mine_ref[block, :].astype(F32) + theirs_ref[block, :].astype(F32)).astype(BF16)
        part = pl.ds(r, CHUNK)
        copies.append(pltpu.make_async_copy(out_ref.at[part, :], out_hbm.at[part, :], sems.at[i]))
        copies[-1].start()
    for copy in copies:
        copy.wait()


def total_call(mine, theirs):
    rows, half = mine.shape
    return call(
        total_kernel,
        "total",
        vmem=4,
        cost=micros(0.8),
        in_specs=[VMEM] * 2,
        out_specs=HBM,
        out_shape=jax.ShapeDtypeStruct((rows, half), BF16),
        scratch=[pltpu.VMEM((rows, half), BF16), pltpu.SemaphoreType.DMA((rows // CHUNK,))],
    )(mine, theirs)


def body(
    tokens,
    hidden,
    embedding,
    w_gate,
    w_inner,
    w_state,
    w_step,
    conv_inner,
    conv_state,
    step_bias,
    decay_rate,
    norm_gain,
    w_output,
):
    swap = [(0, 1), (1, 0)]

    def theirs(a):
        return lax.ppermute(a, "ch", swap)

    core = lax.axis_index("ch").astype(jnp.int32)
    index = lax.axis_index("seq").astype(jnp.int32)
    last = lax.axis_size("seq") - 1
    back = core.reshape(1)
    parity = (index & 1).reshape(1)
    place = (index + core * (last - 2 * index)).reshape(1)
    w_inner_2 = theirs(w_inner)
    normed, tail, small = prepare_call(
        (back, parity, place), hidden, tokens, embedding, conv_inner, norm_gain, step_bias, decay_rate
    )
    halo = onward(tail, 1)
    small_2 = theirs(small)
    w_step_t = w_step.T
    w_step_2 = theirs(w_step_t)
    w_gate_2 = theirs(w_gate)
    w_output_2 = theirs(w_output)
    gate_1 = gate_call("own", normed, w_gate)
    bc, bt = maps_call(place, normed, halo, w_state, conv_state, after=[gate_1])
    xs_1, cum_1, cumt_1, send_1, mine_1 = local_call(
        "own", place, parity, normed, halo, bt, w_inner, w_step_t, small
    )
    chain_1 = Chain("own", place, send_1, mine_1)
    xs_2, cum_2, cumt_2, send_2, mine_2 = local_call(
        "other", place, parity, normed, halo, bt, w_inner_2, w_step_2, small_2, after=[mine_1]
    )
    chain_2 = Chain("other", place, send_2, mine_2)
    done = chain_1.pair(after=[xs_2])
    y_1 = inside_call("own", xs_1, bc, cum_1, cumt_1, after=[done])
    done = chain_1.middle(after=[y_1])
    done = chain_2.pair(after=[done])
    entry_1 = chain_1.entry(after=[done])
    y_2 = inside_call("other", xs_2, bc, cum_2, cumt_2, after=[entry_1[0]])
    done = chain_2.middle(after=[y_2])
    gate_2 = gate_call("other", normed, w_gate_2, after=[done])
    entry_2 = chain_2.entry(after=[gate_2])
    partial = finish_call(
        back, parity, y_1, bc, cum_1, *entry_1, gate_1, small, w_output, after=[entry_2[0]]
    )
    full_width = float(w_inner.shape[1] * lax.axis_size("ch"))
    mine, send = finish_call(
        back, parity, y_2, bc, cum_2, *entry_2, gate_2, small_2, w_output_2, full_width, partial
    )
    return total_call(mine, theirs(send))


def solution(mesh):
    return jax.shard_map(
        body,
        mesh=mesh,
        in_specs=(
            P(("win", "seq")),
            P(("win", "seq"), None),
            P(),
            P(None, "ch"),
            P(None, "ch"),
            P(),
            P(None, "ch"),
            P(None, "ch"),
            P(),
            P("ch"),
            P("ch"),
            P("ch"),
            P("ch", None),
        ),
        out_specs=P(("win", "seq"), "ch"),
        check_vma=False,
    )
```

```python
import functools

import jax
import jax.numpy as jnp
from jax import lax
from jax.experimental import pallas as pl
from jax.experimental.pallas import tpu as pltpu
from jax.sharding import PartitionSpec as P

F32 = jnp.float32
BF16 = jnp.bfloat16
EPS = 1e-05
HALO = 16
EXTRA = 16
CHUNK = 128
TILE = 256
BLOCK = 64
MB = 1024 * 1024
VMEM = pl.BlockSpec(memory_space=pltpu.VMEM)
HBM = pl.BlockSpec(memory_space=pltpu.HBM)


def call(
    kernel, name, *, vmem, cost, scalars=(), grid=(), in_specs, out_specs, out_shape, scratch=(), after=()
):
    flops, moved, special = cost
    first = len(scalars) + len(in_specs)

    def body(*refs):
        kernel(*refs[:first], *refs[first + len(after) :])

    run = pl.pallas_call(
        body,
        grid_spec=pltpu.PrefetchScalarGridSpec(
            num_scalar_prefetch=len(scalars),
            grid=grid,
            in_specs=list(in_specs) + [pl.BlockSpec(memory_space=pl.ANY)] * len(after),
            out_specs=out_specs,
            scratch_shapes=scratch,
        ),
        out_shape=out_shape,
        compiler_params=pltpu.CompilerParams(
            vmem_limit_bytes=vmem * MB, dimension_semantics=("arbitrary",) * len(grid)
        ),
        cost_estimate=pl.CostEstimate(flops=flops, bytes_accessed=moved, transcendentals=special),
        name=name,
    )
    return lambda *arrays: run(*arrays, *after)


def micros(us):
    return (int(us * 1.1e9), int(us * 1e6), 0)


def dot(a, b):
    return jnp.dot(a, b, preferred_element_type=F32)


def dot_nt(a, b):
    return lax.dot_general(a, b, (((1,), (1,)), ((), ())), preferred_element_type=F32)


def dot_tn(a, b):
    return lax.dot_general(a, b, (((0,), (0,)), ((), ())), preferred_element_type=F32)


def flip_matrix(size):
    rows = lax.broadcasted_iota(jnp.int32, (size, size), 0)
    columns = lax.broadcasted_iota(jnp.int32, (size, size), 1)
    return jnp.where(rows + columns == size - 1, 1.0, 0.0).astype(BF16)


def flip_both(value):
    rows, width = value.shape
    turned = dot(flip_matrix(rows), value).astype(BF16)
    anti = flip_matrix(TILE)
    count = width // TILE
    blocks = [
        dot(turned[:, (count - 1 - k) * TILE : (count - k) * TILE], anti).astype(BF16)
        for k in range(count)
    ]
    return jnp.concatenate(blocks, axis=1)


def silu(v):
    half = 0.5 * v
    return half + half * jnp.tanh(half)


def two_parts(value):
    high = value.astype(BF16)
    low = (value - high.astype(F32)).astype(BF16)
    return jnp.concatenate([high, low], axis=1)


def two_rows(value):
    high = value.astype(BF16).astype(F32)
    return jnp.concatenate([high, value - high], axis=0)


def head_matrix(heads, width, head_size, first_head):
    source = lax.broadcasted_iota(jnp.int32, (2 * heads, width), 0)
    source = jnp.where(source >= heads, source - heads, source)
    target = lax.broadcasted_iota(jnp.int32, (2 * heads, width), 1) // head_size + first_head
    return jnp.where(source == target, 1.0, 0.0).astype(BF16)


def prepare_kernel(
    back_ref,
    parity_ref,
    place_ref,
    hidden_hbm,
    tokens_hbm,
    emb_hbm,
    conv_hbm,
    gain_hbm,
    bias_hbm,
    rate_hbm,
    step_hbm,
    out_ref,
    tail_ref,
    small_ref,
    hidden_ref,
    tokens_ref,
    emb_ref,
    conv_ref,
    gain_ref,
    bias_ref,
    rate_ref,
    step_ref,
    base_ref,
    normed_ref,
    sems,
):
    rows = hidden_ref.shape[0]
    kinds = emb_ref.shape[0]
    taps, inner = conv_ref.shape
    heads = bias_ref.shape[1]
    count = rows // CHUNK
    back = back_ref[0] == 1
    whole = [
        (tokens_hbm, tokens_ref),
        (emb_hbm, emb_ref),
        (conv_hbm, conv_ref),
        (gain_hbm, gain_ref),
        (bias_hbm, bias_ref),
        (rate_hbm, rate_ref),
        (step_hbm, step_ref),
    ]
    small_copies = [pltpu.make_async_copy(src, dst, sems.at[count + i]) for i, (src, dst) in enumerate(whole)]
    parts = [pl.ds(r * CHUNK, CHUNK) for r in range(count)]
    copies = [
        pltpu.make_async_copy(hidden_hbm.at[part, :], hidden_ref.at[part, :], sems.at[r])
        for r, part in enumerate(parts)
    ]
    for copy in small_copies[:2] + copies + small_copies[2:]:
        copy.start()
    for copy in small_copies[:2]:
        copy.wait()
    kind = lax.broadcasted_iota(jnp.int32, (kinds, rows), 0)
    onehot = jnp.where(kind == tokens_ref[...], 1.0, 0.0).astype(BF16)
    for r in range(count):
        copies[r].wait()
        low, high = r * CHUNK, (r + 1) * CHUNK
        base_ref[...] = dot_tn(onehot[:, low:high], emb_ref[...])
        for q in range(low, high, HALO):
            block = slice(q, q + HALO)
            merged = hidden_ref[block, :].astype(F32) + base_ref[q - low : q - low + HALO, :]
            merged = merged.astype(BF16).astype(F32)
            mean = jnp.mean(merged * merged, axis=-1, keepdims=True)
            normed_ref[q - low : q - low + HALO, :] = (merged * lax.rsqrt(mean + EPS)).astype(BF16)

        @pl.when(back)
        def _():
            out_ref[rows - high : rows - low, :] = flip_both(normed_ref[...])

        @pl.when(jnp.logical_not(back))
        def _():
            out_ref[low:high, :] = normed_ref[...]

    tail_ref[...] = out_ref[rows - HALO :, :]
    for copy in small_copies[2:]:
        copy.wait()
    small_ref[:taps, :] = conv_ref[...]
    small_ref[taps : taps + 1, :] = gain_ref[...]
    small_ref[taps + 1 : SMALL_ROWS, :] = jnp.zeros((SMALL_ROWS - taps - 1, inner), F32)
    small_ref[taps + 1 : taps + 2, :heads] = bias_ref[...]
    small_ref[taps + 2 : taps + 3, :heads] = rate_ref[...]
    small_ref[SMALL_ROWS:, :] = step_ref[...].astype(F32)


def prepare_call(scalars, hidden, tokens, embedding, conv, gain, bias, rate, step):
    rows, width = hidden.shape
    inner = conv.shape[1]
    arrays = [hidden, tokens.reshape(1, -1), embedding, conv]
    arrays += [a.reshape(1, -1) for a in (gain, bias, rate)] + [step]
    return call(
        prepare_kernel,
        "prepare",
        vmem=12,
        cost=micros(2.7),
        scalars=scalars,
        in_specs=[HBM] * len(arrays),
        out_specs=[VMEM] * 3,
        out_shape=[
            jax.ShapeDtypeStruct((rows, width), BF16),
            jax.ShapeDtypeStruct((HALO, width), BF16),
            jax.ShapeDtypeStruct((SMALL_ROWS + step.shape[0], inner), F32),
        ],
        scratch=[pltpu.VMEM(a.shape, a.dtype) for a in arrays]
        + [pltpu.VMEM((CHUNK, width), F32), pltpu.VMEM((CHUNK, width), BF16)]
        + [pltpu.SemaphoreType.DMA((rows // CHUNK + len(arrays) - 1,))],
    )(*scalars, *(pltpu.with_memory_space_constraint(a, pltpu.HBM) for a in arrays))


def gate_kernel(rows_ref, wg_ref, out_ref, gate_ref):
    rows, inner = out_ref.shape
    for low in range(0, inner, TILE):
        columns = slice(low, low + TILE)
        gate_ref[...] = dot(rows_ref[...], wg_ref[:, columns])
        for r in range(0, rows, BLOCK):
            gate = gate_ref[r : r + BLOCK, :].astype(BF16).astype(F32)
            out_ref[r : r + BLOCK, columns] = silu(gate).astype(BF16)


def gate_call(tag, normed, w_gate, after=()):
    rows = normed.shape[0]
    inner = w_gate.shape[1]
    return call(
        gate_kernel,
        "gate_" + tag,
        vmem=8,
        cost=micros(2.4),
        in_specs=[VMEM] * 2,
        out_specs=VMEM,
        out_shape=jax.ShapeDtypeStruct((rows, inner), BF16),
        scratch=[pltpu.VMEM((rows, TILE), F32)],
        after=after,
    )(normed, w_gate)


def conv_silu(rows_ref, weights, row):
    taps = weights.shape[0]
    ahead = 8
    window = rows_ref[HALO - ahead + row : HALO + row + BLOCK, :]
    total = weights[taps - 1 :, :] * window[ahead:, :]
    for back in range(1, taps):
        total += weights[taps - 1 - back : taps - back, :] * pltpu.roll(window, back, 0)[ahead:, :]
    return silu(total).astype(BF16)


def maps_kernel(place_ref, normed_ref, halo_ref, ws_ref, cs_ref, bc_ref, bt_ref, rows_ref):
    rows = normed_ref.shape[0]
    states = bc_ref.shape[1] // 2
    before = dot(halo_ref[...], ws_ref[...]).astype(BF16).astype(F32)
    rows_ref[:HALO, :] = jnp.where(place_ref[0] >= 1, before, 0.0)
    rows_ref[HALO:, :] = dot(normed_ref[...], ws_ref[...]).astype(BF16).astype(F32)
    weights = cs_ref[...]
    for r in range(0, rows, BLOCK):
        bc_ref[r : r + BLOCK, :] = conv_silu(rows_ref, weights, r)
    bt_ref[...] = bc_ref[:, :states].astype(F32).T.astype(BF16)


def maps_call(place, normed, halo, w_state, conv_state, after=()):
    rows = normed.shape[0]
    both = w_state.shape[1]
    return call(
        maps_kernel,
        "maps",
        vmem=8,
        cost=micros(1.5),
        scalars=(place,),
        in_specs=[VMEM] * 4,
        out_specs=[VMEM] * 2,
        out_shape=[
            jax.ShapeDtypeStruct((rows, both), BF16),
            jax.ShapeDtypeStruct((both // 2, rows), BF16),
        ],
        scratch=[pltpu.VMEM((rows + HALO, both), F32)],
        after=after,
    )(place, normed, halo, w_state, conv_state)


def local_kernel(
    head_size,
    place_ref,
    parity_ref,
    normed_ref,
    halo_ref,
    bt_ref,
    wi_ref,
    small_ref,
    x_ref,
    cum_ref,
    times_ref,
    send_ref,
    mine_ref,
    rows_ref,
    spread_ref,
    scaled_ref,
    left_ref,
    whole_ref,
    payload_ref,
):
    rows = normed_ref.shape[0]
    states = bt_ref.shape[0]
    heads = cum_ref.shape[1]
    taps = SMALL_TAPS
    raw = dot_nt(normed_ref[...], small_ref[SMALL_ROWS:, :].astype(BF16))
    columns = small_ref[:SMALL_ROWS, :CHUNK].T
    raw = raw.T + columns[:heads, taps + 1 : taps + 2]
    step = jnp.maximum(raw, 0.0) + jnp.log1p(jnp.exp(-jnp.abs(raw)))
    logdecay = -step * columns[:heads, taps + 2 : taps + 3]
    high = logdecay.astype(BF16)
    rest = logdecay - high.astype(F32)
    mid = rest.astype(BF16)
    low = (rest - mid.astype(F32)).astype(BF16)
    starts = range(0, rows, CHUNK)
    pieces = [part[:, r : r + CHUNK] for r in starts for part in (high, mid, low)]
    frm = lax.broadcasted_iota(jnp.int32, (CHUNK, CHUNK), 0)
    to = lax.broadcasted_iota(jnp.int32, (CHUNK, CHUNK), 1)
    sums = dot(jnp.concatenate(pieces, axis=0), jnp.where(to >= frm, 1.0, 0.0).astype(BF16))
    run = jnp.zeros((heads, 1), F32)
    cums = []
    for i in range(len(starts)):
        at = 3 * i * heads
        cums.append(sums[at : at + heads] + sums[at + heads : at + 2 * heads] + sums[at + 2 * heads : at + 3 * heads] + run)
        run = cums[-1][:, CHUNK - 1 :]
    cum = jnp.concatenate(cums, axis=1)
    times_ref[:heads, :] = cum
    times_ref[heads:, :] = step
    cum_ref[...] = cum.T
    left_ref[...] = two_rows(step * jnp.exp(run - cum)).T.astype(BF16)
    whole_ref[...] = two_parts(jnp.exp(cum_ref[rows - 1 :, :]))

    inner = x_ref.shape[1]
    half = inner // 2
    tiles = range(inner // TILE)
    onehots = [head_matrix(heads, TILE, head_size, t * (TILE // head_size)) for t in tiles]
    spans = [slice(t * TILE, (t + 1) * TILE) for t in tiles]

    def project(t):
        weights = wi_ref[:, spans[t]]
        before = dot(halo_ref[...], weights).astype(BF16).astype(F32)
        rows_ref[t % 2, :HALO, :] = jnp.where(place_ref[0] >= 1, before, 0.0)
        rows_ref[t % 2, HALO:, :] = dot(normed_ref[...], weights).astype(BF16).astype(F32)
        spread_ref[t % 2] = dot(left_ref[...], onehots[t])

    def combine(t):
        taps_here = small_ref[:taps, spans[t]]
        for r in range(0, rows, BLOCK):
            block = slice(r, r + BLOCK)
            x = conv_silu(rows_ref.at[t % 2], taps_here, r)
            x_ref[block, spans[t]] = x
            scaled_ref[t % 2, block, :] = (x.astype(F32) * spread_ref[t % 2, block, :]).astype(BF16)
        state = dot(bt_ref[...], scaled_ref[t % 2])
        here = slice(t * TILE % half, t * TILE % half + TILE)
        is_mine = jnp.where(parity_ref[0] == t * TILE // half, 1, 0)
        write_payload(payload_ref.at[is_mine], here, state, dot(whole_ref[...], onehots[t]))

    project(0)
    for t in tiles:
        if t + 1 < len(tiles):
            project(t + 1)
        combine(t)
    send_ref[...] = payload_ref[0]
    mine_ref[...] = payload_ref[1]


SMALL_TAPS = 4
SMALL_ROWS = 8


def local_call(tag, place, parity, normed, halo, bt, w_inner, small, after=()):
    rows = normed.shape[0]
    inner = w_inner.shape[1]
    heads = small.shape[0] - SMALL_ROWS
    states = bt.shape[0]
    return call(
        functools.partial(local_kernel, inner // heads),
        "local_" + tag,
        vmem=12,
        cost=micros(5.0),
        scalars=(place, parity),
        in_specs=[VMEM] * 5,
        out_specs=[VMEM] * 5,
        out_shape=[
            jax.ShapeDtypeStruct((rows, inner), BF16),
            jax.ShapeDtypeStruct((rows, heads), F32),
            jax.ShapeDtypeStruct((2 * heads, rows), F32),
            jax.ShapeDtypeStruct((states + EXTRA, inner // 2), BF16),
            jax.ShapeDtypeStruct((states + EXTRA, inner // 2), BF16),
        ],
        scratch=[
            pltpu.VMEM((2, rows + HALO, TILE), F32),
            pltpu.VMEM((2, rows, TILE), F32),
            pltpu.VMEM((2, rows, TILE), BF16),
            pltpu.VMEM((rows, 2 * heads), BF16),
            pltpu.VMEM((1, 2 * heads), BF16),
            pltpu.VMEM((2, states + EXTRA, inner // 2), BF16),
        ],
        after=after,
    )(place, parity, normed, halo, bt, w_inner, small)


def inside_kernel(head_size, x_ref, bc_ref, bt_ref, cum_ref, times_ref, y_ref, state_ref):
    rows, inner = x_ref.shape
    states = bc_ref.shape[1] // 2
    heads = cum_ref.shape[1]
    length = CHUNK
    last = length - 1
    pair = 2 * head_size
    lane = lax.broadcasted_iota(jnp.int32, (length, pair), 1)
    to = lax.broadcasted_iota(jnp.int32, (length, length), 0)
    frm = lax.broadcasted_iota(jnp.int32, (length, length), 1)
    state_ref[...] = jnp.zeros_like(state_ref)

    def chunk(c, before):
        at = slice(c * length, (c + 1) * length)
        bmat = bt_ref[:, at]
        cmat = bc_ref[at, states:]
        scores = jnp.where(to >= frm, dot(cmat, bmat), 0.0)
        cum = cum_ref[at, :]
        cumt = times_ref[:heads, at]
        step = times_ref[heads:, at]
        end = cumt[:, last:]
        since = two_rows(jnp.exp(cumt - before)).T.astype(BF16)
        left = two_rows(step * jnp.exp(end - cumt)).T.astype(BF16)
        for first in range(0, heads, TILE // head_size):
            columns = slice(first * head_size, first * head_size + TILE)
            onehot = head_matrix(heads, TILE, head_size, first)
            since_here = dot(since, onehot)
            state = state_ref[:, columns]
            carried = dot(cmat, state.astype(BF16)) * since_here
            scaled = (x_ref[at, columns].astype(F32) * dot(left, onehot)).astype(BF16)
            state_ref[:, columns] = state * since_here[last:, :] + dot(bmat, scaled)
            for start in range(0, TILE, pair):
                low = first * head_size + start
                weights = []
                for h in (low // head_size, low // head_size + 1):
                    apart = jnp.minimum(cum[:, h : h + 1] - cumt[h : h + 1, :], 0.0)
                    weights.append((jnp.exp(apart) * (scores * step[h : h + 1, :])).astype(BF16))
                mine = x_ref[at, low : low + pair]
                none = jnp.zeros_like(mine)
                stacked = jnp.concatenate(
                    [jnp.where(lane < head_size, mine, none), jnp.where(lane < head_size, none, mine)], axis=0
                )
                inside = dot(jnp.concatenate(weights, axis=1), stacked)
                y_ref[at, low : low + pair] = (inside + carried[:, start : start + pair]).astype(BF16)
        return end

    before = jnp.zeros((heads, 1), F32)
    for c in range(rows // length):
        before = chunk(c, before)


def inside_call(tag, x, bc, bt, cum, times, after=()):
    rows, inner = x.shape
    heads = cum.shape[1]
    both = bc.shape[1]
    return call(
        functools.partial(inside_kernel, inner // heads),
        "inside_" + tag,
        vmem=8,
        cost=micros(3.2),
        in_specs=[VMEM] * 5,
        out_specs=VMEM,
        out_shape=jax.ShapeDtypeStruct((rows, inner), BF16),
        scratch=[pltpu.VMEM((both // 2, inner), F32)],
        after=after,
    )(x, bc, bt, cum, times)


def parts_of(ref, known=None):
    states = ref.shape[0] - EXTRA
    state = ref[:states, :].astype(F32)
    extra = ref[states:, :].astype(F32)
    decay = extra[:1] + extra[1:2]
    if known is None:
        return state, decay
    return jnp.where(known, state, 0.0), jnp.where(known, decay, 0.0)


def write_payload(out_ref, columns, state, decay):
    states = state.shape[0]
    out_ref[:states, columns] = state.astype(BF16)
    decay = jnp.broadcast_to(decay, (EXTRA, decay.shape[1]))
    high = decay.astype(BF16).astype(F32)
    place = lax.broadcasted_iota(jnp.int32, decay.shape, 0)
    out_ref[states:, columns] = jnp.where(place == 0, high, decay - high).astype(BF16)


ALL = slice(None)


def pair_kernel(place_ref, mine_ref, other_ref, out_ref):
    mine, mine_a = parts_of(mine_ref)
    other, other_a = parts_of(other_ref)
    is_first = lax.rem(place_ref[0], 2) == 0
    early = jnp.where(is_first, mine, other)
    late = jnp.where(is_first, other, mine)
    late_a = jnp.where(is_first, other_a, mine_a)
    write_payload(out_ref, ALL, late_a * early + late, mine_a * other_a)


def chain_kernel(reach, place_ref, pair_ref, before_ref, out_ref):
    pair, pair_a = parts_of(pair_ref)
    before, before_a = parts_of(before_ref, place_ref[0] >= reach)
    write_payload(out_ref, ALL, pair_a * before + pair, pair_a * before_a)


def longer_kernel(reach, farther_reach, place_ref, before_ref, farther_ref, out_ref):
    before, before_a = parts_of(before_ref, place_ref[0] >= reach)
    farther, farther_a = parts_of(farther_ref, place_ref[0] >= farther_reach)
    write_payload(out_ref, ALL, before + before_a * farther, before_a * farther_a)


def entry_kernel(reach, farther_reach, place_ref, mine_ref, other_ref, before_ref, farther_ref, keep_ref, send_ref):
    mine, mine_a = parts_of(mine_ref)
    other, other_a = parts_of(other_ref)
    before, before_a = parts_of(before_ref, place_ref[0] >= reach)
    farther, _ = parts_of(farther_ref, place_ref[0] >= farther_reach)
    is_first = lax.rem(place_ref[0], 2) == 0
    entry_first = before + before_a * farther
    early = jnp.where(is_first, mine, other)
    early_a = jnp.where(is_first, mine_a, other_a)
    entry_second = early_a * entry_first + early
    keep_ref[...] = jnp.where(is_first, entry_first, entry_second).astype(BF16)
    send_ref[...] = jnp.where(is_first, entry_second, entry_first).astype(BF16)


def small_call(kernel, name, place, arrays, shapes, after=()):
    return call(
        kernel,
        name,
        vmem=4,
        cost=micros(0.5),
        scalars=(place,),
        in_specs=[VMEM] * len(arrays),
        out_specs=[VMEM] * len(shapes),
        out_shape=[jax.ShapeDtypeStruct(s, BF16) for s in shapes],
        after=after,
    )(place, *arrays)


def onward(value, by):
    count = lax.axis_size("seq")
    pairs = []
    for i in range(count):
        up = (i + by, 0) if i + by < count else (i, 1)
        down = (i - by, 1) if i - by >= 0 else (i, 0)
        pairs += [(2 * i, 2 * up[0] + up[1]), (2 * i + 1, 2 * down[0] + down[1])]
    return lax.ppermute(value, ("seq", "ch"), pairs)


class Chain:
    def __init__(self, tag, place, send, mine):
        self.tag, self.place, self.mine = tag, place, mine
        self.count = lax.axis_size("seq")
        self.swap = [(i, i ^ 1) for i in range(self.count)]
        self.other = lax.ppermute(send, "seq", self.swap)
        self.before = self.farther = None
        self.reach = self.farther_reach = 0
        self.apart = 2

    def pair(self, after):
        (self.pair_state,) = small_call(
            pair_kernel, "pair_" + self.tag, self.place, [self.mine, self.other], [self.mine.shape], after
        )
        self.running = self.pair_state
        self.hop()
        return self.pair_state

    def hop(self):
        if self.apart < self.count:
            self.arrived = onward(self.running, self.apart)

    def middle(self, after):
        while self.apart * 2 < self.count:
            self.take(after)
            (self.running,) = small_call(
                functools.partial(chain_kernel, self.reach),
                "chain_" + self.tag,
                self.place,
                [self.pair_state, self.before],
                [self.mine.shape],
                after,
            )
            self.apart *= 2
            self.hop()
        return self.running

    def take(self, after=()):
        if self.before is None:
            self.before, self.reach = self.arrived, self.apart
        else:
            (self.before,) = small_call(
                functools.partial(longer_kernel, self.reach, self.apart),
                "longer_" + self.tag,
                self.place,
                [self.before, self.arrived],
                [self.mine.shape],
                after,
            )
            self.reach = 0

    def entry(self, after):
        shape = self.mine.shape
        if self.apart < self.count:
            if self.before is None:
                self.before, self.reach = self.arrived, self.apart
                self.farther, self.farther_reach = self.arrived, self.count
            else:
                self.farther, self.farther_reach = self.arrived, self.apart
        else:
            self.before = self.farther = self.mine
            self.reach = self.farther_reach = self.count
        half = (shape[0] - EXTRA, shape[1])
        keep, out = small_call(
            functools.partial(entry_kernel, self.reach, self.farther_reach),
            "entry_" + self.tag,
            self.place,
            [self.mine, self.other, self.before, self.farther],
            [half, half],
            after,
        )
        return keep, lax.ppermute(out, "seq", self.swap)


def gated_part(
    head_size, swap, y_ref, bc_ref, cum_ref, keep_ref, other_ref, gate_ref, small_ref, wo_ref, scaled_ref, tile_ref
):
    rows, inner = y_ref.shape
    states = bc_ref.shape[1] // 2
    heads = cum_ref.shape[1]
    half = inner // 2
    since = two_parts(jnp.exp(cum_ref[...]))
    squares = [0.0] * (rows // BLOCK)
    for low in range(0, inner, TILE):
        columns = slice(low, low + TILE)
        here = slice(low % half, low % half + TILE)
        use_other = swap if low < half else jnp.logical_not(swap)
        entry = jnp.where(use_other, other_ref[:, here], keep_ref[:, here])
        tile_ref[0] = dot(bc_ref[:, states:], entry)
        tile_ref[1] = dot(since, head_matrix(heads, TILE, head_size, low // head_size))
        gain = small_ref[SMALL_TAPS : SMALL_TAPS + 1, columns]
        for i, r in enumerate(range(0, rows, BLOCK)):
            block = slice(r, r + BLOCK)
            gated = y_ref[block, columns].astype(F32) + tile_ref[0, block, :] * tile_ref[1, block, :]
            gated = gated * gate_ref[block, columns].astype(F32)
            squares[i] += jnp.sum(gated * gated, axis=-1, keepdims=True)
            scaled_ref[block, columns] = (gated * gain).astype(BF16)
    return squares


def part_kernel(head_size, parity_ref, *refs):
    *ins, out_ref, sq_ref, scaled_ref, tile_ref = refs
    squares = gated_part(head_size, parity_ref[0] == 1, *ins, scaled_ref, tile_ref)
    for i, square in enumerate(squares):
        sq_ref[i * BLOCK : (i + 1) * BLOCK, :] = jnp.broadcast_to(square, (BLOCK, sq_ref.shape[1]))
    for low in range(0, out_ref.shape[1], TILE):
        out_ref[:, low : low + TILE] = dot(scaled_ref[...], ins[-1][:, low : low + TILE])


def product(back, scaled_ref, weights_ref, part_ref, scale_ref, tile_ref, half_ref, out_ref, first):
    rows, half = out_ref.shape
    for low in range(0, half, TILE):
        columns = slice(first + low, first + low + TILE)
        tile_ref[...] = dot(scaled_ref[...], weights_ref[:, columns])
        for r in range(0, rows, BLOCK):
            block = slice(r, r + BLOCK)
            value = (tile_ref[block, :] + part_ref[block, columns]) * scale_ref[block, :1]
            half_ref[block, low : low + TILE] = value.astype(BF16)

    @pl.when(back == 1)
    def _():
        turn = flip_matrix(TILE)
        for r in range(0, rows, TILE):
            for low in range(0, half, TILE):
                tile = dot(turn, half_ref[r : r + TILE, low : low + TILE]).astype(BF16)
                tile = dot(tile, turn).astype(BF16)
                to_row, to = rows - TILE - r, half - TILE - low
                out_ref[to_row : to_row + TILE, to : to + TILE] = tile

    @pl.when(back != 1)
    def _():
        out_ref[...] = half_ref[...]


def finish_kernel(head_size, full_width, back_ref, parity_ref, *refs):
    *ins, part_ref, psq_ref, send_ref, scaled_ref, scale_ref, tile_ref, half_ref = refs
    squares = gated_part(head_size, parity_ref[0] == 1, *ins, scaled_ref, tile_ref)
    for i, square in enumerate(squares):
        block = slice(i * BLOCK, (i + 1) * BLOCK)
        scale = lax.rsqrt((square + psq_ref[block, :1]) / full_width + EPS)
        scale_ref[block, :] = jnp.broadcast_to(scale, (BLOCK, scale_ref.shape[1]))
    product(back_ref[0], scaled_ref, ins[-1], part_ref, scale_ref, tile_ref.at[0], half_ref, send_ref, send_ref.shape[1])


def own_kernel(back_ref, scaled_ref, weights_ref, part_ref, scale_ref, own_ref, tile_ref, half_ref):
    product(back_ref[0], scaled_ref, weights_ref, part_ref, scale_ref, tile_ref, half_ref, own_ref, 0)


def own_call(back, scaled, w_output, part, scale, after):
    rows, width = part.shape
    half = width // 2
    return call(
        own_kernel,
        "own_half",
        vmem=8,
        cost=micros(0.7),
        scalars=(back,),
        in_specs=[VMEM] * 4,
        out_specs=VMEM,
        out_shape=jax.ShapeDtypeStruct((rows, half), BF16),
        scratch=[pltpu.VMEM((rows, TILE), F32), pltpu.VMEM((rows, half), BF16)],
        after=after,
    )(back, scaled, w_output, part, scale)


def finish_call(back, parity, y, bc, cum, keep, other, gate, small, w_output, full_width=None, partial=None, after=()):
    rows, inner = y.shape
    width = w_output.shape[1]
    half = width // 2
    heads = cum.shape[1]
    arrays = [y, bc, cum, keep, other, gate, small, w_output]
    tiles = pltpu.VMEM((2, rows, TILE), F32)
    if partial is None:
        scratch = [pltpu.VMEM((rows, inner), BF16), tiles]
        scalars = (parity,)
        kernel = functools.partial(part_kernel, inner // heads)
        out_shape = [jax.ShapeDtypeStruct((rows, width), F32), jax.ShapeDtypeStruct((rows, 128), F32)]
    else:
        scalars = (back, parity)
        scratch = [tiles, pltpu.VMEM((rows, half), BF16)]
        kernel = functools.partial(finish_kernel, inner // heads, full_width)
        arrays += list(partial)
        out_shape = [
            jax.ShapeDtypeStruct((rows, half), BF16),
            jax.ShapeDtypeStruct((rows, inner), BF16),
            jax.ShapeDtypeStruct((rows, 128), F32),
        ]
    return call(
        kernel,
        "part" if partial is None else "finish",
        vmem=16,
        cost=micros(3.5),
        scalars=scalars,
        in_specs=[VMEM] * len(arrays),
        out_specs=[VMEM] * len(out_shape),
        out_shape=out_shape,
        scratch=scratch,
        after=after,
    )(*scalars, *arrays)


def total_kernel(mine_ref, theirs_ref, out_hbm, out_ref, sems):
    copies = []
    for i, r in enumerate(range(0, mine_ref.shape[0], CHUNK)):
        for q in range(r, r + CHUNK, BLOCK):
            block = slice(q, q + BLOCK)
            out_ref[block, :] = (mine_ref[block, :].astype(F32) + theirs_ref[block, :].astype(F32)).astype(BF16)
        part = pl.ds(r, CHUNK)
        copies.append(pltpu.make_async_copy(out_ref.at[part, :], out_hbm.at[part, :], sems.at[i]))
        copies[-1].start()
    for copy in copies:
        copy.wait()


def total_call(mine, theirs):
    rows, half = mine.shape
    return call(
        total_kernel,
        "total",
        vmem=4,
        cost=micros(0.8),
        in_specs=[VMEM] * 2,
        out_specs=HBM,
        out_shape=jax.ShapeDtypeStruct((rows, half), BF16),
        scratch=[pltpu.VMEM((rows, half), BF16), pltpu.SemaphoreType.DMA((rows // CHUNK,))],
    )(mine, theirs)


def body(
    tokens,
    hidden,
    embedding,
    w_gate,
    w_inner,
    w_state,
    w_step,
    conv_inner,
    conv_state,
    step_bias,
    decay_rate,
    norm_gain,
    w_output,
):
    swap = [(0, 1), (1, 0)]

    def theirs(a):
        return lax.ppermute(a, "ch", swap)

    core = lax.axis_index("ch").astype(jnp.int32)
    index = lax.axis_index("seq").astype(jnp.int32)
    last = lax.axis_size("seq") - 1
    back = core.reshape(1)
    parity = (index & 1).reshape(1)
    place = (index + core * (last - 2 * index)).reshape(1)
    w_inner_2 = theirs(w_inner)
    normed, tail, small = prepare_call(
        (back, parity, place), hidden, tokens, embedding, conv_inner, norm_gain, step_bias, decay_rate, w_step.T
    )
    halo = onward(tail, 1)
    small_2 = theirs(small)
    w_gate_2 = theirs(w_gate)
    w_output_2 = theirs(w_output)
    gate_1 = gate_call("own", normed, w_gate)
    bc, bt = maps_call(place, normed, halo, w_state, conv_state, after=[gate_1])
    x_1, cum_1, times_1, send_1, mine_1 = local_call(
        "own", place, parity, normed, halo, bt, w_inner, small
    )
    chain_1 = Chain("own", place, send_1, mine_1)
    x_2, cum_2, times_2, send_2, mine_2 = local_call(
        "other", place, parity, normed, halo, bt, w_inner_2, small_2, after=[mine_1]
    )
    chain_2 = Chain("other", place, send_2, mine_2)
    done = chain_1.pair(after=[x_2])
    y_1 = inside_call("own", x_1, bc, bt, cum_1, times_1, after=[done])
    done = chain_1.middle(after=[y_1])
    done = chain_2.pair(after=[done])
    entry_1 = chain_1.entry(after=[done])
    y_2 = inside_call("other", x_2, bc, bt, cum_2, times_2, after=[entry_1[0]])
    done = chain_2.middle(after=[y_2])
    gate_2 = gate_call("other", normed, w_gate_2, after=[done])
    entry_2 = chain_2.entry(after=[gate_2])
    partial = finish_call(
        back, parity, y_1, bc, cum_1, *entry_1, gate_1, small, w_output, after=[entry_2[0]]
    )
    full_width = float(w_inner.shape[1] * lax.axis_size("ch"))
    send, scaled, scale = finish_call(
        back, parity, y_2, bc, cum_2, *entry_2, gate_2, small_2, w_output_2, full_width, partial
    )
    arriving = theirs(send)
    mine = own_call(back, scaled, w_output_2, partial[0], scale, after=[send])
    return total_call(mine, arriving)


def solution(mesh):
    return jax.shard_map(
        body,
        mesh=mesh,
        in_specs=(
            P(("win", "seq")),
            P(("win", "seq"), None),
            P(),
            P(None, "ch"),
            P(None, "ch"),
            P(),
            P(None, "ch"),
            P(None, "ch"),
            P(),
            P("ch"),
            P("ch"),
            P("ch"),
            P("ch", None),
        ),
        out_specs=P(("win", "seq"), "ch"),
        check_vma=False,
    )
```

```python
import functools

import jax
import jax.numpy as jnp
from jax import lax
from jax.experimental import pallas as pl
from jax.experimental.pallas import tpu as pltpu
from jax.sharding import PartitionSpec as P

F32 = jnp.float32
BF16 = jnp.bfloat16
EPS = 1e-05
HALO = 16
EXTRA = 16
CHUNK = 128
TILE = 256
BLOCK = 64
MB = 1024 * 1024
VMEM = pl.BlockSpec(memory_space=pltpu.VMEM)
HBM = pl.BlockSpec(memory_space=pltpu.HBM)


def call(
    kernel, name, *, vmem, cost, scalars=(), grid=(), in_specs, out_specs, out_shape, scratch=(), after=()
):
    flops, moved, special = cost
    first = len(scalars) + len(in_specs)

    def body(*refs):
        kernel(*refs[:first], *refs[first + len(after) :])

    run = pl.pallas_call(
        body,
        grid_spec=pltpu.PrefetchScalarGridSpec(
            num_scalar_prefetch=len(scalars),
            grid=grid,
            in_specs=list(in_specs) + [pl.BlockSpec(memory_space=pl.ANY)] * len(after),
            out_specs=out_specs,
            scratch_shapes=scratch,
        ),
        out_shape=out_shape,
        compiler_params=pltpu.CompilerParams(
            vmem_limit_bytes=vmem * MB, dimension_semantics=("arbitrary",) * len(grid)
        ),
        cost_estimate=pl.CostEstimate(flops=flops, bytes_accessed=moved, transcendentals=special),
        name=name,
    )
    return lambda *arrays: run(*arrays, *after)


def micros(us):
    return (int(us * 1.1e9), int(us * 1e6), 0)


def dot(a, b):
    return jnp.dot(a, b, preferred_element_type=F32)


def dot_nt(a, b):
    return lax.dot_general(a, b, (((1,), (1,)), ((), ())), preferred_element_type=F32)


def dot_tn(a, b):
    return lax.dot_general(a, b, (((0,), (0,)), ((), ())), preferred_element_type=F32)


def flip_matrix(size):
    rows = lax.broadcasted_iota(jnp.int32, (size, size), 0)
    columns = lax.broadcasted_iota(jnp.int32, (size, size), 1)
    return jnp.where(rows + columns == size - 1, 1.0, 0.0).astype(BF16)


def flip_both(value):
    rows, width = value.shape
    turned = dot(flip_matrix(rows), value).astype(BF16)
    anti = flip_matrix(TILE)
    count = width // TILE
    blocks = [
        dot(turned[:, (count - 1 - k) * TILE : (count - k) * TILE], anti).astype(BF16)
        for k in range(count)
    ]
    return jnp.concatenate(blocks, axis=1)


def silu(v):
    half = 0.5 * v
    return half + half * jnp.tanh(half)


def two_parts(value):
    high = value.astype(BF16)
    low = (value - high.astype(F32)).astype(BF16)
    return jnp.concatenate([high, low], axis=1)


def two_rows(value):
    high = value.astype(BF16).astype(F32)
    return jnp.concatenate([high, value - high], axis=0)


def head_matrix(heads, width, head_size, first_head):
    source = lax.broadcasted_iota(jnp.int32, (2 * heads, width), 0)
    source = jnp.where(source >= heads, source - heads, source)
    target = lax.broadcasted_iota(jnp.int32, (2 * heads, width), 1) // head_size + first_head
    return jnp.where(source == target, 1.0, 0.0).astype(BF16)


def prepare_kernel(
    back_ref,
    parity_ref,
    place_ref,
    hidden_hbm,
    tokens_hbm,
    emb_hbm,
    conv_hbm,
    gain_hbm,
    bias_hbm,
    rate_hbm,
    step_hbm,
    out_ref,
    tail_ref,
    small_ref,
    hidden_ref,
    tokens_ref,
    emb_ref,
    conv_ref,
    gain_ref,
    bias_ref,
    rate_ref,
    step_ref,
    base_ref,
    normed_ref,
    sems,
):
    rows = hidden_ref.shape[0]
    kinds = emb_ref.shape[0]
    taps, inner = conv_ref.shape
    heads = bias_ref.shape[1]
    count = rows // CHUNK
    back = back_ref[0] == 1
    whole = [
        (tokens_hbm, tokens_ref),
        (emb_hbm, emb_ref),
        (conv_hbm, conv_ref),
        (gain_hbm, gain_ref),
        (bias_hbm, bias_ref),
        (rate_hbm, rate_ref),
        (step_hbm, step_ref),
    ]
    small_copies = [pltpu.make_async_copy(src, dst, sems.at[count + i]) for i, (src, dst) in enumerate(whole)]
    parts = [pl.ds(r * CHUNK, CHUNK) for r in range(count)]
    copies = [
        pltpu.make_async_copy(hidden_hbm.at[part, :], hidden_ref.at[part, :], sems.at[r])
        for r, part in enumerate(parts)
    ]
    for copy in small_copies[:2] + copies + small_copies[2:]:
        copy.start()
    for copy in small_copies[:2]:
        copy.wait()
    kind = lax.broadcasted_iota(jnp.int32, (kinds, rows), 0)
    onehot = jnp.where(kind == tokens_ref[...], 1.0, 0.0).astype(BF16)
    for r in range(count):
        copies[r].wait()
        low, high = r * CHUNK, (r + 1) * CHUNK
        base_ref[...] = dot_tn(onehot[:, low:high], emb_ref[...])
        for q in range(low, high, HALO):
            block = slice(q, q + HALO)
            merged = hidden_ref[block, :].astype(F32) + base_ref[q - low : q - low + HALO, :]
            merged = merged.astype(BF16).astype(F32)
            mean = jnp.mean(merged * merged, axis=-1, keepdims=True)
            normed_ref[q - low : q - low + HALO, :] = (merged * lax.rsqrt(mean + EPS)).astype(BF16)

        @pl.when(back)
        def _():
            out_ref[rows - high : rows - low, :] = flip_both(normed_ref[...])

        @pl.when(jnp.logical_not(back))
        def _():
            out_ref[low:high, :] = normed_ref[...]

    tail_ref[...] = out_ref[rows - HALO :, :]
    for copy in small_copies[2:]:
        copy.wait()
    small_ref[:taps, :] = conv_ref[...]
    small_ref[taps : taps + 1, :] = gain_ref[...]
    small_ref[taps + 1 : SMALL_ROWS, :] = jnp.zeros((SMALL_ROWS - taps - 1, inner), F32)
    small_ref[taps + 1 : taps + 2, :heads] = bias_ref[...]
    small_ref[taps + 2 : taps + 3, :heads] = rate_ref[...]
    small_ref[SMALL_ROWS:, :] = step_ref[...].astype(F32)


def prepare_call(scalars, hidden, tokens, embedding, conv, gain, bias, rate, step):
    rows, width = hidden.shape
    inner = conv.shape[1]
    arrays = [hidden, tokens.reshape(1, -1), embedding, conv]
    arrays += [a.reshape(1, -1) for a in (gain, bias, rate)] + [step]
    return call(
        prepare_kernel,
        "prepare",
        vmem=12,
        cost=micros(2.7),
        scalars=scalars,
        in_specs=[HBM] * len(arrays),
        out_specs=[VMEM] * 3,
        out_shape=[
            jax.ShapeDtypeStruct((rows, width), BF16),
            jax.ShapeDtypeStruct((HALO, width), BF16),
            jax.ShapeDtypeStruct((SMALL_ROWS + step.shape[0], inner), F32),
        ],
        scratch=[pltpu.VMEM(a.shape, a.dtype) for a in arrays]
        + [pltpu.VMEM((CHUNK, width), F32), pltpu.VMEM((CHUNK, width), BF16)]
        + [pltpu.SemaphoreType.DMA((rows // CHUNK + len(arrays) - 1,))],
    )(*scalars, *(pltpu.with_memory_space_constraint(a, pltpu.HBM) for a in arrays))


def gate_kernel(rows_ref, wg_ref, out_ref, gate_ref):
    rows, inner = out_ref.shape
    for low in range(0, inner, TILE):
        columns = slice(low, low + TILE)
        gate_ref[...] = dot(rows_ref[...], wg_ref[:, columns])
        for r in range(0, rows, BLOCK):
            gate = gate_ref[r : r + BLOCK, :].astype(BF16).astype(F32)
            out_ref[r : r + BLOCK, columns] = silu(gate).astype(BF16)


def gate_call(tag, normed, w_gate, after=()):
    rows = normed.shape[0]
    inner = w_gate.shape[1]
    return call(
        gate_kernel,
        "gate_" + tag,
        vmem=8,
        cost=micros(2.4),
        in_specs=[VMEM] * 2,
        out_specs=VMEM,
        out_shape=jax.ShapeDtypeStruct((rows, inner), BF16),
        scratch=[pltpu.VMEM((rows, TILE), F32)],
        after=after,
    )(normed, w_gate)


def conv_silu(rows_ref, weights, row):
    taps = weights.shape[0]
    ahead = 8
    window = rows_ref[HALO - ahead + row : HALO + row + BLOCK, :]
    total = weights[taps - 1 :, :] * window[ahead:, :]
    for back in range(1, taps):
        total += weights[taps - 1 - back : taps - back, :] * pltpu.roll(window, back, 0)[ahead:, :]
    return silu(total).astype(BF16)


def maps_kernel(place_ref, normed_ref, halo_ref, ws_ref, cs_ref, bc_ref, bt_ref, rows_ref):
    rows = normed_ref.shape[0]
    states = bc_ref.shape[1] // 2
    before = dot(halo_ref[...], ws_ref[...]).astype(BF16).astype(F32)
    rows_ref[:HALO, :] = jnp.where(place_ref[0] >= 1, before, 0.0)
    rows_ref[HALO:, :] = dot(normed_ref[...], ws_ref[...]).astype(BF16).astype(F32)
    weights = cs_ref[...]
    for r in range(0, rows, BLOCK):
        bc_ref[r : r + BLOCK, :] = conv_silu(rows_ref, weights, r)
    bt_ref[...] = bc_ref[:, :states].astype(F32).T.astype(BF16)


def maps_call(place, normed, halo, w_state, conv_state, after=()):
    rows = normed.shape[0]
    both = w_state.shape[1]
    return call(
        maps_kernel,
        "maps",
        vmem=8,
        cost=micros(1.5),
        scalars=(place,),
        in_specs=[VMEM] * 4,
        out_specs=[VMEM] * 2,
        out_shape=[
            jax.ShapeDtypeStruct((rows, both), BF16),
            jax.ShapeDtypeStruct((both // 2, rows), BF16),
        ],
        scratch=[pltpu.VMEM((rows + HALO, both), F32)],
        after=after,
    )(place, normed, halo, w_state, conv_state)


def local_kernel(
    head_size,
    place_ref,
    parity_ref,
    normed_ref,
    halo_ref,
    bt_ref,
    wi_ref,
    small_ref,
    x_ref,
    cum_ref,
    times_ref,
    send_ref,
    mine_ref,
    rows_ref,
    spread_ref,
    scaled_ref,
    left_ref,
    whole_ref,
    payload_ref,
):
    rows = normed_ref.shape[0]
    states = bt_ref.shape[0]
    heads = cum_ref.shape[1]
    taps = SMALL_TAPS
    raw = dot_nt(normed_ref[...], small_ref[SMALL_ROWS:, :].astype(BF16))
    columns = small_ref[:SMALL_ROWS, :CHUNK].T
    raw = raw.T + columns[:heads, taps + 1 : taps + 2]
    step = jnp.maximum(raw, 0.0) + jnp.log1p(jnp.exp(-jnp.abs(raw)))
    logdecay = -step * columns[:heads, taps + 2 : taps + 3]
    high = logdecay.astype(BF16)
    rest = logdecay - high.astype(F32)
    mid = rest.astype(BF16)
    low = (rest - mid.astype(F32)).astype(BF16)
    starts = range(0, rows, CHUNK)
    pieces = [part[:, r : r + CHUNK] for r in starts for part in (high, mid, low)]
    frm = lax.broadcasted_iota(jnp.int32, (CHUNK, CHUNK), 0)
    to = lax.broadcasted_iota(jnp.int32, (CHUNK, CHUNK), 1)
    sums = dot(jnp.concatenate(pieces, axis=0), jnp.where(to >= frm, 1.0, 0.0).astype(BF16))
    run = jnp.zeros((heads, 1), F32)
    cums = []
    for i in range(len(starts)):
        at = 3 * i * heads
        cums.append(sums[at : at + heads] + sums[at + heads : at + 2 * heads] + sums[at + 2 * heads : at + 3 * heads] + run)
        run = cums[-1][:, CHUNK - 1 :]
    cum = jnp.concatenate(cums, axis=1)
    times_ref[:heads, :] = cum
    times_ref[heads:, :] = step
    cum_ref[...] = cum.T
    left_ref[...] = two_rows(step * jnp.exp(run - cum)).T.astype(BF16)
    whole_ref[...] = two_parts(jnp.exp(cum_ref[rows - 1 :, :]))

    inner = x_ref.shape[1]
    half = inner // 2
    tiles = range(inner // TILE)
    onehots = [head_matrix(heads, TILE, head_size, t * (TILE // head_size)) for t in tiles]
    spans = [slice(t * TILE, (t + 1) * TILE) for t in tiles]

    def project(t):
        weights = wi_ref[:, spans[t]]
        before = dot(halo_ref[...], weights).astype(BF16).astype(F32)
        rows_ref[t % 2, :HALO, :] = jnp.where(place_ref[0] >= 1, before, 0.0)
        rows_ref[t % 2, HALO:, :] = dot(normed_ref[...], weights).astype(BF16).astype(F32)
        spread_ref[t % 2] = dot(left_ref[...], onehots[t])

    def combine(t):
        taps_here = small_ref[:taps, spans[t]]
        for r in range(0, rows, BLOCK):
            block = slice(r, r + BLOCK)
            x = conv_silu(rows_ref.at[t % 2], taps_here, r)
            x_ref[block, spans[t]] = x
            scaled_ref[t % 2, block, :] = (x.astype(F32) * spread_ref[t % 2, block, :]).astype(BF16)
        state = dot(bt_ref[...], scaled_ref[t % 2])
        here = slice(t * TILE % half, t * TILE % half + TILE)
        is_mine = jnp.where(parity_ref[0] == t * TILE // half, 1, 0)
        write_payload(payload_ref.at[is_mine], here, state, dot(whole_ref[...], onehots[t]))

    project(0)
    for t in tiles:
        if t + 1 < len(tiles):
            project(t + 1)
        combine(t)
    send_ref[...] = payload_ref[0]
    mine_ref[...] = payload_ref[1]


SMALL_TAPS = 4
SMALL_ROWS = 8


def local_call(tag, place, parity, normed, halo, bt, w_inner, small, after=()):
    rows = normed.shape[0]
    inner = w_inner.shape[1]
    heads = small.shape[0] - SMALL_ROWS
    states = bt.shape[0]
    return call(
        functools.partial(local_kernel, inner // heads),
        "local_" + tag,
        vmem=12,
        cost=micros(5.0),
        scalars=(place, parity),
        in_specs=[VMEM] * 5,
        out_specs=[VMEM] * 5,
        out_shape=[
            jax.ShapeDtypeStruct((rows, inner), BF16),
            jax.ShapeDtypeStruct((rows, heads), F32),
            jax.ShapeDtypeStruct((2 * heads, rows), F32),
            jax.ShapeDtypeStruct((states + EXTRA, inner // 2), BF16),
            jax.ShapeDtypeStruct((states + EXTRA, inner // 2), BF16),
        ],
        scratch=[
            pltpu.VMEM((2, rows + HALO, TILE), F32),
            pltpu.VMEM((2, rows, TILE), F32),
            pltpu.VMEM((2, rows, TILE), BF16),
            pltpu.VMEM((rows, 2 * heads), BF16),
            pltpu.VMEM((1, 2 * heads), BF16),
            pltpu.VMEM((2, states + EXTRA, inner // 2), BF16),
        ],
        after=after,
    )(place, parity, normed, halo, bt, w_inner, small)


def inside_kernel(head_size, x_ref, bc_ref, bt_ref, cum_ref, times_ref, y_ref, state_ref):
    rows, inner = x_ref.shape
    states = bc_ref.shape[1] // 2
    heads = cum_ref.shape[1]
    length = CHUNK
    last = length - 1
    pair = 2 * head_size
    lane = lax.broadcasted_iota(jnp.int32, (length, pair), 1)
    to = lax.broadcasted_iota(jnp.int32, (length, length), 0)
    frm = lax.broadcasted_iota(jnp.int32, (length, length), 1)
    state_ref[...] = jnp.zeros_like(state_ref)

    def chunk(c, before):
        at = slice(c * length, (c + 1) * length)
        bmat = bt_ref[:, at]
        cmat = bc_ref[at, states:]
        scores = jnp.where(to >= frm, dot(cmat, bmat), 0.0)
        cum = cum_ref[at, :]
        cumt = times_ref[:heads, at]
        step = times_ref[heads:, at]
        end = cumt[:, last:]
        since = two_rows(jnp.exp(cumt - before)).T.astype(BF16)
        left = two_rows(step * jnp.exp(end - cumt)).T.astype(BF16)
        for first in range(0, heads, TILE // head_size):
            columns = slice(first * head_size, first * head_size + TILE)
            onehot = head_matrix(heads, TILE, head_size, first)
            since_here = dot(since, onehot)
            state = state_ref[:, columns]
            carried = dot(cmat, state.astype(BF16)) * since_here
            scaled = (x_ref[at, columns].astype(F32) * dot(left, onehot)).astype(BF16)
            state_ref[:, columns] = state * since_here[last:, :] + dot(bmat, scaled)
            for start in range(0, TILE, pair):
                low = first * head_size + start
                weights = []
                for h in (low // head_size, low // head_size + 1):
                    apart = jnp.minimum(cum[:, h : h + 1] - cumt[h : h + 1, :], 0.0)
                    weights.append((jnp.exp(apart) * (scores * step[h : h + 1, :])).astype(BF16))
                mine = x_ref[at, low : low + pair]
                none = jnp.zeros_like(mine)
                stacked = jnp.concatenate(
                    [jnp.where(lane < head_size, mine, none), jnp.where(lane < head_size, none, mine)], axis=0
                )
                inside = dot(jnp.concatenate(weights, axis=1), stacked)
                y_ref[at, low : low + pair] = (inside + carried[:, start : start + pair]).astype(BF16)
        return end

    before = jnp.zeros((heads, 1), F32)
    for c in range(rows // length):
        before = chunk(c, before)


def inside_call(tag, x, bc, bt, cum, times, after=()):
    rows, inner = x.shape
    heads = cum.shape[1]
    both = bc.shape[1]
    return call(
        functools.partial(inside_kernel, inner // heads),
        "inside_" + tag,
        vmem=8,
        cost=micros(3.2),
        in_specs=[VMEM] * 5,
        out_specs=VMEM,
        out_shape=jax.ShapeDtypeStruct((rows, inner), BF16),
        scratch=[pltpu.VMEM((both // 2, inner), F32)],
        after=after,
    )(x, bc, bt, cum, times)


def parts_of(ref, known=None):
    states = ref.shape[0] - EXTRA
    state = ref[:states, :].astype(F32)
    extra = ref[states:, :].astype(F32)
    decay = extra[:1] + extra[1:2]
    if known is None:
        return state, decay
    return jnp.where(known, state, 0.0), jnp.where(known, decay, 0.0)


def write_payload(out_ref, columns, state, decay):
    states = state.shape[0]
    out_ref[:states, columns] = state.astype(BF16)
    decay = jnp.broadcast_to(decay, (EXTRA, decay.shape[1]))
    high = decay.astype(BF16).astype(F32)
    place = lax.broadcasted_iota(jnp.int32, decay.shape, 0)
    out_ref[states:, columns] = jnp.where(place == 0, high, decay - high).astype(BF16)


ALL = slice(None)


def pair_kernel(place_ref, mine_ref, other_ref, out_ref):
    mine, mine_a = parts_of(mine_ref)
    other, other_a = parts_of(other_ref)
    is_first = lax.rem(place_ref[0], 2) == 0
    early = jnp.where(is_first, mine, other)
    late = jnp.where(is_first, other, mine)
    late_a = jnp.where(is_first, other_a, mine_a)
    write_payload(out_ref, ALL, late_a * early + late, mine_a * other_a)


def chain_kernel(reach, place_ref, pair_ref, before_ref, out_ref):
    pair, pair_a = parts_of(pair_ref)
    before, before_a = parts_of(before_ref, place_ref[0] >= reach)
    write_payload(out_ref, ALL, pair_a * before + pair, pair_a * before_a)


def longer_kernel(reach, farther_reach, place_ref, before_ref, farther_ref, out_ref):
    before, before_a = parts_of(before_ref, place_ref[0] >= reach)
    farther, farther_a = parts_of(farther_ref, place_ref[0] >= farther_reach)
    write_payload(out_ref, ALL, before + before_a * farther, before_a * farther_a)


def entry_kernel(reach, farther_reach, place_ref, mine_ref, other_ref, before_ref, farther_ref, keep_ref, send_ref):
    mine, mine_a = parts_of(mine_ref)
    other, other_a = parts_of(other_ref)
    before, before_a = parts_of(before_ref, place_ref[0] >= reach)
    farther, _ = parts_of(farther_ref, place_ref[0] >= farther_reach)
    is_first = lax.rem(place_ref[0], 2) == 0
    entry_first = before + before_a * farther
    early = jnp.where(is_first, mine, other)
    early_a = jnp.where(is_first, mine_a, other_a)
    entry_second = early_a * entry_first + early
    keep_ref[...] = jnp.where(is_first, entry_first, entry_second).astype(BF16)
    send_ref[...] = jnp.where(is_first, entry_second, entry_first).astype(BF16)


def small_call(kernel, name, place, arrays, shapes, after=()):
    return call(
        kernel,
        name,
        vmem=4,
        cost=micros(0.5),
        scalars=(place,),
        in_specs=[VMEM] * len(arrays),
        out_specs=[VMEM] * len(shapes),
        out_shape=[jax.ShapeDtypeStruct(s, BF16) for s in shapes],
        after=after,
    )(place, *arrays)


def onward(value, by):
    count = lax.axis_size("seq")
    pairs = []
    for i in range(count):
        up = (i + by, 0) if i + by < count else (i, 1)
        down = (i - by, 1) if i - by >= 0 else (i, 0)
        pairs += [(2 * i, 2 * up[0] + up[1]), (2 * i + 1, 2 * down[0] + down[1])]
    return lax.ppermute(value, ("seq", "ch"), pairs)


class Chain:
    def __init__(self, tag, place, send, mine):
        self.tag, self.place, self.mine = tag, place, mine
        self.count = lax.axis_size("seq")
        self.swap = [(i, i ^ 1) for i in range(self.count)]
        self.other = lax.ppermute(send, "seq", self.swap)
        self.before = self.farther = None
        self.reach = self.farther_reach = 0
        self.apart = 2

    def pair(self, after):
        (self.pair_state,) = small_call(
            pair_kernel, "pair_" + self.tag, self.place, [self.mine, self.other], [self.mine.shape], after
        )
        self.running = self.pair_state
        self.hop()
        return self.pair_state

    def hop(self):
        if self.apart < self.count:
            self.arrived = onward(self.running, self.apart)

    def middle(self, after):
        while self.apart * 2 < self.count:
            self.take(after)
            (self.running,) = small_call(
                functools.partial(chain_kernel, self.reach),
                "chain_" + self.tag,
                self.place,
                [self.pair_state, self.before],
                [self.mine.shape],
                after,
            )
            self.apart *= 2
            self.hop()
        return self.running

    def take(self, after=()):
        if self.before is None:
            self.before, self.reach = self.arrived, self.apart
        else:
            (self.before,) = small_call(
                functools.partial(longer_kernel, self.reach, self.apart),
                "longer_" + self.tag,
                self.place,
                [self.before, self.arrived],
                [self.mine.shape],
                after,
            )
            self.reach = 0

    def entry(self, after):
        shape = self.mine.shape
        if self.apart < self.count:
            if self.before is None:
                self.before, self.reach = self.arrived, self.apart
                self.farther, self.farther_reach = self.arrived, self.count
            else:
                self.farther, self.farther_reach = self.arrived, self.apart
        else:
            self.before = self.farther = self.mine
            self.reach = self.farther_reach = self.count
        half = (shape[0] - EXTRA, shape[1])
        keep, out = small_call(
            functools.partial(entry_kernel, self.reach, self.farther_reach),
            "entry_" + self.tag,
            self.place,
            [self.mine, self.other, self.before, self.farther],
            [half, half],
            after,
        )
        return keep, lax.ppermute(out, "seq", self.swap)


def gated_part(
    head_size, swap, y_ref, bc_ref, cum_ref, keep_ref, other_ref, gate_ref, small_ref, wo_ref, scaled_ref, tile_ref
):
    rows, inner = y_ref.shape
    states = bc_ref.shape[1] // 2
    heads = cum_ref.shape[1]
    half = inner // 2
    since = two_parts(jnp.exp(cum_ref[...]))
    squares = [0.0] * (rows // BLOCK)
    for low in range(0, inner, TILE):
        columns = slice(low, low + TILE)
        here = slice(low % half, low % half + TILE)
        use_other = swap if low < half else jnp.logical_not(swap)
        entry = jnp.where(use_other, other_ref[:, here], keep_ref[:, here])
        tile_ref[0] = dot(bc_ref[:, states:], entry)
        tile_ref[1] = dot(since, head_matrix(heads, TILE, head_size, low // head_size))
        gain = small_ref[SMALL_TAPS : SMALL_TAPS + 1, columns]
        for i, r in enumerate(range(0, rows, BLOCK)):
            block = slice(r, r + BLOCK)
            gated = y_ref[block, columns].astype(F32) + tile_ref[0, block, :] * tile_ref[1, block, :]
            gated = gated * gate_ref[block, columns].astype(F32)
            squares[i] += jnp.sum(gated * gated, axis=-1, keepdims=True)
            scaled_ref[block, columns] = (gated * gain).astype(BF16)
    return squares


def part_kernel(head_size, parity_ref, *refs):
    *ins, out_ref, sq_ref, scaled_ref, tile_ref = refs
    squares = gated_part(head_size, parity_ref[0] == 1, *ins, scaled_ref, tile_ref)
    for i, square in enumerate(squares):
        sq_ref[i * BLOCK : (i + 1) * BLOCK, :] = jnp.broadcast_to(square, (BLOCK, sq_ref.shape[1]))
    for low in range(0, out_ref.shape[1], TILE):
        out_ref[:, low : low + TILE] = dot(scaled_ref[...], ins[-1][:, low : low + TILE])


def product(back, scaled_ref, weights_ref, part_ref, scale_ref, tile_ref, half_ref, out_ref, first):
    rows, half = out_ref.shape
    for low in range(0, half, TILE):
        columns = slice(first + low, first + low + TILE)
        tile_ref[...] = dot(scaled_ref[...], weights_ref[:, columns])
        for r in range(0, rows, BLOCK):
            block = slice(r, r + BLOCK)
            value = (tile_ref[block, :] + part_ref[block, columns]) * scale_ref[block, :1]
            half_ref[block, low : low + TILE] = value.astype(BF16)

    @pl.when(back == 1)
    def _():
        turn = flip_matrix(TILE)
        for r in range(0, rows, TILE):
            for low in range(0, half, TILE):
                tile = dot(turn, half_ref[r : r + TILE, low : low + TILE]).astype(BF16)
                tile = dot(tile, turn).astype(BF16)
                to_row, to = rows - TILE - r, half - TILE - low
                out_ref[to_row : to_row + TILE, to : to + TILE] = tile

    @pl.when(back != 1)
    def _():
        out_ref[...] = half_ref[...]


def finish_kernel(head_size, full_width, back_ref, parity_ref, *refs):
    *ins, part_ref, psq_ref, send_ref, scaled_ref, scale_ref, tile_ref, half_ref = refs
    squares = gated_part(head_size, parity_ref[0] == 1, *ins, scaled_ref, tile_ref)
    for i, square in enumerate(squares):
        block = slice(i * BLOCK, (i + 1) * BLOCK)
        scale = lax.rsqrt((square + psq_ref[block, :1]) / full_width + EPS)
        scale_ref[block, :] = jnp.broadcast_to(scale, (BLOCK, scale_ref.shape[1]))
    product(back_ref[0], scaled_ref, ins[-1], part_ref, scale_ref, tile_ref.at[0], half_ref, send_ref, send_ref.shape[1])


def own_kernel(back_ref, scaled_ref, weights_ref, part_ref, scale_ref, own_ref, tile_ref, half_ref):
    product(back_ref[0], scaled_ref, weights_ref, part_ref, scale_ref, tile_ref, half_ref, own_ref, 0)


def own_call(back, scaled, w_output, part, scale, after):
    rows, width = part.shape
    half = width // 2
    return call(
        own_kernel,
        "own_half",
        vmem=8,
        cost=micros(0.7),
        scalars=(back,),
        in_specs=[VMEM] * 4,
        out_specs=VMEM,
        out_shape=jax.ShapeDtypeStruct((rows, half), BF16),
        scratch=[pltpu.VMEM((rows, TILE), F32), pltpu.VMEM((rows, half), BF16)],
        after=after,
    )(back, scaled, w_output, part, scale)


def finish_call(back, parity, y, bc, cum, keep, other, gate, small, w_output, full_width=None, partial=None, after=()):
    rows, inner = y.shape
    width = w_output.shape[1]
    half = width // 2
    heads = cum.shape[1]
    arrays = [y, bc, cum, keep, other, gate, small, w_output]
    tiles = pltpu.VMEM((2, rows, TILE), F32)
    if partial is None:
        scratch = [pltpu.VMEM((rows, inner), BF16), tiles]
        scalars = (parity,)
        kernel = functools.partial(part_kernel, inner // heads)
        out_shape = [jax.ShapeDtypeStruct((rows, width), F32), jax.ShapeDtypeStruct((rows, 128), F32)]
    else:
        scalars = (back, parity)
        scratch = [tiles, pltpu.VMEM((rows, half), BF16)]
        kernel = functools.partial(finish_kernel, inner // heads, full_width)
        arrays += list(partial)
        out_shape = [
            jax.ShapeDtypeStruct((rows, half), BF16),
            jax.ShapeDtypeStruct((rows, inner), BF16),
            jax.ShapeDtypeStruct((rows, 128), F32),
        ]
    return call(
        kernel,
        "part" if partial is None else "finish",
        vmem=16,
        cost=micros(3.5),
        scalars=scalars,
        in_specs=[VMEM] * len(arrays),
        out_specs=[VMEM] * len(out_shape),
        out_shape=out_shape,
        scratch=scratch,
        after=after,
    )(*scalars, *arrays)


def total_kernel(mine_ref, theirs_ref, out_hbm, out_ref, sems):
    copies = []
    for i, r in enumerate(range(0, mine_ref.shape[0], CHUNK)):
        for q in range(r, r + CHUNK, BLOCK):
            block = slice(q, q + BLOCK)
            out_ref[block, :] = (mine_ref[block, :].astype(F32) + theirs_ref[block, :].astype(F32)).astype(BF16)
        part = pl.ds(r, CHUNK)
        copies.append(pltpu.make_async_copy(out_ref.at[part, :], out_hbm.at[part, :], sems.at[i]))
        copies[-1].start()
    for copy in copies:
        copy.wait()


def total_call(mine, theirs):
    rows, half = mine.shape
    return call(
        total_kernel,
        "total",
        vmem=4,
        cost=micros(0.8),
        in_specs=[VMEM] * 2,
        out_specs=HBM,
        out_shape=jax.ShapeDtypeStruct((rows, half), BF16),
        scratch=[pltpu.VMEM((rows, half), BF16), pltpu.SemaphoreType.DMA((rows // CHUNK,))],
    )(mine, theirs)


def body(
    tokens,
    hidden,
    embedding,
    w_gate,
    w_inner,
    w_state,
    w_step,
    conv_inner,
    conv_state,
    step_bias,
    decay_rate,
    norm_gain,
    w_output,
):
    swap = [(0, 1), (1, 0)]

    def theirs(a):
        return lax.ppermute(a, "ch", swap)

    core = lax.axis_index("ch").astype(jnp.int32)
    index = lax.axis_index("seq").astype(jnp.int32)
    last = lax.axis_size("seq") - 1
    back = core.reshape(1)
    parity = (index & 1).reshape(1)
    place = (index + core * (last - 2 * index)).reshape(1)
    place, parity, w_inner_3, w_gate_3, w_output_3 = lax.optimization_barrier(
        (place, parity, w_inner, w_gate, w_output)
    )
    w_inner_2 = theirs(w_inner_3)
    normed, tail, small = prepare_call(
        (back, parity, place), hidden, tokens, embedding, conv_inner, norm_gain, step_bias, decay_rate, w_step.T
    )
    halo = onward(tail, 1)
    small_2 = theirs(small)
    w_gate_2 = theirs(w_gate_3)
    w_output_2 = theirs(w_output_3)
    bc, bt = maps_call(place, normed, halo, w_state, conv_state)
    x_1, cum_1, times_1, send_1, mine_1 = local_call("own", place, parity, normed, halo, bt, w_inner, small)
    chain_1 = Chain("own", place, send_1, mine_1)
    x_2, cum_2, times_2, send_2, mine_2 = local_call(
        "other", place, parity, normed, halo, bt, w_inner_2, small_2, after=[mine_1]
    )
    chain_2 = Chain("other", place, send_2, mine_2)
    gate_2 = gate_call("other", normed, w_gate_2, after=[x_2])
    done = chain_1.pair(after=[gate_2])
    y_1 = inside_call("own", x_1, bc, bt, cum_1, times_1, after=[done])
    done = chain_1.middle(after=[y_1])
    done = chain_2.pair(after=[done])
    y_2 = inside_call("other", x_2, bc, bt, cum_2, times_2, after=[done])
    entry_1 = chain_1.entry(after=[y_2])
    done = chain_2.middle(after=[entry_1[0]])
    gate_1 = gate_call("own", normed, w_gate, after=[done])
    entry_2 = chain_2.entry(after=[gate_1])
    partial = finish_call(
        back, parity, y_1, bc, cum_1, *entry_1, gate_1, small, w_output, after=[entry_2[0]]
    )
    full_width = float(w_inner.shape[1] * lax.axis_size("ch"))
    send, scaled, scale = finish_call(
        back, parity, y_2, bc, cum_2, *entry_2, gate_2, small_2, w_output_2, full_width, partial
    )
    arriving = theirs(send)
    mine = own_call(back, scaled, w_output_2, partial[0], scale, after=[send])
    return total_call(mine, arriving)


def solution(mesh):
    return jax.shard_map(
        body,
        mesh=mesh,
        in_specs=(
            P(("win", "seq")),
            P(("win", "seq"), None),
            P(),
            P(None, "ch"),
            P(None, "ch"),
            P(),
            P(None, "ch"),
            P(None, "ch"),
            P(),
            P("ch"),
            P("ch"),
            P("ch"),
            P("ch", None),
        ),
        out_specs=P(("win", "seq"), "ch"),
        check_vma=False,
    )
```

```python
import functools

import jax
import jax.numpy as jnp
from jax import lax
from jax.experimental import pallas as pl
from jax.experimental.pallas import tpu as pltpu
from jax.sharding import PartitionSpec as P

F32 = jnp.float32
BF16 = jnp.bfloat16
EPS = 1e-05
HALO = 16
EXTRA = 16
CHUNK = 128
TILE = 256
BLOCK = 64
MB = 1024 * 1024
VMEM = pl.BlockSpec(memory_space=pltpu.VMEM)
HBM = pl.BlockSpec(memory_space=pltpu.HBM)


def call(
    kernel, name, *, vmem, cost, scalars=(), grid=(), in_specs, out_specs, out_shape, scratch=(), after=()
):
    flops, moved, special = cost
    first = len(scalars) + len(in_specs)

    def body(*refs):
        kernel(*refs[:first], *refs[first + len(after) :])

    run = pl.pallas_call(
        body,
        grid_spec=pltpu.PrefetchScalarGridSpec(
            num_scalar_prefetch=len(scalars),
            grid=grid,
            in_specs=list(in_specs) + [pl.BlockSpec(memory_space=pl.ANY)] * len(after),
            out_specs=out_specs,
            scratch_shapes=scratch,
        ),
        out_shape=out_shape,
        compiler_params=pltpu.CompilerParams(
            vmem_limit_bytes=vmem * MB, dimension_semantics=("arbitrary",) * len(grid)
        ),
        cost_estimate=pl.CostEstimate(flops=flops, bytes_accessed=moved, transcendentals=special),
        name=name,
    )
    return lambda *arrays: run(*arrays, *after)


def micros(us):
    return (int(us * 1.1e9), int(us * 1e6), 0)


def dot(a, b):
    return jnp.dot(a, b, preferred_element_type=F32)


def dot_nt(a, b):
    return lax.dot_general(a, b, (((1,), (1,)), ((), ())), preferred_element_type=F32)


def dot_tn(a, b):
    return lax.dot_general(a, b, (((0,), (0,)), ((), ())), preferred_element_type=F32)


def flip_matrix(size):
    rows = lax.broadcasted_iota(jnp.int32, (size, size), 0)
    columns = lax.broadcasted_iota(jnp.int32, (size, size), 1)
    return jnp.where(rows + columns == size - 1, 1.0, 0.0).astype(BF16)


def flip_both(value):
    rows, width = value.shape
    turned = dot(flip_matrix(rows), value).astype(BF16)
    anti = flip_matrix(TILE)
    count = width // TILE
    blocks = [
        dot(turned[:, (count - 1 - k) * TILE : (count - k) * TILE], anti).astype(BF16)
        for k in range(count)
    ]
    return jnp.concatenate(blocks, axis=1)


def silu(v):
    half = 0.5 * v
    return half + half * jnp.tanh(half)


def two_parts(value):
    high = value.astype(BF16)
    low = (value - high.astype(F32)).astype(BF16)
    return jnp.concatenate([high, low], axis=1)


def two_rows(value):
    high = value.astype(BF16).astype(F32)
    return jnp.concatenate([high, value - high], axis=0)


def head_matrix(heads, width, head_size, first_head):
    source = lax.broadcasted_iota(jnp.int32, (2 * heads, width), 0)
    source = jnp.where(source >= heads, source - heads, source)
    target = lax.broadcasted_iota(jnp.int32, (2 * heads, width), 1) // head_size + first_head
    return jnp.where(source == target, 1.0, 0.0).astype(BF16)


def prepare_kernel(
    back_ref,
    parity_ref,
    place_ref,
    hidden_hbm,
    tokens_hbm,
    emb_hbm,
    conv_hbm,
    gain_hbm,
    bias_hbm,
    rate_hbm,
    step_hbm,
    out_ref,
    tail_ref,
    small_ref,
    hidden_ref,
    tokens_ref,
    emb_ref,
    conv_ref,
    gain_ref,
    bias_ref,
    rate_ref,
    step_ref,
    base_ref,
    normed_ref,
    sems,
):
    rows = hidden_ref.shape[0]
    kinds = emb_ref.shape[0]
    taps, inner = conv_ref.shape
    heads = bias_ref.shape[1]
    count = rows // CHUNK
    back = back_ref[0] == 1
    whole = [
        (tokens_hbm, tokens_ref),
        (emb_hbm, emb_ref),
        (conv_hbm, conv_ref),
        (gain_hbm, gain_ref),
        (bias_hbm, bias_ref),
        (rate_hbm, rate_ref),
        (step_hbm, step_ref),
    ]
    small_copies = [pltpu.make_async_copy(src, dst, sems.at[count + i]) for i, (src, dst) in enumerate(whole)]
    parts = [pl.ds(r * CHUNK, CHUNK) for r in range(count)]
    copies = [
        pltpu.make_async_copy(hidden_hbm.at[part, :], hidden_ref.at[part, :], sems.at[r])
        for r, part in enumerate(parts)
    ]
    for copy in small_copies[:2] + copies + small_copies[2:]:
        copy.start()
    for copy in small_copies[:2]:
        copy.wait()
    kind = lax.broadcasted_iota(jnp.int32, (kinds, rows), 0)
    onehot = jnp.where(kind == tokens_ref[...], 1.0, 0.0).astype(BF16)
    for r in range(count):
        copies[r].wait()
        low, high = r * CHUNK, (r + 1) * CHUNK
        base_ref[...] = dot_tn(onehot[:, low:high], emb_ref[...])
        for q in range(low, high, HALO):
            block = slice(q, q + HALO)
            merged = hidden_ref[block, :].astype(F32) + base_ref[q - low : q - low + HALO, :]
            merged = merged.astype(BF16).astype(F32)
            mean = jnp.mean(merged * merged, axis=-1, keepdims=True)
            normed_ref[q - low : q - low + HALO, :] = (merged * lax.rsqrt(mean + EPS)).astype(BF16)

        @pl.when(back)
        def _():
            out_ref[rows - high : rows - low, :] = flip_both(normed_ref[...])

        @pl.when(jnp.logical_not(back))
        def _():
            out_ref[low:high, :] = normed_ref[...]

    tail_ref[...] = out_ref[rows - HALO :, :]
    for copy in small_copies[2:]:
        copy.wait()
    small_ref[:taps, :] = conv_ref[...]
    small_ref[taps : taps + 1, :] = gain_ref[...]
    small_ref[taps + 1 : SMALL_ROWS, :] = jnp.zeros((SMALL_ROWS - taps - 1, inner), F32)
    small_ref[taps + 1 : taps + 2, :heads] = bias_ref[...]
    small_ref[taps + 2 : taps + 3, :heads] = rate_ref[...]
    small_ref[SMALL_ROWS:, :] = step_ref[...].astype(F32)


def prepare_call(scalars, hidden, tokens, embedding, conv, gain, bias, rate, step):
    rows, width = hidden.shape
    inner = conv.shape[1]
    arrays = [hidden, tokens.reshape(1, -1), embedding, conv]
    arrays += [a.reshape(1, -1) for a in (gain, bias, rate)] + [step]
    return call(
        prepare_kernel,
        "prepare",
        vmem=12,
        cost=micros(2.7),
        scalars=scalars,
        in_specs=[HBM] * len(arrays),
        out_specs=[VMEM] * 3,
        out_shape=[
            jax.ShapeDtypeStruct((rows, width), BF16),
            jax.ShapeDtypeStruct((HALO, width), BF16),
            jax.ShapeDtypeStruct((SMALL_ROWS + step.shape[0], inner), F32),
        ],
        scratch=[pltpu.VMEM(a.shape, a.dtype) for a in arrays]
        + [pltpu.VMEM((CHUNK, width), F32), pltpu.VMEM((CHUNK, width), BF16)]
        + [pltpu.SemaphoreType.DMA((rows // CHUNK + len(arrays) - 1,))],
    )(*scalars, *(pltpu.with_memory_space_constraint(a, pltpu.HBM) for a in arrays))


def gate_kernel(rows_ref, wg_ref, out_ref, gate_ref):
    rows, inner = out_ref.shape
    for low in range(0, inner, TILE):
        columns = slice(low, low + TILE)
        gate_ref[...] = dot(rows_ref[...], wg_ref[:, columns])
        for r in range(0, rows, BLOCK):
            gate = gate_ref[r : r + BLOCK, :].astype(BF16).astype(F32)
            out_ref[r : r + BLOCK, columns] = silu(gate).astype(BF16)


def gate_call(tag, normed, w_gate, after=()):
    rows = normed.shape[0]
    inner = w_gate.shape[1]
    return call(
        gate_kernel,
        "gate_" + tag,
        vmem=8,
        cost=micros(2.4),
        in_specs=[VMEM] * 2,
        out_specs=VMEM,
        out_shape=jax.ShapeDtypeStruct((rows, inner), BF16),
        scratch=[pltpu.VMEM((rows, TILE), F32)],
        after=after,
    )(normed, w_gate)


def conv_silu(rows_ref, weights, row):
    taps = weights.shape[0]
    ahead = 8
    window = rows_ref[HALO - ahead + row : HALO + row + BLOCK, :]
    total = weights[taps - 1 :, :] * window[ahead:, :]
    for back in range(1, taps):
        total += weights[taps - 1 - back : taps - back, :] * pltpu.roll(window, back, 0)[ahead:, :]
    return silu(total).astype(BF16)


def maps_kernel(place_ref, normed_ref, halo_ref, ws_ref, cs_ref, bc_ref, bt_ref, rows_ref):
    rows = normed_ref.shape[0]
    states = bc_ref.shape[1] // 2
    before = dot(halo_ref[...], ws_ref[...]).astype(BF16).astype(F32)
    rows_ref[:HALO, :] = jnp.where(place_ref[0] >= 1, before, 0.0)
    rows_ref[HALO:, :] = dot(normed_ref[...], ws_ref[...]).astype(BF16).astype(F32)
    weights = cs_ref[...]
    for r in range(0, rows, BLOCK):
        bc_ref[r : r + BLOCK, :] = conv_silu(rows_ref, weights, r)
    bt_ref[...] = bc_ref[:, :states].astype(F32).T.astype(BF16)


def maps_call(place, normed, halo, w_state, conv_state, after=()):
    rows = normed.shape[0]
    both = w_state.shape[1]
    return call(
        maps_kernel,
        "maps",
        vmem=8,
        cost=micros(1.5),
        scalars=(place,),
        in_specs=[VMEM] * 4,
        out_specs=[VMEM] * 2,
        out_shape=[
            jax.ShapeDtypeStruct((rows, both), BF16),
            jax.ShapeDtypeStruct((both // 2, rows), BF16),
        ],
        scratch=[pltpu.VMEM((rows + HALO, both), F32)],
        after=after,
    )(place, normed, halo, w_state, conv_state)


def local_kernel(
    head_size,
    place_ref,
    parity_ref,
    normed_ref,
    halo_ref,
    bt_ref,
    wi_ref,
    small_ref,
    x_ref,
    cum_ref,
    times_ref,
    send_ref,
    mine_ref,
    rows_ref,
    spread_ref,
    scaled_ref,
    left_ref,
    whole_ref,
    payload_ref,
):
    rows = normed_ref.shape[0]
    states = bt_ref.shape[0]
    heads = cum_ref.shape[1]
    taps = SMALL_TAPS
    raw = dot_nt(normed_ref[...], small_ref[SMALL_ROWS:, :].astype(BF16))
    columns = small_ref[:SMALL_ROWS, :CHUNK].T
    raw = raw.T + columns[:heads, taps + 1 : taps + 2]
    step = jnp.maximum(raw, 0.0) + jnp.log1p(jnp.exp(-jnp.abs(raw)))
    logdecay = -step * columns[:heads, taps + 2 : taps + 3]
    high = logdecay.astype(BF16)
    rest = logdecay - high.astype(F32)
    mid = rest.astype(BF16)
    low = (rest - mid.astype(F32)).astype(BF16)
    starts = range(0, rows, CHUNK)
    pieces = [part[:, r : r + CHUNK] for r in starts for part in (high, mid, low)]
    frm = lax.broadcasted_iota(jnp.int32, (CHUNK, CHUNK), 0)
    to = lax.broadcasted_iota(jnp.int32, (CHUNK, CHUNK), 1)
    sums = dot(jnp.concatenate(pieces, axis=0), jnp.where(to >= frm, 1.0, 0.0).astype(BF16))
    run = jnp.zeros((heads, 1), F32)
    cums = []
    for i in range(len(starts)):
        at = 3 * i * heads
        cums.append(sums[at : at + heads] + sums[at + heads : at + 2 * heads] + sums[at + 2 * heads : at + 3 * heads] + run)
        run = cums[-1][:, CHUNK - 1 :]
    cum = jnp.concatenate(cums, axis=1)
    times_ref[:heads, :] = cum
    times_ref[heads:, :] = step
    cum_ref[...] = cum.T
    left_ref[...] = two_rows(step * jnp.exp(run - cum)).T.astype(BF16)
    whole_ref[...] = two_parts(jnp.exp(cum_ref[rows - 1 :, :]))

    inner = x_ref.shape[1]
    half = inner // 2
    tiles = range(inner // TILE)
    onehots = [head_matrix(heads, TILE, head_size, t * (TILE // head_size)) for t in tiles]
    spans = [slice(t * TILE, (t + 1) * TILE) for t in tiles]

    def project(t):
        weights = wi_ref[:, spans[t]]
        before = dot(halo_ref[...], weights).astype(BF16).astype(F32)
        rows_ref[t % 2, :HALO, :] = jnp.where(place_ref[0] >= 1, before, 0.0)
        rows_ref[t % 2, HALO:, :] = dot(normed_ref[...], weights).astype(BF16).astype(F32)
        spread_ref[t % 2] = dot(left_ref[...], onehots[t])

    def combine(t):
        taps_here = small_ref[:taps, spans[t]]
        for r in range(0, rows, BLOCK):
            block = slice(r, r + BLOCK)
            x = conv_silu(rows_ref.at[t % 2], taps_here, r)
            x_ref[block, spans[t]] = x
            scaled_ref[t % 2, block, :] = (x.astype(F32) * spread_ref[t % 2, block, :]).astype(BF16)
        state = dot(bt_ref[...], scaled_ref[t % 2])
        here = slice(t * TILE % half, t * TILE % half + TILE)
        is_mine = jnp.where(parity_ref[0] == t * TILE // half, 1, 0)
        write_payload(payload_ref.at[is_mine], here, state, dot(whole_ref[...], onehots[t]))

    project(0)
    for t in tiles:
        if t + 1 < len(tiles):
            project(t + 1)
        combine(t)
    send_ref[...] = payload_ref[0]
    mine_ref[...] = payload_ref[1]


SMALL_TAPS = 4
SMALL_ROWS = 8


def local_call(tag, place, parity, normed, halo, bt, w_inner, small, after=()):
    rows = normed.shape[0]
    inner = w_inner.shape[1]
    heads = small.shape[0] - SMALL_ROWS
    states = bt.shape[0]
    return call(
        functools.partial(local_kernel, inner // heads),
        "local_" + tag,
        vmem=12,
        cost=micros(5.0),
        scalars=(place, parity),
        in_specs=[VMEM] * 5,
        out_specs=[VMEM] * 5,
        out_shape=[
            jax.ShapeDtypeStruct((rows, inner), BF16),
            jax.ShapeDtypeStruct((rows, heads), F32),
            jax.ShapeDtypeStruct((2 * heads, rows), F32),
            jax.ShapeDtypeStruct((states + EXTRA, inner // 2), BF16),
            jax.ShapeDtypeStruct((states + EXTRA, inner // 2), BF16),
        ],
        scratch=[
            pltpu.VMEM((2, rows + HALO, TILE), F32),
            pltpu.VMEM((2, rows, TILE), F32),
            pltpu.VMEM((2, rows, TILE), BF16),
            pltpu.VMEM((rows, 2 * heads), BF16),
            pltpu.VMEM((1, 2 * heads), BF16),
            pltpu.VMEM((2, states + EXTRA, inner // 2), BF16),
        ],
        after=after,
    )(place, parity, normed, halo, bt, w_inner, small)


def inside_kernel(head_size, x_ref, bc_ref, bt_ref, cum_ref, times_ref, y_ref, state_ref):
    rows, inner = x_ref.shape
    states = bc_ref.shape[1] // 2
    heads = cum_ref.shape[1]
    length = CHUNK
    last = length - 1
    pair = 2 * head_size
    lane = lax.broadcasted_iota(jnp.int32, (length, pair), 1)
    to = lax.broadcasted_iota(jnp.int32, (length, length), 0)
    frm = lax.broadcasted_iota(jnp.int32, (length, length), 1)
    state_ref[...] = jnp.zeros_like(state_ref)

    def chunk(c, before):
        at = slice(c * length, (c + 1) * length)
        bmat = bt_ref[:, at]
        cmat = bc_ref[at, states:]
        scores = jnp.where(to >= frm, dot(cmat, bmat), 0.0)
        cum = cum_ref[at, :]
        cumt = times_ref[:heads, at]
        step = times_ref[heads:, at]
        end = cumt[:, last:]
        since = two_rows(jnp.exp(cumt - before)).T.astype(BF16)
        left = two_rows(step * jnp.exp(end - cumt)).T.astype(BF16)
        for first in range(0, heads, TILE // head_size):
            columns = slice(first * head_size, first * head_size + TILE)
            onehot = head_matrix(heads, TILE, head_size, first)
            since_here = dot(since, onehot)
            state = state_ref[:, columns]
            carried = dot(cmat, state.astype(BF16)) * since_here
            scaled = (x_ref[at, columns].astype(F32) * dot(left, onehot)).astype(BF16)
            state_ref[:, columns] = state * since_here[last:, :] + dot(bmat, scaled)
            for start in range(0, TILE, pair):
                low = first * head_size + start
                weights = []
                for h in (low // head_size, low // head_size + 1):
                    apart = jnp.minimum(cum[:, h : h + 1] - cumt[h : h + 1, :], 0.0)
                    weights.append((jnp.exp(apart) * (scores * step[h : h + 1, :])).astype(BF16))
                mine = x_ref[at, low : low + pair]
                none = jnp.zeros_like(mine)
                stacked = jnp.concatenate(
                    [jnp.where(lane < head_size, mine, none), jnp.where(lane < head_size, none, mine)], axis=0
                )
                inside = dot(jnp.concatenate(weights, axis=1), stacked)
                y_ref[at, low : low + pair] = (inside + carried[:, start : start + pair]).astype(BF16)
        return end

    before = jnp.zeros((heads, 1), F32)
    for c in range(rows // length):
        before = chunk(c, before)


def inside_call(tag, x, bc, bt, cum, times, after=()):
    rows, inner = x.shape
    heads = cum.shape[1]
    both = bc.shape[1]
    return call(
        functools.partial(inside_kernel, inner // heads),
        "inside_" + tag,
        vmem=8,
        cost=micros(3.2),
        in_specs=[VMEM] * 5,
        out_specs=VMEM,
        out_shape=jax.ShapeDtypeStruct((rows, inner), BF16),
        scratch=[pltpu.VMEM((both // 2, inner), F32)],
        after=after,
    )(x, bc, bt, cum, times)


def parts_of(ref, known=None):
    states = ref.shape[0] - EXTRA
    state = ref[:states, :].astype(F32)
    extra = ref[states:, :].astype(F32)
    decay = extra[:1] + extra[1:2]
    if known is None:
        return state, decay
    return jnp.where(known, state, 0.0), jnp.where(known, decay, 0.0)


def write_payload(out_ref, columns, state, decay):
    states = state.shape[0]
    out_ref[:states, columns] = state.astype(BF16)
    decay = jnp.broadcast_to(decay, (EXTRA, decay.shape[1]))
    high = decay.astype(BF16).astype(F32)
    place = lax.broadcasted_iota(jnp.int32, decay.shape, 0)
    out_ref[states:, columns] = jnp.where(place == 0, high, decay - high).astype(BF16)


ALL = slice(None)


def pair_kernel(place_ref, mine_ref, other_ref, out_ref):
    mine, mine_a = parts_of(mine_ref)
    other, other_a = parts_of(other_ref)
    is_first = lax.rem(place_ref[0], 2) == 0
    early = jnp.where(is_first, mine, other)
    late = jnp.where(is_first, other, mine)
    late_a = jnp.where(is_first, other_a, mine_a)
    write_payload(out_ref, ALL, late_a * early + late, mine_a * other_a)


def chain_kernel(reach, place_ref, pair_ref, before_ref, out_ref):
    pair, pair_a = parts_of(pair_ref)
    before, before_a = parts_of(before_ref, place_ref[0] >= reach)
    write_payload(out_ref, ALL, pair_a * before + pair, pair_a * before_a)


def longer_kernel(reach, farther_reach, place_ref, before_ref, farther_ref, out_ref):
    before, before_a = parts_of(before_ref, place_ref[0] >= reach)
    farther, farther_a = parts_of(farther_ref, place_ref[0] >= farther_reach)
    write_payload(out_ref, ALL, before + before_a * farther, before_a * farther_a)


def entry_kernel(reach, farther_reach, place_ref, mine_ref, other_ref, before_ref, farther_ref, keep_ref, send_ref):
    mine, mine_a = parts_of(mine_ref)
    other, other_a = parts_of(other_ref)
    before, before_a = parts_of(before_ref, place_ref[0] >= reach)
    farther, _ = parts_of(farther_ref, place_ref[0] >= farther_reach)
    is_first = lax.rem(place_ref[0], 2) == 0
    entry_first = before + before_a * farther
    early = jnp.where(is_first, mine, other)
    early_a = jnp.where(is_first, mine_a, other_a)
    entry_second = early_a * entry_first + early
    keep_ref[...] = jnp.where(is_first, entry_first, entry_second).astype(BF16)
    send_ref[...] = jnp.where(is_first, entry_second, entry_first).astype(BF16)


def small_call(kernel, name, place, arrays, shapes, after=()):
    return call(
        kernel,
        name,
        vmem=4,
        cost=micros(0.5),
        scalars=(place,),
        in_specs=[VMEM] * len(arrays),
        out_specs=[VMEM] * len(shapes),
        out_shape=[jax.ShapeDtypeStruct(s, BF16) for s in shapes],
        after=after,
    )(place, *arrays)


def onward(value, by):
    count = lax.axis_size("seq")
    pairs = []
    for i in range(count):
        up = (i + by, 0) if i + by < count else (i, 1)
        down = (i - by, 1) if i - by >= 0 else (i, 0)
        pairs += [(2 * i, 2 * up[0] + up[1]), (2 * i + 1, 2 * down[0] + down[1])]
    return lax.ppermute(value, ("seq", "ch"), pairs)


class Chain:
    def __init__(self, tag, place, send, mine):
        self.tag, self.place, self.mine = tag, place, mine
        self.count = lax.axis_size("seq")
        self.swap = [(i, i ^ 1) for i in range(self.count)]
        self.other = lax.ppermute(send, "seq", self.swap)
        self.before = self.farther = None
        self.reach = self.farther_reach = 0
        self.apart = 2

    def pair(self, after):
        (self.pair_state,) = small_call(
            pair_kernel, "pair_" + self.tag, self.place, [self.mine, self.other], [self.mine.shape], after
        )
        self.running = self.pair_state
        self.hop()
        return self.pair_state

    def hop(self):
        if self.apart < self.count:
            self.arrived = onward(self.running, self.apart)

    def middle(self, after):
        while self.apart * 2 < self.count:
            self.take(after)
            (self.running,) = small_call(
                functools.partial(chain_kernel, self.reach),
                "chain_" + self.tag,
                self.place,
                [self.pair_state, self.before],
                [self.mine.shape],
                after,
            )
            self.apart *= 2
            self.hop()
        return self.running

    def take(self, after=()):
        if self.before is None:
            self.before, self.reach = self.arrived, self.apart
        else:
            (self.before,) = small_call(
                functools.partial(longer_kernel, self.reach, self.apart),
                "longer_" + self.tag,
                self.place,
                [self.before, self.arrived],
                [self.mine.shape],
                after,
            )
            self.reach = 0

    def entry(self, after):
        shape = self.mine.shape
        if self.apart < self.count:
            if self.before is None:
                self.before, self.reach = self.arrived, self.apart
                self.farther, self.farther_reach = self.arrived, self.count
            else:
                self.farther, self.farther_reach = self.arrived, self.apart
        else:
            self.before = self.farther = self.mine
            self.reach = self.farther_reach = self.count
        half = (shape[0] - EXTRA, shape[1])
        keep, out = small_call(
            functools.partial(entry_kernel, self.reach, self.farther_reach),
            "entry_" + self.tag,
            self.place,
            [self.mine, self.other, self.before, self.farther],
            [half, half],
            after,
        )
        return keep, lax.ppermute(out, "seq", self.swap)


def gated_part(
    head_size, swap, y_ref, bc_ref, cum_ref, keep_ref, other_ref, gate_ref, small_ref, wo_ref, scaled_ref, tile_ref
):
    rows, inner = y_ref.shape
    states = bc_ref.shape[1] // 2
    heads = cum_ref.shape[1]
    half = inner // 2
    since = two_parts(jnp.exp(cum_ref[...]))
    squares = [0.0] * (rows // BLOCK)
    for low in range(0, inner, TILE):
        columns = slice(low, low + TILE)
        here = slice(low % half, low % half + TILE)
        use_other = swap if low < half else jnp.logical_not(swap)
        entry = jnp.where(use_other, other_ref[:, here], keep_ref[:, here])
        tile_ref[0] = dot(bc_ref[:, states:], entry)
        tile_ref[1] = dot(since, head_matrix(heads, TILE, head_size, low // head_size))
        gain = small_ref[SMALL_TAPS : SMALL_TAPS + 1, columns]
        for i, r in enumerate(range(0, rows, BLOCK)):
            block = slice(r, r + BLOCK)
            gated = y_ref[block, columns].astype(F32) + tile_ref[0, block, :] * tile_ref[1, block, :]
            gated = gated * gate_ref[block, columns].astype(F32)
            squares[i] += jnp.sum(gated * gated, axis=-1, keepdims=True)
            scaled_ref[block, columns] = (gated * gain).astype(BF16)
    return squares


def part_kernel(head_size, parity_ref, *refs):
    *ins, out_ref, sq_ref, scaled_ref, tile_ref = refs
    squares = gated_part(head_size, parity_ref[0] == 1, *ins, scaled_ref, tile_ref)
    for i, square in enumerate(squares):
        sq_ref[i * BLOCK : (i + 1) * BLOCK, :] = jnp.broadcast_to(square, (BLOCK, sq_ref.shape[1]))
    for low in range(0, out_ref.shape[1], TILE):
        out_ref[:, low : low + TILE] = dot(scaled_ref[...], ins[-1][:, low : low + TILE])


def product(back, scaled_ref, weights_ref, part_ref, scale_ref, tile_ref, half_ref, out_ref, first):
    rows, half = out_ref.shape
    for low in range(0, half, TILE):
        columns = slice(first + low, first + low + TILE)
        tile_ref[...] = dot(scaled_ref[...], weights_ref[:, columns])
        for r in range(0, rows, BLOCK):
            block = slice(r, r + BLOCK)
            value = (tile_ref[block, :] + part_ref[block, columns]) * scale_ref[block, :1]
            half_ref[block, low : low + TILE] = value.astype(BF16)

    @pl.when(back == 1)
    def _():
        turn = flip_matrix(TILE)
        for r in range(0, rows, TILE):
            for low in range(0, half, TILE):
                tile = dot(turn, half_ref[r : r + TILE, low : low + TILE]).astype(BF16)
                tile = dot(tile, turn).astype(BF16)
                to_row, to = rows - TILE - r, half - TILE - low
                out_ref[to_row : to_row + TILE, to : to + TILE] = tile

    @pl.when(back != 1)
    def _():
        out_ref[...] = half_ref[...]


def finish_kernel(head_size, full_width, back_ref, parity_ref, *refs):
    *ins, part_ref, psq_ref, send_ref, scaled_ref, scale_ref, tile_ref, half_ref = refs
    squares = gated_part(head_size, parity_ref[0] == 1, *ins, scaled_ref, tile_ref)
    for i, square in enumerate(squares):
        block = slice(i * BLOCK, (i + 1) * BLOCK)
        scale = lax.rsqrt((square + psq_ref[block, :1]) / full_width + EPS)
        scale_ref[block, :] = jnp.broadcast_to(scale, (BLOCK, scale_ref.shape[1]))
    product(back_ref[0], scaled_ref, ins[-1], part_ref, scale_ref, tile_ref.at[0], half_ref, send_ref, send_ref.shape[1])


def own_kernel(back_ref, scaled_ref, weights_ref, part_ref, scale_ref, own_ref, tile_ref, half_ref):
    product(back_ref[0], scaled_ref, weights_ref, part_ref, scale_ref, tile_ref, half_ref, own_ref, 0)


def own_call(back, scaled, w_output, part, scale, after):
    rows, width = part.shape
    half = width // 2
    return call(
        own_kernel,
        "own_half",
        vmem=8,
        cost=micros(0.7),
        scalars=(back,),
        in_specs=[VMEM] * 4,
        out_specs=VMEM,
        out_shape=jax.ShapeDtypeStruct((rows, half), BF16),
        scratch=[pltpu.VMEM((rows, TILE), F32), pltpu.VMEM((rows, half), BF16)],
        after=after,
    )(back, scaled, w_output, part, scale)


def finish_call(back, parity, y, bc, cum, keep, other, gate, small, w_output, full_width=None, partial=None, after=()):
    rows, inner = y.shape
    width = w_output.shape[1]
    half = width // 2
    heads = cum.shape[1]
    arrays = [y, bc, cum, keep, other, gate, small, w_output]
    tiles = pltpu.VMEM((2, rows, TILE), F32)
    if partial is None:
        scratch = [pltpu.VMEM((rows, inner), BF16), tiles]
        scalars = (parity,)
        kernel = functools.partial(part_kernel, inner // heads)
        out_shape = [jax.ShapeDtypeStruct((rows, width), F32), jax.ShapeDtypeStruct((rows, 128), F32)]
    else:
        scalars = (back, parity)
        scratch = [tiles, pltpu.VMEM((rows, half), BF16)]
        kernel = functools.partial(finish_kernel, inner // heads, full_width)
        arrays += list(partial)
        out_shape = [
            jax.ShapeDtypeStruct((rows, half), BF16),
            jax.ShapeDtypeStruct((rows, inner), BF16),
            jax.ShapeDtypeStruct((rows, 128), F32),
        ]
    return call(
        kernel,
        "part" if partial is None else "finish",
        vmem=16,
        cost=micros(3.5),
        scalars=scalars,
        in_specs=[VMEM] * len(arrays),
        out_specs=[VMEM] * len(out_shape),
        out_shape=out_shape,
        scratch=scratch,
        after=after,
    )(*scalars, *arrays)


def total_kernel(mine_ref, theirs_ref, out_hbm, out_ref, sems):
    copies = []
    for i, r in enumerate(range(0, mine_ref.shape[0], CHUNK)):
        for q in range(r, r + CHUNK, BLOCK):
            block = slice(q, q + BLOCK)
            out_ref[block, :] = (mine_ref[block, :].astype(F32) + theirs_ref[block, :].astype(F32)).astype(BF16)
        part = pl.ds(r, CHUNK)
        copies.append(pltpu.make_async_copy(out_ref.at[part, :], out_hbm.at[part, :], sems.at[i]))
        copies[-1].start()
    for copy in copies:
        copy.wait()


def total_call(mine, theirs):
    rows, half = mine.shape
    return call(
        total_kernel,
        "total",
        vmem=4,
        cost=micros(0.8),
        in_specs=[VMEM] * 2,
        out_specs=HBM,
        out_shape=jax.ShapeDtypeStruct((rows, half), BF16),
        scratch=[pltpu.VMEM((rows, half), BF16), pltpu.SemaphoreType.DMA((rows // CHUNK,))],
    )(mine, theirs)


def body(
    tokens,
    hidden,
    embedding,
    w_gate,
    w_inner,
    w_state,
    w_step,
    conv_inner,
    conv_state,
    step_bias,
    decay_rate,
    norm_gain,
    w_output,
):
    swap = [(0, 1), (1, 0)]

    def theirs(a):
        return lax.ppermute(a, "ch", swap)

    core = lax.axis_index("ch").astype(jnp.int32)
    index = lax.axis_index("seq").astype(jnp.int32)
    last = lax.axis_size("seq") - 1
    back = core.reshape(1)
    parity = (index & 1).reshape(1)
    place = (index + core * (last - 2 * index)).reshape(1)
    place, parity, w_inner_3, w_gate_3, w_output_3 = lax.optimization_barrier(
        (place, parity, w_inner, w_gate, w_output)
    )
    w_inner_2 = theirs(w_inner_3)
    normed, tail, small = prepare_call(
        (back, parity, place), hidden, tokens, embedding, conv_inner, norm_gain, step_bias, decay_rate, w_step.T
    )
    halo = onward(tail, 1)
    small_2 = theirs(small)
    w_gate_2 = theirs(w_gate_3)
    w_output_2 = theirs(w_output_3)
    gate_1 = gate_call("own", normed, w_gate)
    bc, bt = maps_call(place, normed, halo, w_state, conv_state, after=[gate_1])
    x_1, cum_1, times_1, send_1, mine_1 = local_call("own", place, parity, normed, halo, bt, w_inner, small)
    chain_1 = Chain("own", place, send_1, mine_1)
    x_2, cum_2, times_2, send_2, mine_2 = local_call(
        "other", place, parity, normed, halo, bt, w_inner_2, small_2, after=[mine_1]
    )
    chain_2 = Chain("other", place, send_2, mine_2)
    gate_2 = gate_call("other", normed, w_gate_2, after=[x_2])
    done = chain_1.pair(after=[gate_2])
    y_1 = inside_call("own", x_1, bc, bt, cum_1, times_1, after=[done])
    done = chain_1.middle(after=[y_1])
    done = chain_2.pair(after=[done])
    entry_1 = chain_1.entry(after=[done])
    done = chain_2.middle(after=[entry_1[0]])
    entry_2 = chain_2.entry(after=[done])
    y_2 = inside_call("other", x_2, bc, bt, cum_2, times_2, after=[entry_2[0]])
    partial = finish_call(
        back, parity, y_1, bc, cum_1, *entry_1, gate_1, small, w_output, after=[y_2]
    )
    full_width = float(w_inner.shape[1] * lax.axis_size("ch"))
    send, scaled, scale = finish_call(
        back, parity, y_2, bc, cum_2, *entry_2, gate_2, small_2, w_output_2, full_width, partial
    )
    arriving = theirs(send)
    mine = own_call(back, scaled, w_output_2, partial[0], scale, after=[send])
    return total_call(mine, arriving)


def solution(mesh):
    return jax.shard_map(
        body,
        mesh=mesh,
        in_specs=(
            P(("win", "seq")),
            P(("win", "seq"), None),
            P(),
            P(None, "ch"),
            P(None, "ch"),
            P(),
            P(None, "ch"),
            P(None, "ch"),
            P(),
            P("ch"),
            P("ch"),
            P("ch"),
            P("ch", None),
        ),
        out_specs=P(("win", "seq"), "ch"),
        check_vma=False,
    )
```

```python
import functools

import jax
import jax.numpy as jnp
from jax import lax
from jax.experimental import pallas as pl
from jax.experimental.pallas import tpu as pltpu
from jax.sharding import PartitionSpec as P

F32 = jnp.float32
BF16 = jnp.bfloat16
EPS = 1e-05
HALO = 16
EXTRA = 16
CHUNK = 128
TILE = 256
BLOCK = 64
MB = 1024 * 1024
VMEM = pl.BlockSpec(memory_space=pltpu.VMEM)
HBM = pl.BlockSpec(memory_space=pltpu.HBM)


def call(
    kernel, name, *, vmem, cost, scalars=(), grid=(), in_specs, out_specs, out_shape, scratch=(), after=()
):
    flops, moved, special = cost
    first = len(scalars) + len(in_specs)

    def body(*refs):
        kernel(*refs[:first], *refs[first + len(after) :])

    run = pl.pallas_call(
        body,
        grid_spec=pltpu.PrefetchScalarGridSpec(
            num_scalar_prefetch=len(scalars),
            grid=grid,
            in_specs=list(in_specs) + [pl.BlockSpec(memory_space=pl.ANY)] * len(after),
            out_specs=out_specs,
            scratch_shapes=scratch,
        ),
        out_shape=out_shape,
        compiler_params=pltpu.CompilerParams(
            vmem_limit_bytes=vmem * MB, dimension_semantics=("arbitrary",) * len(grid)
        ),
        cost_estimate=pl.CostEstimate(flops=flops, bytes_accessed=moved, transcendentals=special),
        name=name,
    )
    return lambda *arrays: run(*arrays, *after)


def micros(us):
    return (int(us * 1.1e9), int(us * 1e6), 0)


def dot(a, b):
    return jnp.dot(a, b, preferred_element_type=F32)


def dot_nt(a, b):
    return lax.dot_general(a, b, (((1,), (1,)), ((), ())), preferred_element_type=F32)


def dot_tn(a, b):
    return lax.dot_general(a, b, (((0,), (0,)), ((), ())), preferred_element_type=F32)


def flip_matrix(size):
    rows = lax.broadcasted_iota(jnp.int32, (size, size), 0)
    columns = lax.broadcasted_iota(jnp.int32, (size, size), 1)
    return jnp.where(rows + columns == size - 1, 1.0, 0.0).astype(BF16)


def flip_both(value):
    rows, width = value.shape
    turned = dot(flip_matrix(rows), value).astype(BF16)
    anti = flip_matrix(TILE)
    count = width // TILE
    blocks = [
        dot(turned[:, (count - 1 - k) * TILE : (count - k) * TILE], anti).astype(BF16)
        for k in range(count)
    ]
    return jnp.concatenate(blocks, axis=1)


def silu(v):
    half = 0.5 * v
    return half + half * jnp.tanh(half)


def two_parts(value):
    high = value.astype(BF16)
    low = (value - high.astype(F32)).astype(BF16)
    return jnp.concatenate([high, low], axis=1)


def two_rows(value):
    high = value.astype(BF16).astype(F32)
    return jnp.concatenate([high, value - high], axis=0)


def head_matrix(heads, width, head_size, first_head):
    source = lax.broadcasted_iota(jnp.int32, (2 * heads, width), 0)
    source = jnp.where(source >= heads, source - heads, source)
    target = lax.broadcasted_iota(jnp.int32, (2 * heads, width), 1) // head_size + first_head
    return jnp.where(source == target, 1.0, 0.0).astype(BF16)


def prepare_kernel(
    back_ref,
    parity_ref,
    place_ref,
    hidden_hbm,
    tokens_hbm,
    emb_hbm,
    conv_hbm,
    gain_hbm,
    bias_hbm,
    rate_hbm,
    step_hbm,
    out_ref,
    tail_ref,
    small_ref,
    hidden_ref,
    tokens_ref,
    emb_ref,
    conv_ref,
    gain_ref,
    bias_ref,
    rate_ref,
    step_ref,
    base_ref,
    normed_ref,
    sems,
):
    rows = hidden_ref.shape[0]
    kinds = emb_ref.shape[0]
    taps, inner = conv_ref.shape
    heads = bias_ref.shape[1]
    count = rows // CHUNK
    back = back_ref[0] == 1
    whole = [
        (tokens_hbm, tokens_ref),
        (emb_hbm, emb_ref),
        (conv_hbm, conv_ref),
        (gain_hbm, gain_ref),
        (bias_hbm, bias_ref),
        (rate_hbm, rate_ref),
        (step_hbm, step_ref),
    ]
    small_copies = [pltpu.make_async_copy(src, dst, sems.at[count + i]) for i, (src, dst) in enumerate(whole)]
    parts = [pl.ds(r * CHUNK, CHUNK) for r in range(count)]
    copies = [
        pltpu.make_async_copy(hidden_hbm.at[part, :], hidden_ref.at[part, :], sems.at[r])
        for r, part in enumerate(parts)
    ]
    for copy in small_copies[:2] + copies + small_copies[2:]:
        copy.start()
    for copy in small_copies[:2]:
        copy.wait()
    kind = lax.broadcasted_iota(jnp.int32, (kinds, rows), 0)
    onehot = jnp.where(kind == tokens_ref[...], 1.0, 0.0).astype(BF16)
    for r in range(count):
        copies[r].wait()
        low, high = r * CHUNK, (r + 1) * CHUNK
        base_ref[...] = dot_tn(onehot[:, low:high], emb_ref[...])
        for q in range(low, high, HALO):
            block = slice(q, q + HALO)
            merged = hidden_ref[block, :].astype(F32) + base_ref[q - low : q - low + HALO, :]
            merged = merged.astype(BF16).astype(F32)
            mean = jnp.mean(merged * merged, axis=-1, keepdims=True)
            normed_ref[q - low : q - low + HALO, :] = (merged * lax.rsqrt(mean + EPS)).astype(BF16)

        @pl.when(back)
        def _():
            out_ref[rows - high : rows - low, :] = flip_both(normed_ref[...])

        @pl.when(jnp.logical_not(back))
        def _():
            out_ref[low:high, :] = normed_ref[...]

    tail_ref[...] = out_ref[rows - HALO :, :]
    for copy in small_copies[2:]:
        copy.wait()
    small_ref[:taps, :] = conv_ref[...]
    small_ref[taps : taps + 1, :] = gain_ref[...]
    small_ref[taps + 1 : SMALL_ROWS, :] = jnp.zeros((SMALL_ROWS - taps - 1, inner), F32)
    small_ref[taps + 1 : taps + 2, :heads] = bias_ref[...]
    small_ref[taps + 2 : taps + 3, :heads] = rate_ref[...]
    small_ref[SMALL_ROWS:, :] = step_ref[...].astype(F32)


def prepare_call(scalars, hidden, tokens, embedding, conv, gain, bias, rate, step):
    rows, width = hidden.shape
    inner = conv.shape[1]
    arrays = [hidden, tokens.reshape(1, -1), embedding, conv]
    arrays += [a.reshape(1, -1) for a in (gain, bias, rate)] + [step]
    return call(
        prepare_kernel,
        "prepare",
        vmem=12,
        cost=micros(2.7),
        scalars=scalars,
        in_specs=[HBM] * len(arrays),
        out_specs=[VMEM] * 3,
        out_shape=[
            jax.ShapeDtypeStruct((rows, width), BF16),
            jax.ShapeDtypeStruct((HALO, width), BF16),
            jax.ShapeDtypeStruct((SMALL_ROWS + step.shape[0], inner), F32),
        ],
        scratch=[pltpu.VMEM(a.shape, a.dtype) for a in arrays]
        + [pltpu.VMEM((CHUNK, width), F32), pltpu.VMEM((CHUNK, width), BF16)]
        + [pltpu.SemaphoreType.DMA((rows // CHUNK + len(arrays) - 1,))],
    )(*scalars, *(pltpu.with_memory_space_constraint(a, pltpu.HBM) for a in arrays))


def gate_kernel(rows_ref, wg_ref, out_ref, gate_ref):
    rows, inner = out_ref.shape
    for low in range(0, inner, TILE):
        columns = slice(low, low + TILE)
        gate_ref[...] = dot(rows_ref[...], wg_ref[:, columns])
        for r in range(0, rows, BLOCK):
            gate = gate_ref[r : r + BLOCK, :].astype(BF16).astype(F32)
            out_ref[r : r + BLOCK, columns] = silu(gate).astype(BF16)


def gate_call(tag, normed, w_gate, after=()):
    rows = normed.shape[0]
    inner = w_gate.shape[1]
    return call(
        gate_kernel,
        "gate_" + tag,
        vmem=8,
        cost=micros(2.4),
        in_specs=[VMEM] * 2,
        out_specs=VMEM,
        out_shape=jax.ShapeDtypeStruct((rows, inner), BF16),
        scratch=[pltpu.VMEM((rows, TILE), F32)],
        after=after,
    )(normed, w_gate)


def conv_silu(rows_ref, weights, row):
    taps = weights.shape[0]
    ahead = 8
    window = rows_ref[HALO - ahead + row : HALO + row + BLOCK, :]
    total = weights[taps - 1 :, :] * window[ahead:, :]
    for back in range(1, taps):
        total += weights[taps - 1 - back : taps - back, :] * pltpu.roll(window, back, 0)[ahead:, :]
    return silu(total).astype(BF16)


def maps_kernel(place_ref, normed_ref, halo_ref, ws_ref, cs_ref, bc_ref, bt_ref, rows_ref):
    rows = normed_ref.shape[0]
    states = bc_ref.shape[1] // 2
    before = dot(halo_ref[...], ws_ref[...]).astype(BF16).astype(F32)
    rows_ref[:HALO, :] = jnp.where(place_ref[0] >= 1, before, 0.0)
    rows_ref[HALO:, :] = dot(normed_ref[...], ws_ref[...]).astype(BF16).astype(F32)
    weights = cs_ref[...]
    for r in range(0, rows, BLOCK):
        bc_ref[r : r + BLOCK, :] = conv_silu(rows_ref, weights, r)
    bt_ref[...] = bc_ref[:, :states].astype(F32).T.astype(BF16)


def maps_call(place, normed, halo, w_state, conv_state, after=()):
    rows = normed.shape[0]
    both = w_state.shape[1]
    return call(
        maps_kernel,
        "maps",
        vmem=8,
        cost=micros(1.5),
        scalars=(place,),
        in_specs=[VMEM] * 4,
        out_specs=[VMEM] * 2,
        out_shape=[
            jax.ShapeDtypeStruct((rows, both), BF16),
            jax.ShapeDtypeStruct((both // 2, rows), BF16),
        ],
        scratch=[pltpu.VMEM((rows + HALO, both), F32)],
        after=after,
    )(place, normed, halo, w_state, conv_state)


def local_kernel(
    head_size,
    place_ref,
    parity_ref,
    normed_ref,
    halo_ref,
    bt_ref,
    wi_ref,
    small_ref,
    x_ref,
    cum_ref,
    times_ref,
    send_ref,
    mine_ref,
    rows_ref,
    spread_ref,
    scaled_ref,
    left_ref,
    whole_ref,
    payload_ref,
):
    rows = normed_ref.shape[0]
    states = bt_ref.shape[0]
    heads = cum_ref.shape[1]
    taps = SMALL_TAPS
    raw = dot_nt(normed_ref[...], small_ref[SMALL_ROWS:, :].astype(BF16))
    columns = small_ref[:SMALL_ROWS, :CHUNK].T
    raw = raw.T + columns[:heads, taps + 1 : taps + 2]
    step = jnp.maximum(raw, 0.0) + jnp.log1p(jnp.exp(-jnp.abs(raw)))
    logdecay = -step * columns[:heads, taps + 2 : taps + 3]
    high = logdecay.astype(BF16)
    rest = logdecay - high.astype(F32)
    mid = rest.astype(BF16)
    low = (rest - mid.astype(F32)).astype(BF16)
    starts = range(0, rows, CHUNK)
    pieces = [part[:, r : r + CHUNK] for r in starts for part in (high, mid, low)]
    frm = lax.broadcasted_iota(jnp.int32, (CHUNK, CHUNK), 0)
    to = lax.broadcasted_iota(jnp.int32, (CHUNK, CHUNK), 1)
    sums = dot(jnp.concatenate(pieces, axis=0), jnp.where(to >= frm, 1.0, 0.0).astype(BF16))
    run = jnp.zeros((heads, 1), F32)
    cums = []
    for i in range(len(starts)):
        at = 3 * i * heads
        cums.append(sums[at : at + heads] + sums[at + heads : at + 2 * heads] + sums[at + 2 * heads : at + 3 * heads] + run)
        run = cums[-1][:, CHUNK - 1 :]
    cum = jnp.concatenate(cums, axis=1)
    times_ref[:heads, :] = cum
    times_ref[heads:, :] = step
    cum_ref[...] = cum.T
    left_ref[...] = two_rows(step * jnp.exp(run - cum)).T.astype(BF16)
    whole_ref[...] = two_parts(jnp.exp(cum_ref[rows - 1 :, :]))

    inner = x_ref.shape[1]
    half = inner // 2
    tiles = range(inner // TILE)
    onehots = [head_matrix(heads, TILE, head_size, t * (TILE // head_size)) for t in tiles]
    spans = [slice(t * TILE, (t + 1) * TILE) for t in tiles]

    def project(t):
        weights = wi_ref[:, spans[t]]
        before = dot(halo_ref[...], weights).astype(BF16).astype(F32)
        rows_ref[t % 2, :HALO, :] = jnp.where(place_ref[0] >= 1, before, 0.0)
        rows_ref[t % 2, HALO:, :] = dot(normed_ref[...], weights).astype(BF16).astype(F32)
        spread_ref[t % 2] = dot(left_ref[...], onehots[t])

    def combine(t):
        taps_here = small_ref[:taps, spans[t]]
        for r in range(0, rows, BLOCK):
            block = slice(r, r + BLOCK)
            x = conv_silu(rows_ref.at[t % 2], taps_here, r)
            x_ref[block, spans[t]] = x
            scaled_ref[t % 2, block, :] = (x.astype(F32) * spread_ref[t % 2, block, :]).astype(BF16)
        state = dot(bt_ref[...], scaled_ref[t % 2])
        here = slice(t * TILE % half, t * TILE % half + TILE)
        is_mine = jnp.where(parity_ref[0] == t * TILE // half, 1, 0)
        write_payload(payload_ref.at[is_mine], here, state, dot(whole_ref[...], onehots[t]))

    project(0)
    for t in tiles:
        if t + 1 < len(tiles):
            project(t + 1)
        combine(t)
    send_ref[...] = payload_ref[0]
    mine_ref[...] = payload_ref[1]


SMALL_TAPS = 4
SMALL_ROWS = 8


def local_call(tag, place, parity, normed, halo, bt, w_inner, small, after=()):
    rows = normed.shape[0]
    inner = w_inner.shape[1]
    heads = small.shape[0] - SMALL_ROWS
    states = bt.shape[0]
    return call(
        functools.partial(local_kernel, inner // heads),
        "local_" + tag,
        vmem=12,
        cost=micros(5.0),
        scalars=(place, parity),
        in_specs=[VMEM] * 5,
        out_specs=[VMEM] * 5,
        out_shape=[
            jax.ShapeDtypeStruct((rows, inner), BF16),
            jax.ShapeDtypeStruct((rows, heads), F32),
            jax.ShapeDtypeStruct((2 * heads, rows), F32),
            jax.ShapeDtypeStruct((states + EXTRA, inner // 2), BF16),
            jax.ShapeDtypeStruct((states + EXTRA, inner // 2), BF16),
        ],
        scratch=[
            pltpu.VMEM((2, rows + HALO, TILE), F32),
            pltpu.VMEM((2, rows, TILE), F32),
            pltpu.VMEM((2, rows, TILE), BF16),
            pltpu.VMEM((rows, 2 * heads), BF16),
            pltpu.VMEM((1, 2 * heads), BF16),
            pltpu.VMEM((2, states + EXTRA, inner // 2), BF16),
        ],
        after=after,
    )(place, parity, normed, halo, bt, w_inner, small)


def inside_kernel(head_size, x_ref, bc_ref, bt_ref, cum_ref, times_ref, y_ref, state_ref):
    rows, inner = x_ref.shape
    states = bc_ref.shape[1] // 2
    heads = cum_ref.shape[1]
    length = CHUNK
    last = length - 1
    pair = 2 * head_size
    lane = lax.broadcasted_iota(jnp.int32, (length, pair), 1)
    to = lax.broadcasted_iota(jnp.int32, (length, length), 0)
    frm = lax.broadcasted_iota(jnp.int32, (length, length), 1)
    state_ref[...] = jnp.zeros_like(state_ref)

    def chunk(c, before):
        at = slice(c * length, (c + 1) * length)
        bmat = bt_ref[:, at]
        cmat = bc_ref[at, states:]
        scores = jnp.where(to >= frm, dot(cmat, bmat), 0.0)
        cum = cum_ref[at, :]
        cumt = times_ref[:heads, at]
        step = times_ref[heads:, at]
        end = cumt[:, last:]
        since = two_rows(jnp.exp(cumt - before)).T.astype(BF16)
        left = two_rows(step * jnp.exp(end - cumt)).T.astype(BF16)
        for first in range(0, heads, TILE // head_size):
            columns = slice(first * head_size, first * head_size + TILE)
            onehot = head_matrix(heads, TILE, head_size, first)
            since_here = dot(since, onehot)
            state = state_ref[:, columns]
            carried = dot(cmat, state.astype(BF16)) * since_here
            scaled = (x_ref[at, columns].astype(F32) * dot(left, onehot)).astype(BF16)
            state_ref[:, columns] = state * since_here[last:, :] + dot(bmat, scaled)
            for start in range(0, TILE, pair):
                low = first * head_size + start
                weights = []
                for h in (low // head_size, low // head_size + 1):
                    apart = jnp.minimum(cum[:, h : h + 1] - cumt[h : h + 1, :], 0.0)
                    weights.append((jnp.exp(apart) * (scores * step[h : h + 1, :])).astype(BF16))
                mine = x_ref[at, low : low + pair]
                none = jnp.zeros_like(mine)
                stacked = jnp.concatenate(
                    [jnp.where(lane < head_size, mine, none), jnp.where(lane < head_size, none, mine)], axis=0
                )
                inside = dot(jnp.concatenate(weights, axis=1), stacked)
                y_ref[at, low : low + pair] = (inside + carried[:, start : start + pair]).astype(BF16)
        return end

    before = jnp.zeros((heads, 1), F32)
    for c in range(rows // length):
        before = chunk(c, before)


def inside_call(tag, x, bc, bt, cum, times, after=()):
    rows, inner = x.shape
    heads = cum.shape[1]
    both = bc.shape[1]
    return call(
        functools.partial(inside_kernel, inner // heads),
        "inside_" + tag,
        vmem=8,
        cost=micros(3.2),
        in_specs=[VMEM] * 5,
        out_specs=VMEM,
        out_shape=jax.ShapeDtypeStruct((rows, inner), BF16),
        scratch=[pltpu.VMEM((both // 2, inner), F32)],
        after=after,
    )(x, bc, bt, cum, times)


def parts_of(ref, known=None):
    states = ref.shape[0] - EXTRA
    state = ref[:states, :].astype(F32)
    extra = ref[states:, :].astype(F32)
    decay = extra[:1] + extra[1:2]
    if known is None:
        return state, decay
    return jnp.where(known, state, 0.0), jnp.where(known, decay, 0.0)


def write_payload(out_ref, columns, state, decay):
    states = state.shape[0]
    out_ref[:states, columns] = state.astype(BF16)
    decay = jnp.broadcast_to(decay, (EXTRA, decay.shape[1]))
    high = decay.astype(BF16).astype(F32)
    place = lax.broadcasted_iota(jnp.int32, decay.shape, 0)
    out_ref[states:, columns] = jnp.where(place == 0, high, decay - high).astype(BF16)


ALL = slice(None)


def pair_kernel(place_ref, *refs):
    *ins, out_ref = refs
    is_first = lax.rem(place_ref[0], 2) == 0
    for group in range(len(ins) // 2):
        mine_ref, other_ref = ins[2 * group : 2 * group + 2]
        mine, mine_a = parts_of(mine_ref)
        other, other_a = parts_of(other_ref)
        early = jnp.where(is_first, mine, other)
        late = jnp.where(is_first, other, mine)
        late_a = jnp.where(is_first, other_a, mine_a)
        width = mine_ref.shape[1]
        here = slice(group * width, (group + 1) * width)
        write_payload(out_ref, here, late_a * early + late, mine_a * other_a)


def chain_kernel(reach, place_ref, pair_ref, before_ref, out_ref):
    pair, pair_a = parts_of(pair_ref)
    before, before_a = parts_of(before_ref, place_ref[0] >= reach)
    write_payload(out_ref, ALL, pair_a * before + pair, pair_a * before_a)


def longer_kernel(reach, farther_reach, place_ref, before_ref, farther_ref, out_ref):
    before, before_a = parts_of(before_ref, place_ref[0] >= reach)
    farther, farther_a = parts_of(farther_ref, place_ref[0] >= farther_reach)
    write_payload(out_ref, ALL, before + before_a * farther, before_a * farther_a)


def entry_kernel(reach, farther_reach, place_ref, *refs):
    groups = (len(refs) - 2) // 4
    before_ref, farther_ref = refs[2 * groups : 2 * groups + 2]
    is_first = lax.rem(place_ref[0], 2) == 0
    before, before_a = parts_of(before_ref, place_ref[0] >= reach)
    farther, _ = parts_of(farther_ref, place_ref[0] >= farther_reach)
    entries = before + before_a * farther
    for group in range(groups):
        mine_ref, other_ref = refs[2 * group : 2 * group + 2]
        keep_ref, send_ref = refs[2 * groups + 2 + 2 * group : 2 * groups + 4 + 2 * group]
        mine, mine_a = parts_of(mine_ref)
        other, other_a = parts_of(other_ref)
        width = mine_ref.shape[1]
        entry_first = entries[:, group * width : (group + 1) * width]
        early = jnp.where(is_first, mine, other)
        early_a = jnp.where(is_first, mine_a, other_a)
        entry_second = early_a * entry_first + early
        keep_ref[...] = jnp.where(is_first, entry_first, entry_second).astype(BF16)
        send_ref[...] = jnp.where(is_first, entry_second, entry_first).astype(BF16)


def small_call(kernel, name, place, arrays, shapes, after=()):
    return call(
        kernel,
        name,
        vmem=4,
        cost=micros(0.5),
        scalars=(place,),
        in_specs=[VMEM] * len(arrays),
        out_specs=[VMEM] * len(shapes),
        out_shape=[jax.ShapeDtypeStruct(s, BF16) for s in shapes],
        after=after,
    )(place, *arrays)


def onward(value, by):
    count = lax.axis_size("seq")
    pairs = []
    for i in range(count):
        up = (i + by, 0) if i + by < count else (i, 1)
        down = (i - by, 1) if i - by >= 0 else (i, 0)
        pairs += [(2 * i, 2 * up[0] + up[1]), (2 * i + 1, 2 * down[0] + down[1])]
    return lax.ppermute(value, ("seq", "ch"), pairs)


def in_pairs(value):
    count = lax.axis_size("seq")
    return lax.ppermute(value, "seq", [(i, i ^ 1) for i in range(count)])


class Chain:
    def __init__(self, place, halves):
        self.place, self.halves = place, halves
        self.flat = [a for pair in halves for a in pair]
        height, width = self.flat[0].shape
        self.shape = (height, width * len(halves))
        self.count = lax.axis_size("seq")
        self.before = self.farther = None
        self.reach = self.farther_reach = 0
        self.apart = 2

    def pair(self, after):
        (self.pair_state,) = small_call(pair_kernel, "pair", self.place, self.flat, [self.shape], after)
        self.running = self.pair_state
        self.hop()
        return self.pair_state

    def hop(self):
        if self.apart < self.count:
            self.arrived = onward(self.running, self.apart)

    def middle(self, after):
        while self.apart * 2 < self.count:
            self.take(after)
            (self.running,) = small_call(
                functools.partial(chain_kernel, self.reach),
                "chain",
                self.place,
                [self.pair_state, self.before],
                [self.shape],
                after,
            )
            self.apart *= 2
            self.hop()
        return self.running

    def take(self, after=()):
        if self.before is None:
            self.before, self.reach = self.arrived, self.apart
        else:
            (self.before,) = small_call(
                functools.partial(longer_kernel, self.reach, self.apart),
                "longer",
                self.place,
                [self.before, self.arrived],
                [self.shape],
                after,
            )
            self.reach = 0

    def entry(self, after):
        if self.apart < self.count:
            if self.before is None:
                self.before, self.reach = self.arrived, self.apart
                self.farther, self.farther_reach = self.arrived, self.count
            else:
                self.farther, self.farther_reach = self.arrived, self.apart
        else:
            self.before = self.farther = self.pair_state
            self.reach = self.farther_reach = self.count
        half = (self.shape[0] - EXTRA, self.flat[0].shape[1])
        outs = small_call(
            functools.partial(entry_kernel, self.reach, self.farther_reach),
            "entry",
            self.place,
            self.flat + [self.before, self.farther],
            [half, half] * len(self.halves),
            after,
        )
        return [(outs[2 * i], in_pairs(outs[2 * i + 1])) for i in range(len(self.halves))]


def gated_part(
    head_size, swap, y_ref, bc_ref, cum_ref, keep_ref, other_ref, gate_ref, small_ref, wo_ref, scaled_ref, tile_ref
):
    rows, inner = y_ref.shape
    states = bc_ref.shape[1] // 2
    heads = cum_ref.shape[1]
    half = inner // 2
    since = two_parts(jnp.exp(cum_ref[...]))
    squares = [0.0] * (rows // BLOCK)
    for low in range(0, inner, TILE):
        columns = slice(low, low + TILE)
        here = slice(low % half, low % half + TILE)
        use_other = swap if low < half else jnp.logical_not(swap)
        entry = jnp.where(use_other, other_ref[:, here], keep_ref[:, here])
        tile_ref[0] = dot(bc_ref[:, states:], entry)
        tile_ref[1] = dot(since, head_matrix(heads, TILE, head_size, low // head_size))
        gain = small_ref[SMALL_TAPS : SMALL_TAPS + 1, columns]
        for i, r in enumerate(range(0, rows, BLOCK)):
            block = slice(r, r + BLOCK)
            gated = y_ref[block, columns].astype(F32) + tile_ref[0, block, :] * tile_ref[1, block, :]
            gated = gated * gate_ref[block, columns].astype(F32)
            squares[i] += jnp.sum(gated * gated, axis=-1, keepdims=True)
            scaled_ref[block, columns] = (gated * gain).astype(BF16)
    return squares


def part_kernel(head_size, parity_ref, *refs):
    *ins, out_ref, sq_ref, scaled_ref, tile_ref = refs
    squares = gated_part(head_size, parity_ref[0] == 1, *ins, scaled_ref, tile_ref)
    for i, square in enumerate(squares):
        sq_ref[i * BLOCK : (i + 1) * BLOCK, :] = jnp.broadcast_to(square, (BLOCK, sq_ref.shape[1]))
    for low in range(0, out_ref.shape[1], TILE):
        out_ref[:, low : low + TILE] = dot(scaled_ref[...], ins[-1][:, low : low + TILE])


def product(back, scaled_ref, weights_ref, part_ref, scale_ref, tile_ref, half_ref, out_ref, first):
    rows, half = out_ref.shape
    for low in range(0, half, TILE):
        columns = slice(first + low, first + low + TILE)
        tile_ref[...] = dot(scaled_ref[...], weights_ref[:, columns])
        for r in range(0, rows, BLOCK):
            block = slice(r, r + BLOCK)
            value = (tile_ref[block, :] + part_ref[block, columns]) * scale_ref[block, :1]
            half_ref[block, low : low + TILE] = value.astype(BF16)

    @pl.when(back == 1)
    def _():
        turn = flip_matrix(TILE)
        for r in range(0, rows, TILE):
            for low in range(0, half, TILE):
                tile = dot(turn, half_ref[r : r + TILE, low : low + TILE]).astype(BF16)
                tile = dot(tile, turn).astype(BF16)
                to_row, to = rows - TILE - r, half - TILE - low
                out_ref[to_row : to_row + TILE, to : to + TILE] = tile

    @pl.when(back != 1)
    def _():
        out_ref[...] = half_ref[...]


def finish_kernel(head_size, full_width, back_ref, parity_ref, *refs):
    *ins, part_ref, psq_ref, send_ref, scaled_ref, scale_ref, tile_ref, half_ref = refs
    squares = gated_part(head_size, parity_ref[0] == 1, *ins, scaled_ref, tile_ref)
    for i, square in enumerate(squares):
        block = slice(i * BLOCK, (i + 1) * BLOCK)
        scale = lax.rsqrt((square + psq_ref[block, :1]) / full_width + EPS)
        scale_ref[block, :] = jnp.broadcast_to(scale, (BLOCK, scale_ref.shape[1]))
    product(back_ref[0], scaled_ref, ins[-1], part_ref, scale_ref, tile_ref.at[0], half_ref, send_ref, send_ref.shape[1])


def own_kernel(back_ref, scaled_ref, weights_ref, part_ref, scale_ref, own_ref, tile_ref, half_ref):
    product(back_ref[0], scaled_ref, weights_ref, part_ref, scale_ref, tile_ref, half_ref, own_ref, 0)


def own_call(back, scaled, w_output, part, scale, after):
    rows, width = part.shape
    half = width // 2
    return call(
        own_kernel,
        "own_half",
        vmem=8,
        cost=micros(0.7),
        scalars=(back,),
        in_specs=[VMEM] * 4,
        out_specs=VMEM,
        out_shape=jax.ShapeDtypeStruct((rows, half), BF16),
        scratch=[pltpu.VMEM((rows, TILE), F32), pltpu.VMEM((rows, half), BF16)],
        after=after,
    )(back, scaled, w_output, part, scale)


def finish_call(back, parity, y, bc, cum, keep, other, gate, small, w_output, full_width=None, partial=None, after=()):
    rows, inner = y.shape
    width = w_output.shape[1]
    half = width // 2
    heads = cum.shape[1]
    arrays = [y, bc, cum, keep, other, gate, small, w_output]
    tiles = pltpu.VMEM((2, rows, TILE), F32)
    if partial is None:
        scratch = [pltpu.VMEM((rows, inner), BF16), tiles]
        scalars = (parity,)
        kernel = functools.partial(part_kernel, inner // heads)
        out_shape = [jax.ShapeDtypeStruct((rows, width), F32), jax.ShapeDtypeStruct((rows, 128), F32)]
    else:
        scalars = (back, parity)
        scratch = [tiles, pltpu.VMEM((rows, half), BF16)]
        kernel = functools.partial(finish_kernel, inner // heads, full_width)
        arrays += list(partial)
        out_shape = [
            jax.ShapeDtypeStruct((rows, half), BF16),
            jax.ShapeDtypeStruct((rows, inner), BF16),
            jax.ShapeDtypeStruct((rows, 128), F32),
        ]
    return call(
        kernel,
        "part" if partial is None else "finish",
        vmem=16,
        cost=micros(3.5),
        scalars=scalars,
        in_specs=[VMEM] * len(arrays),
        out_specs=[VMEM] * len(out_shape),
        out_shape=out_shape,
        scratch=scratch,
        after=after,
    )(*scalars, *arrays)


def total_kernel(mine_ref, theirs_ref, out_hbm, out_ref, sems):
    copies = []
    for i, r in enumerate(range(0, mine_ref.shape[0], CHUNK)):
        for q in range(r, r + CHUNK, BLOCK):
            block = slice(q, q + BLOCK)
            out_ref[block, :] = (mine_ref[block, :].astype(F32) + theirs_ref[block, :].astype(F32)).astype(BF16)
        part = pl.ds(r, CHUNK)
        copies.append(pltpu.make_async_copy(out_ref.at[part, :], out_hbm.at[part, :], sems.at[i]))
        copies[-1].start()
    for copy in copies:
        copy.wait()


def total_call(mine, theirs):
    rows, half = mine.shape
    return call(
        total_kernel,
        "total",
        vmem=4,
        cost=micros(0.8),
        in_specs=[VMEM] * 2,
        out_specs=HBM,
        out_shape=jax.ShapeDtypeStruct((rows, half), BF16),
        scratch=[pltpu.VMEM((rows, half), BF16), pltpu.SemaphoreType.DMA((rows // CHUNK,))],
    )(mine, theirs)


def body(
    tokens,
    hidden,
    embedding,
    w_gate,
    w_inner,
    w_state,
    w_step,
    conv_inner,
    conv_state,
    step_bias,
    decay_rate,
    norm_gain,
    w_output,
):
    swap = [(0, 1), (1, 0)]

    def theirs(a):
        return lax.ppermute(a, "ch", swap)

    core = lax.axis_index("ch").astype(jnp.int32)
    index = lax.axis_index("seq").astype(jnp.int32)
    last = lax.axis_size("seq") - 1
    back = core.reshape(1)
    parity = (index & 1).reshape(1)
    place = (index + core * (last - 2 * index)).reshape(1)
    place, parity, w_inner_3, w_gate_3, w_output_3 = lax.optimization_barrier(
        (place, parity, w_inner, w_gate, w_output)
    )
    w_inner_2 = theirs(w_inner_3)
    normed, tail, small = prepare_call(
        (back, parity, place), hidden, tokens, embedding, conv_inner, norm_gain, step_bias, decay_rate, w_step.T
    )
    halo = onward(tail, 1)
    small_2 = theirs(small)
    w_gate_2 = theirs(w_gate_3)
    w_output_2 = theirs(w_output_3)
    gate_1 = gate_call("own", normed, w_gate)
    bc, bt = maps_call(place, normed, halo, w_state, conv_state, after=[gate_1])
    x_1, cum_1, times_1, send_1, mine_1 = local_call("own", place, parity, normed, halo, bt, w_inner, small)
    other_1 = in_pairs(send_1)
    x_2, cum_2, times_2, send_2, mine_2 = local_call(
        "other", place, parity, normed, halo, bt, w_inner_2, small_2, after=[mine_1]
    )
    other_2 = in_pairs(send_2)
    gate_2 = gate_call("other", normed, w_gate_2, after=[x_2])
    y_1 = inside_call("own", x_1, bc, bt, cum_1, times_1, after=[gate_2])
    chain = Chain(place, [(mine_1, other_1), (mine_2, other_2)])
    done = chain.pair(after=[y_1])
    y_2 = inside_call("other", x_2, bc, bt, cum_2, times_2, after=[done])
    done = chain.middle(after=[y_2])
    entry_1, entry_2 = chain.entry(after=[done])
    partial = finish_call(
        back, parity, y_1, bc, cum_1, *entry_1, gate_1, small, w_output
    )
    full_width = float(w_inner.shape[1] * lax.axis_size("ch"))
    send, scaled, scale = finish_call(
        back, parity, y_2, bc, cum_2, *entry_2, gate_2, small_2, w_output_2, full_width, partial
    )
    arriving = theirs(send)
    mine = own_call(back, scaled, w_output_2, partial[0], scale, after=[send])
    return total_call(mine, arriving)


def solution(mesh):
    return jax.shard_map(
        body,
        mesh=mesh,
        in_specs=(
            P(("win", "seq")),
            P(("win", "seq"), None),
            P(),
            P(None, "ch"),
            P(None, "ch"),
            P(),
            P(None, "ch"),
            P(None, "ch"),
            P(),
            P("ch"),
            P("ch"),
            P("ch"),
            P("ch", None),
        ),
        out_specs=P(("win", "seq"), "ch"),
        check_vma=False,
    )
```

```python
import functools

import jax
import jax.numpy as jnp
from jax import lax
from jax.experimental import pallas as pl
from jax.experimental.pallas import tpu as pltpu
from jax.sharding import PartitionSpec as P

F32 = jnp.float32
BF16 = jnp.bfloat16
EPS = 1e-05
HALO = 16
EXTRA = 16
CHUNK = 128
TILE = 256
BLOCK = 64
MB = 1024 * 1024
VMEM = pl.BlockSpec(memory_space=pltpu.VMEM)
HBM = pl.BlockSpec(memory_space=pltpu.HBM)


def call(
    kernel, name, *, vmem, cost, scalars=(), grid=(), in_specs, out_specs, out_shape, scratch=(), after=()
):
    flops, moved, special = cost
    first = len(scalars) + len(in_specs)

    def body(*refs):
        kernel(*refs[:first], *refs[first + len(after) :])

    run = pl.pallas_call(
        body,
        grid_spec=pltpu.PrefetchScalarGridSpec(
            num_scalar_prefetch=len(scalars),
            grid=grid,
            in_specs=list(in_specs) + [pl.BlockSpec(memory_space=pl.ANY)] * len(after),
            out_specs=out_specs,
            scratch_shapes=scratch,
        ),
        out_shape=out_shape,
        compiler_params=pltpu.CompilerParams(
            vmem_limit_bytes=vmem * MB, dimension_semantics=("arbitrary",) * len(grid)
        ),
        cost_estimate=pl.CostEstimate(flops=flops, bytes_accessed=moved, transcendentals=special),
        name=name,
    )
    return lambda *arrays: run(*arrays, *after)


def micros(us):
    return (int(us * 1.1e9), int(us * 1e6), 0)


def dot(a, b):
    return jnp.dot(a, b, preferred_element_type=F32)


def dot_nt(a, b):
    return lax.dot_general(a, b, (((1,), (1,)), ((), ())), preferred_element_type=F32)


def dot_tn(a, b):
    return lax.dot_general(a, b, (((0,), (0,)), ((), ())), preferred_element_type=F32)


def flip_matrix(size):
    rows = lax.broadcasted_iota(jnp.int32, (size, size), 0)
    columns = lax.broadcasted_iota(jnp.int32, (size, size), 1)
    return jnp.where(rows + columns == size - 1, 1.0, 0.0).astype(BF16)


def flip_both(value):
    rows, width = value.shape
    turned = dot(flip_matrix(rows), value).astype(BF16)
    anti = flip_matrix(TILE)
    count = width // TILE
    blocks = [
        dot(turned[:, (count - 1 - k) * TILE : (count - k) * TILE], anti).astype(BF16)
        for k in range(count)
    ]
    return jnp.concatenate(blocks, axis=1)


def silu(v):
    half = 0.5 * v
    return half + half * jnp.tanh(half)


def two_parts(value):
    high = value.astype(BF16)
    low = (value - high.astype(F32)).astype(BF16)
    return jnp.concatenate([high, low], axis=1)


def two_rows(value):
    high = value.astype(BF16).astype(F32)
    return jnp.concatenate([high, value - high], axis=0)


def head_matrix(heads, width, head_size, first_head):
    source = lax.broadcasted_iota(jnp.int32, (2 * heads, width), 0)
    source = jnp.where(source >= heads, source - heads, source)
    target = lax.broadcasted_iota(jnp.int32, (2 * heads, width), 1) // head_size + first_head
    return jnp.where(source == target, 1.0, 0.0).astype(BF16)


def prepare_kernel(
    back_ref,
    parity_ref,
    place_ref,
    hidden_hbm,
    tokens_hbm,
    emb_hbm,
    conv_hbm,
    gain_hbm,
    bias_hbm,
    rate_hbm,
    step_hbm,
    out_ref,
    tail_ref,
    small_ref,
    hidden_ref,
    tokens_ref,
    emb_ref,
    conv_ref,
    gain_ref,
    bias_ref,
    rate_ref,
    step_ref,
    base_ref,
    normed_ref,
    sems,
):
    rows = hidden_ref.shape[0]
    kinds = emb_ref.shape[0]
    taps, inner = conv_ref.shape
    heads = bias_ref.shape[1]
    count = rows // CHUNK
    back = back_ref[0] == 1
    whole = [
        (tokens_hbm, tokens_ref),
        (emb_hbm, emb_ref),
        (conv_hbm, conv_ref),
        (gain_hbm, gain_ref),
        (bias_hbm, bias_ref),
        (rate_hbm, rate_ref),
        (step_hbm, step_ref),
    ]
    small_copies = [pltpu.make_async_copy(src, dst, sems.at[count + i]) for i, (src, dst) in enumerate(whole)]
    parts = [pl.ds(r * CHUNK, CHUNK) for r in range(count)]
    copies = [
        pltpu.make_async_copy(hidden_hbm.at[part, :], hidden_ref.at[part, :], sems.at[r])
        for r, part in enumerate(parts)
    ]
    for copy in small_copies[:2] + copies + small_copies[2:]:
        copy.start()
    for copy in small_copies[:2]:
        copy.wait()
    kind = lax.broadcasted_iota(jnp.int32, (kinds, rows), 0)
    onehot = jnp.where(kind == tokens_ref[...], 1.0, 0.0).astype(BF16)
    for r in range(count):
        copies[r].wait()
        low, high = r * CHUNK, (r + 1) * CHUNK
        base_ref[...] = dot_tn(onehot[:, low:high], emb_ref[...])
        for q in range(low, high, HALO):
            block = slice(q, q + HALO)
            merged = hidden_ref[block, :].astype(F32) + base_ref[q - low : q - low + HALO, :]
            merged = merged.astype(BF16).astype(F32)
            mean = jnp.mean(merged * merged, axis=-1, keepdims=True)
            normed_ref[q - low : q - low + HALO, :] = (merged * lax.rsqrt(mean + EPS)).astype(BF16)

        @pl.when(back)
        def _():
            out_ref[rows - high : rows - low, :] = flip_both(normed_ref[...])

        @pl.when(jnp.logical_not(back))
        def _():
            out_ref[low:high, :] = normed_ref[...]

    tail_ref[...] = out_ref[rows - HALO :, :]
    for copy in small_copies[2:]:
        copy.wait()
    small_ref[:taps, :] = conv_ref[...]
    small_ref[taps : taps + 1, :] = gain_ref[...]
    small_ref[taps + 1 : SMALL_ROWS, :] = jnp.zeros((SMALL_ROWS - taps - 1, inner), F32)
    small_ref[taps + 1 : taps + 2, :heads] = bias_ref[...]
    small_ref[taps + 2 : taps + 3, :heads] = rate_ref[...]
    small_ref[SMALL_ROWS:, :] = step_ref[...].astype(F32)


def prepare_call(scalars, hidden, tokens, embedding, conv, gain, bias, rate, step):
    rows, width = hidden.shape
    inner = conv.shape[1]
    arrays = [hidden, tokens.reshape(1, -1), embedding, conv]
    arrays += [a.reshape(1, -1) for a in (gain, bias, rate)] + [step]
    return call(
        prepare_kernel,
        "prepare",
        vmem=12,
        cost=micros(2.7),
        scalars=scalars,
        in_specs=[HBM] * len(arrays),
        out_specs=[VMEM] * 3,
        out_shape=[
            jax.ShapeDtypeStruct((rows, width), BF16),
            jax.ShapeDtypeStruct((HALO, width), BF16),
            jax.ShapeDtypeStruct((SMALL_ROWS + step.shape[0], inner), F32),
        ],
        scratch=[pltpu.VMEM(a.shape, a.dtype) for a in arrays]
        + [pltpu.VMEM((CHUNK, width), F32), pltpu.VMEM((CHUNK, width), BF16)]
        + [pltpu.SemaphoreType.DMA((rows // CHUNK + len(arrays) - 1,))],
    )(*scalars, *(pltpu.with_memory_space_constraint(a, pltpu.HBM) for a in arrays))


def gate_kernel(rows_ref, wg_ref, out_ref, gate_ref):
    rows, inner = out_ref.shape
    for low in range(0, inner, TILE):
        columns = slice(low, low + TILE)
        gate_ref[...] = dot(rows_ref[...], wg_ref[:, columns])
        for r in range(0, rows, BLOCK):
            gate = gate_ref[r : r + BLOCK, :].astype(BF16).astype(F32)
            out_ref[r : r + BLOCK, columns] = silu(gate).astype(BF16)


def gate_call(tag, normed, w_gate, after=()):
    rows = normed.shape[0]
    inner = w_gate.shape[1]
    return call(
        gate_kernel,
        "gate_" + tag,
        vmem=8,
        cost=micros(2.4),
        in_specs=[VMEM] * 2,
        out_specs=VMEM,
        out_shape=jax.ShapeDtypeStruct((rows, inner), BF16),
        scratch=[pltpu.VMEM((rows, TILE), F32)],
        after=after,
    )(normed, w_gate)


def conv_silu(rows_ref, weights, row):
    taps = weights.shape[0]
    ahead = 8
    window = rows_ref[HALO - ahead + row : HALO + row + BLOCK, :]
    total = weights[taps - 1 :, :] * window[ahead:, :]
    for back in range(1, taps):
        total += weights[taps - 1 - back : taps - back, :] * pltpu.roll(window, back, 0)[ahead:, :]
    return silu(total).astype(BF16)


def maps_kernel(place_ref, normed_ref, halo_ref, ws_ref, cs_ref, bc_ref, bt_ref, rows_ref):
    rows = normed_ref.shape[0]
    states = bc_ref.shape[1] // 2
    before = dot(halo_ref[...], ws_ref[...]).astype(BF16).astype(F32)
    rows_ref[:HALO, :] = jnp.where(place_ref[0] >= 1, before, 0.0)
    rows_ref[HALO:, :] = dot(normed_ref[...], ws_ref[...]).astype(BF16).astype(F32)
    weights = cs_ref[...]
    for r in range(0, rows, BLOCK):
        bc_ref[r : r + BLOCK, :] = conv_silu(rows_ref, weights, r)
    bt_ref[...] = bc_ref[:, :states].astype(F32).T.astype(BF16)


def maps_call(place, normed, halo, w_state, conv_state, after=()):
    rows = normed.shape[0]
    both = w_state.shape[1]
    return call(
        maps_kernel,
        "maps",
        vmem=8,
        cost=micros(1.5),
        scalars=(place,),
        in_specs=[VMEM] * 4,
        out_specs=[VMEM] * 2,
        out_shape=[
            jax.ShapeDtypeStruct((rows, both), BF16),
            jax.ShapeDtypeStruct((both // 2, rows), BF16),
        ],
        scratch=[pltpu.VMEM((rows + HALO, both), F32)],
        after=after,
    )(place, normed, halo, w_state, conv_state)


def local_kernel(
    head_size,
    place_ref,
    parity_ref,
    normed_ref,
    halo_ref,
    bt_ref,
    wi_ref,
    small_ref,
    x_ref,
    cum_ref,
    times_ref,
    send_ref,
    mine_ref,
    rows_ref,
    spread_ref,
    scaled_ref,
    left_ref,
    whole_ref,
    payload_ref,
):
    rows = normed_ref.shape[0]
    states = bt_ref.shape[0]
    heads = cum_ref.shape[1]
    taps = SMALL_TAPS
    raw = dot_nt(normed_ref[...], small_ref[SMALL_ROWS:, :].astype(BF16))
    columns = small_ref[:SMALL_ROWS, :CHUNK].T
    raw = raw.T + columns[:heads, taps + 1 : taps + 2]
    step = jnp.maximum(raw, 0.0) + jnp.log1p(jnp.exp(-jnp.abs(raw)))
    logdecay = -step * columns[:heads, taps + 2 : taps + 3]
    high = logdecay.astype(BF16)
    rest = logdecay - high.astype(F32)
    mid = rest.astype(BF16)
    low = (rest - mid.astype(F32)).astype(BF16)
    starts = range(0, rows, CHUNK)
    pieces = [part[:, r : r + CHUNK] for r in starts for part in (high, mid, low)]
    frm = lax.broadcasted_iota(jnp.int32, (CHUNK, CHUNK), 0)
    to = lax.broadcasted_iota(jnp.int32, (CHUNK, CHUNK), 1)
    sums = dot(jnp.concatenate(pieces, axis=0), jnp.where(to >= frm, 1.0, 0.0).astype(BF16))
    run = jnp.zeros((heads, 1), F32)
    cums = []
    for i in range(len(starts)):
        at = 3 * i * heads
        cums.append(sums[at : at + heads] + sums[at + heads : at + 2 * heads] + sums[at + 2 * heads : at + 3 * heads] + run)
        run = cums[-1][:, CHUNK - 1 :]
    cum = jnp.concatenate(cums, axis=1)
    times_ref[:heads, :] = cum
    times_ref[heads:, :] = step
    cum_ref[...] = cum.T
    left_ref[...] = two_rows(step * jnp.exp(run - cum)).T.astype(BF16)
    whole_ref[...] = two_parts(jnp.exp(cum_ref[rows - 1 :, :]))

    inner = x_ref.shape[1]
    half = inner // 2
    tiles = range(inner // TILE)
    onehots = [head_matrix(heads, TILE, head_size, t * (TILE // head_size)) for t in tiles]
    spans = [slice(t * TILE, (t + 1) * TILE) for t in tiles]

    def project(t):
        weights = wi_ref[:, spans[t]]
        before = dot(halo_ref[...], weights).astype(BF16).astype(F32)
        rows_ref[t % 2, :HALO, :] = jnp.where(place_ref[0] >= 1, before, 0.0)
        rows_ref[t % 2, HALO:, :] = dot(normed_ref[...], weights).astype(BF16).astype(F32)
        spread_ref[t % 2] = dot(left_ref[...], onehots[t])

    def combine(t):
        taps_here = small_ref[:taps, spans[t]]
        for r in range(0, rows, BLOCK):
            block = slice(r, r + BLOCK)
            x = conv_silu(rows_ref.at[t % 2], taps_here, r)
            x_ref[block, spans[t]] = x
            scaled_ref[t % 2, block, :] = (x.astype(F32) * spread_ref[t % 2, block, :]).astype(BF16)
        state = dot(bt_ref[...], scaled_ref[t % 2])
        here = slice(t * TILE % half, t * TILE % half + TILE)
        is_mine = jnp.where(parity_ref[0] == t * TILE // half, 1, 0)
        write_payload(payload_ref.at[is_mine], here, state, dot(whole_ref[...], onehots[t]))

    project(0)
    for t in tiles:
        if t + 1 < len(tiles):
            project(t + 1)
        combine(t)
    send_ref[...] = payload_ref[0]
    mine_ref[...] = payload_ref[1]


SMALL_TAPS = 4
SMALL_ROWS = 8


def local_call(tag, place, parity, normed, halo, bt, w_inner, small, after=()):
    rows = normed.shape[0]
    inner = w_inner.shape[1]
    heads = small.shape[0] - SMALL_ROWS
    states = bt.shape[0]
    return call(
        functools.partial(local_kernel, inner // heads),
        "local_" + tag,
        vmem=12,
        cost=micros(5.0),
        scalars=(place, parity),
        in_specs=[VMEM] * 5,
        out_specs=[VMEM] * 5,
        out_shape=[
            jax.ShapeDtypeStruct((rows, inner), BF16),
            jax.ShapeDtypeStruct((rows, heads), F32),
            jax.ShapeDtypeStruct((2 * heads, rows), F32),
            jax.ShapeDtypeStruct((states + EXTRA, inner // 2), BF16),
            jax.ShapeDtypeStruct((states + EXTRA, inner // 2), BF16),
        ],
        scratch=[
            pltpu.VMEM((2, rows + HALO, TILE), F32),
            pltpu.VMEM((2, rows, TILE), F32),
            pltpu.VMEM((2, rows, TILE), BF16),
            pltpu.VMEM((rows, 2 * heads), BF16),
            pltpu.VMEM((1, 2 * heads), BF16),
            pltpu.VMEM((2, states + EXTRA, inner // 2), BF16),
        ],
        after=after,
    )(place, parity, normed, halo, bt, w_inner, small)


def inside_kernel(head_size, x_ref, bc_ref, bt_ref, cum_ref, times_ref, y_ref, state_ref):
    rows, inner = x_ref.shape
    states = bc_ref.shape[1] // 2
    heads = cum_ref.shape[1]
    length = CHUNK
    last = length - 1
    pair = 2 * head_size
    lane = lax.broadcasted_iota(jnp.int32, (length, pair), 1)
    to = lax.broadcasted_iota(jnp.int32, (length, length), 0)
    frm = lax.broadcasted_iota(jnp.int32, (length, length), 1)
    state_ref[...] = jnp.zeros_like(state_ref)

    def chunk(c, before):
        at = slice(c * length, (c + 1) * length)
        bmat = bt_ref[:, at]
        cmat = bc_ref[at, states:]
        scores = jnp.where(to >= frm, dot(cmat, bmat), 0.0)
        cum = cum_ref[at, :]
        cumt = times_ref[:heads, at]
        step = times_ref[heads:, at]
        end = cumt[:, last:]
        since = two_rows(jnp.exp(cumt - before)).T.astype(BF16)
        left = two_rows(step * jnp.exp(end - cumt)).T.astype(BF16)
        for first in range(0, heads, TILE // head_size):
            columns = slice(first * head_size, first * head_size + TILE)
            onehot = head_matrix(heads, TILE, head_size, first)
            since_here = dot(since, onehot)
            state = state_ref[:, columns]
            carried = dot(cmat, state.astype(BF16)) * since_here
            scaled = (x_ref[at, columns].astype(F32) * dot(left, onehot)).astype(BF16)
            state_ref[:, columns] = state * since_here[last:, :] + dot(bmat, scaled)
            for start in range(0, TILE, pair):
                low = first * head_size + start
                weights = []
                for h in (low // head_size, low // head_size + 1):
                    apart = jnp.minimum(cum[:, h : h + 1] - cumt[h : h + 1, :], 0.0)
                    weights.append((jnp.exp(apart) * (scores * step[h : h + 1, :])).astype(BF16))
                mine = x_ref[at, low : low + pair]
                none = jnp.zeros_like(mine)
                stacked = jnp.concatenate(
                    [jnp.where(lane < head_size, mine, none), jnp.where(lane < head_size, none, mine)], axis=0
                )
                inside = dot(jnp.concatenate(weights, axis=1), stacked)
                y_ref[at, low : low + pair] = (inside + carried[:, start : start + pair]).astype(BF16)
        return end

    before = jnp.zeros((heads, 1), F32)
    for c in range(rows // length):
        before = chunk(c, before)


def inside_call(tag, x, bc, bt, cum, times, after=()):
    rows, inner = x.shape
    heads = cum.shape[1]
    both = bc.shape[1]
    return call(
        functools.partial(inside_kernel, inner // heads),
        "inside_" + tag,
        vmem=8,
        cost=micros(3.2),
        in_specs=[VMEM] * 5,
        out_specs=VMEM,
        out_shape=jax.ShapeDtypeStruct((rows, inner), BF16),
        scratch=[pltpu.VMEM((both // 2, inner), F32)],
        after=after,
    )(x, bc, bt, cum, times)


def parts_of(ref, known=None):
    states = ref.shape[0] - EXTRA
    state = ref[:states, :].astype(F32)
    extra = ref[states:, :].astype(F32)
    decay = extra[:1] + extra[1:2]
    if known is None:
        return state, decay
    return jnp.where(known, state, 0.0), jnp.where(known, decay, 0.0)


def write_payload(out_ref, columns, state, decay):
    states = state.shape[0]
    out_ref[:states, columns] = state.astype(BF16)
    decay = jnp.broadcast_to(decay, (EXTRA, decay.shape[1]))
    high = decay.astype(BF16).astype(F32)
    place = lax.broadcasted_iota(jnp.int32, decay.shape, 0)
    out_ref[states:, columns] = jnp.where(place == 0, high, decay - high).astype(BF16)


ALL = slice(None)


def pair_kernel(place_ref, mine_ref, other_ref, out_ref):
    mine, mine_a = parts_of(mine_ref)
    other, other_a = parts_of(other_ref)
    is_first = lax.rem(place_ref[0], 2) == 0
    early = jnp.where(is_first, mine, other)
    late = jnp.where(is_first, other, mine)
    late_a = jnp.where(is_first, other_a, mine_a)
    write_payload(out_ref, ALL, late_a * early + late, mine_a * other_a)


def chain_kernel(reach, place_ref, pair_ref, before_ref, out_ref):
    pair, pair_a = parts_of(pair_ref)
    before, before_a = parts_of(before_ref, place_ref[0] >= reach)
    write_payload(out_ref, ALL, pair_a * before + pair, pair_a * before_a)


def longer_kernel(reach, farther_reach, place_ref, before_ref, farther_ref, out_ref):
    before, before_a = parts_of(before_ref, place_ref[0] >= reach)
    farther, farther_a = parts_of(farther_ref, place_ref[0] >= farther_reach)
    write_payload(out_ref, ALL, before + before_a * farther, before_a * farther_a)


def entry_kernel(reach, farther_reach, place_ref, mine_ref, other_ref, before_ref, farther_ref, keep_ref, send_ref):
    mine, mine_a = parts_of(mine_ref)
    other, other_a = parts_of(other_ref)
    before, before_a = parts_of(before_ref, place_ref[0] >= reach)
    farther, _ = parts_of(farther_ref, place_ref[0] >= farther_reach)
    is_first = lax.rem(place_ref[0], 2) == 0
    entry_first = before + before_a * farther
    early = jnp.where(is_first, mine, other)
    early_a = jnp.where(is_first, mine_a, other_a)
    entry_second = early_a * entry_first + early
    keep_ref[...] = jnp.where(is_first, entry_first, entry_second).astype(BF16)
    send_ref[...] = jnp.where(is_first, entry_second, entry_first).astype(BF16)


def small_call(kernel, name, place, arrays, shapes, after=()):
    return call(
        kernel,
        name,
        vmem=4,
        cost=micros(0.5),
        scalars=(place,),
        in_specs=[VMEM] * len(arrays),
        out_specs=[VMEM] * len(shapes),
        out_shape=[jax.ShapeDtypeStruct(s, BF16) for s in shapes],
        after=after,
    )(place, *arrays)


def onward(value, by):
    count = lax.axis_size("seq")
    pairs = []
    for i in range(count):
        up = (i + by, 0) if i + by < count else (i, 1)
        down = (i - by, 1) if i - by >= 0 else (i, 0)
        pairs += [(2 * i, 2 * up[0] + up[1]), (2 * i + 1, 2 * down[0] + down[1])]
    return lax.ppermute(value, ("seq", "ch"), pairs)


class Chain:
    def __init__(self, tag, place, send, mine):
        self.tag, self.place, self.mine = tag, place, mine
        self.count = lax.axis_size("seq")
        self.swap = [(i, i ^ 1) for i in range(self.count)]
        self.other = lax.ppermute(send, "seq", self.swap)
        self.before = self.farther = None
        self.reach = self.farther_reach = 0
        self.apart = 2

    def pair(self, after):
        (self.pair_state,) = small_call(
            pair_kernel, "pair_" + self.tag, self.place, [self.mine, self.other], [self.mine.shape], after
        )
        self.running = self.pair_state
        self.hop()
        return self.pair_state

    def hop(self):
        if self.apart < self.count:
            self.arrived = onward(self.running, self.apart)

    def middle(self, after):
        while self.apart * 2 < self.count:
            self.take(after)
            (self.running,) = small_call(
                functools.partial(chain_kernel, self.reach),
                "chain_" + self.tag,
                self.place,
                [self.pair_state, self.before],
                [self.mine.shape],
                after,
            )
            self.apart *= 2
            self.hop()
        return self.running

    def take(self, after=()):
        if self.before is None:
            self.before, self.reach = self.arrived, self.apart
        else:
            (self.before,) = small_call(
                functools.partial(longer_kernel, self.reach, self.apart),
                "longer_" + self.tag,
                self.place,
                [self.before, self.arrived],
                [self.mine.shape],
                after,
            )
            self.reach = 0

    def entry(self, after):
        shape = self.mine.shape
        if self.apart < self.count:
            if self.before is None:
                self.before, self.reach = self.arrived, self.apart
                self.farther, self.farther_reach = self.arrived, self.count
            else:
                self.farther, self.farther_reach = self.arrived, self.apart
        else:
            self.before = self.farther = self.mine
            self.reach = self.farther_reach = self.count
        half = (shape[0] - EXTRA, shape[1])
        keep, out = small_call(
            functools.partial(entry_kernel, self.reach, self.farther_reach),
            "entry_" + self.tag,
            self.place,
            [self.mine, self.other, self.before, self.farther],
            [half, half],
            after,
        )
        return keep, lax.ppermute(out, "seq", self.swap)


def gated_part(
    head_size, swap, y_ref, bc_ref, cum_ref, keep_ref, other_ref, gate_ref, small_ref, wo_ref, scaled_ref, tile_ref
):
    rows, inner = y_ref.shape
    states = bc_ref.shape[1] // 2
    heads = cum_ref.shape[1]
    half = inner // 2
    since = two_parts(jnp.exp(cum_ref[...]))
    squares = [0.0] * (rows // BLOCK)
    for low in range(0, inner, TILE):
        columns = slice(low, low + TILE)
        here = slice(low % half, low % half + TILE)
        use_other = swap if low < half else jnp.logical_not(swap)
        entry = jnp.where(use_other, other_ref[:, here], keep_ref[:, here])
        tile_ref[0] = dot(bc_ref[:, states:], entry)
        tile_ref[1] = dot(since, head_matrix(heads, TILE, head_size, low // head_size))
        gain = small_ref[SMALL_TAPS : SMALL_TAPS + 1, columns]
        for i, r in enumerate(range(0, rows, BLOCK)):
            block = slice(r, r + BLOCK)
            gated = y_ref[block, columns].astype(F32) + tile_ref[0, block, :] * tile_ref[1, block, :]
            gated = gated * gate_ref[block, columns].astype(F32)
            squares[i] += jnp.sum(gated * gated, axis=-1, keepdims=True)
            scaled_ref[block, columns] = (gated * gain).astype(BF16)
    return squares


def part_kernel(head_size, parity_ref, *refs):
    *ins, out_ref, sq_ref, scaled_ref, tile_ref = refs
    squares = gated_part(head_size, parity_ref[0] == 1, *ins, scaled_ref, tile_ref)
    for i, square in enumerate(squares):
        sq_ref[i * BLOCK : (i + 1) * BLOCK, :] = jnp.broadcast_to(square, (BLOCK, sq_ref.shape[1]))
    for low in range(0, out_ref.shape[1], TILE):
        out_ref[:, low : low + TILE] = dot(scaled_ref[...], ins[-1][:, low : low + TILE])


def product(back, scaled_ref, weights_ref, part_ref, scale_ref, tile_ref, half_ref, out_ref, first):
    rows, half = out_ref.shape
    for low in range(0, half, TILE):
        columns = slice(first + low, first + low + TILE)
        tile_ref[...] = dot(scaled_ref[...], weights_ref[:, columns])
        for r in range(0, rows, BLOCK):
            block = slice(r, r + BLOCK)
            value = (tile_ref[block, :] + part_ref[block, columns]) * scale_ref[block, :1]
            half_ref[block, low : low + TILE] = value.astype(BF16)

    @pl.when(back == 1)
    def _():
        turn = flip_matrix(TILE)
        for r in range(0, rows, TILE):
            for low in range(0, half, TILE):
                tile = dot(turn, half_ref[r : r + TILE, low : low + TILE]).astype(BF16)
                tile = dot(tile, turn).astype(BF16)
                to_row, to = rows - TILE - r, half - TILE - low
                out_ref[to_row : to_row + TILE, to : to + TILE] = tile

    @pl.when(back != 1)
    def _():
        out_ref[...] = half_ref[...]


def finish_kernel(head_size, full_width, back_ref, parity_ref, *refs):
    *ins, part_ref, psq_ref, send_ref, scaled_ref, scale_ref, tile_ref, half_ref = refs
    squares = gated_part(head_size, parity_ref[0] == 1, *ins, scaled_ref, tile_ref)
    for i, square in enumerate(squares):
        block = slice(i * BLOCK, (i + 1) * BLOCK)
        scale = lax.rsqrt((square + psq_ref[block, :1]) / full_width + EPS)
        scale_ref[block, :] = jnp.broadcast_to(scale, (BLOCK, scale_ref.shape[1]))
    product(back_ref[0], scaled_ref, ins[-1], part_ref, scale_ref, tile_ref.at[0], half_ref, send_ref, send_ref.shape[1])


def own_kernel(back_ref, scaled_ref, weights_ref, part_ref, scale_ref, own_ref, tile_ref, half_ref):
    product(back_ref[0], scaled_ref, weights_ref, part_ref, scale_ref, tile_ref, half_ref, own_ref, 0)


def own_call(back, scaled, w_output, part, scale, after):
    rows, width = part.shape
    half = width // 2
    return call(
        own_kernel,
        "own_half",
        vmem=8,
        cost=micros(0.7),
        scalars=(back,),
        in_specs=[VMEM] * 4,
        out_specs=VMEM,
        out_shape=jax.ShapeDtypeStruct((rows, half), BF16),
        scratch=[pltpu.VMEM((rows, TILE), F32), pltpu.VMEM((rows, half), BF16)],
        after=after,
    )(back, scaled, w_output, part, scale)


def finish_call(back, parity, y, bc, cum, keep, other, gate, small, w_output, full_width=None, partial=None, after=()):
    rows, inner = y.shape
    width = w_output.shape[1]
    half = width // 2
    heads = cum.shape[1]
    arrays = [y, bc, cum, keep, other, gate, small, w_output]
    tiles = pltpu.VMEM((2, rows, TILE), F32)
    if partial is None:
        scratch = [pltpu.VMEM((rows, inner), BF16), tiles]
        scalars = (parity,)
        kernel = functools.partial(part_kernel, inner // heads)
        out_shape = [jax.ShapeDtypeStruct((rows, width), F32), jax.ShapeDtypeStruct((rows, 128), F32)]
    else:
        scalars = (back, parity)
        scratch = [tiles, pltpu.VMEM((rows, half), BF16)]
        kernel = functools.partial(finish_kernel, inner // heads, full_width)
        arrays += list(partial)
        out_shape = [
            jax.ShapeDtypeStruct((rows, half), BF16),
            jax.ShapeDtypeStruct((rows, inner), BF16),
            jax.ShapeDtypeStruct((rows, 128), F32),
        ]
    return call(
        kernel,
        "part" if partial is None else "finish",
        vmem=16,
        cost=micros(3.5),
        scalars=scalars,
        in_specs=[VMEM] * len(arrays),
        out_specs=[VMEM] * len(out_shape),
        out_shape=out_shape,
        scratch=scratch,
        after=after,
    )(*scalars, *arrays)


def total_kernel(mine_ref, theirs_ref, out_hbm, out_ref, sems):
    copies = []
    for i, r in enumerate(range(0, mine_ref.shape[0], CHUNK)):
        for q in range(r, r + CHUNK, BLOCK):
            block = slice(q, q + BLOCK)
            out_ref[block, :] = (mine_ref[block, :].astype(F32) + theirs_ref[block, :].astype(F32)).astype(BF16)
        part = pl.ds(r, CHUNK)
        copies.append(pltpu.make_async_copy(out_ref.at[part, :], out_hbm.at[part, :], sems.at[i]))
        copies[-1].start()
    for copy in copies:
        copy.wait()


def total_call(mine, theirs):
    rows, half = mine.shape
    return call(
        total_kernel,
        "total",
        vmem=4,
        cost=micros(0.8),
        in_specs=[VMEM] * 2,
        out_specs=HBM,
        out_shape=jax.ShapeDtypeStruct((rows, half), BF16),
        scratch=[pltpu.VMEM((rows, half), BF16), pltpu.SemaphoreType.DMA((rows // CHUNK,))],
    )(mine, theirs)


def body(
    tokens,
    hidden,
    embedding,
    w_gate,
    w_inner,
    w_state,
    w_step,
    conv_inner,
    conv_state,
    step_bias,
    decay_rate,
    norm_gain,
    w_output,
):
    swap = [(0, 1), (1, 0)]

    def theirs(a):
        return lax.ppermute(a, "ch", swap)

    core = lax.axis_index("ch").astype(jnp.int32)
    index = lax.axis_index("seq").astype(jnp.int32)
    last = lax.axis_size("seq") - 1
    back = core.reshape(1)
    parity = (index & 1).reshape(1)
    place = (index + core * (last - 2 * index)).reshape(1)
    place, parity, w_inner_3, w_gate_3, w_output_3 = lax.optimization_barrier(
        (place, parity, w_inner, w_gate, w_output)
    )
    w_inner_2 = theirs(w_inner_3)
    normed, tail, small = prepare_call(
        (back, parity, place), hidden, tokens, embedding, conv_inner, norm_gain, step_bias, decay_rate, w_step.T
    )
    halo = onward(tail, 1)
    small_2 = theirs(small)
    w_gate_2 = theirs(w_gate_3)
    w_output_2 = theirs(w_output_3)
    gate_1 = gate_call("own", normed, w_gate)
    bc, bt = maps_call(place, normed, halo, w_state, conv_state, after=[gate_1])
    x_1, cum_1, times_1, send_1, mine_1 = local_call("own", place, parity, normed, halo, bt, w_inner, small)
    chain_1 = Chain("own", place, send_1, mine_1)
    x_2, cum_2, times_2, send_2, mine_2 = local_call(
        "other", place, parity, normed, halo, bt, w_inner_2, small_2, after=[mine_1]
    )
    chain_2 = Chain("other", place, send_2, mine_2)
    gate_2 = gate_call("other", normed, w_gate_2, after=[x_2])
    done = chain_1.pair(after=[gate_2])
    y_1 = inside_call("own", x_1, bc, bt, cum_1, times_1, after=[done])
    done = chain_2.pair(after=[y_1])
    done = chain_1.middle(after=[done])
    done = chain_2.middle(after=[done])
    entry_1 = chain_1.entry(after=[done])
    entry_2 = chain_2.entry(after=[entry_1[0]])
    y_2 = inside_call("other", x_2, bc, bt, cum_2, times_2, after=[entry_2[0]])
    partial = finish_call(
        back, parity, y_1, bc, cum_1, *entry_1, gate_1, small, w_output, after=[y_2]
    )
    full_width = float(w_inner.shape[1] * lax.axis_size("ch"))
    send, scaled, scale = finish_call(
        back, parity, y_2, bc, cum_2, *entry_2, gate_2, small_2, w_output_2, full_width, partial
    )
    arriving = theirs(send)
    mine = own_call(back, scaled, w_output_2, partial[0], scale, after=[send])
    return total_call(mine, arriving)


def solution(mesh):
    return jax.shard_map(
        body,
        mesh=mesh,
        in_specs=(
            P(("win", "seq")),
            P(("win", "seq"), None),
            P(),
            P(None, "ch"),
            P(None, "ch"),
            P(),
            P(None, "ch"),
            P(None, "ch"),
            P(),
            P("ch"),
            P("ch"),
            P("ch"),
            P("ch", None),
        ),
        out_specs=P(("win", "seq"), "ch"),
        check_vma=False,
    )
```

```python
import functools

import jax
import jax.numpy as jnp
from jax import lax
from jax.experimental import pallas as pl
from jax.experimental.pallas import tpu as pltpu
from jax.sharding import PartitionSpec as P

F32 = jnp.float32
BF16 = jnp.bfloat16
EPS = 1e-05
HALO = 16
EXTRA = 16
CHUNK = 128
TILE = 256
BLOCK = 64
MB = 1024 * 1024
VMEM = pl.BlockSpec(memory_space=pltpu.VMEM)
HBM = pl.BlockSpec(memory_space=pltpu.HBM)


def call(
    kernel, name, *, vmem, cost, scalars=(), grid=(), in_specs, out_specs, out_shape, scratch=(), after=()
):
    flops, moved, special = cost
    first = len(scalars) + len(in_specs)

    def body(*refs):
        kernel(*refs[:first], *refs[first + len(after) :])

    run = pl.pallas_call(
        body,
        grid_spec=pltpu.PrefetchScalarGridSpec(
            num_scalar_prefetch=len(scalars),
            grid=grid,
            in_specs=list(in_specs) + [pl.BlockSpec(memory_space=pl.ANY)] * len(after),
            out_specs=out_specs,
            scratch_shapes=scratch,
        ),
        out_shape=out_shape,
        compiler_params=pltpu.CompilerParams(
            vmem_limit_bytes=vmem * MB, dimension_semantics=("arbitrary",) * len(grid)
        ),
        cost_estimate=pl.CostEstimate(flops=flops, bytes_accessed=moved, transcendentals=special),
        name=name,
    )
    return lambda *arrays: run(*arrays, *after)


def micros(us):
    return (int(us * 1.1e9), int(us * 1e6), 0)


def dot(a, b):
    return jnp.dot(a, b, preferred_element_type=F32)


def dot_nt(a, b):
    return lax.dot_general(a, b, (((1,), (1,)), ((), ())), preferred_element_type=F32)


def dot_tn(a, b):
    return lax.dot_general(a, b, (((0,), (0,)), ((), ())), preferred_element_type=F32)


def flip_matrix(size):
    rows = lax.broadcasted_iota(jnp.int32, (size, size), 0)
    columns = lax.broadcasted_iota(jnp.int32, (size, size), 1)
    return jnp.where(rows + columns == size - 1, 1.0, 0.0).astype(BF16)


def flip_both(value):
    rows, width = value.shape
    turned = dot(flip_matrix(rows), value).astype(BF16)
    anti = flip_matrix(TILE)
    count = width // TILE
    blocks = [
        dot(turned[:, (count - 1 - k) * TILE : (count - k) * TILE], anti).astype(BF16)
        for k in range(count)
    ]
    return jnp.concatenate(blocks, axis=1)


def silu(v):
    half = 0.5 * v
    return half + half * jnp.tanh(half)


def two_parts(value):
    high = value.astype(BF16)
    low = (value - high.astype(F32)).astype(BF16)
    return jnp.concatenate([high, low], axis=1)


def two_rows(value):
    high = value.astype(BF16).astype(F32)
    return jnp.concatenate([high, value - high], axis=0)


def head_matrix(heads, width, head_size, first_head):
    source = lax.broadcasted_iota(jnp.int32, (2 * heads, width), 0)
    source = jnp.where(source >= heads, source - heads, source)
    target = lax.broadcasted_iota(jnp.int32, (2 * heads, width), 1) // head_size + first_head
    return jnp.where(source == target, 1.0, 0.0).astype(BF16)


def prepare_kernel(
    back_ref,
    parity_ref,
    place_ref,
    hidden_hbm,
    tokens_hbm,
    emb_hbm,
    conv_hbm,
    gain_hbm,
    bias_hbm,
    rate_hbm,
    step_hbm,
    out_ref,
    tail_ref,
    small_ref,
    hidden_ref,
    tokens_ref,
    emb_ref,
    conv_ref,
    gain_ref,
    bias_ref,
    rate_ref,
    step_ref,
    base_ref,
    normed_ref,
    sems,
):
    rows = hidden_ref.shape[0]
    kinds = emb_ref.shape[0]
    taps, inner = conv_ref.shape
    heads = bias_ref.shape[1]
    count = rows // CHUNK
    back = back_ref[0] == 1
    whole = [
        (tokens_hbm, tokens_ref),
        (emb_hbm, emb_ref),
        (conv_hbm, conv_ref),
        (gain_hbm, gain_ref),
        (bias_hbm, bias_ref),
        (rate_hbm, rate_ref),
        (step_hbm, step_ref),
    ]
    small_copies = [pltpu.make_async_copy(src, dst, sems.at[count + i]) for i, (src, dst) in enumerate(whole)]
    parts = [pl.ds(r * CHUNK, CHUNK) for r in range(count)]
    copies = [
        pltpu.make_async_copy(hidden_hbm.at[part, :], hidden_ref.at[part, :], sems.at[r])
        for r, part in enumerate(parts)
    ]
    for copy in small_copies[:2] + copies + small_copies[2:]:
        copy.start()
    for copy in small_copies[:2]:
        copy.wait()
    kind = lax.broadcasted_iota(jnp.int32, (kinds, rows), 0)
    onehot = jnp.where(kind == tokens_ref[...], 1.0, 0.0).astype(BF16)
    for r in range(count):
        copies[r].wait()
        low, high = r * CHUNK, (r + 1) * CHUNK
        base_ref[...] = dot_tn(onehot[:, low:high], emb_ref[...])
        for q in range(low, high, HALO):
            block = slice(q, q + HALO)
            merged = hidden_ref[block, :].astype(F32) + base_ref[q - low : q - low + HALO, :]
            merged = merged.astype(BF16).astype(F32)
            mean = jnp.mean(merged * merged, axis=-1, keepdims=True)
            normed_ref[q - low : q - low + HALO, :] = (merged * lax.rsqrt(mean + EPS)).astype(BF16)

        @pl.when(back)
        def _():
            out_ref[rows - high : rows - low, :] = flip_both(normed_ref[...])

        @pl.when(jnp.logical_not(back))
        def _():
            out_ref[low:high, :] = normed_ref[...]

    tail_ref[...] = out_ref[rows - HALO :, :]
    for copy in small_copies[2:]:
        copy.wait()
    small_ref[:taps, :] = conv_ref[...]
    small_ref[taps : taps + 1, :] = gain_ref[...]
    small_ref[taps + 1 : SMALL_ROWS, :] = jnp.zeros((SMALL_ROWS - taps - 1, inner), F32)
    small_ref[taps + 1 : taps + 2, :heads] = bias_ref[...]
    small_ref[taps + 2 : taps + 3, :heads] = rate_ref[...]
    small_ref[SMALL_ROWS:, :] = step_ref[...].astype(F32)


def prepare_call(scalars, hidden, tokens, embedding, conv, gain, bias, rate, step):
    rows, width = hidden.shape
    inner = conv.shape[1]
    arrays = [hidden, tokens.reshape(1, -1), embedding, conv]
    arrays += [a.reshape(1, -1) for a in (gain, bias, rate)] + [step]
    return call(
        prepare_kernel,
        "prepare",
        vmem=12,
        cost=micros(2.7),
        scalars=scalars,
        in_specs=[HBM] * len(arrays),
        out_specs=[VMEM] * 3,
        out_shape=[
            jax.ShapeDtypeStruct((rows, width), BF16),
            jax.ShapeDtypeStruct((HALO, width), BF16),
            jax.ShapeDtypeStruct((SMALL_ROWS + step.shape[0], inner), F32),
        ],
        scratch=[pltpu.VMEM(a.shape, a.dtype) for a in arrays]
        + [pltpu.VMEM((CHUNK, width), F32), pltpu.VMEM((CHUNK, width), BF16)]
        + [pltpu.SemaphoreType.DMA((rows // CHUNK + len(arrays) - 1,))],
    )(*scalars, *(pltpu.with_memory_space_constraint(a, pltpu.HBM) for a in arrays))


def gate_kernel(rows_ref, wg_ref, out_ref, gate_ref):
    rows, inner = out_ref.shape
    for low in range(0, inner, TILE):
        columns = slice(low, low + TILE)
        gate_ref[...] = dot(rows_ref[...], wg_ref[:, columns])
        for r in range(0, rows, BLOCK):
            gate = gate_ref[r : r + BLOCK, :].astype(BF16).astype(F32)
            out_ref[r : r + BLOCK, columns] = silu(gate).astype(BF16)


def gate_call(tag, normed, w_gate, after=()):
    rows = normed.shape[0]
    inner = w_gate.shape[1]
    return call(
        gate_kernel,
        "gate_" + tag,
        vmem=8,
        cost=micros(2.4),
        in_specs=[VMEM] * 2,
        out_specs=VMEM,
        out_shape=jax.ShapeDtypeStruct((rows, inner), BF16),
        scratch=[pltpu.VMEM((rows, TILE), F32)],
        after=after,
    )(normed, w_gate)


def conv_silu(rows_ref, weights, row):
    taps = weights.shape[0]
    ahead = 8
    window = rows_ref[HALO - ahead + row : HALO + row + BLOCK, :]
    total = weights[taps - 1 :, :] * window[ahead:, :]
    for back in range(1, taps):
        total += weights[taps - 1 - back : taps - back, :] * pltpu.roll(window, back, 0)[ahead:, :]
    return silu(total).astype(BF16)


def maps_kernel(place_ref, normed_ref, halo_ref, ws_ref, cs_ref, bc_ref, bt_ref, rows_ref):
    rows = normed_ref.shape[0]
    states = bc_ref.shape[1] // 2
    before = dot(halo_ref[...], ws_ref[...]).astype(BF16).astype(F32)
    rows_ref[:HALO, :] = jnp.where(place_ref[0] >= 1, before, 0.0)
    rows_ref[HALO:, :] = dot(normed_ref[...], ws_ref[...]).astype(BF16).astype(F32)
    weights = cs_ref[...]
    for r in range(0, rows, BLOCK):
        bc_ref[r : r + BLOCK, :] = conv_silu(rows_ref, weights, r)
    bt_ref[...] = bc_ref[:, :states].astype(F32).T.astype(BF16)


def maps_call(place, normed, halo, w_state, conv_state, after=()):
    rows = normed.shape[0]
    both = w_state.shape[1]
    return call(
        maps_kernel,
        "maps",
        vmem=8,
        cost=micros(1.5),
        scalars=(place,),
        in_specs=[VMEM] * 4,
        out_specs=[VMEM] * 2,
        out_shape=[
            jax.ShapeDtypeStruct((rows, both), BF16),
            jax.ShapeDtypeStruct((both // 2, rows), BF16),
        ],
        scratch=[pltpu.VMEM((rows + HALO, both), F32)],
        after=after,
    )(place, normed, halo, w_state, conv_state)


def local_kernel(
    head_size,
    place_ref,
    parity_ref,
    normed_ref,
    halo_ref,
    bt_ref,
    wi_ref,
    small_ref,
    x_ref,
    cum_ref,
    times_ref,
    send_ref,
    mine_ref,
    rows_ref,
    spread_ref,
    scaled_ref,
    left_ref,
    whole_ref,
    payload_ref,
):
    rows = normed_ref.shape[0]
    states = bt_ref.shape[0]
    heads = cum_ref.shape[1]
    taps = SMALL_TAPS
    raw = dot_nt(normed_ref[...], small_ref[SMALL_ROWS:, :].astype(BF16))
    columns = small_ref[:SMALL_ROWS, :CHUNK].T
    raw = raw.T + columns[:heads, taps + 1 : taps + 2]
    step = jnp.maximum(raw, 0.0) + jnp.log1p(jnp.exp(-jnp.abs(raw)))
    logdecay = -step * columns[:heads, taps + 2 : taps + 3]
    high = logdecay.astype(BF16)
    rest = logdecay - high.astype(F32)
    mid = rest.astype(BF16)
    low = (rest - mid.astype(F32)).astype(BF16)
    starts = range(0, rows, CHUNK)
    pieces = [part[:, r : r + CHUNK] for r in starts for part in (high, mid, low)]
    frm = lax.broadcasted_iota(jnp.int32, (CHUNK, CHUNK), 0)
    to = lax.broadcasted_iota(jnp.int32, (CHUNK, CHUNK), 1)
    sums = dot(jnp.concatenate(pieces, axis=0), jnp.where(to >= frm, 1.0, 0.0).astype(BF16))
    run = jnp.zeros((heads, 1), F32)
    cums = []
    for i in range(len(starts)):
        at = 3 * i * heads
        cums.append(sums[at : at + heads] + sums[at + heads : at + 2 * heads] + sums[at + 2 * heads : at + 3 * heads] + run)
        run = cums[-1][:, CHUNK - 1 :]
    cum = jnp.concatenate(cums, axis=1)
    times_ref[:heads, :] = cum
    times_ref[heads:, :] = step
    cum_ref[...] = cum.T
    left_ref[...] = two_rows(step * jnp.exp(run - cum)).T.astype(BF16)
    whole_ref[...] = two_parts(jnp.exp(cum_ref[rows - 1 :, :]))

    inner = x_ref.shape[1]
    half = inner // 2
    tiles = range(inner // TILE)
    onehots = [head_matrix(heads, TILE, head_size, t * (TILE // head_size)) for t in tiles]
    spans = [slice(t * TILE, (t + 1) * TILE) for t in tiles]

    def project(t):
        weights = wi_ref[:, spans[t]]
        before = dot(halo_ref[...], weights).astype(BF16).astype(F32)
        rows_ref[t % 2, :HALO, :] = jnp.where(place_ref[0] >= 1, before, 0.0)
        rows_ref[t % 2, HALO:, :] = dot(normed_ref[...], weights).astype(BF16).astype(F32)
        spread_ref[t % 2] = dot(left_ref[...], onehots[t])

    def combine(t):
        taps_here = small_ref[:taps, spans[t]]
        for r in range(0, rows, BLOCK):
            block = slice(r, r + BLOCK)
            x = conv_silu(rows_ref.at[t % 2], taps_here, r)
            x_ref[block, spans[t]] = x
            scaled_ref[t % 2, block, :] = (x.astype(F32) * spread_ref[t % 2, block, :]).astype(BF16)
        state = dot(bt_ref[...], scaled_ref[t % 2])
        here = slice(t * TILE % half, t * TILE % half + TILE)
        is_mine = jnp.where(parity_ref[0] == t * TILE // half, 1, 0)
        write_payload(payload_ref.at[is_mine], here, state, dot(whole_ref[...], onehots[t]))

    project(0)
    for t in tiles:
        if t + 1 < len(tiles):
            project(t + 1)
        combine(t)
    send_ref[...] = payload_ref[0]
    mine_ref[...] = payload_ref[1]


SMALL_TAPS = 4
SMALL_ROWS = 8


def local_call(tag, place, parity, normed, halo, bt, w_inner, small, after=()):
    rows = normed.shape[0]
    inner = w_inner.shape[1]
    heads = small.shape[0] - SMALL_ROWS
    states = bt.shape[0]
    return call(
        functools.partial(local_kernel, inner // heads),
        "local_" + tag,
        vmem=12,
        cost=micros(5.0),
        scalars=(place, parity),
        in_specs=[VMEM] * 5,
        out_specs=[VMEM] * 5,
        out_shape=[
            jax.ShapeDtypeStruct((rows, inner), BF16),
            jax.ShapeDtypeStruct((rows, heads), F32),
            jax.ShapeDtypeStruct((2 * heads, rows), F32),
            jax.ShapeDtypeStruct((states + EXTRA, inner // 2), BF16),
            jax.ShapeDtypeStruct((states + EXTRA, inner // 2), BF16),
        ],
        scratch=[
            pltpu.VMEM((2, rows + HALO, TILE), F32),
            pltpu.VMEM((2, rows, TILE), F32),
            pltpu.VMEM((2, rows, TILE), BF16),
            pltpu.VMEM((rows, 2 * heads), BF16),
            pltpu.VMEM((1, 2 * heads), BF16),
            pltpu.VMEM((2, states + EXTRA, inner // 2), BF16),
        ],
        after=after,
    )(place, parity, normed, halo, bt, w_inner, small)


def inside_kernel(head_size, head, x_ref, bc_ref, bt_ref, cum_ref, times_ref, y_ref, state_ref):
    rows, width = y_ref.shape
    states = bc_ref.shape[1] // 2
    heads = cum_ref.shape[1]
    length = CHUNK
    last = length - 1
    pair = 2 * head_size
    lane = lax.broadcasted_iota(jnp.int32, (length, pair), 1)
    to = lax.broadcasted_iota(jnp.int32, (length, length), 0)
    frm = lax.broadcasted_iota(jnp.int32, (length, length), 1)
    state_ref[...] = jnp.zeros_like(state_ref)

    def chunk(c, before):
        at = slice(c * length, (c + 1) * length)
        bmat = bt_ref[:, at]
        cmat = bc_ref[at, states:]
        scores = jnp.where(to >= frm, dot(cmat, bmat), 0.0)
        cum = cum_ref[at, :]
        cumt = times_ref[:heads, at]
        step = times_ref[heads:, at]
        end = cumt[:, last:]
        since = two_rows(jnp.exp(cumt - before)).T.astype(BF16)
        left = two_rows(step * jnp.exp(end - cumt)).T.astype(BF16)
        for offset in range(0, width, TILE):
            first = head + offset // head_size
            columns = slice(first * head_size, first * head_size + TILE)
            here = slice(offset, offset + TILE)
            onehot = head_matrix(heads, TILE, head_size, first)
            since_here = dot(since, onehot)
            state = state_ref[:, here]
            carried = dot(cmat, state.astype(BF16)) * since_here
            scaled = (x_ref[at, columns].astype(F32) * dot(left, onehot)).astype(BF16)
            state_ref[:, here] = state * since_here[last:, :] + dot(bmat, scaled)
            for start in range(0, TILE, pair):
                low = first * head_size + start
                weights = []
                for h in (low // head_size, low // head_size + 1):
                    apart = jnp.minimum(cum[:, h : h + 1] - cumt[h : h + 1, :], 0.0)
                    weights.append((jnp.exp(apart) * (scores * step[h : h + 1, :])).astype(BF16))
                mine = x_ref[at, low : low + pair]
                none = jnp.zeros_like(mine)
                stacked = jnp.concatenate(
                    [jnp.where(lane < head_size, mine, none), jnp.where(lane < head_size, none, mine)], axis=0
                )
                inside = dot(jnp.concatenate(weights, axis=1), stacked)
                y_ref[at, offset + start : offset + start + pair] = (
                    inside + carried[:, start : start + pair]
                ).astype(BF16)
        return end

    before = jnp.zeros((heads, 1), F32)
    for c in range(rows // length):
        before = chunk(c, before)


def inside_call(tag, x, bc, bt, cum, times, after=(), part=0, parts=1):
    rows, inner = x.shape
    heads = cum.shape[1]
    both = bc.shape[1]
    width = inner // parts
    return call(
        functools.partial(inside_kernel, inner // heads, part * heads // parts),
        "inside_" + tag,
        vmem=8,
        cost=micros(3.2 / parts),
        in_specs=[VMEM] * 5,
        out_specs=VMEM,
        out_shape=jax.ShapeDtypeStruct((rows, width), BF16),
        scratch=[pltpu.VMEM((both // 2, width), F32)],
        after=after,
    )(x, bc, bt, cum, times)


def mark_kernel(rows_ref, out_ref):
    out_ref[...] = rows_ref[: out_ref.shape[0], : out_ref.shape[1]]


def mark_call(value, after):
    return call(
        mark_kernel,
        "mark",
        vmem=4,
        cost=micros(2.4),
        in_specs=[VMEM],
        out_specs=VMEM,
        out_shape=jax.ShapeDtypeStruct((HALO, 128), value.dtype),
        after=after,
    )(value)


def parts_of(ref, known=None):
    states = ref.shape[0] - EXTRA
    state = ref[:states, :].astype(F32)
    extra = ref[states:, :].astype(F32)
    decay = extra[:1] + extra[1:2]
    if known is None:
        return state, decay
    return jnp.where(known, state, 0.0), jnp.where(known, decay, 0.0)


def write_payload(out_ref, columns, state, decay):
    states = state.shape[0]
    out_ref[:states, columns] = state.astype(BF16)
    decay = jnp.broadcast_to(decay, (EXTRA, decay.shape[1]))
    high = decay.astype(BF16).astype(F32)
    place = lax.broadcasted_iota(jnp.int32, decay.shape, 0)
    out_ref[states:, columns] = jnp.where(place == 0, high, decay - high).astype(BF16)


ALL = slice(None)


def pair_kernel(place_ref, mine_ref, other_ref, out_ref):
    mine, mine_a = parts_of(mine_ref)
    other, other_a = parts_of(other_ref)
    is_first = lax.rem(place_ref[0], 2) == 0
    early = jnp.where(is_first, mine, other)
    late = jnp.where(is_first, other, mine)
    late_a = jnp.where(is_first, other_a, mine_a)
    write_payload(out_ref, ALL, late_a * early + late, mine_a * other_a)


def chain_kernel(reach, place_ref, pair_ref, before_ref, out_ref):
    pair, pair_a = parts_of(pair_ref)
    before, before_a = parts_of(before_ref, place_ref[0] >= reach)
    write_payload(out_ref, ALL, pair_a * before + pair, pair_a * before_a)


def longer_kernel(reach, farther_reach, place_ref, before_ref, farther_ref, out_ref):
    before, before_a = parts_of(before_ref, place_ref[0] >= reach)
    farther, farther_a = parts_of(farther_ref, place_ref[0] >= farther_reach)
    write_payload(out_ref, ALL, before + before_a * farther, before_a * farther_a)


def entry_kernel(reach, farther_reach, place_ref, mine_ref, other_ref, before_ref, farther_ref, keep_ref, send_ref):
    mine, mine_a = parts_of(mine_ref)
    other, other_a = parts_of(other_ref)
    before, before_a = parts_of(before_ref, place_ref[0] >= reach)
    farther, _ = parts_of(farther_ref, place_ref[0] >= farther_reach)
    is_first = lax.rem(place_ref[0], 2) == 0
    entry_first = before + before_a * farther
    early = jnp.where(is_first, mine, other)
    early_a = jnp.where(is_first, mine_a, other_a)
    entry_second = early_a * entry_first + early
    keep_ref[...] = jnp.where(is_first, entry_first, entry_second).astype(BF16)
    send_ref[...] = jnp.where(is_first, entry_second, entry_first).astype(BF16)


def small_call(kernel, name, place, arrays, shapes, after=()):
    return call(
        kernel,
        name,
        vmem=4,
        cost=micros(0.5),
        scalars=(place,),
        in_specs=[VMEM] * len(arrays),
        out_specs=[VMEM] * len(shapes),
        out_shape=[jax.ShapeDtypeStruct(s, BF16) for s in shapes],
        after=after,
    )(place, *arrays)


def onward(value, by):
    count = lax.axis_size("seq")
    pairs = []
    for i in range(count):
        up = (i + by, 0) if i + by < count else (i, 1)
        down = (i - by, 1) if i - by >= 0 else (i, 0)
        pairs += [(2 * i, 2 * up[0] + up[1]), (2 * i + 1, 2 * down[0] + down[1])]
    return lax.ppermute(value, ("seq", "ch"), pairs)


class Chain:
    def __init__(self, tag, place, send, mine):
        self.tag, self.place, self.mine = tag, place, mine
        self.count = lax.axis_size("seq")
        self.swap = [(i, i ^ 1) for i in range(self.count)]
        self.other = lax.ppermute(send, "seq", self.swap)
        self.before = self.farther = None
        self.reach = self.farther_reach = 0
        self.apart = 2

    def pair(self, after):
        (self.pair_state,) = small_call(
            pair_kernel, "pair_" + self.tag, self.place, [self.mine, self.other], [self.mine.shape], after
        )
        self.running = self.pair_state
        self.hop()
        return self.pair_state

    def hop(self):
        if self.apart < self.count:
            self.arrived = onward(self.running, self.apart)

    def middle(self, after):
        while self.apart * 2 < self.count:
            self.take(after)
            (self.running,) = small_call(
                functools.partial(chain_kernel, self.reach),
                "chain_" + self.tag,
                self.place,
                [self.pair_state, self.before],
                [self.mine.shape],
                after,
            )
            self.apart *= 2
            self.hop()
        return self.running

    def take(self, after=()):
        if self.before is None:
            self.before, self.reach = self.arrived, self.apart
        else:
            (self.before,) = small_call(
                functools.partial(longer_kernel, self.reach, self.apart),
                "longer_" + self.tag,
                self.place,
                [self.before, self.arrived],
                [self.mine.shape],
                after,
            )
            self.reach = 0

    def entry(self, after):
        shape = self.mine.shape
        if self.apart < self.count:
            if self.before is None:
                self.before, self.reach = self.arrived, self.apart
                self.farther, self.farther_reach = self.arrived, self.count
            else:
                self.farther, self.farther_reach = self.arrived, self.apart
        else:
            self.before = self.farther = self.mine
            self.reach = self.farther_reach = self.count
        half = (shape[0] - EXTRA, shape[1])
        keep, out = small_call(
            functools.partial(entry_kernel, self.reach, self.farther_reach),
            "entry_" + self.tag,
            self.place,
            [self.mine, self.other, self.before, self.farther],
            [half, half],
            after,
        )
        return keep, lax.ppermute(out, "seq", self.swap)


def gated_part(
    head_size, swap, y_refs, bc_ref, cum_ref, keep_ref, other_ref, gate_ref, small_ref, wo_ref, scaled_ref, tile_ref
):
    rows, share = y_refs[0].shape
    inner = share * len(y_refs)
    states = bc_ref.shape[1] // 2
    heads = cum_ref.shape[1]
    half = inner // 2
    since = two_parts(jnp.exp(cum_ref[...]))
    squares = [0.0] * (rows // BLOCK)
    for low in range(0, inner, TILE):
        columns = slice(low, low + TILE)
        y_ref = y_refs[low // share]
        of_share = slice(low % share, low % share + TILE)
        here = slice(low % half, low % half + TILE)
        use_other = swap if low < half else jnp.logical_not(swap)
        entry = jnp.where(use_other, other_ref[:, here], keep_ref[:, here])
        tile_ref[0] = dot(bc_ref[:, states:], entry)
        tile_ref[1] = dot(since, head_matrix(heads, TILE, head_size, low // head_size))
        gain = small_ref[SMALL_TAPS : SMALL_TAPS + 1, columns]
        for i, r in enumerate(range(0, rows, BLOCK)):
            block = slice(r, r + BLOCK)
            gated = y_ref[block, of_share].astype(F32) + tile_ref[0, block, :] * tile_ref[1, block, :]
            gated = gated * gate_ref[block, columns].astype(F32)
            squares[i] += jnp.sum(gated * gated, axis=-1, keepdims=True)
            scaled_ref[block, columns] = (gated * gain).astype(BF16)
    return squares


def part_kernel(head_size, shares, parity_ref, *refs):
    *ins, out_ref, sq_ref, scaled_ref, tile_ref = refs
    squares = gated_part(head_size, parity_ref[0] == 1, ins[:shares], *ins[shares:], scaled_ref, tile_ref)
    for i, square in enumerate(squares):
        sq_ref[i * BLOCK : (i + 1) * BLOCK, :] = jnp.broadcast_to(square, (BLOCK, sq_ref.shape[1]))
    for low in range(0, out_ref.shape[1], TILE):
        out_ref[:, low : low + TILE] = dot(scaled_ref[...], ins[-1][:, low : low + TILE])


def product(back, scaled_ref, weights_ref, part_ref, scale_ref, tile_ref, half_ref, out_ref, first):
    rows, half = out_ref.shape
    for low in range(0, half, TILE):
        columns = slice(first + low, first + low + TILE)
        tile_ref[...] = dot(scaled_ref[...], weights_ref[:, columns])
        for r in range(0, rows, BLOCK):
            block = slice(r, r + BLOCK)
            value = (tile_ref[block, :] + part_ref[block, columns]) * scale_ref[block, :1]
            half_ref[block, low : low + TILE] = value.astype(BF16)

    @pl.when(back == 1)
    def _():
        turn = flip_matrix(TILE)
        for r in range(0, rows, TILE):
            for low in range(0, half, TILE):
                tile = dot(turn, half_ref[r : r + TILE, low : low + TILE]).astype(BF16)
                tile = dot(tile, turn).astype(BF16)
                to_row, to = rows - TILE - r, half - TILE - low
                out_ref[to_row : to_row + TILE, to : to + TILE] = tile

    @pl.when(back != 1)
    def _():
        out_ref[...] = half_ref[...]


def finish_kernel(head_size, shares, full_width, back_ref, parity_ref, *refs):
    *ins, part_ref, psq_ref, send_ref, scaled_ref, scale_ref, tile_ref, half_ref = refs
    squares = gated_part(head_size, parity_ref[0] == 1, ins[:shares], *ins[shares:], scaled_ref, tile_ref)
    for i, square in enumerate(squares):
        block = slice(i * BLOCK, (i + 1) * BLOCK)
        scale = lax.rsqrt((square + psq_ref[block, :1]) / full_width + EPS)
        scale_ref[block, :] = jnp.broadcast_to(scale, (BLOCK, scale_ref.shape[1]))
    product(back_ref[0], scaled_ref, ins[-1], part_ref, scale_ref, tile_ref.at[0], half_ref, send_ref, send_ref.shape[1])


def own_kernel(back_ref, scaled_ref, weights_ref, part_ref, scale_ref, own_ref, tile_ref, half_ref):
    product(back_ref[0], scaled_ref, weights_ref, part_ref, scale_ref, tile_ref, half_ref, own_ref, 0)


def own_call(back, scaled, w_output, part, scale, after):
    rows, width = part.shape
    half = width // 2
    return call(
        own_kernel,
        "own_half",
        vmem=8,
        cost=micros(0.7),
        scalars=(back,),
        in_specs=[VMEM] * 4,
        out_specs=VMEM,
        out_shape=jax.ShapeDtypeStruct((rows, half), BF16),
        scratch=[pltpu.VMEM((rows, TILE), F32), pltpu.VMEM((rows, half), BF16)],
        after=after,
    )(back, scaled, w_output, part, scale)


def finish_call(back, parity, ys, bc, cum, keep, other, gate, small, w_output, full_width=None, partial=None, after=()):
    rows = ys[0].shape[0]
    inner = ys[0].shape[1] * len(ys)
    width = w_output.shape[1]
    half = width // 2
    heads = cum.shape[1]
    arrays = [*ys, bc, cum, keep, other, gate, small, w_output]
    tiles = pltpu.VMEM((2, rows, TILE), F32)
    if partial is None:
        scratch = [pltpu.VMEM((rows, inner), BF16), tiles]
        scalars = (parity,)
        kernel = functools.partial(part_kernel, inner // heads, len(ys))
        out_shape = [jax.ShapeDtypeStruct((rows, width), F32), jax.ShapeDtypeStruct((rows, 128), F32)]
    else:
        scalars = (back, parity)
        scratch = [tiles, pltpu.VMEM((rows, half), BF16)]
        kernel = functools.partial(finish_kernel, inner // heads, len(ys), full_width)
        arrays += list(partial)
        out_shape = [
            jax.ShapeDtypeStruct((rows, half), BF16),
            jax.ShapeDtypeStruct((rows, inner), BF16),
            jax.ShapeDtypeStruct((rows, 128), F32),
        ]
    return call(
        kernel,
        "part" if partial is None else "finish",
        vmem=16,
        cost=micros(3.5),
        scalars=scalars,
        in_specs=[VMEM] * len(arrays),
        out_specs=[VMEM] * len(out_shape),
        out_shape=out_shape,
        scratch=scratch,
        after=after,
    )(*scalars, *arrays)


def total_kernel(mine_ref, theirs_ref, out_hbm, out_ref, sems):
    copies = []
    for i, r in enumerate(range(0, mine_ref.shape[0], CHUNK)):
        for q in range(r, r + CHUNK, BLOCK):
            block = slice(q, q + BLOCK)
            out_ref[block, :] = (mine_ref[block, :].astype(F32) + theirs_ref[block, :].astype(F32)).astype(BF16)
        part = pl.ds(r, CHUNK)
        copies.append(pltpu.make_async_copy(out_ref.at[part, :], out_hbm.at[part, :], sems.at[i]))
        copies[-1].start()
    for copy in copies:
        copy.wait()


def total_call(mine, theirs):
    rows, half = mine.shape
    return call(
        total_kernel,
        "total",
        vmem=4,
        cost=micros(0.8),
        in_specs=[VMEM] * 2,
        out_specs=HBM,
        out_shape=jax.ShapeDtypeStruct((rows, half), BF16),
        scratch=[pltpu.VMEM((rows, half), BF16), pltpu.SemaphoreType.DMA((rows // CHUNK,))],
    )(mine, theirs)


def body(
    tokens,
    hidden,
    embedding,
    w_gate,
    w_inner,
    w_state,
    w_step,
    conv_inner,
    conv_state,
    step_bias,
    decay_rate,
    norm_gain,
    w_output,
):
    swap = [(0, 1), (1, 0)]

    def theirs(a):
        return lax.ppermute(a, "ch", swap)

    core = lax.axis_index("ch").astype(jnp.int32)
    index = lax.axis_index("seq").astype(jnp.int32)
    last = lax.axis_size("seq") - 1
    back = core.reshape(1)
    parity = (index & 1).reshape(1)
    place = (index + core * (last - 2 * index)).reshape(1)
    place, parity, w_inner_3, w_gate_3, w_output_3 = lax.optimization_barrier(
        (place, parity, w_inner, w_gate, w_output)
    )
    w_inner_2 = theirs(w_inner_3)
    normed, tail, small = prepare_call(
        (back, parity, place), hidden, tokens, embedding, conv_inner, norm_gain, step_bias, decay_rate, w_step.T
    )
    halo = onward(tail, 1)
    small_2 = theirs(small)
    w_gate_2 = theirs(w_gate_3)
    w_output_2 = theirs(w_output_3)
    gate_1 = gate_call("own", normed, w_gate)
    bc, bt = maps_call(place, normed, halo, w_state, conv_state, after=[gate_1])
    x_1, cum_1, times_1, send_1, mine_1 = local_call("own", place, parity, normed, halo, bt, w_inner, small)
    chain_1 = Chain("own", place, send_1, mine_1)
    x_2, cum_2, times_2, send_2, mine_2 = local_call(
        "other", place, parity, normed, halo, bt, w_inner_2, small_2, after=[mine_1]
    )
    chain_2 = Chain("other", place, send_2, mine_2)
    done = mark_call(normed, after=[x_2])
    done = chain_1.pair(after=[done])
    y_1 = inside_call("own", x_1, bc, bt, cum_1, times_1, after=[done])
    done = chain_2.pair(after=[y_1])
    done = chain_1.middle(after=[done])
    gate_2 = gate_call("other", normed, w_gate_2, after=[done])
    done = chain_2.middle(after=[gate_2])
    entry_1 = chain_1.entry(after=[done])
    scan_2 = ("other", x_2, bc, bt, cum_2, times_2)
    y_2 = [inside_call(*scan_2, after=[entry_1[0]], part=0, parts=2)]
    entry_2 = chain_2.entry(after=y_2)
    y_2.append(inside_call(*scan_2, after=[entry_2[0]], part=1, parts=2))
    partial = finish_call(
        back, parity, [y_1], bc, cum_1, *entry_1, gate_1, small, w_output, after=y_2
    )
    full_width = float(w_inner.shape[1] * lax.axis_size("ch"))
    send, scaled, scale = finish_call(
        back, parity, y_2, bc, cum_2, *entry_2, gate_2, small_2, w_output_2, full_width, partial
    )
    arriving = theirs(send)
    mine = own_call(back, scaled, w_output_2, partial[0], scale, after=[send])
    return total_call(mine, arriving)


def solution(mesh):
    return jax.shard_map(
        body,
        mesh=mesh,
        in_specs=(
            P(("win", "seq")),
            P(("win", "seq"), None),
            P(),
            P(None, "ch"),
            P(None, "ch"),
            P(),
            P(None, "ch"),
            P(None, "ch"),
            P(),
            P("ch"),
            P("ch"),
            P("ch"),
            P("ch", None),
        ),
        out_specs=P(("win", "seq"), "ch"),
        check_vma=False,
    )
```

```python
import functools

import jax
import jax.numpy as jnp
from jax import lax
from jax.experimental import pallas as pl
from jax.experimental.pallas import tpu as pltpu
from jax.sharding import PartitionSpec as P

F32 = jnp.float32
BF16 = jnp.bfloat16
EPS = 1e-05
HALO = 16
EXTRA = 16
CHUNK = 128
TILE = 256
BLOCK = 64
MB = 1024 * 1024
VMEM = pl.BlockSpec(memory_space=pltpu.VMEM)
HBM = pl.BlockSpec(memory_space=pltpu.HBM)


def call(
    kernel, name, *, vmem, cost, scalars=(), grid=(), in_specs, out_specs, out_shape, scratch=(), after=()
):
    flops, moved, special = cost
    first = len(scalars) + len(in_specs)

    def body(*refs):
        kernel(*refs[:first], *refs[first + len(after) :])

    run = pl.pallas_call(
        body,
        grid_spec=pltpu.PrefetchScalarGridSpec(
            num_scalar_prefetch=len(scalars),
            grid=grid,
            in_specs=list(in_specs) + [pl.BlockSpec(memory_space=pl.ANY)] * len(after),
            out_specs=out_specs,
            scratch_shapes=scratch,
        ),
        out_shape=out_shape,
        compiler_params=pltpu.CompilerParams(
            vmem_limit_bytes=vmem * MB, dimension_semantics=("arbitrary",) * len(grid)
        ),
        cost_estimate=pl.CostEstimate(flops=flops, bytes_accessed=moved, transcendentals=special),
        name=name,
    )
    return lambda *arrays: run(*arrays, *after)


def micros(us):
    return (int(us * 1.1e9), int(us * 1e6), 0)


def dot(a, b):
    return jnp.dot(a, b, preferred_element_type=F32)


def dot_nt(a, b):
    return lax.dot_general(a, b, (((1,), (1,)), ((), ())), preferred_element_type=F32)


def dot_tn(a, b):
    return lax.dot_general(a, b, (((0,), (0,)), ((), ())), preferred_element_type=F32)


def flip_matrix(size):
    rows = lax.broadcasted_iota(jnp.int32, (size, size), 0)
    columns = lax.broadcasted_iota(jnp.int32, (size, size), 1)
    return jnp.where(rows + columns == size - 1, 1.0, 0.0).astype(BF16)


def flip_both(value):
    rows, width = value.shape
    turned = dot(flip_matrix(rows), value).astype(BF16)
    anti = flip_matrix(TILE)
    count = width // TILE
    blocks = [
        dot(turned[:, (count - 1 - k) * TILE : (count - k) * TILE], anti).astype(BF16)
        for k in range(count)
    ]
    return jnp.concatenate(blocks, axis=1)


def silu(v):
    half = 0.5 * v
    return half + half * jnp.tanh(half)


def two_parts(value):
    high = value.astype(BF16)
    low = (value - high.astype(F32)).astype(BF16)
    return jnp.concatenate([high, low], axis=1)


def two_rows(value):
    high = value.astype(BF16).astype(F32)
    return jnp.concatenate([high, value - high], axis=0)


def head_matrix(heads, width, head_size, first_head):
    source = lax.broadcasted_iota(jnp.int32, (2 * heads, width), 0)
    source = jnp.where(source >= heads, source - heads, source)
    target = lax.broadcasted_iota(jnp.int32, (2 * heads, width), 1) // head_size + first_head
    return jnp.where(source == target, 1.0, 0.0).astype(BF16)


def prepare_kernel(
    back_ref,
    parity_ref,
    place_ref,
    hidden_hbm,
    tokens_hbm,
    emb_hbm,
    conv_hbm,
    gain_hbm,
    bias_hbm,
    rate_hbm,
    step_hbm,
    out_ref,
    tail_ref,
    small_ref,
    hidden_ref,
    tokens_ref,
    emb_ref,
    conv_ref,
    gain_ref,
    bias_ref,
    rate_ref,
    step_ref,
    base_ref,
    normed_ref,
    sems,
):
    rows = hidden_ref.shape[0]
    kinds = emb_ref.shape[0]
    taps, inner = conv_ref.shape
    heads = bias_ref.shape[1]
    count = rows // CHUNK
    back = back_ref[0] == 1
    whole = [
        (tokens_hbm, tokens_ref),
        (emb_hbm, emb_ref),
        (conv_hbm, conv_ref),
        (gain_hbm, gain_ref),
        (bias_hbm, bias_ref),
        (rate_hbm, rate_ref),
        (step_hbm, step_ref),
    ]
    small_copies = [pltpu.make_async_copy(src, dst, sems.at[count + i]) for i, (src, dst) in enumerate(whole)]
    parts = [pl.ds(r * CHUNK, CHUNK) for r in range(count)]
    copies = [
        pltpu.make_async_copy(hidden_hbm.at[part, :], hidden_ref.at[part, :], sems.at[r])
        for r, part in enumerate(parts)
    ]
    for copy in small_copies[:2] + copies + small_copies[2:]:
        copy.start()
    for copy in small_copies[:2]:
        copy.wait()
    kind = lax.broadcasted_iota(jnp.int32, (kinds, rows), 0)
    onehot = jnp.where(kind == tokens_ref[...], 1.0, 0.0).astype(BF16)
    for r in range(count):
        copies[r].wait()
        low, high = r * CHUNK, (r + 1) * CHUNK
        base_ref[...] = dot_tn(onehot[:, low:high], emb_ref[...])
        for q in range(low, high, HALO):
            block = slice(q, q + HALO)
            merged = hidden_ref[block, :].astype(F32) + base_ref[q - low : q - low + HALO, :]
            merged = merged.astype(BF16).astype(F32)
            mean = jnp.mean(merged * merged, axis=-1, keepdims=True)
            normed_ref[q - low : q - low + HALO, :] = (merged * lax.rsqrt(mean + EPS)).astype(BF16)

        @pl.when(back)
        def _():
            out_ref[rows - high : rows - low, :] = flip_both(normed_ref[...])

        @pl.when(jnp.logical_not(back))
        def _():
            out_ref[low:high, :] = normed_ref[...]

    tail_ref[...] = out_ref[rows - HALO :, :]
    for copy in small_copies[2:]:
        copy.wait()
    small_ref[:taps, :] = conv_ref[...]
    small_ref[taps : taps + 1, :] = gain_ref[...]
    small_ref[taps + 1 : SMALL_ROWS, :] = jnp.zeros((SMALL_ROWS - taps - 1, inner), F32)
    small_ref[taps + 1 : taps + 2, :heads] = bias_ref[...]
    small_ref[taps + 2 : taps + 3, :heads] = rate_ref[...]
    small_ref[SMALL_ROWS:, :] = step_ref[...].astype(F32)


def prepare_call(scalars, hidden, tokens, embedding, conv, gain, bias, rate, step):
    rows, width = hidden.shape
    inner = conv.shape[1]
    arrays = [hidden, tokens.reshape(1, -1), embedding, conv]
    arrays += [a.reshape(1, -1) for a in (gain, bias, rate)] + [step]
    return call(
        prepare_kernel,
        "prepare",
        vmem=12,
        cost=micros(2.7),
        scalars=scalars,
        in_specs=[HBM] * len(arrays),
        out_specs=[VMEM] * 3,
        out_shape=[
            jax.ShapeDtypeStruct((rows, width), BF16),
            jax.ShapeDtypeStruct((HALO, width), BF16),
            jax.ShapeDtypeStruct((SMALL_ROWS + step.shape[0], inner), F32),
        ],
        scratch=[pltpu.VMEM(a.shape, a.dtype) for a in arrays]
        + [pltpu.VMEM((CHUNK, width), F32), pltpu.VMEM((CHUNK, width), BF16)]
        + [pltpu.SemaphoreType.DMA((rows // CHUNK + len(arrays) - 1,))],
    )(*scalars, *(pltpu.with_memory_space_constraint(a, pltpu.HBM) for a in arrays))


def gate_kernel(rows_ref, wg_ref, out_ref, gate_ref):
    rows, inner = out_ref.shape
    for low in range(0, inner, TILE):
        columns = slice(low, low + TILE)
        gate_ref[...] = dot(rows_ref[...], wg_ref[:, columns])
        for r in range(0, rows, BLOCK):
            gate = gate_ref[r : r + BLOCK, :].astype(BF16).astype(F32)
            out_ref[r : r + BLOCK, columns] = silu(gate).astype(BF16)


def gate_call(tag, normed, w_gate, after=()):
    rows = normed.shape[0]
    inner = w_gate.shape[1]
    return call(
        gate_kernel,
        "gate_" + tag,
        vmem=8,
        cost=micros(2.4),
        in_specs=[VMEM] * 2,
        out_specs=VMEM,
        out_shape=jax.ShapeDtypeStruct((rows, inner), BF16),
        scratch=[pltpu.VMEM((rows, TILE), F32)],
        after=after,
    )(normed, w_gate)


def conv_silu(rows_ref, weights, row):
    taps = weights.shape[0]
    ahead = 8
    window = rows_ref[HALO - ahead + row : HALO + row + BLOCK, :]
    total = weights[taps - 1 :, :] * window[ahead:, :]
    for back in range(1, taps):
        total += weights[taps - 1 - back : taps - back, :] * pltpu.roll(window, back, 0)[ahead:, :]
    return silu(total).astype(BF16)


def maps_kernel(place_ref, normed_ref, halo_ref, ws_ref, cs_ref, bc_ref, bt_ref, rows_ref):
    rows = normed_ref.shape[0]
    states = bc_ref.shape[1] // 2
    before = dot(halo_ref[...], ws_ref[...]).astype(BF16).astype(F32)
    rows_ref[:HALO, :] = jnp.where(place_ref[0] >= 1, before, 0.0)
    rows_ref[HALO:, :] = dot(normed_ref[...], ws_ref[...]).astype(BF16).astype(F32)
    weights = cs_ref[...]
    for r in range(0, rows, BLOCK):
        bc_ref[r : r + BLOCK, :] = conv_silu(rows_ref, weights, r)
    bt_ref[...] = bc_ref[:, :states].astype(F32).T.astype(BF16)


def maps_call(place, normed, halo, w_state, conv_state, after=()):
    rows = normed.shape[0]
    both = w_state.shape[1]
    return call(
        maps_kernel,
        "maps",
        vmem=8,
        cost=micros(0.3),
        scalars=(place,),
        in_specs=[VMEM] * 4,
        out_specs=[VMEM] * 2,
        out_shape=[
            jax.ShapeDtypeStruct((rows, both), BF16),
            jax.ShapeDtypeStruct((both // 2, rows), BF16),
        ],
        scratch=[pltpu.VMEM((rows + HALO, both), F32)],
        after=after,
    )(place, normed, halo, w_state, conv_state)


def local_kernel(
    head_size,
    place_ref,
    parity_ref,
    normed_ref,
    halo_ref,
    bt_ref,
    wi_ref,
    small_ref,
    x_ref,
    cum_ref,
    times_ref,
    send_ref,
    mine_ref,
    rows_ref,
    spread_ref,
    scaled_ref,
    left_ref,
    whole_ref,
    payload_ref,
):
    rows = normed_ref.shape[0]
    states = bt_ref.shape[0]
    heads = cum_ref.shape[1]
    taps = SMALL_TAPS
    raw = dot_nt(normed_ref[...], small_ref[SMALL_ROWS:, :].astype(BF16))
    columns = small_ref[:SMALL_ROWS, :CHUNK].T
    raw = raw.T + columns[:heads, taps + 1 : taps + 2]
    step = jnp.maximum(raw, 0.0) + jnp.log1p(jnp.exp(-jnp.abs(raw)))
    logdecay = -step * columns[:heads, taps + 2 : taps + 3]
    high = logdecay.astype(BF16)
    rest = logdecay - high.astype(F32)
    mid = rest.astype(BF16)
    low = (rest - mid.astype(F32)).astype(BF16)
    starts = range(0, rows, CHUNK)
    pieces = [part[:, r : r + CHUNK] for r in starts for part in (high, mid, low)]
    frm = lax.broadcasted_iota(jnp.int32, (CHUNK, CHUNK), 0)
    to = lax.broadcasted_iota(jnp.int32, (CHUNK, CHUNK), 1)
    sums = dot(jnp.concatenate(pieces, axis=0), jnp.where(to >= frm, 1.0, 0.0).astype(BF16))
    run = jnp.zeros((heads, 1), F32)
    cums = []
    for i in range(len(starts)):
        at = 3 * i * heads
        cums.append(sums[at : at + heads] + sums[at + heads : at + 2 * heads] + sums[at + 2 * heads : at + 3 * heads] + run)
        run = cums[-1][:, CHUNK - 1 :]
    cum = jnp.concatenate(cums, axis=1)
    times_ref[:heads, :] = cum
    times_ref[heads:, :] = step
    cum_ref[...] = cum.T
    left_ref[...] = two_rows(step * jnp.exp(run - cum)).T.astype(BF16)
    whole_ref[...] = two_parts(jnp.exp(cum_ref[rows - 1 :, :]))

    inner = x_ref.shape[1]
    half = inner // 2
    tiles = range(inner // TILE)
    onehots = [head_matrix(heads, TILE, head_size, t * (TILE // head_size)) for t in tiles]
    spans = [slice(t * TILE, (t + 1) * TILE) for t in tiles]

    def project(t):
        weights = wi_ref[:, spans[t]]
        before = dot(halo_ref[...], weights).astype(BF16).astype(F32)
        rows_ref[t % 2, :HALO, :] = jnp.where(place_ref[0] >= 1, before, 0.0)
        rows_ref[t % 2, HALO:, :] = dot(normed_ref[...], weights).astype(BF16).astype(F32)
        spread_ref[t % 2] = dot(left_ref[...], onehots[t])

    def combine(t):
        taps_here = small_ref[:taps, spans[t]]
        for r in range(0, rows, BLOCK):
            block = slice(r, r + BLOCK)
            x = conv_silu(rows_ref.at[t % 2], taps_here, r)
            x_ref[block, spans[t]] = x
            scaled_ref[t % 2, block, :] = (x.astype(F32) * spread_ref[t % 2, block, :]).astype(BF16)
        state = dot(bt_ref[...], scaled_ref[t % 2])
        here = slice(t * TILE % half, t * TILE % half + TILE)
        is_mine = jnp.where(parity_ref[0] == t * TILE // half, 1, 0)
        write_payload(payload_ref.at[is_mine], here, state, dot(whole_ref[...], onehots[t]))

    project(0)
    for t in tiles:
        if t + 1 < len(tiles):
            project(t + 1)
        combine(t)
    send_ref[...] = payload_ref[0]
    mine_ref[...] = payload_ref[1]


SMALL_TAPS = 4
SMALL_ROWS = 8


def local_call(tag, place, parity, normed, halo, bt, w_inner, small, after=()):
    rows = normed.shape[0]
    inner = w_inner.shape[1]
    heads = small.shape[0] - SMALL_ROWS
    states = bt.shape[0]
    return call(
        functools.partial(local_kernel, inner // heads),
        "local_" + tag,
        vmem=12,
        cost=micros(5.0),
        scalars=(place, parity),
        in_specs=[VMEM] * 5,
        out_specs=[VMEM] * 5,
        out_shape=[
            jax.ShapeDtypeStruct((rows, inner), BF16),
            jax.ShapeDtypeStruct((rows, heads), F32),
            jax.ShapeDtypeStruct((2 * heads, rows), F32),
            jax.ShapeDtypeStruct((states + EXTRA, inner // 2), BF16),
            jax.ShapeDtypeStruct((states + EXTRA, inner // 2), BF16),
        ],
        scratch=[
            pltpu.VMEM((2, rows + HALO, TILE), F32),
            pltpu.VMEM((2, rows, TILE), F32),
            pltpu.VMEM((2, rows, TILE), BF16),
            pltpu.VMEM((rows, 2 * heads), BF16),
            pltpu.VMEM((1, 2 * heads), BF16),
            pltpu.VMEM((2, states + EXTRA, inner // 2), BF16),
        ],
        after=after,
    )(place, parity, normed, halo, bt, w_inner, small)


def inside_kernel(head_size, head, x_ref, bc_ref, bt_ref, cum_ref, times_ref, y_ref, state_ref):
    rows, width = y_ref.shape
    states = bc_ref.shape[1] // 2
    heads = cum_ref.shape[1]
    length = CHUNK
    last = length - 1
    pair = 2 * head_size
    lane = lax.broadcasted_iota(jnp.int32, (length, pair), 1)
    to = lax.broadcasted_iota(jnp.int32, (length, length), 0)
    frm = lax.broadcasted_iota(jnp.int32, (length, length), 1)

    def chunk(c, before):
        at = slice(c * length, (c + 1) * length)
        bmat = bt_ref[:, at]
        cmat = bc_ref[at, states:]
        scores = jnp.where(to >= frm, dot(cmat, bmat), 0.0)
        cum = cum_ref[at, :]
        cumt = times_ref[:heads, at]
        step = times_ref[heads:, at]
        end = cumt[:, last:]
        entered = c > 0
        leaves = (c + 1) * length < rows
        if entered:
            since = two_rows(jnp.exp(cumt - before)).T.astype(BF16)
        if leaves:
            left = two_rows(step * jnp.exp(end - cumt)).T.astype(BF16)
        for offset in range(0, width, TILE):
            first = head + offset // head_size
            columns = slice(first * head_size, first * head_size + TILE)
            here = slice(offset, offset + TILE)
            onehot = head_matrix(heads, TILE, head_size, first)
            if entered:
                since_here = dot(since, onehot)
                state = state_ref[:, here]
                carried = dot(cmat, state.astype(BF16)) * since_here
            if leaves:
                scaled = (x_ref[at, columns].astype(F32) * dot(left, onehot)).astype(BF16)
                added = dot(bmat, scaled)
                state_ref[:, here] = state * since_here[last:, :] + added if entered else added
            for start in range(0, TILE, pair):
                low = first * head_size + start
                weights = []
                for h in (low // head_size, low // head_size + 1):
                    apart = jnp.minimum(cum[:, h : h + 1] - cumt[h : h + 1, :], 0.0)
                    weights.append((jnp.exp(apart) * (scores * step[h : h + 1, :])).astype(BF16))
                mine = x_ref[at, low : low + pair]
                none = jnp.zeros_like(mine)
                stacked = jnp.concatenate(
                    [jnp.where(lane < head_size, mine, none), jnp.where(lane < head_size, none, mine)], axis=0
                )
                inside = dot(jnp.concatenate(weights, axis=1), stacked)
                if entered:
                    inside += carried[:, start : start + pair]
                y_ref[at, offset + start : offset + start + pair] = inside.astype(BF16)
        return end

    before = jnp.zeros((heads, 1), F32)
    for c in range(rows // length):
        before = chunk(c, before)


def inside_call(tag, x, bc, bt, cum, times, after=(), part=0, parts=1):
    rows, inner = x.shape
    heads = cum.shape[1]
    both = bc.shape[1]
    width = inner // parts
    return call(
        functools.partial(inside_kernel, inner // heads, part * heads // parts),
        "inside_" + tag,
        vmem=8,
        cost=micros(3.2 / parts),
        in_specs=[VMEM] * 5,
        out_specs=VMEM,
        out_shape=jax.ShapeDtypeStruct((rows, width), BF16),
        scratch=[pltpu.VMEM((both // 2, width), F32)],
        after=after,
    )(x, bc, bt, cum, times)


def mark_kernel(rows_ref, out_ref):
    out_ref[...] = rows_ref[: out_ref.shape[0], : out_ref.shape[1]]


def mark_call(value, after):
    return call(
        mark_kernel,
        "mark",
        vmem=4,
        cost=micros(2.4),
        in_specs=[VMEM],
        out_specs=VMEM,
        out_shape=jax.ShapeDtypeStruct((HALO, 128), value.dtype),
        after=after,
    )(value)


def parts_of(ref, known=None):
    states = ref.shape[0] - EXTRA
    state = ref[:states, :].astype(F32)
    extra = ref[states:, :].astype(F32)
    decay = extra[:1] + extra[1:2]
    if known is None:
        return state, decay
    return jnp.where(known, state, 0.0), jnp.where(known, decay, 0.0)


def write_payload(out_ref, columns, state, decay):
    states = state.shape[0]
    out_ref[:states, columns] = state.astype(BF16)
    decay = jnp.broadcast_to(decay, (EXTRA, decay.shape[1]))
    high = decay.astype(BF16).astype(F32)
    place = lax.broadcasted_iota(jnp.int32, decay.shape, 0)
    out_ref[states:, columns] = jnp.where(place == 0, high, decay - high).astype(BF16)


ALL = slice(None)


def pair_kernel(place_ref, mine_ref, other_ref, out_ref):
    mine, mine_a = parts_of(mine_ref)
    other, other_a = parts_of(other_ref)
    is_first = lax.rem(place_ref[0], 2) == 0
    early = jnp.where(is_first, mine, other)
    late = jnp.where(is_first, other, mine)
    late_a = jnp.where(is_first, other_a, mine_a)
    write_payload(out_ref, ALL, late_a * early + late, mine_a * other_a)


def chain_kernel(reach, place_ref, pair_ref, before_ref, out_ref):
    pair, pair_a = parts_of(pair_ref)
    before, before_a = parts_of(before_ref, place_ref[0] >= reach)
    write_payload(out_ref, ALL, pair_a * before + pair, pair_a * before_a)


def longer_kernel(reach, farther_reach, place_ref, before_ref, farther_ref, out_ref):
    before, before_a = parts_of(before_ref, place_ref[0] >= reach)
    farther, farther_a = parts_of(farther_ref, place_ref[0] >= farther_reach)
    write_payload(out_ref, ALL, before + before_a * farther, before_a * farther_a)


def entry_kernel(reach, farther_reach, place_ref, mine_ref, other_ref, before_ref, farther_ref, keep_ref, send_ref):
    mine, mine_a = parts_of(mine_ref)
    other, other_a = parts_of(other_ref)
    before, before_a = parts_of(before_ref, place_ref[0] >= reach)
    farther, _ = parts_of(farther_ref, place_ref[0] >= farther_reach)
    is_first = lax.rem(place_ref[0], 2) == 0
    entry_first = before + before_a * farther
    early = jnp.where(is_first, mine, other)
    early_a = jnp.where(is_first, mine_a, other_a)
    entry_second = early_a * entry_first + early
    keep_ref[...] = jnp.where(is_first, entry_first, entry_second).astype(BF16)
    send_ref[...] = jnp.where(is_first, entry_second, entry_first).astype(BF16)


def small_call(kernel, name, place, arrays, shapes, after=()):
    return call(
        kernel,
        name,
        vmem=4,
        cost=micros(0.5),
        scalars=(place,),
        in_specs=[VMEM] * len(arrays),
        out_specs=[VMEM] * len(shapes),
        out_shape=[jax.ShapeDtypeStruct(s, BF16) for s in shapes],
        after=after,
    )(place, *arrays)


def onward(value, by):
    count = lax.axis_size("seq")
    pairs = []
    for i in range(count):
        up = (i + by, 0) if i + by < count else (i, 1)
        down = (i - by, 1) if i - by >= 0 else (i, 0)
        pairs += [(2 * i, 2 * up[0] + up[1]), (2 * i + 1, 2 * down[0] + down[1])]
    return lax.ppermute(value, ("seq", "ch"), pairs)


class Chain:
    def __init__(self, tag, place, send, mine):
        self.tag, self.place, self.mine = tag, place, mine
        self.count = lax.axis_size("seq")
        self.swap = [(i, i ^ 1) for i in range(self.count)]
        self.other = lax.ppermute(send, "seq", self.swap)
        self.before = self.farther = None
        self.reach = self.farther_reach = 0
        self.apart = 2

    def pair(self, after):
        (self.pair_state,) = small_call(
            pair_kernel, "pair_" + self.tag, self.place, [self.mine, self.other], [self.mine.shape], after
        )
        self.running = self.pair_state
        self.hop()
        return self.pair_state

    def hop(self):
        if self.apart < self.count:
            self.arrived = onward(self.running, self.apart)

    def middle(self, after):
        while self.apart * 2 < self.count:
            self.take(after)
            (self.running,) = small_call(
                functools.partial(chain_kernel, self.reach),
                "chain_" + self.tag,
                self.place,
                [self.pair_state, self.before],
                [self.mine.shape],
                after,
            )
            self.apart *= 2
            self.hop()
        return self.running

    def take(self, after=()):
        if self.before is None:
            self.before, self.reach = self.arrived, self.apart
        else:
            (self.before,) = small_call(
                functools.partial(longer_kernel, self.reach, self.apart),
                "longer_" + self.tag,
                self.place,
                [self.before, self.arrived],
                [self.mine.shape],
                after,
            )
            self.reach = 0

    def entry(self, after):
        shape = self.mine.shape
        if self.apart < self.count:
            if self.before is None:
                self.before, self.reach = self.arrived, self.apart
                self.farther, self.farther_reach = self.arrived, self.count
            else:
                self.farther, self.farther_reach = self.arrived, self.apart
        else:
            self.before = self.farther = self.mine
            self.reach = self.farther_reach = self.count
        half = (shape[0] - EXTRA, shape[1])
        keep, out = small_call(
            functools.partial(entry_kernel, self.reach, self.farther_reach),
            "entry_" + self.tag,
            self.place,
            [self.mine, self.other, self.before, self.farther],
            [half, half],
            after,
        )
        return keep, lax.ppermute(out, "seq", self.swap)


def gated_part(
    head_size, swap, y_refs, bc_ref, cum_ref, keep_ref, other_ref, gate_ref, small_ref, wo_ref, scaled_ref, tile_ref
):
    rows, share = y_refs[0].shape
    inner = share * len(y_refs)
    states = bc_ref.shape[1] // 2
    heads = cum_ref.shape[1]
    half = inner // 2
    since = two_parts(jnp.exp(cum_ref[...]))
    squares = [0.0] * (rows // BLOCK)
    for low in range(0, inner, TILE):
        columns = slice(low, low + TILE)
        y_ref = y_refs[low // share]
        of_share = slice(low % share, low % share + TILE)
        here = slice(low % half, low % half + TILE)
        use_other = swap if low < half else jnp.logical_not(swap)
        entry = jnp.where(use_other, other_ref[:, here], keep_ref[:, here])
        tile_ref[0] = dot(bc_ref[:, states:], entry)
        tile_ref[1] = dot(since, head_matrix(heads, TILE, head_size, low // head_size))
        gain = small_ref[SMALL_TAPS : SMALL_TAPS + 1, columns]
        for i, r in enumerate(range(0, rows, BLOCK)):
            block = slice(r, r + BLOCK)
            gated = y_ref[block, of_share].astype(F32) + tile_ref[0, block, :] * tile_ref[1, block, :]
            gated = gated * gate_ref[block, columns].astype(F32)
            squares[i] += jnp.sum(gated * gated, axis=-1, keepdims=True)
            scaled_ref[block, columns] = (gated * gain).astype(BF16)
    return squares


def part_kernel(head_size, shares, parity_ref, *refs):
    *ins, out_ref, sq_ref, scaled_ref, tile_ref = refs
    squares = gated_part(head_size, parity_ref[0] == 1, ins[:shares], *ins[shares:], scaled_ref, tile_ref)
    for i, square in enumerate(squares):
        sq_ref[i * BLOCK : (i + 1) * BLOCK, :] = jnp.broadcast_to(square, (BLOCK, sq_ref.shape[1]))
    for low in range(0, out_ref.shape[1], TILE):
        out_ref[:, low : low + TILE] = dot(scaled_ref[...], ins[-1][:, low : low + TILE])


def product(back, scaled_ref, weights_ref, part_ref, scale_ref, tile_ref, half_ref, out_ref, first):
    rows, half = out_ref.shape
    for low in range(0, half, TILE):
        columns = slice(first + low, first + low + TILE)
        tile_ref[...] = dot(scaled_ref[...], weights_ref[:, columns])
        for r in range(0, rows, BLOCK):
            block = slice(r, r + BLOCK)
            value = (tile_ref[block, :] + part_ref[block, columns]) * scale_ref[block, :1]
            half_ref[block, low : low + TILE] = value.astype(BF16)

    @pl.when(back == 1)
    def _():
        turn = flip_matrix(TILE)
        for r in range(0, rows, TILE):
            for low in range(0, half, TILE):
                tile = dot(turn, half_ref[r : r + TILE, low : low + TILE]).astype(BF16)
                tile = dot(tile, turn).astype(BF16)
                to_row, to = rows - TILE - r, half - TILE - low
                out_ref[to_row : to_row + TILE, to : to + TILE] = tile

    @pl.when(back != 1)
    def _():
        out_ref[...] = half_ref[...]


def finish_kernel(head_size, shares, full_width, back_ref, parity_ref, *refs):
    *ins, part_ref, psq_ref, send_ref, scaled_ref, scale_ref, tile_ref, half_ref = refs
    squares = gated_part(head_size, parity_ref[0] == 1, ins[:shares], *ins[shares:], scaled_ref, tile_ref)
    for i, square in enumerate(squares):
        block = slice(i * BLOCK, (i + 1) * BLOCK)
        scale = lax.rsqrt((square + psq_ref[block, :1]) / full_width + EPS)
        scale_ref[block, :] = jnp.broadcast_to(scale, (BLOCK, scale_ref.shape[1]))
    product(back_ref[0], scaled_ref, ins[-1], part_ref, scale_ref, tile_ref.at[0], half_ref, send_ref, send_ref.shape[1])


def own_kernel(back_ref, scaled_ref, weights_ref, part_ref, scale_ref, own_ref, tile_ref, half_ref):
    product(back_ref[0], scaled_ref, weights_ref, part_ref, scale_ref, tile_ref, half_ref, own_ref, 0)


def own_call(back, scaled, w_output, part, scale, after):
    rows, width = part.shape
    half = width // 2
    return call(
        own_kernel,
        "own_half",
        vmem=8,
        cost=micros(0.7),
        scalars=(back,),
        in_specs=[VMEM] * 4,
        out_specs=VMEM,
        out_shape=jax.ShapeDtypeStruct((rows, half), BF16),
        scratch=[pltpu.VMEM((rows, TILE), F32), pltpu.VMEM((rows, half), BF16)],
        after=after,
    )(back, scaled, w_output, part, scale)


def finish_call(back, parity, ys, bc, cum, keep, other, gate, small, w_output, full_width=None, partial=None, after=()):
    rows = ys[0].shape[0]
    inner = ys[0].shape[1] * len(ys)
    width = w_output.shape[1]
    half = width // 2
    heads = cum.shape[1]
    arrays = [*ys, bc, cum, keep, other, gate, small, w_output]
    tiles = pltpu.VMEM((2, rows, TILE), F32)
    if partial is None:
        scratch = [pltpu.VMEM((rows, inner), BF16), tiles]
        scalars = (parity,)
        kernel = functools.partial(part_kernel, inner // heads, len(ys))
        out_shape = [jax.ShapeDtypeStruct((rows, width), F32), jax.ShapeDtypeStruct((rows, 128), F32)]
    else:
        scalars = (back, parity)
        scratch = [tiles, pltpu.VMEM((rows, half), BF16)]
        kernel = functools.partial(finish_kernel, inner // heads, len(ys), full_width)
        arrays += list(partial)
        out_shape = [
            jax.ShapeDtypeStruct((rows, half), BF16),
            jax.ShapeDtypeStruct((rows, inner), BF16),
            jax.ShapeDtypeStruct((rows, 128), F32),
        ]
    return call(
        kernel,
        "part" if partial is None else "finish",
        vmem=16,
        cost=micros(3.5),
        scalars=scalars,
        in_specs=[VMEM] * len(arrays),
        out_specs=[VMEM] * len(out_shape),
        out_shape=out_shape,
        scratch=scratch,
        after=after,
    )(*scalars, *arrays)


def total_kernel(mine_ref, theirs_ref, out_hbm, out_ref, sems):
    copies = []
    for i, r in enumerate(range(0, mine_ref.shape[0], CHUNK)):
        for q in range(r, r + CHUNK, BLOCK):
            block = slice(q, q + BLOCK)
            out_ref[block, :] = (mine_ref[block, :].astype(F32) + theirs_ref[block, :].astype(F32)).astype(BF16)
        part = pl.ds(r, CHUNK)
        copies.append(pltpu.make_async_copy(out_ref.at[part, :], out_hbm.at[part, :], sems.at[i]))
        copies[-1].start()
    for copy in copies:
        copy.wait()


def total_call(mine, theirs):
    rows, half = mine.shape
    return call(
        total_kernel,
        "total",
        vmem=4,
        cost=micros(0.8),
        in_specs=[VMEM] * 2,
        out_specs=HBM,
        out_shape=jax.ShapeDtypeStruct((rows, half), BF16),
        scratch=[pltpu.VMEM((rows, half), BF16), pltpu.SemaphoreType.DMA((rows // CHUNK,))],
    )(mine, theirs)


def body(
    tokens,
    hidden,
    embedding,
    w_gate,
    w_inner,
    w_state,
    w_step,
    conv_inner,
    conv_state,
    step_bias,
    decay_rate,
    norm_gain,
    w_output,
):
    swap = [(0, 1), (1, 0)]

    def theirs(a):
        return lax.ppermute(a, "ch", swap)

    core = lax.axis_index("ch").astype(jnp.int32)
    index = lax.axis_index("seq").astype(jnp.int32)
    last = lax.axis_size("seq") - 1
    back = core.reshape(1)
    parity = (index & 1).reshape(1)
    place = (index + core * (last - 2 * index)).reshape(1)
    place, parity, w_inner_3, w_gate_3, w_output_3 = lax.optimization_barrier(
        (place, parity, w_inner, w_gate, w_output)
    )
    w_inner_2 = theirs(w_inner_3)
    normed, tail, small = prepare_call(
        (back, parity, place), hidden, tokens, embedding, conv_inner, norm_gain, step_bias, decay_rate, w_step.T
    )
    halo = onward(tail, 1)
    small_2 = theirs(small)
    w_gate_2 = theirs(w_gate_3)
    w_output_2 = theirs(w_output_3)
    gate_1 = gate_call("own", normed, w_gate)
    bc, bt = maps_call(place, normed, halo, w_state, conv_state, after=[gate_1])
    x_1, cum_1, times_1, send_1, mine_1 = local_call("own", place, parity, normed, halo, bt, w_inner, small)
    chain_1 = Chain("own", place, send_1, mine_1)
    x_2, cum_2, times_2, send_2, mine_2 = local_call(
        "other", place, parity, normed, halo, bt, w_inner_2, small_2, after=[mine_1]
    )
    chain_2 = Chain("other", place, send_2, mine_2)
    done = mark_call(normed, after=[x_2])
    done = chain_1.pair(after=[done])
    y_1 = inside_call("own", x_1, bc, bt, cum_1, times_1, after=[done])
    done = chain_2.pair(after=[y_1])
    done = chain_1.middle(after=[done])
    gate_2 = gate_call("other", normed, w_gate_2, after=[done])
    done = chain_2.middle(after=[gate_2])
    entry_1 = chain_1.entry(after=[done])
    scan_2 = ("other", x_2, bc, bt, cum_2, times_2)
    y_2 = [inside_call(*scan_2, after=[entry_1[0]], part=0, parts=2)]
    entry_2 = chain_2.entry(after=y_2)
    y_2.append(inside_call(*scan_2, after=[entry_2[0]], part=1, parts=2))
    partial = finish_call(
        back, parity, [y_1], bc, cum_1, *entry_1, gate_1, small, w_output, after=y_2
    )
    full_width = float(w_inner.shape[1] * lax.axis_size("ch"))
    send, scaled, scale = finish_call(
        back, parity, y_2, bc, cum_2, *entry_2, gate_2, small_2, w_output_2, full_width, partial
    )
    arriving = theirs(send)
    mine = own_call(back, scaled, w_output_2, partial[0], scale, after=[send])
    return total_call(mine, arriving)


def solution(mesh):
    return jax.shard_map(
        body,
        mesh=mesh,
        in_specs=(
            P(("win", "seq")),
            P(("win", "seq"), None),
            P(),
            P(None, "ch"),
            P(None, "ch"),
            P(),
            P(None, "ch"),
            P(None, "ch"),
            P(),
            P("ch"),
            P("ch"),
            P("ch"),
            P("ch", None),
        ),
        out_specs=P(("win", "seq"), "ch"),
        check_vma=False,
    )
```

```python
import functools

import jax
import jax.numpy as jnp
from jax import lax
from jax.experimental import pallas as pl
from jax.experimental.pallas import tpu as pltpu
from jax.sharding import PartitionSpec as P

F32 = jnp.float32
BF16 = jnp.bfloat16
EPS = 1e-05
HALO = 16
EXTRA = 16
CHUNK = 128
TILE = 256
BLOCK = 64
MB = 1024 * 1024
VMEM = pl.BlockSpec(memory_space=pltpu.VMEM)
HBM = pl.BlockSpec(memory_space=pltpu.HBM)


def call(
    kernel, name, *, vmem, cost, scalars=(), grid=(), in_specs, out_specs, out_shape, scratch=(), after=()
):
    flops, moved, special = cost
    first = len(scalars) + len(in_specs)

    def body(*refs):
        kernel(*refs[:first], *refs[first + len(after) :])

    run = pl.pallas_call(
        body,
        grid_spec=pltpu.PrefetchScalarGridSpec(
            num_scalar_prefetch=len(scalars),
            grid=grid,
            in_specs=list(in_specs) + [pl.BlockSpec(memory_space=pl.ANY)] * len(after),
            out_specs=out_specs,
            scratch_shapes=scratch,
        ),
        out_shape=out_shape,
        compiler_params=pltpu.CompilerParams(
            vmem_limit_bytes=vmem * MB, dimension_semantics=("arbitrary",) * len(grid)
        ),
        cost_estimate=pl.CostEstimate(flops=flops, bytes_accessed=moved, transcendentals=special),
        name=name,
    )
    return lambda *arrays: run(*arrays, *after)


def micros(us):
    return (int(us * 1.1e9), int(us * 1e6), 0)


def dot(a, b):
    return jnp.dot(a, b, preferred_element_type=F32)


def dot_nt(a, b):
    return lax.dot_general(a, b, (((1,), (1,)), ((), ())), preferred_element_type=F32)


def dot_tn(a, b):
    return lax.dot_general(a, b, (((0,), (0,)), ((), ())), preferred_element_type=F32)


def flip_matrix(size):
    rows = lax.broadcasted_iota(jnp.int32, (size, size), 0)
    columns = lax.broadcasted_iota(jnp.int32, (size, size), 1)
    return jnp.where(rows + columns == size - 1, 1.0, 0.0).astype(BF16)


def flip_both(value):
    rows, width = value.shape
    turned = dot(flip_matrix(rows), value).astype(BF16)
    anti = flip_matrix(TILE)
    count = width // TILE
    blocks = [
        dot(turned[:, (count - 1 - k) * TILE : (count - k) * TILE], anti).astype(BF16)
        for k in range(count)
    ]
    return jnp.concatenate(blocks, axis=1)


def silu(v):
    half = 0.5 * v
    return half + half * jnp.tanh(half)


def two_parts(value):
    high = value.astype(BF16)
    low = (value - high.astype(F32)).astype(BF16)
    return jnp.concatenate([high, low], axis=1)


def two_rows(value):
    high = value.astype(BF16).astype(F32)
    return jnp.concatenate([high, value - high], axis=0)


def head_matrix(heads, width, head_size, first_head):
    source = lax.broadcasted_iota(jnp.int32, (2 * heads, width), 0)
    source = jnp.where(source >= heads, source - heads, source)
    target = lax.broadcasted_iota(jnp.int32, (2 * heads, width), 1) // head_size + first_head
    return jnp.where(source == target, 1.0, 0.0).astype(BF16)


def prepare_kernel(
    back_ref,
    parity_ref,
    place_ref,
    hidden_hbm,
    tokens_hbm,
    emb_hbm,
    conv_hbm,
    gain_hbm,
    bias_hbm,
    rate_hbm,
    step_hbm,
    out_ref,
    tail_ref,
    small_ref,
    hidden_ref,
    tokens_ref,
    emb_ref,
    conv_ref,
    gain_ref,
    bias_ref,
    rate_ref,
    step_ref,
    base_ref,
    normed_ref,
    turned_ref,
    sems,
):
    rows = hidden_ref.shape[0]
    kinds = emb_ref.shape[0]
    taps, inner = conv_ref.shape
    heads = bias_ref.shape[1]
    count = rows // CHUNK
    back = back_ref[0] == 1
    whole = [
        (tokens_hbm, tokens_ref),
        (emb_hbm, emb_ref),
        (conv_hbm, conv_ref),
        (gain_hbm, gain_ref),
        (bias_hbm, bias_ref),
        (rate_hbm, rate_ref),
        (step_hbm, step_ref),
    ]
    small_copies = [pltpu.make_async_copy(src, dst, sems.at[count + i]) for i, (src, dst) in enumerate(whole)]
    parts = [pl.ds(r * CHUNK, CHUNK) for r in range(count)]
    copies = [
        pltpu.make_async_copy(hidden_hbm.at[part, :], hidden_ref.at[part, :], sems.at[r])
        for r, part in enumerate(parts)
    ]
    for copy in small_copies[:2] + copies + small_copies[2:]:
        copy.start()
    for copy in small_copies[:2]:
        copy.wait()
    kind = lax.broadcasted_iota(jnp.int32, (kinds, rows), 0)
    onehot = jnp.where(kind == tokens_ref[...], 1.0, 0.0).astype(BF16)
    for r in range(count):
        copies[r].wait()
        low, high = r * CHUNK, (r + 1) * CHUNK
        base_ref[...] = dot_tn(onehot[:, low:high], emb_ref[...])
        for q in range(low, high, HALO):
            block = slice(q, q + HALO)
            merged = hidden_ref[block, :].astype(F32) + base_ref[q - low : q - low + HALO, :]
            merged = merged.astype(BF16).astype(F32)
            mean = jnp.mean(merged * merged, axis=-1, keepdims=True)
            normed_ref[block, :] = (merged * lax.rsqrt(mean + EPS)).astype(BF16)

    @pl.when(back)
    def _():
        turn = flip_matrix(TILE)
        for c in range(0, hidden_ref.shape[1], TILE):
            to = hidden_ref.shape[1] - TILE - c
            for r in range(0, rows, TILE):
                turned = dot(turn, normed_ref[r : r + TILE, c : c + TILE]).astype(BF16)
                turned_ref[r : r + TILE, c : c + TILE] = turned
            for r in range(0, rows, TILE):
                out_ref[rows - TILE - r : rows - r, to : to + TILE] = dot(
                    turned_ref[r : r + TILE, c : c + TILE], turn
                ).astype(BF16)

    @pl.when(jnp.logical_not(back))
    def _():
        out_ref[...] = normed_ref[...]

    tail_ref[...] = out_ref[rows - HALO :, :]
    for copy in small_copies[2:]:
        copy.wait()
    small_ref[:taps, :] = conv_ref[...]
    small_ref[taps : taps + 1, :] = gain_ref[...]
    small_ref[taps + 1 : SMALL_ROWS, :] = jnp.zeros((SMALL_ROWS - taps - 1, inner), F32)
    small_ref[taps + 1 : taps + 2, :heads] = bias_ref[...]
    small_ref[taps + 2 : taps + 3, :heads] = rate_ref[...]
    small_ref[SMALL_ROWS:, :] = step_ref[...].astype(F32)


def prepare_call(scalars, hidden, tokens, embedding, conv, gain, bias, rate, step):
    rows, width = hidden.shape
    inner = conv.shape[1]
    arrays = [hidden, tokens.reshape(1, -1), embedding, conv]
    arrays += [a.reshape(1, -1) for a in (gain, bias, rate)] + [step]
    return call(
        prepare_kernel,
        "prepare",
        vmem=12,
        cost=micros(2.7),
        scalars=scalars,
        in_specs=[HBM] * len(arrays),
        out_specs=[VMEM] * 3,
        out_shape=[
            jax.ShapeDtypeStruct((rows, width), BF16),
            jax.ShapeDtypeStruct((HALO, width), BF16),
            jax.ShapeDtypeStruct((SMALL_ROWS + step.shape[0], inner), F32),
        ],
        scratch=[pltpu.VMEM(a.shape, a.dtype) for a in arrays]
        + [pltpu.VMEM((CHUNK, width), F32)]
        + [pltpu.VMEM((rows, width), BF16)] * 2
        + [pltpu.SemaphoreType.DMA((rows // CHUNK + len(arrays) - 1,))],
    )(*scalars, *(pltpu.with_memory_space_constraint(a, pltpu.HBM) for a in arrays))


def gate_kernel(rows_ref, wg_ref, out_ref, gate_ref):
    rows, inner = out_ref.shape
    for low in range(0, inner, TILE):
        columns = slice(low, low + TILE)
        gate_ref[...] = dot(rows_ref[...], wg_ref[:, columns])
        for r in range(0, rows, BLOCK):
            gate = gate_ref[r : r + BLOCK, :].astype(BF16).astype(F32)
            out_ref[r : r + BLOCK, columns] = silu(gate).astype(BF16)


def gate_call(tag, normed, w_gate, after=()):
    rows = normed.shape[0]
    inner = w_gate.shape[1]
    return call(
        gate_kernel,
        "gate_" + tag,
        vmem=8,
        cost=micros(2.4),
        in_specs=[VMEM] * 2,
        out_specs=VMEM,
        out_shape=jax.ShapeDtypeStruct((rows, inner), BF16),
        scratch=[pltpu.VMEM((rows, TILE), F32)],
        after=after,
    )(normed, w_gate)


def conv_silu(rows_ref, weights, row):
    taps = weights.shape[0]
    ahead = 8
    window = rows_ref[HALO - ahead + row : HALO + row + BLOCK, :]
    total = weights[taps - 1 :, :] * window[ahead:, :]
    for back in range(1, taps):
        total += weights[taps - 1 - back : taps - back, :] * pltpu.roll(window, back, 0)[ahead:, :]
    return silu(total).astype(BF16)


def maps_kernel(place_ref, normed_ref, halo_ref, ws_ref, cs_ref, bc_ref, bt_ref, rows_ref):
    rows = normed_ref.shape[0]
    states = bc_ref.shape[1] // 2
    before = dot(halo_ref[...], ws_ref[...]).astype(BF16).astype(F32)
    rows_ref[:HALO, :] = jnp.where(place_ref[0] >= 1, before, 0.0)
    rows_ref[HALO:, :] = dot(normed_ref[...], ws_ref[...]).astype(BF16).astype(F32)
    weights = cs_ref[...]
    for r in range(0, rows, BLOCK):
        bc_ref[r : r + BLOCK, :] = conv_silu(rows_ref, weights, r)
    bt_ref[...] = bc_ref[:, :states].astype(F32).T.astype(BF16)


def maps_call(place, normed, halo, w_state, conv_state, after=()):
    rows = normed.shape[0]
    both = w_state.shape[1]
    return call(
        maps_kernel,
        "maps",
        vmem=8,
        cost=micros(0.3),
        scalars=(place,),
        in_specs=[VMEM] * 4,
        out_specs=[VMEM] * 2,
        out_shape=[
            jax.ShapeDtypeStruct((rows, both), BF16),
            jax.ShapeDtypeStruct((both // 2, rows), BF16),
        ],
        scratch=[pltpu.VMEM((rows + HALO, both), F32)],
        after=after,
    )(place, normed, halo, w_state, conv_state)


def local_kernel(
    head_size,
    place_ref,
    parity_ref,
    normed_ref,
    halo_ref,
    bt_ref,
    wi_ref,
    small_ref,
    x_ref,
    cum_ref,
    times_ref,
    send_ref,
    mine_ref,
    rows_ref,
    spread_ref,
    scaled_ref,
    left_ref,
    whole_ref,
    payload_ref,
):
    rows = normed_ref.shape[0]
    states = bt_ref.shape[0]
    heads = cum_ref.shape[1]
    taps = SMALL_TAPS

    def project_rows(t):
        weights = wi_ref[:, t * TILE : (t + 1) * TILE]
        before = dot(halo_ref[...], weights).astype(BF16).astype(F32)
        rows_ref[t % 2, :HALO, :] = jnp.where(place_ref[0] >= 1, before, 0.0)
        rows_ref[t % 2, HALO:, :] = dot(normed_ref[...], weights).astype(BF16).astype(F32)

    raw = dot_nt(normed_ref[...], small_ref[SMALL_ROWS:, :].astype(BF16))
    columns = small_ref[:SMALL_ROWS, :CHUNK].T
    raw = raw.T + columns[:heads, taps + 1 : taps + 2]
    step = jnp.maximum(raw, 0.0) + jnp.log1p(jnp.exp(-jnp.abs(raw)))
    logdecay = -step * columns[:heads, taps + 2 : taps + 3]
    high = logdecay.astype(BF16)
    rest = logdecay - high.astype(F32)
    mid = rest.astype(BF16)
    low = (rest - mid.astype(F32)).astype(BF16)
    starts = range(0, rows, CHUNK)
    pieces = [part[:, r : r + CHUNK] for r in starts for part in (high, mid, low)]
    project_rows(0)
    frm = lax.broadcasted_iota(jnp.int32, (CHUNK, CHUNK), 0)
    to = lax.broadcasted_iota(jnp.int32, (CHUNK, CHUNK), 1)
    sums = dot(jnp.concatenate(pieces, axis=0), jnp.where(to >= frm, 1.0, 0.0).astype(BF16))
    run = jnp.zeros((heads, 1), F32)
    cums = []
    for i in range(len(starts)):
        at = 3 * i * heads
        cums.append(sums[at : at + heads] + sums[at + heads : at + 2 * heads] + sums[at + 2 * heads : at + 3 * heads] + run)
        run = cums[-1][:, CHUNK - 1 :]
    cum = jnp.concatenate(cums, axis=1)
    times_ref[:heads, :] = cum
    times_ref[heads:, :] = step
    cum_ref[...] = cum.T
    left_ref[...] = two_rows(step * jnp.exp(run - cum)).T.astype(BF16)
    whole_ref[...] = two_parts(jnp.exp(cum_ref[rows - 1 :, :]))

    inner = x_ref.shape[1]
    half = inner // 2
    tiles = range(inner // TILE)
    onehots = [head_matrix(heads, TILE, head_size, t * (TILE // head_size)) for t in tiles]
    spans = [slice(t * TILE, (t + 1) * TILE) for t in tiles]

    def project(t):
        project_rows(t)
        spread_ref[t % 2] = dot(left_ref[...], onehots[t])

    def combine(t):
        taps_here = small_ref[:taps, spans[t]]
        for r in range(0, rows, BLOCK):
            block = slice(r, r + BLOCK)
            x = conv_silu(rows_ref.at[t % 2], taps_here, r)
            x_ref[block, spans[t]] = x
            scaled_ref[t % 2, block, :] = (x.astype(F32) * spread_ref[t % 2, block, :]).astype(BF16)
        state = dot(bt_ref[...], scaled_ref[t % 2])
        here = slice(t * TILE % half, t * TILE % half + TILE)
        is_mine = jnp.where(parity_ref[0] == t * TILE // half, 1, 0)
        write_payload(payload_ref.at[is_mine], here, state, dot(whole_ref[...], onehots[t]))

    spread_ref[0] = dot(left_ref[...], onehots[0])
    for t in tiles:
        if t + 1 < len(tiles):
            project(t + 1)
        combine(t)
    send_ref[...] = payload_ref[0]
    mine_ref[...] = payload_ref[1]


SMALL_TAPS = 4
SMALL_ROWS = 8


def local_call(tag, place, parity, normed, halo, bt, w_inner, small, after=()):
    rows = normed.shape[0]
    inner = w_inner.shape[1]
    heads = small.shape[0] - SMALL_ROWS
    states = bt.shape[0]
    return call(
        functools.partial(local_kernel, inner // heads),
        "local_" + tag,
        vmem=12,
        cost=micros(5.0),
        scalars=(place, parity),
        in_specs=[VMEM] * 5,
        out_specs=[VMEM] * 5,
        out_shape=[
            jax.ShapeDtypeStruct((rows, inner), BF16),
            jax.ShapeDtypeStruct((rows, heads), F32),
            jax.ShapeDtypeStruct((2 * heads, rows), F32),
            jax.ShapeDtypeStruct((states + EXTRA, inner // 2), BF16),
            jax.ShapeDtypeStruct((states + EXTRA, inner // 2), BF16),
        ],
        scratch=[
            pltpu.VMEM((2, rows + HALO, TILE), F32),
            pltpu.VMEM((2, rows, TILE), F32),
            pltpu.VMEM((2, rows, TILE), BF16),
            pltpu.VMEM((rows, 2 * heads), BF16),
            pltpu.VMEM((1, 2 * heads), BF16),
            pltpu.VMEM((2, states + EXTRA, inner // 2), BF16),
        ],
        after=after,
    )(place, parity, normed, halo, bt, w_inner, small)


def inside_kernel(head_size, head, x_ref, bc_ref, bt_ref, cum_ref, times_ref, y_ref, state_ref):
    rows, width = y_ref.shape
    states = bc_ref.shape[1] // 2
    heads = cum_ref.shape[1]
    length = CHUNK
    last = length - 1
    pair = 2 * head_size
    lane = lax.broadcasted_iota(jnp.int32, (length, pair), 1)
    to = lax.broadcasted_iota(jnp.int32, (length, length), 0)
    frm = lax.broadcasted_iota(jnp.int32, (length, length), 1)

    def chunk(c, before):
        at = slice(c * length, (c + 1) * length)
        bmat = bt_ref[:, at]
        cmat = bc_ref[at, states:]
        scores = jnp.where(to >= frm, dot(cmat, bmat), 0.0)
        cum = cum_ref[at, :]
        cumt = times_ref[:heads, at]
        step = times_ref[heads:, at]
        end = cumt[:, last:]
        entered = c > 0
        leaves = (c + 1) * length < rows
        if entered:
            since = two_rows(jnp.exp(cumt - before)).T.astype(BF16)
        if leaves:
            left = two_rows(step * jnp.exp(end - cumt)).T.astype(BF16)
        for offset in range(0, width, TILE):
            first = head + offset // head_size
            columns = slice(first * head_size, first * head_size + TILE)
            here = slice(offset, offset + TILE)
            onehot = head_matrix(heads, TILE, head_size, first)
            if entered:
                since_here = dot(since, onehot)
                state = state_ref[:, here]
                carried = dot(cmat, state.astype(BF16)) * since_here
            if leaves:
                scaled = (x_ref[at, columns].astype(F32) * dot(left, onehot)).astype(BF16)
                added = dot(bmat, scaled)
                state_ref[:, here] = state * since_here[last:, :] + added if entered else added
            for start in range(0, TILE, pair):
                low = first * head_size + start
                weights = []
                for h in (low // head_size, low // head_size + 1):
                    apart = jnp.minimum(cum[:, h : h + 1] - cumt[h : h + 1, :], 0.0)
                    weights.append((jnp.exp(apart) * (scores * step[h : h + 1, :])).astype(BF16))
                mine = x_ref[at, low : low + pair]
                none = jnp.zeros_like(mine)
                stacked = jnp.concatenate(
                    [jnp.where(lane < head_size, mine, none), jnp.where(lane < head_size, none, mine)], axis=0
                )
                inside = dot(jnp.concatenate(weights, axis=1), stacked)
                if entered:
                    inside += carried[:, start : start + pair]
                y_ref[at, offset + start : offset + start + pair] = inside.astype(BF16)
        return end

    before = jnp.zeros((heads, 1), F32)
    for c in range(rows // length):
        before = chunk(c, before)


def inside_call(tag, x, bc, bt, cum, times, after=(), part=0, parts=1):
    rows, inner = x.shape
    heads = cum.shape[1]
    both = bc.shape[1]
    width = inner // parts
    return call(
        functools.partial(inside_kernel, inner // heads, part * heads // parts),
        "inside_" + tag,
        vmem=8,
        cost=micros(3.2 / parts),
        in_specs=[VMEM] * 5,
        out_specs=VMEM,
        out_shape=jax.ShapeDtypeStruct((rows, width), BF16),
        scratch=[pltpu.VMEM((both // 2, width), F32)],
        after=after,
    )(x, bc, bt, cum, times)


def mark_kernel(rows_ref, out_ref):
    out_ref[...] = rows_ref[: out_ref.shape[0], : out_ref.shape[1]]


def mark_call(value, after):
    return call(
        mark_kernel,
        "mark",
        vmem=4,
        cost=micros(2.4),
        in_specs=[VMEM],
        out_specs=VMEM,
        out_shape=jax.ShapeDtypeStruct((HALO, 128), value.dtype),
        after=after,
    )(value)


def parts_of(ref, known=None):
    states = ref.shape[0] - EXTRA
    state = ref[:states, :].astype(F32)
    extra = ref[states:, :].astype(F32)
    decay = extra[:1] + extra[1:2]
    if known is None:
        return state, decay
    return jnp.where(known, state, 0.0), jnp.where(known, decay, 0.0)


def write_payload(out_ref, columns, state, decay):
    states = state.shape[0]
    out_ref[:states, columns] = state.astype(BF16)
    decay = jnp.broadcast_to(decay, (EXTRA, decay.shape[1]))
    high = decay.astype(BF16).astype(F32)
    place = lax.broadcasted_iota(jnp.int32, decay.shape, 0)
    out_ref[states:, columns] = jnp.where(place == 0, high, decay - high).astype(BF16)


ALL = slice(None)


def pair_kernel(place_ref, mine_ref, other_ref, out_ref):
    mine, mine_a = parts_of(mine_ref)
    other, other_a = parts_of(other_ref)
    is_first = lax.rem(place_ref[0], 2) == 0
    early = jnp.where(is_first, mine, other)
    late = jnp.where(is_first, other, mine)
    late_a = jnp.where(is_first, other_a, mine_a)
    write_payload(out_ref, ALL, late_a * early + late, mine_a * other_a)


def chain_kernel(reach, place_ref, pair_ref, before_ref, out_ref):
    pair, pair_a = parts_of(pair_ref)
    before, before_a = parts_of(before_ref, place_ref[0] >= reach)
    write_payload(out_ref, ALL, pair_a * before + pair, pair_a * before_a)


def longer_kernel(reach, farther_reach, place_ref, before_ref, farther_ref, out_ref):
    before, before_a = parts_of(before_ref, place_ref[0] >= reach)
    farther, farther_a = parts_of(farther_ref, place_ref[0] >= farther_reach)
    write_payload(out_ref, ALL, before + before_a * farther, before_a * farther_a)


def entry_kernel(reach, farther_reach, place_ref, mine_ref, other_ref, before_ref, farther_ref, keep_ref, send_ref):
    mine, mine_a = parts_of(mine_ref)
    other, other_a = parts_of(other_ref)
    before, before_a = parts_of(before_ref, place_ref[0] >= reach)
    farther, _ = parts_of(farther_ref, place_ref[0] >= farther_reach)
    is_first = lax.rem(place_ref[0], 2) == 0
    entry_first = before + before_a * farther
    early = jnp.where(is_first, mine, other)
    early_a = jnp.where(is_first, mine_a, other_a)
    entry_second = early_a * entry_first + early
    keep_ref[...] = jnp.where(is_first, entry_first, entry_second).astype(BF16)
    send_ref[...] = jnp.where(is_first, entry_second, entry_first).astype(BF16)


def small_call(kernel, name, place, arrays, shapes, after=()):
    return call(
        kernel,
        name,
        vmem=4,
        cost=micros(0.5),
        scalars=(place,),
        in_specs=[VMEM] * len(arrays),
        out_specs=[VMEM] * len(shapes),
        out_shape=[jax.ShapeDtypeStruct(s, BF16) for s in shapes],
        after=after,
    )(place, *arrays)


def onward(value, by):
    count = lax.axis_size("seq")
    pairs = []
    for i in range(count):
        up = (i + by, 0) if i + by < count else (i, 1)
        down = (i - by, 1) if i - by >= 0 else (i, 0)
        pairs += [(2 * i, 2 * up[0] + up[1]), (2 * i + 1, 2 * down[0] + down[1])]
    return lax.ppermute(value, ("seq", "ch"), pairs)


class Chain:
    def __init__(self, tag, place, send, mine):
        self.tag, self.place, self.mine = tag, place, mine
        self.count = lax.axis_size("seq")
        self.swap = [(i, i ^ 1) for i in range(self.count)]
        self.other = lax.ppermute(send, "seq", self.swap)
        self.before = self.farther = None
        self.reach = self.farther_reach = 0
        self.apart = 2

    def pair(self, after):
        (self.pair_state,) = small_call(
            pair_kernel, "pair_" + self.tag, self.place, [self.mine, self.other], [self.mine.shape], after
        )
        self.running = self.pair_state
        self.hop()
        return self.pair_state

    def hop(self):
        if self.apart < self.count:
            self.arrived = onward(self.running, self.apart)

    def middle(self, after):
        while self.apart * 2 < self.count:
            self.take(after)
            (self.running,) = small_call(
                functools.partial(chain_kernel, self.reach),
                "chain_" + self.tag,
                self.place,
                [self.pair_state, self.before],
                [self.mine.shape],
                after,
            )
            self.apart *= 2
            self.hop()
        return self.running

    def take(self, after=()):
        if self.before is None:
            self.before, self.reach = self.arrived, self.apart
        else:
            (self.before,) = small_call(
                functools.partial(longer_kernel, self.reach, self.apart),
                "longer_" + self.tag,
                self.place,
                [self.before, self.arrived],
                [self.mine.shape],
                after,
            )
            self.reach = 0

    def entry(self, after):
        shape = self.mine.shape
        if self.apart < self.count:
            if self.before is None:
                self.before, self.reach = self.arrived, self.apart
                self.farther, self.farther_reach = self.arrived, self.count
            else:
                self.farther, self.farther_reach = self.arrived, self.apart
        else:
            self.before = self.farther = self.mine
            self.reach = self.farther_reach = self.count
        half = (shape[0] - EXTRA, shape[1])
        keep, out = small_call(
            functools.partial(entry_kernel, self.reach, self.farther_reach),
            "entry_" + self.tag,
            self.place,
            [self.mine, self.other, self.before, self.farther],
            [half, half],
            after,
        )
        return keep, lax.ppermute(out, "seq", self.swap)


def gated_part(
    head_size, swap, y_refs, bc_ref, cum_ref, keep_ref, other_ref, gate_ref, small_ref, wo_ref, scaled_ref, tile_ref
):
    rows, share = y_refs[0].shape
    inner = share * len(y_refs)
    states = bc_ref.shape[1] // 2
    heads = cum_ref.shape[1]
    half = inner // 2
    since = two_parts(jnp.exp(cum_ref[...]))
    squares = [0.0] * (rows // BLOCK)
    for low in range(0, inner, TILE):
        columns = slice(low, low + TILE)
        y_ref = y_refs[low // share]
        of_share = slice(low % share, low % share + TILE)
        here = slice(low % half, low % half + TILE)
        use_other = swap if low < half else jnp.logical_not(swap)
        entry = jnp.where(use_other, other_ref[:, here], keep_ref[:, here])
        tile_ref[0] = dot(bc_ref[:, states:], entry)
        tile_ref[1] = dot(since, head_matrix(heads, TILE, head_size, low // head_size))
        gain = small_ref[SMALL_TAPS : SMALL_TAPS + 1, columns]
        for i, r in enumerate(range(0, rows, BLOCK)):
            block = slice(r, r + BLOCK)
            gated = y_ref[block, of_share].astype(F32) + tile_ref[0, block, :] * tile_ref[1, block, :]
            gated = gated * gate_ref[block, columns].astype(F32)
            squares[i] += jnp.sum(gated * gated, axis=-1, keepdims=True)
            scaled_ref[block, columns] = (gated * gain).astype(BF16)
    return squares


def part_kernel(head_size, shares, parity_ref, *refs):
    *ins, out_ref, sq_ref, scaled_ref, tile_ref = refs
    squares = gated_part(head_size, parity_ref[0] == 1, ins[:shares], *ins[shares:], scaled_ref, tile_ref)
    for i, square in enumerate(squares):
        sq_ref[i * BLOCK : (i + 1) * BLOCK, :] = jnp.broadcast_to(square, (BLOCK, sq_ref.shape[1]))
    for low in range(0, out_ref.shape[1], TILE):
        out_ref[:, low : low + TILE] = dot(scaled_ref[...], ins[-1][:, low : low + TILE])


def product(back, scaled_ref, weights_ref, part_ref, scale_ref, tile_ref, half_ref, out_ref, first):
    rows, half = out_ref.shape
    for low in range(0, half, TILE):
        columns = slice(first + low, first + low + TILE)
        tile_ref[...] = dot(scaled_ref[...], weights_ref[:, columns])
        for r in range(0, rows, BLOCK):
            block = slice(r, r + BLOCK)
            value = (tile_ref[block, :] + part_ref[block, columns]) * scale_ref[block, :1]
            half_ref[block, low : low + TILE] = value.astype(BF16)

    @pl.when(back == 1)
    def _():
        turn = flip_matrix(TILE)
        for r in range(0, rows, TILE):
            for low in range(0, half, TILE):
                tile = dot(turn, half_ref[r : r + TILE, low : low + TILE]).astype(BF16)
                tile = dot(tile, turn).astype(BF16)
                to_row, to = rows - TILE - r, half - TILE - low
                out_ref[to_row : to_row + TILE, to : to + TILE] = tile

    @pl.when(back != 1)
    def _():
        out_ref[...] = half_ref[...]


def finish_kernel(head_size, shares, full_width, back_ref, parity_ref, *refs):
    *ins, part_ref, psq_ref, send_ref, scaled_ref, scale_ref, tile_ref, half_ref = refs
    squares = gated_part(head_size, parity_ref[0] == 1, ins[:shares], *ins[shares:], scaled_ref, tile_ref)
    for i, square in enumerate(squares):
        block = slice(i * BLOCK, (i + 1) * BLOCK)
        scale = lax.rsqrt((square + psq_ref[block, :1]) / full_width + EPS)
        scale_ref[block, :] = jnp.broadcast_to(scale, (BLOCK, scale_ref.shape[1]))
    product(back_ref[0], scaled_ref, ins[-1], part_ref, scale_ref, tile_ref.at[0], half_ref, send_ref, send_ref.shape[1])


def own_kernel(back_ref, scaled_ref, weights_ref, part_ref, scale_ref, own_ref, tile_ref, half_ref):
    product(back_ref[0], scaled_ref, weights_ref, part_ref, scale_ref, tile_ref, half_ref, own_ref, 0)


def own_call(back, scaled, w_output, part, scale, after):
    rows, width = part.shape
    half = width // 2
    return call(
        own_kernel,
        "own_half",
        vmem=8,
        cost=micros(0.7),
        scalars=(back,),
        in_specs=[VMEM] * 4,
        out_specs=VMEM,
        out_shape=jax.ShapeDtypeStruct((rows, half), BF16),
        scratch=[pltpu.VMEM((rows, TILE), F32), pltpu.VMEM((rows, half), BF16)],
        after=after,
    )(back, scaled, w_output, part, scale)


def finish_call(back, parity, ys, bc, cum, keep, other, gate, small, w_output, full_width=None, partial=None, after=()):
    rows = ys[0].shape[0]
    inner = ys[0].shape[1] * len(ys)
    width = w_output.shape[1]
    half = width // 2
    heads = cum.shape[1]
    arrays = [*ys, bc, cum, keep, other, gate, small, w_output]
    tiles = pltpu.VMEM((2, rows, TILE), F32)
    if partial is None:
        scratch = [pltpu.VMEM((rows, inner), BF16), tiles]
        scalars = (parity,)
        kernel = functools.partial(part_kernel, inner // heads, len(ys))
        out_shape = [jax.ShapeDtypeStruct((rows, width), F32), jax.ShapeDtypeStruct((rows, 128), F32)]
    else:
        scalars = (back, parity)
        scratch = [tiles, pltpu.VMEM((rows, half), BF16)]
        kernel = functools.partial(finish_kernel, inner // heads, len(ys), full_width)
        arrays += list(partial)
        out_shape = [
            jax.ShapeDtypeStruct((rows, half), BF16),
            jax.ShapeDtypeStruct((rows, inner), BF16),
            jax.ShapeDtypeStruct((rows, 128), F32),
        ]
    return call(
        kernel,
        "part" if partial is None else "finish",
        vmem=16,
        cost=micros(3.5),
        scalars=scalars,
        in_specs=[VMEM] * len(arrays),
        out_specs=[VMEM] * len(out_shape),
        out_shape=out_shape,
        scratch=scratch,
        after=after,
    )(*scalars, *arrays)


def total_kernel(mine_ref, theirs_ref, out_hbm, out_ref, sems):
    copies = []
    for i, r in enumerate(range(0, mine_ref.shape[0], CHUNK)):
        for q in range(r, r + CHUNK, BLOCK):
            block = slice(q, q + BLOCK)
            out_ref[block, :] = (mine_ref[block, :].astype(F32) + theirs_ref[block, :].astype(F32)).astype(BF16)
        part = pl.ds(r, CHUNK)
        copies.append(pltpu.make_async_copy(out_ref.at[part, :], out_hbm.at[part, :], sems.at[i]))
        copies[-1].start()
    for copy in copies:
        copy.wait()


def total_call(mine, theirs):
    rows, half = mine.shape
    return call(
        total_kernel,
        "total",
        vmem=4,
        cost=micros(0.8),
        in_specs=[VMEM] * 2,
        out_specs=HBM,
        out_shape=jax.ShapeDtypeStruct((rows, half), BF16),
        scratch=[pltpu.VMEM((rows, half), BF16), pltpu.SemaphoreType.DMA((rows // CHUNK,))],
    )(mine, theirs)


def body(
    tokens,
    hidden,
    embedding,
    w_gate,
    w_inner,
    w_state,
    w_step,
    conv_inner,
    conv_state,
    step_bias,
    decay_rate,
    norm_gain,
    w_output,
):
    swap = [(0, 1), (1, 0)]

    def theirs(a):
        return lax.ppermute(a, "ch", swap)

    core = lax.axis_index("ch").astype(jnp.int32)
    index = lax.axis_index("seq").astype(jnp.int32)
    last = lax.axis_size("seq") - 1
    back = core.reshape(1)
    parity = (index & 1).reshape(1)
    place = (index + core * (last - 2 * index)).reshape(1)
    place, parity, w_inner_3, w_gate_3, w_output_3 = lax.optimization_barrier(
        (place, parity, w_inner, w_gate, w_output)
    )
    w_inner_2 = theirs(w_inner_3)
    normed, tail, small = prepare_call(
        (back, parity, place), hidden, tokens, embedding, conv_inner, norm_gain, step_bias, decay_rate, w_step.T
    )
    halo = onward(tail, 1)
    small_2 = theirs(small)
    w_gate_2 = theirs(w_gate_3)
    w_output_2 = theirs(w_output_3)
    gate_1 = gate_call("own", normed, w_gate)
    bc, bt = maps_call(place, normed, halo, w_state, conv_state, after=[gate_1])
    x_1, cum_1, times_1, send_1, mine_1 = local_call("own", place, parity, normed, halo, bt, w_inner, small)
    chain_1 = Chain("own", place, send_1, mine_1)
    x_2, cum_2, times_2, send_2, mine_2 = local_call(
        "other", place, parity, normed, halo, bt, w_inner_2, small_2, after=[mine_1]
    )
    chain_2 = Chain("other", place, send_2, mine_2)
    done = mark_call(normed, after=[x_2])
    done = chain_1.pair(after=[done])
    y_1 = inside_call("own", x_1, bc, bt, cum_1, times_1, after=[done])
    gate_2 = gate_call("other", normed, w_gate_2, after=[y_1])
    done = chain_2.pair(after=[gate_2])
    done = chain_1.middle(after=[done])
    done = chain_2.middle(after=[done])
    entry_1 = chain_1.entry(after=[done])
    scan_2 = ("other", x_2, bc, bt, cum_2, times_2)
    y_2 = [inside_call(*scan_2, after=[entry_1[0]], part=0, parts=2)]
    entry_2 = chain_2.entry(after=y_2)
    y_2.append(inside_call(*scan_2, after=[entry_2[0]], part=1, parts=2))
    partial = finish_call(
        back, parity, [y_1], bc, cum_1, *entry_1, gate_1, small, w_output, after=y_2
    )
    full_width = float(w_inner.shape[1] * lax.axis_size("ch"))
    send, scaled, scale = finish_call(
        back, parity, y_2, bc, cum_2, *entry_2, gate_2, small_2, w_output_2, full_width, partial
    )
    arriving = theirs(send)
    mine = own_call(back, scaled, w_output_2, partial[0], scale, after=[send])
    return total_call(mine, arriving)


def solution(mesh):
    return jax.shard_map(
        body,
        mesh=mesh,
        in_specs=(
            P(("win", "seq")),
            P(("win", "seq"), None),
            P(),
            P(None, "ch"),
            P(None, "ch"),
            P(),
            P(None, "ch"),
            P(None, "ch"),
            P(),
            P("ch"),
            P("ch"),
            P("ch"),
            P("ch", None),
        ),
        out_specs=P(("win", "seq"), "ch"),
        check_vma=False,
    )
```

```python
import functools

import jax
import jax.numpy as jnp
from jax import lax
from jax.experimental import pallas as pl
from jax.experimental.pallas import tpu as pltpu
from jax.sharding import PartitionSpec as P

F32 = jnp.float32
BF16 = jnp.bfloat16
EPS = 1e-05
HALO = 16
EXTRA = 16
CHUNK = 128
TILE = 256
BLOCK = 64
MB = 1024 * 1024
VMEM = pl.BlockSpec(memory_space=pltpu.VMEM)
HBM = pl.BlockSpec(memory_space=pltpu.HBM)


def call(
    kernel, name, *, vmem, cost, scalars=(), grid=(), in_specs, out_specs, out_shape, scratch=(), after=()
):
    flops, moved, special = cost
    first = len(scalars) + len(in_specs)

    def body(*refs):
        kernel(*refs[:first], *refs[first + len(after) :])

    run = pl.pallas_call(
        body,
        grid_spec=pltpu.PrefetchScalarGridSpec(
            num_scalar_prefetch=len(scalars),
            grid=grid,
            in_specs=list(in_specs) + [pl.BlockSpec(memory_space=pl.ANY)] * len(after),
            out_specs=out_specs,
            scratch_shapes=scratch,
        ),
        out_shape=out_shape,
        compiler_params=pltpu.CompilerParams(
            vmem_limit_bytes=vmem * MB, dimension_semantics=("arbitrary",) * len(grid)
        ),
        cost_estimate=pl.CostEstimate(flops=flops, bytes_accessed=moved, transcendentals=special),
        name=name,
    )
    return lambda *arrays: run(*arrays, *after)


def micros(us):
    return (int(us * 1.1e9), int(us * 1e6), 0)


def dot(a, b):
    return jnp.dot(a, b, preferred_element_type=F32)


def dot_nt(a, b):
    return lax.dot_general(a, b, (((1,), (1,)), ((), ())), preferred_element_type=F32)


def dot_tn(a, b):
    return lax.dot_general(a, b, (((0,), (0,)), ((), ())), preferred_element_type=F32)


def flip_matrix(size):
    rows = lax.broadcasted_iota(jnp.int32, (size, size), 0)
    columns = lax.broadcasted_iota(jnp.int32, (size, size), 1)
    return jnp.where(rows + columns == size - 1, 1.0, 0.0).astype(BF16)


def flip_both(value):
    rows, width = value.shape
    turned = dot(flip_matrix(rows), value).astype(BF16)
    anti = flip_matrix(TILE)
    count = width // TILE
    blocks = [
        dot(turned[:, (count - 1 - k) * TILE : (count - k) * TILE], anti).astype(BF16)
        for k in range(count)
    ]
    return jnp.concatenate(blocks, axis=1)


def silu(v):
    half = 0.5 * v
    return half + half * jnp.tanh(half)


def two_parts(value):
    high = value.astype(BF16)
    low = (value - high.astype(F32)).astype(BF16)
    return jnp.concatenate([high, low], axis=1)


def two_rows(value):
    high = value.astype(BF16).astype(F32)
    return jnp.concatenate([high, value - high], axis=0)


def head_matrix(heads, width, head_size, first_head):
    source = lax.broadcasted_iota(jnp.int32, (2 * heads, width), 0)
    source = jnp.where(source >= heads, source - heads, source)
    target = lax.broadcasted_iota(jnp.int32, (2 * heads, width), 1) // head_size + first_head
    return jnp.where(source == target, 1.0, 0.0).astype(BF16)


def prepare_kernel(
    back_ref,
    parity_ref,
    place_ref,
    hidden_hbm,
    tokens_hbm,
    emb_hbm,
    conv_hbm,
    gain_hbm,
    bias_hbm,
    rate_hbm,
    step_hbm,
    out_ref,
    tail_ref,
    small_ref,
    hidden_ref,
    tokens_ref,
    emb_ref,
    conv_ref,
    gain_ref,
    bias_ref,
    rate_ref,
    step_ref,
    base_ref,
    normed_ref,
    turned_ref,
    sems,
):
    rows = hidden_ref.shape[0]
    kinds = emb_ref.shape[0]
    taps, inner = conv_ref.shape
    heads = bias_ref.shape[1]
    count = rows // CHUNK
    back = back_ref[0] == 1
    whole = [
        (tokens_hbm, tokens_ref),
        (emb_hbm, emb_ref),
        (conv_hbm, conv_ref),
        (gain_hbm, gain_ref),
        (bias_hbm, bias_ref),
        (rate_hbm, rate_ref),
        (step_hbm, step_ref),
    ]
    small_copies = [pltpu.make_async_copy(src, dst, sems.at[count + i]) for i, (src, dst) in enumerate(whole)]
    parts = [pl.ds(r * CHUNK, CHUNK) for r in range(count)]
    copies = [
        pltpu.make_async_copy(hidden_hbm.at[part, :], hidden_ref.at[part, :], sems.at[r])
        for r, part in enumerate(parts)
    ]
    for copy in small_copies[:2] + copies + small_copies[2:]:
        copy.start()
    for copy in small_copies[:2]:
        copy.wait()
    kind = lax.broadcasted_iota(jnp.int32, (kinds, rows), 0)
    onehot = jnp.where(kind == tokens_ref[...], 1.0, 0.0).astype(BF16)
    for r in range(count):
        copies[r].wait()
        low, high = r * CHUNK, (r + 1) * CHUNK
        base_ref[...] = dot_tn(onehot[:, low:high], emb_ref[...])
        for q in range(low, high, HALO):
            block = slice(q, q + HALO)
            merged = hidden_ref[block, :].astype(F32) + base_ref[q - low : q - low + HALO, :]
            merged = merged.astype(BF16).astype(F32)
            mean = jnp.mean(merged * merged, axis=-1, keepdims=True)
            normed_ref[block, :] = (merged * lax.rsqrt(mean + EPS)).astype(BF16)

    @pl.when(back)
    def _():
        turn = flip_matrix(TILE)
        for c in range(0, hidden_ref.shape[1], TILE):
            to = hidden_ref.shape[1] - TILE - c
            for r in range(0, rows, TILE):
                turned = dot(turn, normed_ref[r : r + TILE, c : c + TILE]).astype(BF16)
                turned_ref[r : r + TILE, c : c + TILE] = turned
            for r in range(0, rows, TILE):
                out_ref[rows - TILE - r : rows - r, to : to + TILE] = dot(
                    turned_ref[r : r + TILE, c : c + TILE], turn
                ).astype(BF16)

    @pl.when(jnp.logical_not(back))
    def _():
        out_ref[...] = normed_ref[...]

    tail_ref[...] = out_ref[rows - HALO :, :]
    for copy in small_copies[2:]:
        copy.wait()
    small_ref[:taps, :] = conv_ref[...]
    small_ref[taps : taps + 1, :] = gain_ref[...]
    small_ref[taps + 1 : SMALL_ROWS, :] = jnp.zeros((SMALL_ROWS - taps - 1, inner), F32)
    small_ref[taps + 1 : taps + 2, :heads] = bias_ref[...]
    small_ref[taps + 2 : taps + 3, :heads] = rate_ref[...]
    small_ref[SMALL_ROWS:, :] = step_ref[...].astype(F32)


def prepare_call(scalars, hidden, tokens, embedding, conv, gain, bias, rate, step):
    rows, width = hidden.shape
    inner = conv.shape[1]
    arrays = [hidden, tokens.reshape(1, -1), embedding, conv]
    arrays += [a.reshape(1, -1) for a in (gain, bias, rate)] + [step]
    return call(
        prepare_kernel,
        "prepare",
        vmem=12,
        cost=micros(2.7),
        scalars=scalars,
        in_specs=[HBM] * len(arrays),
        out_specs=[VMEM] * 3,
        out_shape=[
            jax.ShapeDtypeStruct((rows, width), BF16),
            jax.ShapeDtypeStruct((HALO, width), BF16),
            jax.ShapeDtypeStruct((SMALL_ROWS + step.shape[0], inner), F32),
        ],
        scratch=[pltpu.VMEM(a.shape, a.dtype) for a in arrays]
        + [pltpu.VMEM((CHUNK, width), F32)]
        + [pltpu.VMEM((rows, width), BF16)] * 2
        + [pltpu.SemaphoreType.DMA((rows // CHUNK + len(arrays) - 1,))],
    )(*scalars, *(pltpu.with_memory_space_constraint(a, pltpu.HBM) for a in arrays))


def gate_kernel(rows_ref, wg_ref, out_ref, gate_ref):
    rows, inner = out_ref.shape
    for low in range(0, inner, TILE):
        columns = slice(low, low + TILE)
        gate_ref[...] = dot(rows_ref[...], wg_ref[:, columns])
        for r in range(0, rows, BLOCK):
            gate = gate_ref[r : r + BLOCK, :].astype(BF16).astype(F32)
            out_ref[r : r + BLOCK, columns] = silu(gate).astype(BF16)


def gate_call(tag, normed, w_gate, after=()):
    rows = normed.shape[0]
    inner = w_gate.shape[1]
    return call(
        gate_kernel,
        "gate_" + tag,
        vmem=8,
        cost=micros(2.4),
        in_specs=[VMEM] * 2,
        out_specs=VMEM,
        out_shape=jax.ShapeDtypeStruct((rows, inner), BF16),
        scratch=[pltpu.VMEM((rows, TILE), F32)],
        after=after,
    )(normed, w_gate)


def conv_silu(rows_ref, weights, row):
    taps = weights.shape[0]
    ahead = 8
    window = rows_ref[HALO - ahead + row : HALO + row + BLOCK, :]
    total = weights[taps - 1 :, :] * window[ahead:, :]
    for back in range(1, taps):
        total += weights[taps - 1 - back : taps - back, :] * pltpu.roll(window, back, 0)[ahead:, :]
    return silu(total).astype(BF16)


def maps_kernel(place_ref, normed_ref, halo_ref, ws_ref, cs_ref, bc_ref, bt_ref, rows_ref):
    rows = normed_ref.shape[0]
    states = bc_ref.shape[1] // 2
    before = dot(halo_ref[...], ws_ref[...]).astype(BF16).astype(F32)
    rows_ref[:HALO, :] = jnp.where(place_ref[0] >= 1, before, 0.0)
    rows_ref[HALO:, :] = dot(normed_ref[...], ws_ref[...]).astype(BF16).astype(F32)
    weights = cs_ref[...]
    for r in range(0, rows, BLOCK):
        bc_ref[r : r + BLOCK, :] = conv_silu(rows_ref, weights, r)
    bt_ref[...] = bc_ref[:, :states].astype(F32).T.astype(BF16)


def maps_call(place, normed, halo, w_state, conv_state, after=()):
    rows = normed.shape[0]
    both = w_state.shape[1]
    return call(
        maps_kernel,
        "maps",
        vmem=8,
        cost=micros(0.3),
        scalars=(place,),
        in_specs=[VMEM] * 4,
        out_specs=[VMEM] * 2,
        out_shape=[
            jax.ShapeDtypeStruct((rows, both), BF16),
            jax.ShapeDtypeStruct((both // 2, rows), BF16),
        ],
        scratch=[pltpu.VMEM((rows + HALO, both), F32)],
        after=after,
    )(place, normed, halo, w_state, conv_state)


def local_kernel(
    head_size,
    place_ref,
    parity_ref,
    normed_ref,
    halo_ref,
    bt_ref,
    wi_ref,
    small_ref,
    x_ref,
    cum_ref,
    times_ref,
    send_ref,
    mine_ref,
    rows_ref,
    spread_ref,
    scaled_ref,
    left_ref,
    whole_ref,
    payload_ref,
):
    rows = normed_ref.shape[0]
    states = bt_ref.shape[0]
    heads = cum_ref.shape[1]
    taps = SMALL_TAPS

    def project_rows(t):
        weights = wi_ref[:, t * TILE : (t + 1) * TILE]
        before = dot(halo_ref[...], weights).astype(BF16).astype(F32)
        rows_ref[t % 2, :HALO, :] = jnp.where(place_ref[0] >= 1, before, 0.0)
        rows_ref[t % 2, HALO:, :] = dot(normed_ref[...], weights).astype(BF16).astype(F32)

    raw = dot_nt(normed_ref[...], small_ref[SMALL_ROWS:, :].astype(BF16))
    columns = small_ref[:SMALL_ROWS, :CHUNK].T
    raw = raw.T + columns[:heads, taps + 1 : taps + 2]
    step = jnp.maximum(raw, 0.0) + jnp.log1p(jnp.exp(-jnp.abs(raw)))
    logdecay = -step * columns[:heads, taps + 2 : taps + 3]
    high = logdecay.astype(BF16)
    rest = logdecay - high.astype(F32)
    mid = rest.astype(BF16)
    low = (rest - mid.astype(F32)).astype(BF16)
    starts = range(0, rows, CHUNK)
    pieces = [part[:, r : r + CHUNK] for r in starts for part in (high, mid, low)]
    project_rows(0)
    frm = lax.broadcasted_iota(jnp.int32, (CHUNK, CHUNK), 0)
    to = lax.broadcasted_iota(jnp.int32, (CHUNK, CHUNK), 1)
    sums = dot(jnp.concatenate(pieces, axis=0), jnp.where(to >= frm, 1.0, 0.0).astype(BF16))
    run = jnp.zeros((heads, 1), F32)
    cums = []
    for i in range(len(starts)):
        at = 3 * i * heads
        cums.append(sums[at : at + heads] + sums[at + heads : at + 2 * heads] + sums[at + 2 * heads : at + 3 * heads] + run)
        run = cums[-1][:, CHUNK - 1 :]
    cum = jnp.concatenate(cums, axis=1)
    times_ref[:heads, :] = cum
    times_ref[heads:, :] = step
    cum_ref[...] = cum.T
    left_ref[...] = two_rows(step * jnp.exp(run - cum)).T.astype(BF16)
    whole_ref[...] = two_parts(jnp.exp(cum_ref[rows - 1 :, :]))

    inner = x_ref.shape[1]
    half = inner // 2
    tiles = range(inner // TILE)
    onehots = [head_matrix(heads, TILE, head_size, t * (TILE // head_size)) for t in tiles]
    spans = [slice(t * TILE, (t + 1) * TILE) for t in tiles]

    def project(t):
        project_rows(t)
        spread_ref[t % 2] = dot(left_ref[...], onehots[t])

    def combine(t):
        taps_here = small_ref[:taps, spans[t]]
        for r in range(0, rows, BLOCK):
            block = slice(r, r + BLOCK)
            x = conv_silu(rows_ref.at[t % 2], taps_here, r)
            x_ref[block, spans[t]] = x
            scaled_ref[t % 2, block, :] = (x.astype(F32) * spread_ref[t % 2, block, :]).astype(BF16)
        state = dot(bt_ref[...], scaled_ref[t % 2])
        here = slice(t * TILE % half, t * TILE % half + TILE)
        is_mine = jnp.where(parity_ref[0] == t * TILE // half, 1, 0)
        write_payload(payload_ref.at[is_mine], here, state, dot(whole_ref[...], onehots[t]))

    spread_ref[0] = dot(left_ref[...], onehots[0])
    for t in tiles:
        if t + 1 < len(tiles):
            project(t + 1)
        combine(t)
    send_ref[...] = payload_ref[0]
    mine_ref[...] = payload_ref[1]


SMALL_TAPS = 4
SMALL_ROWS = 8


def local_call(tag, place, parity, normed, halo, bt, w_inner, small, after=()):
    rows = normed.shape[0]
    inner = w_inner.shape[1]
    heads = small.shape[0] - SMALL_ROWS
    states = bt.shape[0]
    return call(
        functools.partial(local_kernel, inner // heads),
        "local_" + tag,
        vmem=12,
        cost=micros(5.0),
        scalars=(place, parity),
        in_specs=[VMEM] * 5,
        out_specs=[VMEM] * 5,
        out_shape=[
            jax.ShapeDtypeStruct((rows, inner), BF16),
            jax.ShapeDtypeStruct((rows, heads), F32),
            jax.ShapeDtypeStruct((2 * heads, rows), F32),
            jax.ShapeDtypeStruct((states + EXTRA, inner // 2), BF16),
            jax.ShapeDtypeStruct((states + EXTRA, inner // 2), BF16),
        ],
        scratch=[
            pltpu.VMEM((2, rows + HALO, TILE), F32),
            pltpu.VMEM((2, rows, TILE), F32),
            pltpu.VMEM((2, rows, TILE), BF16),
            pltpu.VMEM((rows, 2 * heads), BF16),
            pltpu.VMEM((1, 2 * heads), BF16),
            pltpu.VMEM((2, states + EXTRA, inner // 2), BF16),
        ],
        after=after,
    )(place, parity, normed, halo, bt, w_inner, small)


def inside_kernel(head_size, head, x_ref, bc_ref, bt_ref, cum_ref, times_ref, y_ref, state_ref):
    rows, width = y_ref.shape
    states = bc_ref.shape[1] // 2
    heads = cum_ref.shape[1]
    length = CHUNK
    last = length - 1
    pair = 2 * head_size
    lane = lax.broadcasted_iota(jnp.int32, (length, pair), 1)
    to = lax.broadcasted_iota(jnp.int32, (length, length), 0)
    frm = lax.broadcasted_iota(jnp.int32, (length, length), 1)

    def chunk(c, before):
        at = slice(c * length, (c + 1) * length)
        bmat = bt_ref[:, at]
        cmat = bc_ref[at, states:]
        scores = jnp.where(to >= frm, dot(cmat, bmat), 0.0)
        cum = cum_ref[at, :]
        cumt = times_ref[:heads, at]
        step = times_ref[heads:, at]
        end = cumt[:, last:]
        entered = c > 0
        leaves = (c + 1) * length < rows
        if entered:
            since = two_rows(jnp.exp(cumt - before)).T.astype(BF16)
        if leaves:
            left = two_rows(step * jnp.exp(end - cumt)).T.astype(BF16)
        for offset in range(0, width, TILE):
            first = head + offset // head_size
            columns = slice(first * head_size, first * head_size + TILE)
            here = slice(offset, offset + TILE)
            onehot = head_matrix(heads, TILE, head_size, first)
            if entered:
                since_here = dot(since, onehot)
                state = state_ref[:, here]
                carried = dot(cmat, state.astype(BF16)) * since_here
            if leaves:
                scaled = (x_ref[at, columns].astype(F32) * dot(left, onehot)).astype(BF16)
                added = dot(bmat, scaled)
                state_ref[:, here] = state * since_here[last:, :] + added if entered else added
            for start in range(0, TILE, pair):
                low = first * head_size + start
                weights = []
                for h in (low // head_size, low // head_size + 1):
                    apart = jnp.minimum(cum[:, h : h + 1] - cumt[h : h + 1, :], 0.0)
                    weights.append((jnp.exp(apart) * (scores * step[h : h + 1, :])).astype(BF16))
                mine = x_ref[at, low : low + pair]
                none = jnp.zeros_like(mine)
                stacked = jnp.concatenate(
                    [jnp.where(lane < head_size, mine, none), jnp.where(lane < head_size, none, mine)], axis=0
                )
                inside = dot(jnp.concatenate(weights, axis=1), stacked)
                if entered:
                    inside += carried[:, start : start + pair]
                y_ref[at, offset + start : offset + start + pair] = inside.astype(BF16)
        return end

    before = jnp.zeros((heads, 1), F32)
    for c in range(rows // length):
        before = chunk(c, before)


def inside_call(tag, x, bc, bt, cum, times, after=(), part=0, parts=1):
    rows, inner = x.shape
    heads = cum.shape[1]
    both = bc.shape[1]
    width = inner // parts
    return call(
        functools.partial(inside_kernel, inner // heads, part * heads // parts),
        "inside_" + tag,
        vmem=8,
        cost=micros(3.2 / parts),
        in_specs=[VMEM] * 5,
        out_specs=VMEM,
        out_shape=jax.ShapeDtypeStruct((rows, width), BF16),
        scratch=[pltpu.VMEM((both // 2, width), F32)],
        after=after,
    )(x, bc, bt, cum, times)


def mark_kernel(rows_ref, out_ref):
    out_ref[...] = rows_ref[: out_ref.shape[0], : out_ref.shape[1]]


def mark_call(value, after):
    return call(
        mark_kernel,
        "mark",
        vmem=4,
        cost=micros(2.4),
        in_specs=[VMEM],
        out_specs=VMEM,
        out_shape=jax.ShapeDtypeStruct((HALO, 128), value.dtype),
        after=after,
    )(value)


def parts_of(ref, known=None):
    states = ref.shape[0] - EXTRA
    state = ref[:states, :].astype(F32)
    extra = ref[states:, :].astype(F32)
    decay = extra[:1] + extra[1:2]
    if known is None:
        return state, decay
    return jnp.where(known, state, 0.0), jnp.where(known, decay, 0.0)


def write_payload(out_ref, columns, state, decay):
    states = state.shape[0]
    out_ref[:states, columns] = state.astype(BF16)
    decay = jnp.broadcast_to(decay, (EXTRA, decay.shape[1]))
    high = decay.astype(BF16).astype(F32)
    place = lax.broadcasted_iota(jnp.int32, decay.shape, 0)
    out_ref[states:, columns] = jnp.where(place == 0, high, decay - high).astype(BF16)


ALL = slice(None)


def pair_kernel(place_ref, mine_ref, other_ref, out_ref):
    mine, mine_a = parts_of(mine_ref)
    other, other_a = parts_of(other_ref)
    is_first = lax.rem(place_ref[0], 2) == 0
    early = jnp.where(is_first, mine, other)
    late = jnp.where(is_first, other, mine)
    late_a = jnp.where(is_first, other_a, mine_a)
    write_payload(out_ref, ALL, late_a * early + late, mine_a * other_a)


def chain_kernel(reach, place_ref, pair_ref, before_ref, out_ref):
    pair, pair_a = parts_of(pair_ref)
    before, before_a = parts_of(before_ref, place_ref[0] >= reach)
    write_payload(out_ref, ALL, pair_a * before + pair, pair_a * before_a)


def longer_kernel(reach, farther_reach, place_ref, before_ref, farther_ref, out_ref):
    before, before_a = parts_of(before_ref, place_ref[0] >= reach)
    farther, farther_a = parts_of(farther_ref, place_ref[0] >= farther_reach)
    write_payload(out_ref, ALL, before + before_a * farther, before_a * farther_a)


def entry_kernel(reach, farther_reach, place_ref, mine_ref, other_ref, before_ref, farther_ref, keep_ref, send_ref):
    mine, mine_a = parts_of(mine_ref)
    other, other_a = parts_of(other_ref)
    before, before_a = parts_of(before_ref, place_ref[0] >= reach)
    farther, _ = parts_of(farther_ref, place_ref[0] >= farther_reach)
    is_first = lax.rem(place_ref[0], 2) == 0
    entry_first = before + before_a * farther
    early = jnp.where(is_first, mine, other)
    early_a = jnp.where(is_first, mine_a, other_a)
    entry_second = early_a * entry_first + early
    keep_ref[...] = jnp.where(is_first, entry_first, entry_second).astype(BF16)
    send_ref[...] = jnp.where(is_first, entry_second, entry_first).astype(BF16)


def small_call(kernel, name, place, arrays, shapes, after=()):
    return call(
        kernel,
        name,
        vmem=4,
        cost=micros(0.5),
        scalars=(place,),
        in_specs=[VMEM] * len(arrays),
        out_specs=[VMEM] * len(shapes),
        out_shape=[jax.ShapeDtypeStruct(s, BF16) for s in shapes],
        after=after,
    )(place, *arrays)


def onward(value, by):
    count = lax.axis_size("seq")
    pairs = []
    for i in range(count):
        up = (i + by, 0) if i + by < count else (i, 1)
        down = (i - by, 1) if i - by >= 0 else (i, 0)
        pairs += [(2 * i, 2 * up[0] + up[1]), (2 * i + 1, 2 * down[0] + down[1])]
    return lax.ppermute(value, ("seq", "ch"), pairs)


class Chain:
    def __init__(self, tag, place, send, mine):
        self.tag, self.place, self.mine = tag, place, mine
        self.count = lax.axis_size("seq")
        self.swap = [(i, i ^ 1) for i in range(self.count)]
        self.other = lax.ppermute(send, "seq", self.swap)
        self.before = self.farther = None
        self.reach = self.farther_reach = 0
        self.apart = 2

    def pair(self, after):
        (self.pair_state,) = small_call(
            pair_kernel, "pair_" + self.tag, self.place, [self.mine, self.other], [self.mine.shape], after
        )
        self.running = self.pair_state
        self.hop()
        return self.pair_state

    def hop(self):
        if self.apart < self.count:
            self.arrived = onward(self.running, self.apart)

    def middle(self, after):
        while self.apart * 2 < self.count:
            self.take(after)
            (self.running,) = small_call(
                functools.partial(chain_kernel, self.reach),
                "chain_" + self.tag,
                self.place,
                [self.pair_state, self.before],
                [self.mine.shape],
                after,
            )
            self.apart *= 2
            self.hop()
        return self.running

    def take(self, after=()):
        if self.before is None:
            self.before, self.reach = self.arrived, self.apart
        else:
            (self.before,) = small_call(
                functools.partial(longer_kernel, self.reach, self.apart),
                "longer_" + self.tag,
                self.place,
                [self.before, self.arrived],
                [self.mine.shape],
                after,
            )
            self.reach = 0

    def entry(self, after):
        shape = self.mine.shape
        if self.apart < self.count:
            if self.before is None:
                self.before, self.reach = self.arrived, self.apart
                self.farther, self.farther_reach = self.arrived, self.count
            else:
                self.farther, self.farther_reach = self.arrived, self.apart
        else:
            self.before = self.farther = self.mine
            self.reach = self.farther_reach = self.count
        half = (shape[0] - EXTRA, shape[1])
        keep, out = small_call(
            functools.partial(entry_kernel, self.reach, self.farther_reach),
            "entry_" + self.tag,
            self.place,
            [self.mine, self.other, self.before, self.farther],
            [half, half],
            after,
        )
        return keep, lax.ppermute(out, "seq", self.swap)


def gated_part(
    head_size, swap, y_refs, bc_ref, cum_ref, keep_ref, other_ref, gate_ref, small_ref, wo_ref, scaled_ref, tile_ref
):
    rows, share = y_refs[0].shape
    inner = share * len(y_refs)
    states = bc_ref.shape[1] // 2
    heads = cum_ref.shape[1]
    half = inner // 2
    since = two_parts(jnp.exp(cum_ref[...]))
    squares = [0.0] * (rows // BLOCK)
    for low in range(0, inner, TILE):
        columns = slice(low, low + TILE)
        y_ref = y_refs[low // share]
        of_share = slice(low % share, low % share + TILE)
        here = slice(low % half, low % half + TILE)
        use_other = swap if low < half else jnp.logical_not(swap)
        entry = jnp.where(use_other, other_ref[:, here], keep_ref[:, here])
        tile_ref[0] = dot(bc_ref[:, states:], entry)
        tile_ref[1] = dot(since, head_matrix(heads, TILE, head_size, low // head_size))
        gain = small_ref[SMALL_TAPS : SMALL_TAPS + 1, columns]
        for i, r in enumerate(range(0, rows, BLOCK)):
            block = slice(r, r + BLOCK)
            gated = y_ref[block, of_share].astype(F32) + tile_ref[0, block, :] * tile_ref[1, block, :]
            gated = gated * gate_ref[block, columns].astype(F32)
            squares[i] += jnp.sum(gated * gated, axis=-1, keepdims=True)
            scaled_ref[block, columns] = (gated * gain).astype(BF16)
    return squares


def part_kernel(head_size, shares, parity_ref, *refs):
    *ins, out_ref, sq_ref, scaled_ref, tile_ref = refs
    squares = gated_part(head_size, parity_ref[0] == 1, ins[:shares], *ins[shares:], scaled_ref, tile_ref)
    for i, square in enumerate(squares):
        sq_ref[i * BLOCK : (i + 1) * BLOCK, :] = jnp.broadcast_to(square, (BLOCK, sq_ref.shape[1]))
    for low in range(0, out_ref.shape[1], TILE):
        out_ref[:, low : low + TILE] = dot(scaled_ref[...], ins[-1][:, low : low + TILE])


def product(back, scaled_ref, weights_ref, part_ref, scale_ref, tile_ref, half_ref, out_ref, first):
    rows, half = out_ref.shape
    for low in range(0, half, TILE):
        columns = slice(first + low, first + low + TILE)
        tile_ref[...] = dot(scaled_ref[...], weights_ref[:, columns])
        for r in range(0, rows, BLOCK):
            block = slice(r, r + BLOCK)
            value = (tile_ref[block, :] + part_ref[block, columns]) * scale_ref[block, :1]
            half_ref[block, low : low + TILE] = value.astype(BF16)

    @pl.when(back == 1)
    def _():
        turn = flip_matrix(TILE)
        for r in range(0, rows, TILE):
            for low in range(0, half, TILE):
                tile = dot(turn, half_ref[r : r + TILE, low : low + TILE]).astype(BF16)
                tile = dot(tile, turn).astype(BF16)
                to_row, to = rows - TILE - r, half - TILE - low
                out_ref[to_row : to_row + TILE, to : to + TILE] = tile

    @pl.when(back != 1)
    def _():
        out_ref[...] = half_ref[...]


def finish_kernel(head_size, shares, full_width, back_ref, parity_ref, *refs):
    *ins, part_ref, psq_ref, send_ref, scaled_ref, scale_ref, tile_ref, half_ref = refs
    squares = gated_part(head_size, parity_ref[0] == 1, ins[:shares], *ins[shares:], scaled_ref, tile_ref)
    for i, square in enumerate(squares):
        block = slice(i * BLOCK, (i + 1) * BLOCK)
        scale = lax.rsqrt((square + psq_ref[block, :1]) / full_width + EPS)
        scale_ref[block, :] = jnp.broadcast_to(scale, (BLOCK, scale_ref.shape[1]))
    product(back_ref[0], scaled_ref, ins[-1], part_ref, scale_ref, tile_ref.at[0], half_ref, send_ref, send_ref.shape[1])


def own_kernel(back_ref, scaled_ref, weights_ref, part_ref, scale_ref, own_ref, tile_ref, half_ref):
    product(back_ref[0], scaled_ref, weights_ref, part_ref, scale_ref, tile_ref, half_ref, own_ref, 0)


def own_call(back, scaled, w_output, part, scale, after):
    rows, width = part.shape
    half = width // 2
    return call(
        own_kernel,
        "own_half",
        vmem=8,
        cost=micros(0.7),
        scalars=(back,),
        in_specs=[VMEM] * 4,
        out_specs=VMEM,
        out_shape=jax.ShapeDtypeStruct((rows, half), BF16),
        scratch=[pltpu.VMEM((rows, TILE), F32), pltpu.VMEM((rows, half), BF16)],
        after=after,
    )(back, scaled, w_output, part, scale)


def finish_call(back, parity, ys, bc, cum, keep, other, gate, small, w_output, full_width=None, partial=None, after=()):
    rows = ys[0].shape[0]
    inner = ys[0].shape[1] * len(ys)
    width = w_output.shape[1]
    half = width // 2
    heads = cum.shape[1]
    arrays = [*ys, bc, cum, keep, other, gate, small, w_output]
    tiles = pltpu.VMEM((2, rows, TILE), F32)
    if partial is None:
        scratch = [pltpu.VMEM((rows, inner), BF16), tiles]
        scalars = (parity,)
        kernel = functools.partial(part_kernel, inner // heads, len(ys))
        out_shape = [jax.ShapeDtypeStruct((rows, width), F32), jax.ShapeDtypeStruct((rows, 128), F32)]
    else:
        scalars = (back, parity)
        scratch = [tiles, pltpu.VMEM((rows, half), BF16)]
        kernel = functools.partial(finish_kernel, inner // heads, len(ys), full_width)
        arrays += list(partial)
        out_shape = [
            jax.ShapeDtypeStruct((rows, half), BF16),
            jax.ShapeDtypeStruct((rows, inner), BF16),
            jax.ShapeDtypeStruct((rows, 128), F32),
        ]
    return call(
        kernel,
        "part" if partial is None else "finish",
        vmem=16,
        cost=micros(3.5),
        scalars=scalars,
        in_specs=[VMEM] * len(arrays),
        out_specs=[VMEM] * len(out_shape),
        out_shape=out_shape,
        scratch=scratch,
        after=after,
    )(*scalars, *arrays)


def total_kernel(mine_ref, theirs_ref, out_hbm, out_ref, sems):
    copies = []
    for i, r in enumerate(range(0, mine_ref.shape[0], CHUNK)):
        for q in range(r, r + CHUNK, BLOCK):
            block = slice(q, q + BLOCK)
            out_ref[block, :] = (mine_ref[block, :].astype(F32) + theirs_ref[block, :].astype(F32)).astype(BF16)
        part = pl.ds(r, CHUNK)
        copies.append(pltpu.make_async_copy(out_ref.at[part, :], out_hbm.at[part, :], sems.at[i]))
        copies[-1].start()
    for copy in copies:
        copy.wait()


def total_call(mine, theirs):
    rows, half = mine.shape
    return call(
        total_kernel,
        "total",
        vmem=4,
        cost=micros(0.8),
        in_specs=[VMEM] * 2,
        out_specs=HBM,
        out_shape=jax.ShapeDtypeStruct((rows, half), BF16),
        scratch=[pltpu.VMEM((rows, half), BF16), pltpu.SemaphoreType.DMA((rows // CHUNK,))],
    )(mine, theirs)


def body(
    tokens,
    hidden,
    embedding,
    w_gate,
    w_inner,
    w_state,
    w_step,
    conv_inner,
    conv_state,
    step_bias,
    decay_rate,
    norm_gain,
    w_output,
):
    swap = [(0, 1), (1, 0)]

    def theirs(a):
        return lax.ppermute(a, "ch", swap)

    core = lax.axis_index("ch").astype(jnp.int32)
    index = lax.axis_index("seq").astype(jnp.int32)
    last = lax.axis_size("seq") - 1
    back = core.reshape(1)
    parity = (index & 1).reshape(1)
    place = (index + core * (last - 2 * index)).reshape(1)
    place, parity, w_inner_3, w_gate_3, w_output_3 = lax.optimization_barrier(
        (place, parity, w_inner, w_gate, w_output)
    )
    w_inner_2 = theirs(w_inner_3)
    normed, tail, small = prepare_call(
        (back, parity, place), hidden, tokens, embedding, conv_inner, norm_gain, step_bias, decay_rate, w_step.T
    )
    halo = onward(tail, 1)
    small_2 = theirs(small)
    w_gate_2 = theirs(w_gate_3)
    w_output_2 = theirs(w_output_3)
    gate_1 = gate_call("own", normed, w_gate)
    bc, bt = maps_call(place, normed, halo, w_state, conv_state, after=[gate_1])
    x_1, cum_1, times_1, send_1, mine_1 = local_call("own", place, parity, normed, halo, bt, w_inner, small)
    chain_1 = Chain("own", place, send_1, mine_1)
    x_2, cum_2, times_2, send_2, mine_2 = local_call(
        "other", place, parity, normed, halo, bt, w_inner_2, small_2, after=[mine_1]
    )
    chain_2 = Chain("other", place, send_2, mine_2)
    done = mark_call(normed, after=[x_2])
    done = chain_1.pair(after=[done])
    y_1 = inside_call("own", x_1, bc, bt, cum_1, times_1, after=[done])
    done = chain_2.pair(after=[y_1])
    done = chain_1.middle(after=[done])
    gate_2 = gate_call("other", normed, w_gate_2, after=[done])
    done = chain_2.middle(after=[gate_2])
    entry_1 = chain_1.entry(after=[done])
    scan_2 = ("other", x_2, bc, bt, cum_2, times_2)
    y_2 = [inside_call(*scan_2, after=[entry_1[0]], part=0, parts=2)]
    entry_2 = chain_2.entry(after=y_2)
    y_2.append(inside_call(*scan_2, after=[entry_2[0]], part=1, parts=2))
    partial = finish_call(
        back, parity, [y_1], bc, cum_1, *entry_1, gate_1, small, w_output, after=y_2
    )
    full_width = float(w_inner.shape[1] * lax.axis_size("ch"))
    send, scaled, scale = finish_call(
        back, parity, y_2, bc, cum_2, *entry_2, gate_2, small_2, w_output_2, full_width, partial
    )
    arriving = theirs(send)
    mine = own_call(back, scaled, w_output_2, partial[0], scale, after=[send])
    return total_call(mine, arriving)


def solution(mesh):
    return jax.shard_map(
        body,
        mesh=mesh,
        in_specs=(
            P(("win", "seq")),
            P(("win", "seq"), None),
            P(),
            P(None, "ch"),
            P(None, "ch"),
            P(),
            P(None, "ch"),
            P(None, "ch"),
            P(),
            P("ch"),
            P("ch"),
            P("ch"),
            P("ch", None),
        ),
        out_specs=P(("win", "seq"), "ch"),
        check_vma=False,
    )
```

```python
import functools

import jax
import jax.numpy as jnp
from jax import lax
from jax.experimental import pallas as pl
from jax.experimental.pallas import tpu as pltpu
from jax.sharding import PartitionSpec as P

F32 = jnp.float32
BF16 = jnp.bfloat16
EPS = 1e-05
HALO = 16
EXTRA = 16
CHUNK = 128
TILE = 256
BLOCK = 64
MB = 1024 * 1024
VMEM = pl.BlockSpec(memory_space=pltpu.VMEM)
HBM = pl.BlockSpec(memory_space=pltpu.HBM)


def call(
    kernel, name, *, vmem, cost, scalars=(), grid=(), in_specs, out_specs, out_shape, scratch=(), after=()
):
    flops, moved, special = cost
    first = len(scalars) + len(in_specs)

    def body(*refs):
        kernel(*refs[:first], *refs[first + len(after) :])

    run = pl.pallas_call(
        body,
        grid_spec=pltpu.PrefetchScalarGridSpec(
            num_scalar_prefetch=len(scalars),
            grid=grid,
            in_specs=list(in_specs) + [pl.BlockSpec(memory_space=pl.ANY)] * len(after),
            out_specs=out_specs,
            scratch_shapes=scratch,
        ),
        out_shape=out_shape,
        compiler_params=pltpu.CompilerParams(
            vmem_limit_bytes=vmem * MB, dimension_semantics=("arbitrary",) * len(grid)
        ),
        cost_estimate=pl.CostEstimate(flops=flops, bytes_accessed=moved, transcendentals=special),
        name=name,
    )
    return lambda *arrays: run(*arrays, *after)


def micros(us):
    return (int(us * 1.1e9), int(us * 1e6), 0)


def dot(a, b):
    return jnp.dot(a, b, preferred_element_type=F32)


def dot_nt(a, b):
    return lax.dot_general(a, b, (((1,), (1,)), ((), ())), preferred_element_type=F32)


def dot_tn(a, b):
    return lax.dot_general(a, b, (((0,), (0,)), ((), ())), preferred_element_type=F32)


def flip_matrix(size):
    rows = lax.broadcasted_iota(jnp.int32, (size, size), 0)
    columns = lax.broadcasted_iota(jnp.int32, (size, size), 1)
    return jnp.where(rows + columns == size - 1, 1.0, 0.0).astype(BF16)


def flip_both(value):
    rows, width = value.shape
    turned = dot(flip_matrix(rows), value).astype(BF16)
    anti = flip_matrix(TILE)
    count = width // TILE
    blocks = [
        dot(turned[:, (count - 1 - k) * TILE : (count - k) * TILE], anti).astype(BF16)
        for k in range(count)
    ]
    return jnp.concatenate(blocks, axis=1)


def silu(v):
    half = 0.5 * v
    return half + half * jnp.tanh(half)


def two_parts(value):
    high = value.astype(BF16)
    low = (value - high.astype(F32)).astype(BF16)
    return jnp.concatenate([high, low], axis=1)


def two_rows(value):
    high = value.astype(BF16).astype(F32)
    return jnp.concatenate([high, value - high], axis=0)


def head_matrix(heads, width, head_size, first_head):
    source = lax.broadcasted_iota(jnp.int32, (2 * heads, width), 0)
    source = jnp.where(source >= heads, source - heads, source)
    target = lax.broadcasted_iota(jnp.int32, (2 * heads, width), 1) // head_size + first_head
    return jnp.where(source == target, 1.0, 0.0).astype(BF16)


def prepare_kernel(
    back_ref,
    parity_ref,
    place_ref,
    hidden_hbm,
    tokens_hbm,
    emb_hbm,
    conv_hbm,
    gain_hbm,
    bias_hbm,
    rate_hbm,
    step_hbm,
    out_ref,
    tail_ref,
    small_ref,
    hidden_ref,
    tokens_ref,
    emb_ref,
    conv_ref,
    gain_ref,
    bias_ref,
    rate_ref,
    step_ref,
    base_ref,
    normed_ref,
    turned_ref,
    sems,
):
    rows = hidden_ref.shape[0]
    kinds = emb_ref.shape[0]
    taps, inner = conv_ref.shape
    heads = bias_ref.shape[1]
    count = rows // CHUNK
    back = back_ref[0] == 1
    whole = [
        (tokens_hbm, tokens_ref),
        (emb_hbm, emb_ref),
        (conv_hbm, conv_ref),
        (gain_hbm, gain_ref),
        (bias_hbm, bias_ref),
        (rate_hbm, rate_ref),
        (step_hbm, step_ref),
    ]
    small_copies = [pltpu.make_async_copy(src, dst, sems.at[count + i]) for i, (src, dst) in enumerate(whole)]
    parts = [pl.ds(r * CHUNK, CHUNK) for r in range(count)]
    copies = [
        pltpu.make_async_copy(hidden_hbm.at[part, :], hidden_ref.at[part, :], sems.at[r])
        for r, part in enumerate(parts)
    ]
    for copy in small_copies[:2] + copies + small_copies[2:]:
        copy.start()
    for copy in small_copies[:2]:
        copy.wait()
    kind = lax.broadcasted_iota(jnp.int32, (kinds, rows), 0)
    onehot = jnp.where(kind == tokens_ref[...], 1.0, 0.0).astype(BF16)
    for r in range(count):
        copies[r].wait()
        low, high = r * CHUNK, (r + 1) * CHUNK
        base_ref[...] = dot_tn(onehot[:, low:high], emb_ref[...])
        for q in range(low, high, HALO):
            block = slice(q, q + HALO)
            merged = hidden_ref[block, :].astype(F32) + base_ref[q - low : q - low + HALO, :]
            merged = merged.astype(BF16).astype(F32)
            mean = jnp.mean(merged * merged, axis=-1, keepdims=True)
            normed_ref[block, :] = (merged * lax.rsqrt(mean + EPS)).astype(BF16)

    @pl.when(back)
    def _():
        turn = flip_matrix(TILE)
        for c in range(0, hidden_ref.shape[1], TILE):
            to = hidden_ref.shape[1] - TILE - c
            for r in range(0, rows, TILE):
                turned = dot(turn, normed_ref[r : r + TILE, c : c + TILE]).astype(BF16)
                turned_ref[r : r + TILE, c : c + TILE] = turned
            for r in range(0, rows, TILE):
                out_ref[rows - TILE - r : rows - r, to : to + TILE] = dot(
                    turned_ref[r : r + TILE, c : c + TILE], turn
                ).astype(BF16)

    @pl.when(jnp.logical_not(back))
    def _():
        out_ref[...] = normed_ref[...]

    tail_ref[...] = out_ref[rows - HALO :, :]
    for copy in small_copies[2:]:
        copy.wait()
    small_ref[:taps, :] = conv_ref[...]
    small_ref[taps : taps + 1, :] = gain_ref[...]
    small_ref[taps + 1 : SMALL_ROWS, :] = jnp.zeros((SMALL_ROWS - taps - 1, inner), F32)
    small_ref[taps + 1 : taps + 2, :heads] = bias_ref[...]
    small_ref[taps + 2 : taps + 3, :heads] = rate_ref[...]
    small_ref[SMALL_ROWS:, :] = step_ref[...].astype(F32)


def prepare_call(scalars, hidden, tokens, embedding, conv, gain, bias, rate, step):
    rows, width = hidden.shape
    inner = conv.shape[1]
    arrays = [hidden, tokens.reshape(1, -1), embedding, conv]
    arrays += [a.reshape(1, -1) for a in (gain, bias, rate)] + [step]
    return call(
        prepare_kernel,
        "prepare",
        vmem=12,
        cost=micros(2.7),
        scalars=scalars,
        in_specs=[HBM] * len(arrays),
        out_specs=[VMEM] * 3,
        out_shape=[
            jax.ShapeDtypeStruct((rows, width), BF16),
            jax.ShapeDtypeStruct((HALO, width), BF16),
            jax.ShapeDtypeStruct((SMALL_ROWS + step.shape[0], inner), F32),
        ],
        scratch=[pltpu.VMEM(a.shape, a.dtype) for a in arrays]
        + [pltpu.VMEM((CHUNK, width), F32)]
        + [pltpu.VMEM((rows, width), BF16)] * 2
        + [pltpu.SemaphoreType.DMA((rows // CHUNK + len(arrays) - 1,))],
    )(*scalars, *(pltpu.with_memory_space_constraint(a, pltpu.HBM) for a in arrays))


def gate_kernel(rows_ref, wg_ref, out_ref, gate_ref):
    rows, inner = out_ref.shape
    for low in range(0, inner, TILE):
        columns = slice(low, low + TILE)
        gate_ref[...] = dot(rows_ref[...], wg_ref[:, columns])
        for r in range(0, rows, BLOCK):
            gate = gate_ref[r : r + BLOCK, :].astype(BF16).astype(F32)
            out_ref[r : r + BLOCK, columns] = silu(gate).astype(BF16)


def gate_call(tag, normed, w_gate, after=()):
    rows = normed.shape[0]
    inner = w_gate.shape[1]
    return call(
        gate_kernel,
        "gate_" + tag,
        vmem=8,
        cost=micros(2.4),
        in_specs=[VMEM] * 2,
        out_specs=VMEM,
        out_shape=jax.ShapeDtypeStruct((rows, inner), BF16),
        scratch=[pltpu.VMEM((rows, TILE), F32)],
        after=after,
    )(normed, w_gate)


def conv_silu(rows_ref, weights, row):
    taps = weights.shape[0]
    ahead = 8
    window = rows_ref[HALO - ahead + row : HALO + row + BLOCK, :]
    total = weights[taps - 1 :, :] * window[ahead:, :]
    for back in range(1, taps):
        total += weights[taps - 1 - back : taps - back, :] * pltpu.roll(window, back, 0)[ahead:, :]
    return silu(total).astype(BF16)


def maps_kernel(place_ref, normed_ref, halo_ref, ws_ref, cs_ref, bc_ref, bt_ref, rows_ref):
    rows = normed_ref.shape[0]
    states = bc_ref.shape[1] // 2
    before = dot(halo_ref[...], ws_ref[...]).astype(BF16).astype(F32)
    rows_ref[:HALO, :] = jnp.where(place_ref[0] >= 1, before, 0.0)
    rows_ref[HALO:, :] = dot(normed_ref[...], ws_ref[...]).astype(BF16).astype(F32)
    weights = cs_ref[...]
    for r in range(0, rows, BLOCK):
        bc_ref[r : r + BLOCK, :] = conv_silu(rows_ref, weights, r)
    bt_ref[...] = bc_ref[:, :states].astype(F32).T.astype(BF16)


def maps_call(place, normed, halo, w_state, conv_state, after=()):
    rows = normed.shape[0]
    both = w_state.shape[1]
    return call(
        maps_kernel,
        "maps",
        vmem=8,
        cost=micros(0.3),
        scalars=(place,),
        in_specs=[VMEM] * 4,
        out_specs=[VMEM] * 2,
        out_shape=[
            jax.ShapeDtypeStruct((rows, both), BF16),
            jax.ShapeDtypeStruct((both // 2, rows), BF16),
        ],
        scratch=[pltpu.VMEM((rows + HALO, both), F32)],
        after=after,
    )(place, normed, halo, w_state, conv_state)


def local_kernel(
    head_size,
    place_ref,
    parity_ref,
    normed_ref,
    halo_ref,
    bt_ref,
    wi_ref,
    small_ref,
    x_ref,
    cum_ref,
    times_ref,
    send_ref,
    mine_ref,
    rows_ref,
    spread_ref,
    scaled_ref,
    left_ref,
    whole_ref,
    payload_ref,
):
    rows = normed_ref.shape[0]
    states = bt_ref.shape[0]
    heads = cum_ref.shape[1]
    taps = SMALL_TAPS

    def project_rows(t):
        weights = wi_ref[:, t * TILE : (t + 1) * TILE]
        before = dot(halo_ref[...], weights).astype(BF16).astype(F32)
        rows_ref[t % 2, :HALO, :] = jnp.where(place_ref[0] >= 1, before, 0.0)
        rows_ref[t % 2, HALO:, :] = dot(normed_ref[...], weights).astype(BF16).astype(F32)

    raw = dot_nt(normed_ref[...], small_ref[SMALL_ROWS:, :].astype(BF16))
    columns = small_ref[:SMALL_ROWS, :CHUNK].T
    raw = raw.T + columns[:heads, taps + 1 : taps + 2]
    step = jnp.maximum(raw, 0.0) + jnp.log1p(jnp.exp(-jnp.abs(raw)))
    logdecay = -step * columns[:heads, taps + 2 : taps + 3]
    high = logdecay.astype(BF16)
    rest = logdecay - high.astype(F32)
    mid = rest.astype(BF16)
    low = (rest - mid.astype(F32)).astype(BF16)
    starts = range(0, rows, CHUNK)
    pieces = [part[:, r : r + CHUNK] for r in starts for part in (high, mid, low)]
    project_rows(0)
    frm = lax.broadcasted_iota(jnp.int32, (CHUNK, CHUNK), 0)
    to = lax.broadcasted_iota(jnp.int32, (CHUNK, CHUNK), 1)
    sums = dot(jnp.concatenate(pieces, axis=0), jnp.where(to >= frm, 1.0, 0.0).astype(BF16))
    run = jnp.zeros((heads, 1), F32)
    cums = []
    for i in range(len(starts)):
        at = 3 * i * heads
        cums.append(sums[at : at + heads] + sums[at + heads : at + 2 * heads] + sums[at + 2 * heads : at + 3 * heads] + run)
        run = cums[-1][:, CHUNK - 1 :]
    cum = jnp.concatenate(cums, axis=1)
    times_ref[:heads, :] = cum
    times_ref[heads:, :] = step
    cum_ref[...] = cum.T
    left_ref[...] = two_rows(step * jnp.exp(run - cum)).T.astype(BF16)
    whole_ref[...] = two_parts(jnp.exp(cum_ref[rows - 1 :, :]))

    inner = x_ref.shape[1]
    half = inner // 2
    tiles = range(inner // TILE)
    onehots = [head_matrix(heads, TILE, head_size, t * (TILE // head_size)) for t in tiles]
    spans = [slice(t * TILE, (t + 1) * TILE) for t in tiles]

    def project(t):
        project_rows(t)
        spread_ref[t % 2] = dot(left_ref[...], onehots[t])

    def combine(t):
        taps_here = small_ref[:taps, spans[t]]
        for r in range(0, rows, BLOCK):
            block = slice(r, r + BLOCK)
            x = conv_silu(rows_ref.at[t % 2], taps_here, r)
            x_ref[block, spans[t]] = x
            scaled_ref[t % 2, block, :] = (x.astype(F32) * spread_ref[t % 2, block, :]).astype(BF16)
        state = dot(bt_ref[...], scaled_ref[t % 2])
        here = slice(t * TILE % half, t * TILE % half + TILE)
        is_mine = jnp.where(parity_ref[0] == t * TILE // half, 1, 0)
        write_payload(payload_ref.at[is_mine], here, state, dot(whole_ref[...], onehots[t]))

    spread_ref[0] = dot(left_ref[...], onehots[0])
    for t in tiles:
        if t + 1 < len(tiles):
            project(t + 1)
        combine(t)
    send_ref[...] = payload_ref[0]
    mine_ref[...] = payload_ref[1]


SMALL_TAPS = 4
SMALL_ROWS = 8


def local_call(tag, place, parity, normed, halo, bt, w_inner, small, after=()):
    rows = normed.shape[0]
    inner = w_inner.shape[1]
    heads = small.shape[0] - SMALL_ROWS
    states = bt.shape[0]
    return call(
        functools.partial(local_kernel, inner // heads),
        "local_" + tag,
        vmem=12,
        cost=micros(5.0),
        scalars=(place, parity),
        in_specs=[VMEM] * 5,
        out_specs=[VMEM] * 5,
        out_shape=[
            jax.ShapeDtypeStruct((rows, inner), BF16),
            jax.ShapeDtypeStruct((rows, heads), F32),
            jax.ShapeDtypeStruct((2 * heads, rows), F32),
            jax.ShapeDtypeStruct((states + EXTRA, inner // 2), BF16),
            jax.ShapeDtypeStruct((states + EXTRA, inner // 2), BF16),
        ],
        scratch=[
            pltpu.VMEM((2, rows + HALO, TILE), F32),
            pltpu.VMEM((2, rows, TILE), F32),
            pltpu.VMEM((2, rows, TILE), BF16),
            pltpu.VMEM((rows, 2 * heads), BF16),
            pltpu.VMEM((1, 2 * heads), BF16),
            pltpu.VMEM((2, states + EXTRA, inner // 2), BF16),
        ],
        after=after,
    )(place, parity, normed, halo, bt, w_inner, small)


def inside_kernel(head_size, head, x_ref, bc_ref, bt_ref, cum_ref, times_ref, y_ref, state_ref):
    rows, width = y_ref.shape
    states = bc_ref.shape[1] // 2
    heads = cum_ref.shape[1]
    length = CHUNK
    last = length - 1
    pair = 2 * head_size
    lane = lax.broadcasted_iota(jnp.int32, (length, pair), 1)
    to = lax.broadcasted_iota(jnp.int32, (length, length), 0)
    frm = lax.broadcasted_iota(jnp.int32, (length, length), 1)

    def chunk(c, before):
        at = slice(c * length, (c + 1) * length)
        bmat = bt_ref[:, at]
        cmat = bc_ref[at, states:]
        scores = jnp.where(to >= frm, dot(cmat, bmat), 0.0)
        cum = cum_ref[at, :]
        cumt = times_ref[:heads, at]
        step = times_ref[heads:, at]
        end = cumt[:, last:]
        entered = c > 0
        leaves = (c + 1) * length < rows
        if entered:
            since = two_rows(jnp.exp(cumt - before)).T.astype(BF16)
        if leaves:
            left = two_rows(step * jnp.exp(end - cumt)).T.astype(BF16)
        for offset in range(0, width, TILE):
            first = head + offset // head_size
            columns = slice(first * head_size, first * head_size + TILE)
            here = slice(offset, offset + TILE)
            onehot = head_matrix(heads, TILE, head_size, first)
            if entered:
                since_here = dot(since, onehot)
                state = state_ref[:, here]
                carried = dot(cmat, state.astype(BF16)) * since_here
            if leaves:
                scaled = (x_ref[at, columns].astype(F32) * dot(left, onehot)).astype(BF16)
                added = dot(bmat, scaled)
                state_ref[:, here] = state * since_here[last:, :] + added if entered else added
            for start in range(0, TILE, pair):
                low = first * head_size + start
                weights = []
                for h in (low // head_size, low // head_size + 1):
                    apart = jnp.minimum(cum[:, h : h + 1] - cumt[h : h + 1, :], 0.0)
                    weights.append((jnp.exp(apart) * (scores * step[h : h + 1, :])).astype(BF16))
                mine = x_ref[at, low : low + pair]
                none = jnp.zeros_like(mine)
                stacked = jnp.concatenate(
                    [jnp.where(lane < head_size, mine, none), jnp.where(lane < head_size, none, mine)], axis=0
                )
                inside = dot(jnp.concatenate(weights, axis=1), stacked)
                if entered:
                    inside += carried[:, start : start + pair]
                y_ref[at, offset + start : offset + start + pair] = inside.astype(BF16)
        return end

    before = jnp.zeros((heads, 1), F32)
    for c in range(rows // length):
        before = chunk(c, before)


def inside_call(tag, x, bc, bt, cum, times, after=(), part=0, parts=1):
    rows, inner = x.shape
    heads = cum.shape[1]
    both = bc.shape[1]
    width = inner // parts
    return call(
        functools.partial(inside_kernel, inner // heads, part * heads // parts),
        "inside_" + tag,
        vmem=8,
        cost=micros(3.2 / parts),
        in_specs=[VMEM] * 5,
        out_specs=VMEM,
        out_shape=jax.ShapeDtypeStruct((rows, width), BF16),
        scratch=[pltpu.VMEM((both // 2, width), F32)],
        after=after,
    )(x, bc, bt, cum, times)


def mark_kernel(rows_ref, out_ref):
    out_ref[...] = rows_ref[: out_ref.shape[0], : out_ref.shape[1]]


def mark_call(value, after):
    return call(
        mark_kernel,
        "mark",
        vmem=4,
        cost=micros(2.4),
        in_specs=[VMEM],
        out_specs=VMEM,
        out_shape=jax.ShapeDtypeStruct((HALO, 128), value.dtype),
        after=after,
    )(value)


def parts_of(ref, known=None):
    states = ref.shape[0] - EXTRA
    state = ref[:states, :].astype(F32)
    extra = ref[states:, :].astype(F32)
    decay = extra[:1] + extra[1:2]
    if known is None:
        return state, decay
    return jnp.where(known, state, 0.0), jnp.where(known, decay, 0.0)


def write_payload(out_ref, columns, state, decay):
    states = state.shape[0]
    out_ref[:states, columns] = state.astype(BF16)
    decay = jnp.broadcast_to(decay, (EXTRA, decay.shape[1]))
    high = decay.astype(BF16).astype(F32)
    place = lax.broadcasted_iota(jnp.int32, decay.shape, 0)
    out_ref[states:, columns] = jnp.where(place == 0, high, decay - high).astype(BF16)


ALL = slice(None)


def pair_kernel(place_ref, mine_ref, other_ref, out_ref):
    mine, mine_a = parts_of(mine_ref)
    other, other_a = parts_of(other_ref)
    is_first = lax.rem(place_ref[0], 2) == 0
    early = jnp.where(is_first, mine, other)
    late = jnp.where(is_first, other, mine)
    late_a = jnp.where(is_first, other_a, mine_a)
    write_payload(out_ref, ALL, late_a * early + late, mine_a * other_a)


def chain_kernel(reach, place_ref, pair_ref, before_ref, out_ref):
    pair, pair_a = parts_of(pair_ref)
    before, before_a = parts_of(before_ref, place_ref[0] >= reach)
    write_payload(out_ref, ALL, pair_a * before + pair, pair_a * before_a)


def longer_kernel(reach, farther_reach, place_ref, before_ref, farther_ref, out_ref):
    before, before_a = parts_of(before_ref, place_ref[0] >= reach)
    farther, farther_a = parts_of(farther_ref, place_ref[0] >= farther_reach)
    write_payload(out_ref, ALL, before + before_a * farther, before_a * farther_a)


def entry_kernel(reach, farther_reach, place_ref, mine_ref, other_ref, before_ref, farther_ref, keep_ref, send_ref):
    mine, mine_a = parts_of(mine_ref)
    other, other_a = parts_of(other_ref)
    before, before_a = parts_of(before_ref, place_ref[0] >= reach)
    farther, _ = parts_of(farther_ref, place_ref[0] >= farther_reach)
    is_first = lax.rem(place_ref[0], 2) == 0
    entry_first = before + before_a * farther
    early = jnp.where(is_first, mine, other)
    early_a = jnp.where(is_first, mine_a, other_a)
    entry_second = early_a * entry_first + early
    keep_ref[...] = jnp.where(is_first, entry_first, entry_second).astype(BF16)
    send_ref[...] = jnp.where(is_first, entry_second, entry_first).astype(BF16)


def small_call(kernel, name, place, arrays, shapes, after=()):
    return call(
        kernel,
        name,
        vmem=4,
        cost=micros(0.5),
        scalars=(place,),
        in_specs=[VMEM] * len(arrays),
        out_specs=[VMEM] * len(shapes),
        out_shape=[jax.ShapeDtypeStruct(s, BF16) for s in shapes],
        after=after,
    )(place, *arrays)


def onward(value, by):
    count = lax.axis_size("seq")
    pairs = []
    for i in range(count):
        up = (i + by, 0) if i + by < count else (i, 1)
        down = (i - by, 1) if i - by >= 0 else (i, 0)
        pairs += [(2 * i, 2 * up[0] + up[1]), (2 * i + 1, 2 * down[0] + down[1])]
    return lax.ppermute(value, ("seq", "ch"), pairs)


class Chain:
    def __init__(self, tag, place, send, mine):
        self.tag, self.place, self.mine = tag, place, mine
        self.count = lax.axis_size("seq")
        self.swap = [(i, i ^ 1) for i in range(self.count)]
        self.other = lax.ppermute(send, "seq", self.swap)
        self.before = self.farther = None
        self.reach = self.farther_reach = 0
        self.apart = 2

    def pair(self, after):
        (self.pair_state,) = small_call(
            pair_kernel, "pair_" + self.tag, self.place, [self.mine, self.other], [self.mine.shape], after
        )
        self.running = self.pair_state
        self.hop()
        return self.pair_state

    def hop(self):
        if self.apart < self.count:
            self.arrived = onward(self.running, self.apart)

    def middle(self, after):
        while self.apart * 2 < self.count:
            self.take(after)
            (self.running,) = small_call(
                functools.partial(chain_kernel, self.reach),
                "chain_" + self.tag,
                self.place,
                [self.pair_state, self.before],
                [self.mine.shape],
                after,
            )
            self.apart *= 2
            self.hop()
        return self.running

    def take(self, after=()):
        if self.before is None:
            self.before, self.reach = self.arrived, self.apart
        else:
            (self.before,) = small_call(
                functools.partial(longer_kernel, self.reach, self.apart),
                "longer_" + self.tag,
                self.place,
                [self.before, self.arrived],
                [self.mine.shape],
                after,
            )
            self.reach = 0

    def entry(self, after):
        shape = self.mine.shape
        if self.apart < self.count:
            if self.before is None:
                self.before, self.reach = self.arrived, self.apart
                self.farther, self.farther_reach = self.arrived, self.count
            else:
                self.farther, self.farther_reach = self.arrived, self.apart
        else:
            self.before = self.farther = self.mine
            self.reach = self.farther_reach = self.count
        half = (shape[0] - EXTRA, shape[1])
        keep, out = small_call(
            functools.partial(entry_kernel, self.reach, self.farther_reach),
            "entry_" + self.tag,
            self.place,
            [self.mine, self.other, self.before, self.farther],
            [half, half],
            after,
        )
        return keep, lax.ppermute(out, "seq", self.swap)


def gated_part(
    head_size, swap, y_refs, bc_ref, cum_ref, keep_ref, other_ref, gate_ref, small_ref, wo_ref, scaled_ref, tile_ref
):
    rows, share = y_refs[0].shape
    inner = share * len(y_refs)
    states = bc_ref.shape[1] // 2
    heads = cum_ref.shape[1]
    half = inner // 2
    since = two_parts(jnp.exp(cum_ref[...]))
    squares = [0.0] * (rows // BLOCK)
    for low in range(0, inner, TILE):
        columns = slice(low, low + TILE)
        y_ref = y_refs[low // share]
        of_share = slice(low % share, low % share + TILE)
        here = slice(low % half, low % half + TILE)
        use_other = swap if low < half else jnp.logical_not(swap)
        entry = jnp.where(use_other, other_ref[:, here], keep_ref[:, here])
        tile_ref[0] = dot(bc_ref[:, states:], entry)
        tile_ref[1] = dot(since, head_matrix(heads, TILE, head_size, low // head_size))
        gain = small_ref[SMALL_TAPS : SMALL_TAPS + 1, columns]
        for i, r in enumerate(range(0, rows, BLOCK)):
            block = slice(r, r + BLOCK)
            gated = y_ref[block, of_share].astype(F32) + tile_ref[0, block, :] * tile_ref[1, block, :]
            gated = gated * gate_ref[block, columns].astype(F32)
            squares[i] += jnp.sum(gated * gated, axis=-1, keepdims=True)
            scaled_ref[block, columns] = (gated * gain).astype(BF16)
    return squares


def part_kernel(head_size, shares, parity_ref, *refs):
    *ins, out_ref, sq_ref, scaled_ref, tile_ref = refs
    squares = gated_part(head_size, parity_ref[0] == 1, ins[:shares], *ins[shares:], scaled_ref, tile_ref)
    for i, square in enumerate(squares):
        sq_ref[i * BLOCK : (i + 1) * BLOCK, :] = jnp.broadcast_to(square, (BLOCK, sq_ref.shape[1]))
    for low in range(0, out_ref.shape[1], TILE):
        out_ref[:, low : low + TILE] = dot(scaled_ref[...], ins[-1][:, low : low + TILE])


def product(back, scaled_ref, weights_ref, part_ref, scale_ref, tile_ref, half_ref, out_ref, first):
    rows, half = out_ref.shape
    for low in range(0, half, TILE):
        columns = slice(first + low, first + low + TILE)
        tile_ref[...] = dot(scaled_ref[...], weights_ref[:, columns])
        for r in range(0, rows, BLOCK):
            block = slice(r, r + BLOCK)
            value = (tile_ref[block, :] + part_ref[block, columns]) * scale_ref[block, :1]
            half_ref[block, low : low + TILE] = value.astype(BF16)

    @pl.when(back == 1)
    def _():
        turn = flip_matrix(TILE)
        for r in range(0, rows, TILE):
            for low in range(0, half, TILE):
                tile = dot(turn, half_ref[r : r + TILE, low : low + TILE]).astype(BF16)
                tile = dot(tile, turn).astype(BF16)
                to_row, to = rows - TILE - r, half - TILE - low
                out_ref[to_row : to_row + TILE, to : to + TILE] = tile

    @pl.when(back != 1)
    def _():
        out_ref[...] = half_ref[...]


def finish_kernel(head_size, shares, full_width, back_ref, parity_ref, *refs):
    *ins, part_ref, psq_ref, send_ref, scaled_ref, scale_ref, tile_ref, half_ref = refs
    squares = gated_part(head_size, parity_ref[0] == 1, ins[:shares], *ins[shares:], scaled_ref, tile_ref)
    for i, square in enumerate(squares):
        block = slice(i * BLOCK, (i + 1) * BLOCK)
        scale = lax.rsqrt((square + psq_ref[block, :1]) / full_width + EPS)
        scale_ref[block, :] = jnp.broadcast_to(scale, (BLOCK, scale_ref.shape[1]))
    product(back_ref[0], scaled_ref, ins[-1], part_ref, scale_ref, tile_ref.at[0], half_ref, send_ref, send_ref.shape[1])


def own_kernel(back_ref, scaled_ref, weights_ref, part_ref, scale_ref, own_ref, tile_ref, half_ref):
    product(back_ref[0], scaled_ref, weights_ref, part_ref, scale_ref, tile_ref, half_ref, own_ref, 0)


def own_call(back, scaled, w_output, part, scale, after):
    rows, width = part.shape
    half = width // 2
    return call(
        own_kernel,
        "own_half",
        vmem=8,
        cost=micros(0.7),
        scalars=(back,),
        in_specs=[VMEM] * 4,
        out_specs=VMEM,
        out_shape=jax.ShapeDtypeStruct((rows, half), BF16),
        scratch=[pltpu.VMEM((rows, TILE), F32), pltpu.VMEM((rows, half), BF16)],
        after=after,
    )(back, scaled, w_output, part, scale)


def finish_call(back, parity, ys, bc, cum, keep, other, gate, small, w_output, full_width=None, partial=None, after=()):
    rows = ys[0].shape[0]
    inner = ys[0].shape[1] * len(ys)
    width = w_output.shape[1]
    half = width // 2
    heads = cum.shape[1]
    arrays = [*ys, bc, cum, keep, other, gate, small, w_output]
    tiles = pltpu.VMEM((2, rows, TILE), F32)
    if partial is None:
        scratch = [pltpu.VMEM((rows, inner), BF16), tiles]
        scalars = (parity,)
        kernel = functools.partial(part_kernel, inner // heads, len(ys))
        out_shape = [jax.ShapeDtypeStruct((rows, width), F32), jax.ShapeDtypeStruct((rows, 128), F32)]
    else:
        scalars = (back, parity)
        scratch = [tiles, pltpu.VMEM((rows, half), BF16)]
        kernel = functools.partial(finish_kernel, inner // heads, len(ys), full_width)
        arrays += list(partial)
        out_shape = [
            jax.ShapeDtypeStruct((rows, half), BF16),
            jax.ShapeDtypeStruct((rows, inner), BF16),
            jax.ShapeDtypeStruct((rows, 128), F32),
        ]
    return call(
        kernel,
        "part" if partial is None else "finish",
        vmem=16,
        cost=micros(3.5),
        scalars=scalars,
        in_specs=[VMEM] * len(arrays),
        out_specs=[VMEM] * len(out_shape),
        out_shape=out_shape,
        scratch=scratch,
        after=after,
    )(*scalars, *arrays)


def total_kernel(mine_ref, theirs_ref, out_hbm, out_ref, sems):
    copies = []
    for i, r in enumerate(range(0, mine_ref.shape[0], CHUNK)):
        for q in range(r, r + CHUNK, BLOCK):
            block = slice(q, q + BLOCK)
            out_ref[block, :] = (mine_ref[block, :].astype(F32) + theirs_ref[block, :].astype(F32)).astype(BF16)
        part = pl.ds(r, CHUNK)
        copies.append(pltpu.make_async_copy(out_ref.at[part, :], out_hbm.at[part, :], sems.at[i]))
        copies[-1].start()
    for copy in copies:
        copy.wait()


def total_call(mine, theirs):
    rows, half = mine.shape
    return call(
        total_kernel,
        "total",
        vmem=4,
        cost=micros(0.8),
        in_specs=[VMEM] * 2,
        out_specs=HBM,
        out_shape=jax.ShapeDtypeStruct((rows, half), BF16),
        scratch=[pltpu.VMEM((rows, half), BF16), pltpu.SemaphoreType.DMA((rows // CHUNK,))],
    )(mine, theirs)


def body(
    tokens,
    hidden,
    embedding,
    w_gate,
    w_inner,
    w_state,
    w_step,
    conv_inner,
    conv_state,
    step_bias,
    decay_rate,
    norm_gain,
    w_output,
):
    swap = [(0, 1), (1, 0)]

    def theirs(a):
        return lax.ppermute(a, "ch", swap)

    core = lax.axis_index("ch").astype(jnp.int32)
    index = lax.axis_index("seq").astype(jnp.int32)
    last = lax.axis_size("seq") - 1
    back = core.reshape(1)
    parity = (index & 1).reshape(1)
    place = (index + core * (last - 2 * index)).reshape(1)
    place, parity, w_inner_3, w_gate_3, w_output_3 = lax.optimization_barrier(
        (place, parity, w_inner, w_gate, w_output)
    )
    w_inner_2 = theirs(w_inner_3)
    normed, tail, small = prepare_call(
        (back, parity, place), hidden, tokens, embedding, conv_inner, norm_gain, step_bias, decay_rate, w_step.T
    )
    halo = onward(tail, 1)
    small_2 = theirs(small)
    w_gate_2 = theirs(w_gate_3)
    w_output_2 = theirs(w_output_3)
    gate_1 = gate_call("own", normed, w_gate, after=[w_inner])
    bc, bt = maps_call(place, normed, halo, w_state, conv_state, after=[gate_1])
    x_1, cum_1, times_1, send_1, mine_1 = local_call("own", place, parity, normed, halo, bt, w_inner, small)
    chain_1 = Chain("own", place, send_1, mine_1)
    x_2, cum_2, times_2, send_2, mine_2 = local_call(
        "other", place, parity, normed, halo, bt, w_inner_2, small_2, after=[mine_1]
    )
    chain_2 = Chain("other", place, send_2, mine_2)
    done = mark_call(normed, after=[x_2])
    done = chain_1.pair(after=[done])
    y_1 = inside_call("own", x_1, bc, bt, cum_1, times_1, after=[done])
    done = chain_2.pair(after=[y_1])
    done = chain_1.middle(after=[done])
    gate_2 = gate_call("other", normed, w_gate_2, after=[done])
    done = chain_2.middle(after=[gate_2])
    entry_1 = chain_1.entry(after=[done])
    scan_2 = ("other", x_2, bc, bt, cum_2, times_2)
    y_2 = [inside_call(*scan_2, after=[entry_1[0]], part=0, parts=2)]
    entry_2 = chain_2.entry(after=y_2)
    y_2.append(inside_call(*scan_2, after=[entry_2[0]], part=1, parts=2))
    partial = finish_call(
        back, parity, [y_1], bc, cum_1, *entry_1, gate_1, small, w_output, after=y_2
    )
    full_width = float(w_inner.shape[1] * lax.axis_size("ch"))
    send, scaled, scale = finish_call(
        back, parity, y_2, bc, cum_2, *entry_2, gate_2, small_2, w_output_2, full_width, partial
    )
    arriving = theirs(send)
    mine = own_call(back, scaled, w_output_2, partial[0], scale, after=[send])
    return total_call(mine, arriving)


def solution(mesh):
    return jax.shard_map(
        body,
        mesh=mesh,
        in_specs=(
            P(("win", "seq")),
            P(("win", "seq"), None),
            P(),
            P(None, "ch"),
            P(None, "ch"),
            P(),
            P(None, "ch"),
            P(None, "ch"),
            P(),
            P("ch"),
            P("ch"),
            P("ch"),
            P("ch", None),
        ),
        out_specs=P(("win", "seq"), "ch"),
        check_vma=False,
    )
```

```python
import functools

import jax
import jax.numpy as jnp
from jax import lax
from jax.experimental import pallas as pl
from jax.experimental.pallas import tpu as pltpu
from jax.sharding import PartitionSpec as P

F32 = jnp.float32
BF16 = jnp.bfloat16
EPS = 1e-05
HALO = 16
EXTRA = 16
CHUNK = 128
TILE = 256
BLOCK = 64
MB = 1024 * 1024
VMEM = pl.BlockSpec(memory_space=pltpu.VMEM)
HBM = pl.BlockSpec(memory_space=pltpu.HBM)


def call(
    kernel, name, *, vmem, cost, scalars=(), grid=(), in_specs, out_specs, out_shape, scratch=(), after=()
):
    flops, moved, special = cost
    first = len(scalars) + len(in_specs)

    def body(*refs):
        kernel(*refs[:first], *refs[first + len(after) :])

    run = pl.pallas_call(
        body,
        grid_spec=pltpu.PrefetchScalarGridSpec(
            num_scalar_prefetch=len(scalars),
            grid=grid,
            in_specs=list(in_specs) + [pl.BlockSpec(memory_space=pl.ANY)] * len(after),
            out_specs=out_specs,
            scratch_shapes=scratch,
        ),
        out_shape=out_shape,
        compiler_params=pltpu.CompilerParams(
            vmem_limit_bytes=vmem * MB, dimension_semantics=("arbitrary",) * len(grid)
        ),
        cost_estimate=pl.CostEstimate(flops=flops, bytes_accessed=moved, transcendentals=special),
        name=name,
    )
    return lambda *arrays: run(*arrays, *after)


def micros(us):
    return (int(us * 1.1e9), int(us * 1e6), 0)


def dot(a, b):
    return jnp.dot(a, b, preferred_element_type=F32)


def dot_nt(a, b):
    return lax.dot_general(a, b, (((1,), (1,)), ((), ())), preferred_element_type=F32)


def dot_tn(a, b):
    return lax.dot_general(a, b, (((0,), (0,)), ((), ())), preferred_element_type=F32)


def flip_matrix(size):
    rows = lax.broadcasted_iota(jnp.int32, (size, size), 0)
    columns = lax.broadcasted_iota(jnp.int32, (size, size), 1)
    return jnp.where(rows + columns == size - 1, 1.0, 0.0).astype(BF16)


def flip_both(value):
    rows, width = value.shape
    turned = dot(flip_matrix(rows), value).astype(BF16)
    anti = flip_matrix(TILE)
    count = width // TILE
    blocks = [
        dot(turned[:, (count - 1 - k) * TILE : (count - k) * TILE], anti).astype(BF16)
        for k in range(count)
    ]
    return jnp.concatenate(blocks, axis=1)


def silu(v):
    half = 0.5 * v
    return half + half * jnp.tanh(half)


def two_parts(value):
    high = value.astype(BF16)
    low = (value - high.astype(F32)).astype(BF16)
    return jnp.concatenate([high, low], axis=1)


def two_rows(value):
    high = value.astype(BF16).astype(F32)
    return jnp.concatenate([high, value - high], axis=0)


def head_matrix(heads, width, head_size, first_head):
    source = lax.broadcasted_iota(jnp.int32, (2 * heads, width), 0)
    source = jnp.where(source >= heads, source - heads, source)
    target = lax.broadcasted_iota(jnp.int32, (2 * heads, width), 1) // head_size + first_head
    return jnp.where(source == target, 1.0, 0.0).astype(BF16)


def prepare_kernel(
    back_ref,
    parity_ref,
    place_ref,
    hidden_hbm,
    tokens_hbm,
    emb_hbm,
    conv_hbm,
    gain_hbm,
    bias_hbm,
    rate_hbm,
    step_hbm,
    out_ref,
    tail_ref,
    small_ref,
    hidden_ref,
    tokens_ref,
    emb_ref,
    conv_ref,
    gain_ref,
    bias_ref,
    rate_ref,
    step_ref,
    base_ref,
    normed_ref,
    turned_ref,
    sems,
):
    rows = hidden_ref.shape[0]
    kinds = emb_ref.shape[0]
    taps, inner = conv_ref.shape
    heads = bias_ref.shape[1]
    count = rows // CHUNK
    back = back_ref[0] == 1
    whole = [
        (tokens_hbm, tokens_ref),
        (emb_hbm, emb_ref),
        (conv_hbm, conv_ref),
        (gain_hbm, gain_ref),
        (bias_hbm, bias_ref),
        (rate_hbm, rate_ref),
        (step_hbm, step_ref),
    ]
    small_copies = [pltpu.make_async_copy(src, dst, sems.at[count + i]) for i, (src, dst) in enumerate(whole)]
    parts = [pl.ds(r * CHUNK, CHUNK) for r in range(count)]
    copies = [
        pltpu.make_async_copy(hidden_hbm.at[part, :], hidden_ref.at[part, :], sems.at[r])
        for r, part in enumerate(parts)
    ]
    for copy in small_copies[:2] + copies + small_copies[2:]:
        copy.start()
    for copy in small_copies[:2]:
        copy.wait()
    kind = lax.broadcasted_iota(jnp.int32, (kinds, rows), 0)
    onehot = jnp.where(kind == tokens_ref[...], 1.0, 0.0).astype(BF16)
    for r in range(count):
        copies[r].wait()
        low, high = r * CHUNK, (r + 1) * CHUNK
        base_ref[...] = dot_tn(onehot[:, low:high], emb_ref[...])
        for q in range(low, high, HALO):
            block = slice(q, q + HALO)
            merged = hidden_ref[block, :].astype(F32) + base_ref[q - low : q - low + HALO, :]
            merged = merged.astype(BF16).astype(F32)
            mean = jnp.mean(merged * merged, axis=-1, keepdims=True)
            normed_ref[block, :] = (merged * lax.rsqrt(mean + EPS)).astype(BF16)

    @pl.when(back)
    def _():
        turn = flip_matrix(TILE)
        for c in range(0, hidden_ref.shape[1], TILE):
            to = hidden_ref.shape[1] - TILE - c
            for r in range(0, rows, TILE):
                turned = dot(turn, normed_ref[r : r + TILE, c : c + TILE]).astype(BF16)
                turned_ref[r : r + TILE, c : c + TILE] = turned
            for r in range(0, rows, TILE):
                out_ref[rows - TILE - r : rows - r, to : to + TILE] = dot(
                    turned_ref[r : r + TILE, c : c + TILE], turn
                ).astype(BF16)

    @pl.when(jnp.logical_not(back))
    def _():
        out_ref[...] = normed_ref[...]

    tail_ref[...] = out_ref[rows - HALO :, :]
    for copy in small_copies[2:]:
        copy.wait()
    small_ref[:taps, :] = conv_ref[...]
    small_ref[taps : taps + 1, :] = gain_ref[...]
    small_ref[taps + 1 : SMALL_ROWS, :] = jnp.zeros((SMALL_ROWS - taps - 1, inner), F32)
    small_ref[taps + 1 : taps + 2, :heads] = bias_ref[...]
    small_ref[taps + 2 : taps + 3, :heads] = rate_ref[...]
    small_ref[SMALL_ROWS:, :] = step_ref[...].astype(F32)


def prepare_call(scalars, hidden, tokens, embedding, conv, gain, bias, rate, step):
    rows, width = hidden.shape
    inner = conv.shape[1]
    arrays = [hidden, tokens.reshape(1, -1), embedding, conv]
    arrays += [a.reshape(1, -1) for a in (gain, bias, rate)] + [step]
    return call(
        prepare_kernel,
        "prepare",
        vmem=12,
        cost=micros(2.7),
        scalars=scalars,
        in_specs=[HBM] * len(arrays),
        out_specs=[VMEM] * 3,
        out_shape=[
            jax.ShapeDtypeStruct((rows, width), BF16),
            jax.ShapeDtypeStruct((HALO, width), BF16),
            jax.ShapeDtypeStruct((SMALL_ROWS + step.shape[0], inner), F32),
        ],
        scratch=[pltpu.VMEM(a.shape, a.dtype) for a in arrays]
        + [pltpu.VMEM((CHUNK, width), F32)]
        + [pltpu.VMEM((rows, width), BF16)] * 2
        + [pltpu.SemaphoreType.DMA((rows // CHUNK + len(arrays) - 1,))],
    )(*scalars, *(pltpu.with_memory_space_constraint(a, pltpu.HBM) for a in arrays))


def gate_kernel(rows_ref, wg_ref, out_ref, gate_ref):
    rows, inner = out_ref.shape
    for low in range(0, inner, TILE):
        columns = slice(low, low + TILE)
        gate_ref[...] = dot(rows_ref[...], wg_ref[:, columns])
        for r in range(0, rows, BLOCK):
            gate = gate_ref[r : r + BLOCK, :].astype(BF16).astype(F32)
            out_ref[r : r + BLOCK, columns] = silu(gate).astype(BF16)


def gate_call(tag, normed, w_gate, after=()):
    rows = normed.shape[0]
    inner = w_gate.shape[1]
    return call(
        gate_kernel,
        "gate_" + tag,
        vmem=8,
        cost=micros(2.4),
        in_specs=[VMEM] * 2,
        out_specs=VMEM,
        out_shape=jax.ShapeDtypeStruct((rows, inner), BF16),
        scratch=[pltpu.VMEM((rows, TILE), F32)],
        after=after,
    )(normed, w_gate)


def conv_silu(rows_ref, weights, row):
    taps = weights.shape[0]
    ahead = 8
    window = rows_ref[HALO - ahead + row : HALO + row + BLOCK, :]
    total = weights[taps - 1 :, :] * window[ahead:, :]
    for back in range(1, taps):
        total += weights[taps - 1 - back : taps - back, :] * pltpu.roll(window, back, 0)[ahead:, :]
    return silu(total).astype(BF16)


def maps_kernel(place_ref, normed_ref, halo_ref, ws_ref, cs_ref, bc_ref, bt_ref, rows_ref):
    rows = normed_ref.shape[0]
    states = bc_ref.shape[1] // 2
    before = dot(halo_ref[...], ws_ref[...]).astype(BF16).astype(F32)
    rows_ref[:HALO, :] = jnp.where(place_ref[0] >= 1, before, 0.0)
    rows_ref[HALO:, :] = dot(normed_ref[...], ws_ref[...]).astype(BF16).astype(F32)
    weights = cs_ref[...]
    for r in range(0, rows, BLOCK):
        bc_ref[r : r + BLOCK, :] = conv_silu(rows_ref, weights, r)
    bt_ref[...] = bc_ref[:, :states].astype(F32).T.astype(BF16)


def maps_call(place, normed, halo, w_state, conv_state, after=()):
    rows = normed.shape[0]
    both = w_state.shape[1]
    return call(
        maps_kernel,
        "maps",
        vmem=8,
        cost=micros(0.3),
        scalars=(place,),
        in_specs=[VMEM] * 4,
        out_specs=[VMEM] * 2,
        out_shape=[
            jax.ShapeDtypeStruct((rows, both), BF16),
            jax.ShapeDtypeStruct((both // 2, rows), BF16),
        ],
        scratch=[pltpu.VMEM((rows + HALO, both), F32)],
        after=after,
    )(place, normed, halo, w_state, conv_state)


def local_kernel(
    head_size,
    place_ref,
    parity_ref,
    normed_ref,
    halo_ref,
    bt_ref,
    wi_ref,
    small_ref,
    x_ref,
    cum_ref,
    times_ref,
    send_ref,
    mine_ref,
    rows_ref,
    spread_ref,
    scaled_ref,
    left_ref,
    whole_ref,
    payload_ref,
):
    rows = normed_ref.shape[0]
    states = bt_ref.shape[0]
    heads = cum_ref.shape[1]
    taps = SMALL_TAPS

    def project_rows(t):
        weights = wi_ref[:, t * TILE : (t + 1) * TILE]
        before = dot(halo_ref[...], weights).astype(BF16).astype(F32)
        rows_ref[t % 2, :HALO, :] = jnp.where(place_ref[0] >= 1, before, 0.0)
        rows_ref[t % 2, HALO:, :] = dot(normed_ref[...], weights).astype(BF16).astype(F32)

    raw = dot_nt(normed_ref[...], small_ref[SMALL_ROWS:, :].astype(BF16))
    columns = small_ref[:SMALL_ROWS, :CHUNK].T
    raw = raw.T + columns[:heads, taps + 1 : taps + 2]
    step = jnp.maximum(raw, 0.0) + jnp.log1p(jnp.exp(-jnp.abs(raw)))
    logdecay = -step * columns[:heads, taps + 2 : taps + 3]
    high = logdecay.astype(BF16)
    rest = logdecay - high.astype(F32)
    mid = rest.astype(BF16)
    low = (rest - mid.astype(F32)).astype(BF16)
    starts = range(0, rows, CHUNK)
    pieces = [part[:, r : r + CHUNK] for r in starts for part in (high, mid, low)]
    project_rows(0)
    frm = lax.broadcasted_iota(jnp.int32, (CHUNK, CHUNK), 0)
    to = lax.broadcasted_iota(jnp.int32, (CHUNK, CHUNK), 1)
    sums = dot(jnp.concatenate(pieces, axis=0), jnp.where(to >= frm, 1.0, 0.0).astype(BF16))
    run = jnp.zeros((heads, 1), F32)
    cums = []
    for i in range(len(starts)):
        at = 3 * i * heads
        cums.append(sums[at : at + heads] + sums[at + heads : at + 2 * heads] + sums[at + 2 * heads : at + 3 * heads] + run)
        run = cums[-1][:, CHUNK - 1 :]
    cum = jnp.concatenate(cums, axis=1)
    times_ref[:heads, :] = cum
    times_ref[heads:, :] = step
    cum_ref[...] = cum.T
    left_ref[...] = two_rows(step * jnp.exp(run - cum)).T.astype(BF16)
    whole_ref[...] = two_parts(jnp.exp(cum_ref[rows - 1 :, :]))

    inner = x_ref.shape[1]
    half = inner // 2
    tiles = range(inner // TILE)
    onehots = [head_matrix(heads, TILE, head_size, t * (TILE // head_size)) for t in tiles]
    spans = [slice(t * TILE, (t + 1) * TILE) for t in tiles]

    def project(t):
        project_rows(t)
        spread_ref[t % 2] = dot(left_ref[...], onehots[t])

    def combine(t):
        taps_here = small_ref[:taps, spans[t]]
        for r in range(0, rows, BLOCK):
            block = slice(r, r + BLOCK)
            x = conv_silu(rows_ref.at[t % 2], taps_here, r)
            x_ref[block, spans[t]] = x
            scaled_ref[t % 2, block, :] = (x.astype(F32) * spread_ref[t % 2, block, :]).astype(BF16)
        state = dot(bt_ref[...], scaled_ref[t % 2])
        here = slice(t * TILE % half, t * TILE % half + TILE)
        is_mine = jnp.where(parity_ref[0] == t * TILE // half, 1, 0)
        write_payload(payload_ref.at[is_mine], here, state, dot(whole_ref[...], onehots[t]))

    spread_ref[0] = dot(left_ref[...], onehots[0])
    for t in tiles:
        if t + 1 < len(tiles):
            project(t + 1)
        combine(t)
    send_ref[...] = payload_ref[0]
    mine_ref[...] = payload_ref[1]


SMALL_TAPS = 4
SMALL_ROWS = 8


def local_call(tag, place, parity, normed, halo, bt, w_inner, small, after=()):
    rows = normed.shape[0]
    inner = w_inner.shape[1]
    heads = small.shape[0] - SMALL_ROWS
    states = bt.shape[0]
    return call(
        functools.partial(local_kernel, inner // heads),
        "local_" + tag,
        vmem=12,
        cost=micros(5.0),
        scalars=(place, parity),
        in_specs=[VMEM] * 5,
        out_specs=[VMEM] * 5,
        out_shape=[
            jax.ShapeDtypeStruct((rows, inner), BF16),
            jax.ShapeDtypeStruct((rows, heads), F32),
            jax.ShapeDtypeStruct((2 * heads, rows), F32),
            jax.ShapeDtypeStruct((states + EXTRA, inner // 2), BF16),
            jax.ShapeDtypeStruct((states + EXTRA, inner // 2), BF16),
        ],
        scratch=[
            pltpu.VMEM((2, rows + HALO, TILE), F32),
            pltpu.VMEM((2, rows, TILE), F32),
            pltpu.VMEM((2, rows, TILE), BF16),
            pltpu.VMEM((rows, 2 * heads), BF16),
            pltpu.VMEM((1, 2 * heads), BF16),
            pltpu.VMEM((2, states + EXTRA, inner // 2), BF16),
        ],
        after=after,
    )(place, parity, normed, halo, bt, w_inner, small)


def inside_kernel(head_size, head, x_ref, bc_ref, bt_ref, cum_ref, times_ref, y_ref, state_ref):
    rows, width = y_ref.shape
    states = bc_ref.shape[1] // 2
    heads = cum_ref.shape[1]
    length = CHUNK
    last = length - 1
    pair = 2 * head_size
    lane = lax.broadcasted_iota(jnp.int32, (length, pair), 1)
    to = lax.broadcasted_iota(jnp.int32, (length, length), 0)
    frm = lax.broadcasted_iota(jnp.int32, (length, length), 1)

    def chunk(c, before):
        at = slice(c * length, (c + 1) * length)
        bmat = bt_ref[:, at]
        cmat = bc_ref[at, states:]
        scores = jnp.where(to >= frm, dot(cmat, bmat), 0.0)
        cum = cum_ref[at, :]
        cumt = times_ref[:heads, at]
        step = times_ref[heads:, at]
        end = cumt[:, last:]
        entered = c > 0
        leaves = (c + 1) * length < rows
        if entered:
            since = two_rows(jnp.exp(cumt - before)).T.astype(BF16)
        if leaves:
            left = two_rows(step * jnp.exp(end - cumt)).T.astype(BF16)
        for offset in range(0, width, TILE):
            first = head + offset // head_size
            columns = slice(first * head_size, first * head_size + TILE)
            here = slice(offset, offset + TILE)
            onehot = head_matrix(heads, TILE, head_size, first)
            if entered:
                since_here = dot(since, onehot)
                state = state_ref[:, here]
                carried = dot(cmat, state.astype(BF16)) * since_here
            if leaves:
                scaled = (x_ref[at, columns].astype(F32) * dot(left, onehot)).astype(BF16)
                added = dot(bmat, scaled)
                state_ref[:, here] = state * since_here[last:, :] + added if entered else added
            for start in range(0, TILE, pair):
                low = first * head_size + start
                weights = []
                for h in (low // head_size, low // head_size + 1):
                    apart = jnp.minimum(cum[:, h : h + 1] - cumt[h : h + 1, :], 0.0)
                    weights.append((jnp.exp(apart) * (scores * step[h : h + 1, :])).astype(BF16))
                mine = x_ref[at, low : low + pair]
                none = jnp.zeros_like(mine)
                stacked = jnp.concatenate(
                    [jnp.where(lane < head_size, mine, none), jnp.where(lane < head_size, none, mine)], axis=0
                )
                inside = dot(jnp.concatenate(weights, axis=1), stacked)
                if entered:
                    inside += carried[:, start : start + pair]
                y_ref[at, offset + start : offset + start + pair] = inside.astype(BF16)
        return end

    before = jnp.zeros((heads, 1), F32)
    for c in range(rows // length):
        before = chunk(c, before)


def inside_call(tag, x, bc, bt, cum, times, after=(), part=0, parts=1):
    rows, inner = x.shape
    heads = cum.shape[1]
    both = bc.shape[1]
    width = inner // parts
    return call(
        functools.partial(inside_kernel, inner // heads, part * heads // parts),
        "inside_" + tag,
        vmem=8,
        cost=micros(3.2 / parts),
        in_specs=[VMEM] * 5,
        out_specs=VMEM,
        out_shape=jax.ShapeDtypeStruct((rows, width), BF16),
        scratch=[pltpu.VMEM((both // 2, width), F32)],
        after=after,
    )(x, bc, bt, cum, times)


def mark_kernel(rows_ref, out_ref):
    out_ref[...] = rows_ref[: out_ref.shape[0], : out_ref.shape[1]]


def mark_call(value, after):
    return call(
        mark_kernel,
        "mark",
        vmem=4,
        cost=micros(2.4),
        in_specs=[VMEM],
        out_specs=VMEM,
        out_shape=jax.ShapeDtypeStruct((HALO, 128), value.dtype),
        after=after,
    )(value)


def parts_of(ref, known=None):
    states = ref.shape[0] - EXTRA
    state = ref[:states, :].astype(F32)
    extra = ref[states:, :].astype(F32)
    decay = extra[:1] + extra[1:2]
    if known is None:
        return state, decay
    return jnp.where(known, state, 0.0), jnp.where(known, decay, 0.0)


def write_payload(out_ref, columns, state, decay):
    states = state.shape[0]
    out_ref[:states, columns] = state.astype(BF16)
    decay = jnp.broadcast_to(decay, (EXTRA, decay.shape[1]))
    high = decay.astype(BF16).astype(F32)
    place = lax.broadcasted_iota(jnp.int32, decay.shape, 0)
    out_ref[states:, columns] = jnp.where(place == 0, high, decay - high).astype(BF16)


ALL = slice(None)


def pair_kernel(place_ref, mine_ref, other_ref, out_ref):
    mine, mine_a = parts_of(mine_ref)
    other, other_a = parts_of(other_ref)
    is_first = lax.rem(place_ref[0], 2) == 0
    early = jnp.where(is_first, mine, other)
    late = jnp.where(is_first, other, mine)
    late_a = jnp.where(is_first, other_a, mine_a)
    write_payload(out_ref, ALL, late_a * early + late, mine_a * other_a)


def chain_kernel(reach, place_ref, pair_ref, before_ref, out_ref):
    pair, pair_a = parts_of(pair_ref)
    before, before_a = parts_of(before_ref, place_ref[0] >= reach)
    write_payload(out_ref, ALL, pair_a * before + pair, pair_a * before_a)


def longer_kernel(reach, farther_reach, place_ref, before_ref, farther_ref, out_ref):
    before, before_a = parts_of(before_ref, place_ref[0] >= reach)
    farther, farther_a = parts_of(farther_ref, place_ref[0] >= farther_reach)
    write_payload(out_ref, ALL, before + before_a * farther, before_a * farther_a)


def entry_kernel(reach, farther_reach, place_ref, mine_ref, other_ref, before_ref, farther_ref, keep_ref, send_ref):
    mine, mine_a = parts_of(mine_ref)
    other, other_a = parts_of(other_ref)
    before, before_a = parts_of(before_ref, place_ref[0] >= reach)
    farther, _ = parts_of(farther_ref, place_ref[0] >= farther_reach)
    is_first = lax.rem(place_ref[0], 2) == 0
    entry_first = before + before_a * farther
    early = jnp.where(is_first, mine, other)
    early_a = jnp.where(is_first, mine_a, other_a)
    entry_second = early_a * entry_first + early
    keep_ref[...] = jnp.where(is_first, entry_first, entry_second).astype(BF16)
    send_ref[...] = jnp.where(is_first, entry_second, entry_first).astype(BF16)


def small_call(kernel, name, place, arrays, shapes, after=()):
    return call(
        kernel,
        name,
        vmem=4,
        cost=micros(0.5),
        scalars=(place,),
        in_specs=[VMEM] * len(arrays),
        out_specs=[VMEM] * len(shapes),
        out_shape=[jax.ShapeDtypeStruct(s, BF16) for s in shapes],
        after=after,
    )(place, *arrays)


def onward(value, by):
    count = lax.axis_size("seq")
    pairs = []
    for i in range(count):
        up = (i + by, 0) if i + by < count else (i, 1)
        down = (i - by, 1) if i - by >= 0 else (i, 0)
        pairs += [(2 * i, 2 * up[0] + up[1]), (2 * i + 1, 2 * down[0] + down[1])]
    return lax.ppermute(value, ("seq", "ch"), pairs)


class Chain:
    def __init__(self, tag, place, send, mine):
        self.tag, self.place, self.mine = tag, place, mine
        self.count = lax.axis_size("seq")
        self.swap = [(i, i ^ 1) for i in range(self.count)]
        self.other = lax.ppermute(send, "seq", self.swap)
        self.before = self.farther = None
        self.reach = self.farther_reach = 0
        self.apart = 2

    def pair(self, after):
        (self.pair_state,) = small_call(
            pair_kernel, "pair_" + self.tag, self.place, [self.mine, self.other], [self.mine.shape], after
        )
        self.running = self.pair_state
        self.hop()
        return self.pair_state

    def hop(self):
        if self.apart < self.count:
            self.arrived = onward(self.running, self.apart)

    def middle(self, after):
        while self.apart * 2 < self.count:
            self.take(after)
            (self.running,) = small_call(
                functools.partial(chain_kernel, self.reach),
                "chain_" + self.tag,
                self.place,
                [self.pair_state, self.before],
                [self.mine.shape],
                after,
            )
            self.apart *= 2
            self.hop()
        return self.running

    def take(self, after=()):
        if self.before is None:
            self.before, self.reach = self.arrived, self.apart
        else:
            (self.before,) = small_call(
                functools.partial(longer_kernel, self.reach, self.apart),
                "longer_" + self.tag,
                self.place,
                [self.before, self.arrived],
                [self.mine.shape],
                after,
            )
            self.reach = 0

    def entry(self, after):
        shape = self.mine.shape
        if self.apart < self.count:
            if self.before is None:
                self.before, self.reach = self.arrived, self.apart
                self.farther, self.farther_reach = self.arrived, self.count
            else:
                self.farther, self.farther_reach = self.arrived, self.apart
        else:
            self.before = self.farther = self.mine
            self.reach = self.farther_reach = self.count
        half = (shape[0] - EXTRA, shape[1])
        keep, out = small_call(
            functools.partial(entry_kernel, self.reach, self.farther_reach),
            "entry_" + self.tag,
            self.place,
            [self.mine, self.other, self.before, self.farther],
            [half, half],
            after,
        )
        return keep, lax.ppermute(out, "seq", self.swap)


def gated_part(
    head_size, swap, y_refs, bc_ref, cum_ref, keep_ref, other_ref, gate_ref, small_ref, wo_ref, scaled_ref, tile_ref
):
    rows, share = y_refs[0].shape
    inner = share * len(y_refs)
    states = bc_ref.shape[1] // 2
    heads = cum_ref.shape[1]
    half = inner // 2
    since = two_parts(jnp.exp(cum_ref[...]))
    squares = [0.0] * (rows // BLOCK)
    for low in range(0, inner, TILE):
        columns = slice(low, low + TILE)
        y_ref = y_refs[low // share]
        of_share = slice(low % share, low % share + TILE)
        here = slice(low % half, low % half + TILE)
        use_other = swap if low < half else jnp.logical_not(swap)
        entry = jnp.where(use_other, other_ref[:, here], keep_ref[:, here])
        tile_ref[0] = dot(bc_ref[:, states:], entry)
        tile_ref[1] = dot(since, head_matrix(heads, TILE, head_size, low // head_size))
        gain = small_ref[SMALL_TAPS : SMALL_TAPS + 1, columns]
        for i, r in enumerate(range(0, rows, BLOCK)):
            block = slice(r, r + BLOCK)
            gated = y_ref[block, of_share].astype(F32) + tile_ref[0, block, :] * tile_ref[1, block, :]
            gated = gated * gate_ref[block, columns].astype(F32)
            squares[i] += jnp.sum(gated * gated, axis=-1, keepdims=True)
            scaled_ref[block, columns] = (gated * gain).astype(BF16)
    return squares


def part_kernel(head_size, shares, parity_ref, *refs):
    *ins, out_ref, sq_ref, scaled_ref, tile_ref = refs
    squares = gated_part(head_size, parity_ref[0] == 1, ins[:shares], *ins[shares:], scaled_ref, tile_ref)
    for i, square in enumerate(squares):
        sq_ref[i * BLOCK : (i + 1) * BLOCK, :] = jnp.broadcast_to(square, (BLOCK, sq_ref.shape[1]))
    for low in range(0, out_ref.shape[1], TILE):
        out_ref[:, low : low + TILE] = dot(scaled_ref[...], ins[-1][:, low : low + TILE])


def product(back, scaled_ref, weights_ref, part_ref, scale_ref, tile_ref, half_ref, out_ref, first):
    rows, half = out_ref.shape

    def compute(low, target_ref):
        columns = slice(first + low, first + low + TILE)
        tile_ref[...] = dot(scaled_ref[...], weights_ref[:, columns])
        for r in range(0, rows, BLOCK):
            block = slice(r, r + BLOCK)
            value = (tile_ref[block, :] + part_ref[block, columns]) * scale_ref[block, :1]
            target_ref[block, low : low + TILE] = value.astype(BF16)

    @pl.when(back == 1)
    def _():
        turn = flip_matrix(TILE)
        for low in range(0, half, TILE):
            compute(low, half_ref)
            to = half - TILE - low
            for r in range(0, rows, TILE):
                tile = dot(turn, half_ref[r : r + TILE, low : low + TILE]).astype(BF16)
                out_ref[rows - TILE - r : rows - r, to : to + TILE] = dot(tile, turn).astype(BF16)

    @pl.when(back != 1)
    def _():
        for low in range(0, half, TILE):
            compute(low, out_ref)


def finish_kernel(head_size, shares, full_width, back_ref, parity_ref, *refs):
    *ins, part_ref, psq_ref, send_ref, scaled_ref, scale_ref, tile_ref, half_ref = refs
    squares = gated_part(head_size, parity_ref[0] == 1, ins[:shares], *ins[shares:], scaled_ref, tile_ref)
    for i, square in enumerate(squares):
        block = slice(i * BLOCK, (i + 1) * BLOCK)
        scale = lax.rsqrt((square + psq_ref[block, :1]) / full_width + EPS)
        scale_ref[block, :] = jnp.broadcast_to(scale, (BLOCK, scale_ref.shape[1]))
    product(back_ref[0], scaled_ref, ins[-1], part_ref, scale_ref, tile_ref.at[0], half_ref, send_ref, send_ref.shape[1])


def own_kernel(back_ref, scaled_ref, weights_ref, part_ref, scale_ref, own_ref, tile_ref, half_ref):
    product(back_ref[0], scaled_ref, weights_ref, part_ref, scale_ref, tile_ref, half_ref, own_ref, 0)


def own_call(back, scaled, w_output, part, scale, after):
    rows, width = part.shape
    half = width // 2
    return call(
        own_kernel,
        "own_half",
        vmem=8,
        cost=micros(0.7),
        scalars=(back,),
        in_specs=[VMEM] * 4,
        out_specs=VMEM,
        out_shape=jax.ShapeDtypeStruct((rows, half), BF16),
        scratch=[pltpu.VMEM((rows, TILE), F32), pltpu.VMEM((rows, half), BF16)],
        after=after,
    )(back, scaled, w_output, part, scale)


def finish_call(back, parity, ys, bc, cum, keep, other, gate, small, w_output, full_width=None, partial=None, after=()):
    rows = ys[0].shape[0]
    inner = ys[0].shape[1] * len(ys)
    width = w_output.shape[1]
    half = width // 2
    heads = cum.shape[1]
    arrays = [*ys, bc, cum, keep, other, gate, small, w_output]
    tiles = pltpu.VMEM((2, rows, TILE), F32)
    if partial is None:
        scratch = [pltpu.VMEM((rows, inner), BF16), tiles]
        scalars = (parity,)
        kernel = functools.partial(part_kernel, inner // heads, len(ys))
        out_shape = [jax.ShapeDtypeStruct((rows, width), F32), jax.ShapeDtypeStruct((rows, 128), F32)]
    else:
        scalars = (back, parity)
        scratch = [tiles, pltpu.VMEM((rows, half), BF16)]
        kernel = functools.partial(finish_kernel, inner // heads, len(ys), full_width)
        arrays += list(partial)
        out_shape = [
            jax.ShapeDtypeStruct((rows, half), BF16),
            jax.ShapeDtypeStruct((rows, inner), BF16),
            jax.ShapeDtypeStruct((rows, 128), F32),
        ]
    return call(
        kernel,
        "part" if partial is None else "finish",
        vmem=16,
        cost=micros(3.5),
        scalars=scalars,
        in_specs=[VMEM] * len(arrays),
        out_specs=[VMEM] * len(out_shape),
        out_shape=out_shape,
        scratch=scratch,
        after=after,
    )(*scalars, *arrays)


def total_kernel(mine_ref, theirs_ref, out_hbm, out_ref, sems):
    copies = []
    for i, r in enumerate(range(0, mine_ref.shape[0], CHUNK)):
        for q in range(r, r + CHUNK, BLOCK):
            block = slice(q, q + BLOCK)
            out_ref[block, :] = (mine_ref[block, :].astype(F32) + theirs_ref[block, :].astype(F32)).astype(BF16)
        part = pl.ds(r, CHUNK)
        copies.append(pltpu.make_async_copy(out_ref.at[part, :], out_hbm.at[part, :], sems.at[i]))
        copies[-1].start()
    for copy in copies:
        copy.wait()


def total_call(mine, theirs):
    rows, half = mine.shape
    return call(
        total_kernel,
        "total",
        vmem=4,
        cost=micros(0.8),
        in_specs=[VMEM] * 2,
        out_specs=HBM,
        out_shape=jax.ShapeDtypeStruct((rows, half), BF16),
        scratch=[pltpu.VMEM((rows, half), BF16), pltpu.SemaphoreType.DMA((rows // CHUNK,))],
    )(mine, theirs)


def body(
    tokens,
    hidden,
    embedding,
    w_gate,
    w_inner,
    w_state,
    w_step,
    conv_inner,
    conv_state,
    step_bias,
    decay_rate,
    norm_gain,
    w_output,
):
    swap = [(0, 1), (1, 0)]

    def theirs(a):
        return lax.ppermute(a, "ch", swap)

    core = lax.axis_index("ch").astype(jnp.int32)
    index = lax.axis_index("seq").astype(jnp.int32)
    last = lax.axis_size("seq") - 1
    back = core.reshape(1)
    parity = (index & 1).reshape(1)
    place = (index + core * (last - 2 * index)).reshape(1)
    place, parity, w_inner_3, w_gate_3, w_output_3 = lax.optimization_barrier(
        (place, parity, w_inner, w_gate, w_output)
    )
    w_inner_2 = theirs(w_inner_3)
    normed, tail, small = prepare_call(
        (back, parity, place), hidden, tokens, embedding, conv_inner, norm_gain, step_bias, decay_rate, w_step.T
    )
    halo = onward(tail, 1)
    small_2 = theirs(small)
    w_gate_2 = theirs(w_gate_3)
    w_output_2 = theirs(w_output_3)
    gate_1 = gate_call("own", normed, w_gate)
    bc, bt = maps_call(place, normed, halo, w_state, conv_state, after=[gate_1])
    x_1, cum_1, times_1, send_1, mine_1 = local_call("own", place, parity, normed, halo, bt, w_inner, small)
    chain_1 = Chain("own", place, send_1, mine_1)
    x_2, cum_2, times_2, send_2, mine_2 = local_call(
        "other", place, parity, normed, halo, bt, w_inner_2, small_2, after=[mine_1]
    )
    chain_2 = Chain("other", place, send_2, mine_2)
    done = mark_call(normed, after=[x_2])
    done = chain_1.pair(after=[done])
    y_1 = inside_call("own", x_1, bc, bt, cum_1, times_1, after=[done])
    done = chain_2.pair(after=[y_1])
    done = chain_1.middle(after=[done])
    gate_2 = gate_call("other", normed, w_gate_2, after=[done])
    done = chain_2.middle(after=[gate_2])
    entry_1 = chain_1.entry(after=[done])
    scan_2 = ("other", x_2, bc, bt, cum_2, times_2)
    y_2 = [inside_call(*scan_2, after=[entry_1[0]], part=0, parts=2)]
    entry_2 = chain_2.entry(after=y_2)
    y_2.append(inside_call(*scan_2, after=[entry_2[0]], part=1, parts=2))
    partial = finish_call(
        back, parity, [y_1], bc, cum_1, *entry_1, gate_1, small, w_output, after=y_2
    )
    full_width = float(w_inner.shape[1] * lax.axis_size("ch"))
    send, scaled, scale = finish_call(
        back, parity, y_2, bc, cum_2, *entry_2, gate_2, small_2, w_output_2, full_width, partial
    )
    arriving = theirs(send)
    mine = own_call(back, scaled, w_output_2, partial[0], scale, after=[send])
    return total_call(mine, arriving)


def solution(mesh):
    return jax.shard_map(
        body,
        mesh=mesh,
        in_specs=(
            P(("win", "seq")),
            P(("win", "seq"), None),
            P(),
            P(None, "ch"),
            P(None, "ch"),
            P(),
            P(None, "ch"),
            P(None, "ch"),
            P(),
            P("ch"),
            P("ch"),
            P("ch"),
            P("ch", None),
        ),
        out_specs=P(("win", "seq"), "ch"),
        check_vma=False,
    )
```
